32 devices in a mesh: img: 16 (over z, y, x), row: 2 (over core).
Axes of the slice: x: 2, y: 2, z: 4, core: 2. Of those that a mesh axis runs over, the one named last changes fastest.
Arguments:
- features: bfloat16 [32, 32, 32, 512], P('img', 'row'), may hold values from -6 to 6
- validity: int32 [32, 32, 32], P('img', 'row'), may hold values from 0 to 1, as said below
- upstream: bfloat16 [32, 32, 32, 512], P('img', 'row'), may hold values from -6 to 6
- normgain: bfloat16 [512], replicated, may hold values from 0.25 to 1.75
- normshift: bfloat16 [512], replicated, may hold values from -1.75 to 1.75
- inweight: bfloat16 [512, 1024], P(('img', 'row')), may hold values from -0.25 to 0.25
- inbias: bfloat16 [1024], replicated, may hold values from -1.75 to 1.75
- dwkernel: bfloat16 [7, 7, 992], replicated, may hold values from -2.5 to 2.5
- dwbias: bfloat16 [992], replicated, may hold values from -3 to 3
- gatefirst: bfloat16 [32, 64], replicated, may hold values from -1 to 1
- gatesecond: bfloat16 [64, 128], replicated, may hold values from -0.75 to 0.75
- gatethird: bfloat16 [128, 256], replicated, may hold values from -0.5 to 0.5
- gatefourth: bfloat16 [256, 512], replicated, may hold values from -0.375 to 0.375
- gatebias: bfloat16 [960], replicated, may hold values from -1.75 to 1.75
- outweight: bfloat16 [512, 512], P(('img', 'row')), may hold values from -0.25 to 0.25
- outbias: bfloat16 [512], replicated, may hold values from -1.75 to 1.75
- mixscale: bfloat16 [512], replicated, may hold values from 0.5 to 2
- mlpgain: bfloat16 [512], replicated, may hold values from 0.25 to 1.75
- mlpshift: bfloat16 [512], replicated, may hold values from -1.75 to 1.75
- expandweight: bfloat16 [512, 2048], P(('img', 'row')), may hold values from -0.25 to 0.25
- expandbias: bfloat16 [2048], replicated, may hold values from -1.75 to 1.75
- reduceweight: bfloat16 [2048, 512], P(('img', 'row')), may hold values from -0.125 to 0.125
- reducebias: bfloat16 [512], replicated, may hold values from -1.75 to 1.75
- mlpscale: bfloat16 [512], replicated, may hold values from 0.5 to 2
Outputs:
- produced: bfloat16 [32, 32, 32, 512], P('img', 'row')
- features_grad: bfloat16 [32, 32, 32, 512], P('img', 'row')
- normgain_grad: float32 [512], replicated
- normshift_grad: float32 [512], replicated
- inweight_grad: float32 [512, 1024], P(('img', 'row'))
- inbias_grad: float32 [1024], replicated
- dwkernel_grad: float32 [7, 7, 992], replicated
- dwbias_grad: float32 [992], replicated
- gatefirst_grad: float32 [32, 64], replicated
- gatesecond_grad: float32 [64, 128], replicated
- gatethird_grad: float32 [128, 256], replicated
- gatefourth_grad: float32 [256, 512], replicated
- gatebias_grad: float32 [960], replicated
- outweight_grad: float32 [512, 512], P(('img', 'row'))
- outbias_grad: float32 [512], replicated
- mixscale_grad: float32 [512], replicated
- mlpgain_grad: float32 [512], replicated
- mlpshift_grad: float32 [512], replicated
- expandweight_grad: float32 [512, 2048], P(('img', 'row'))
- expandbias_grad: float32 [2048], replicated
- reduceweight_grad: float32 [2048, 512], P(('img', 'row'))
- reducebias_grad: float32 [512], replicated
- mlpscale_grad: float32 [512], replicated
The draws below stay inside these ranges and needn't reach their ends.
Inputs may be any that keep to these rules, and one draw needn't show every extreme that they name: `validity`: in every image the pixels marked 1 form one rectangle at the top-left corner of the grid, more than 16 rows high.
All inputs are finite; a program needn't handle non-finite values.
Results may differ from the reference program's by a relative error of at most 0.015.
Values may be sent and summed in bfloat16 or wider, within the bound.
No kernel may reach another device: no remote copies, remote signals or barrier semaphores. Data moves between devices by JAX's collectives and lax.ppermute only.
A program may use at most 320 MiB of HBM per device.

```python
import math
import jax
import jax.numpy as jnp
from jax import lax

D = 512
FF = 2048
H = 32
W = 32
KS = 7
IMAGES = 32
ROWS = 16
G0 = 32
G1 = 64
G2 = 128
G3 = 256
G4 = 512
ABC = 992


def draw_validity(key, part):
    first_key, second_key = jax.random.split(jax.random.fold_in(key, 17))
    heights = jax.random.randint(first_key, (IMAGES,), H - ROWS + 1, H + 1)
    widths = jax.random.randint(second_key, (IMAGES,), W // 4, W + 1)
    row_ok = jnp.arange(H)[None, :, None] < heights[:, None, None]
    col_ok = jnp.arange(W)[None, None, :] < widths[:, None, None]
    return (row_ok & col_ok).astype(jnp.int32)


def spiked(entries, rng, source, target, shards_of, factor):
    def block_of(position):
        return (jnp.arange(entries.shape[position]) // (entries.shape[position] // shards_of)).reshape((-1,) + (1,) * (entries.ndim - 1 - position))

    one_side = jax.random.permutation(rng, shards_of)[block_of(target)]
    far = (block_of(target) + shards_of // 2) % shards_of
    return jnp.where((block_of(source) == one_side) | (block_of(source) == far), factor * entries, entries)


def steps_of(key, extent, cuts, smallest, top_value):
    level = 1.0
    for axis_at, shards_of in cuts:
        draws = jax.random.uniform(jax.random.fold_in(jax.random.fold_in(key, 6), axis_at), (shards_of,), jnp.float32, smallest / len(cuts), top_value / len(cuts))
        level = level * jnp.repeat(jnp.exp(draws), extent[axis_at] // shards_of).reshape((-1,) + (1,) * (len(extent) - 1 - axis_at))
    return level


def scatter_about(stream_key, dims, scale, limit, pieces=(), dtype=jnp.bfloat16):
    array = jax.random.normal(stream_key, dims, jnp.float32) * scale
    if len(pieces) > 0:
        array = steps_of(stream_key, dims, pieces, -0.22, 0.18) * array
    return jnp.clip(array, min=-limit, max=limit).astype(dtype)


def gaussian_with(rng, extent, scale, limit, cuts, heavy, dtype=jnp.bfloat16):
    values = scale * jax.random.normal(rng, extent, jnp.float32)
    if cuts:
        values = values * steps_of(rng, extent, cuts, -0.22, 0.18)
    return jnp.clip(spiked(values, jax.random.fold_in(rng, 3), *heavy), -limit, limit).astype(dtype)


def setup_inputs(seed: int = 0) -> dict:
    keys = jax.random.split(jax.random.key(seed), 25)
    return {
        "features": gaussian_with(keys[0], (IMAGES, H, W, D), 1.0, 6.0, ((0, 16), (1, 2)), (0, 3, 16, 2.0)),
        "validity": draw_validity(jax.random.fold_in(keys[24], 71), 0),
        "upstream": scatter_about(keys[2], (IMAGES, H, W, D), 1.0, 6.0, ((0, 16), (1, 2))),
        "normgain": jnp.clip(1.0 + 0.15 * jax.random.normal(keys[3], (D,), jnp.float32), 0.25, 1.75).astype(jnp.bfloat16),
        "normshift": scatter_about(keys[4], (D,), 0.3, 1.75),
        "inweight": scatter_about(keys[5], (D, 2 * D), D ** -0.5, 0.25, ((0, 32),)),
        "inbias": scatter_about(keys[6], (2 * D,), 0.3, 1.75),
        "dwkernel": scatter_about(keys[7], (KS, KS, ABC), (KS * KS // 9) ** -0.5, 2.5),
        "dwbias": scatter_about(keys[8], (ABC,), 0.5, 3.0),
        "gatefirst": scatter_about(keys[9], (G0, G1), G0 ** -0.5, 1.0),
        "gatesecond": scatter_about(keys[10], (G1, G2), G1 ** -0.5, 0.75),
        "gatethird": scatter_about(keys[11], (G2, G3), G2 ** -0.5, 0.5),
        "gatefourth": scatter_about(keys[12], (G3, G4), G3 ** -0.5, 0.375),
        "gatebias": scatter_about(keys[13], (ABC - G0,), 0.3, 1.75),
        "outweight": scatter_about(keys[14], (D, D), D ** -0.5, 0.25, ((0, 32),)),
        "outbias": scatter_about(keys[15], (D,), 0.3, 1.75),
        "mixscale": jnp.clip(jnp.exp(jax.random.uniform(keys[16], (D,), jnp.float32, math.log(0.5), math.log(2.0))), 0.5, 2.0).astype(jnp.bfloat16),
        "mlpgain": jnp.clip(1.0 + 0.15 * jax.random.normal(keys[17], (D,), jnp.float32), 0.25, 1.75).astype(jnp.bfloat16),
        "mlpshift": scatter_about(keys[18], (D,), 0.3, 1.75),
        "expandweight": scatter_about(keys[19], (D, FF), D ** -0.5, 0.25, ((0, 32),)),
        "expandbias": scatter_about(keys[20], (FF,), 0.3, 1.75),
        "reduceweight": scatter_about(keys[21], (FF, D), FF ** -0.5, 0.125, ((0, 32),)),
        "reducebias": scatter_about(keys[22], (D,), 0.3, 1.75),
        "mlpscale": jnp.clip(jnp.exp(jax.random.uniform(keys[23], (D,), jnp.float32, math.log(0.5), math.log(2.0))), 0.5, 2.0).astype(jnp.bfloat16),
    }


@jax.custom_vjp
def low(v):
    return lax.optimization_barrier(v.astype(jnp.bfloat16)).astype(jnp.float32)

@jax.custom_vjp
def low_back(v):
    return v

def low_keep(v):
    return (low(v), None)

def low_pass(kept, grad):
    return (grad,)

def back_keep(v):
    return (v, None)

def back_low(kept, grad):
    return (low(grad),)
low.defvjp(low_keep, low_pass)
low_back.defvjp(back_keep, back_low)
norm_eps = 1e-06
conv_scale = 1.0 / 3.0

def layer_norm(values, gain, shift):
    center = lax.optimization_barrier(jnp.mean(values, axis=-1, keepdims=True))
    shifted = values - center
    spread = lax.optimization_barrier(jnp.mean(shifted * shifted, axis=-1, keepdims=True))
    return shifted * lax.rsqrt(spread + norm_eps) * gain + shift

def project(values, weight):
    return jnp.einsum('...c,cd->...d', values, weight, precision=lax.Precision.HIGHEST)

def depthwise(conv_in, kernel):
    half = KS // 2
    padded = jnp.pad(conv_in, ((0, 0), (half, half), (half, half), (0, 0)))
    height = conv_in.shape[1]
    width = conv_in.shape[2]
    total = jnp.zeros(conv_in.shape, jnp.float32)
    for row_tap in range(KS):
        for col_tap in range(KS):
            total = total + padded[:, row_tap:row_tap + height, col_tap:col_tap + width, :] * kernel[row_tap, col_tap]
    return total

def forward(params, features, maskf):
    normgain, normshift, inweight, inbias, dwkernel, dwbias, gatefirst, gatesecond, gatethird, gatefourth, gatebias, outweight, outbias, mixscale, mlpgain, mlpshift, expandweight, expandbias, reduceweight, reducebias, mlpscale = params
    widths = [D // 16, D // 8, D // 4, D // 2, D]
    gates = [gatefirst, gatesecond, gatethird, gatefourth]
    first_in = low(maskf * layer_norm(features, normgain, normshift))
    joined = low_back(project(first_in, inweight) + inbias)
    pointwise = joined[..., :widths[0]]
    conv_in = low(joined[..., widths[0]:] * maskf)
    depth = low_back((depthwise(conv_in, dwkernel) + dwbias) * conv_scale)
    factors = []
    start = 0
    for level in range(5):
        factors.append(depth[..., start:start + widths[level]])
        start = start + widths[level]
    current = pointwise * factors[0]
    bias_start = 0
    for level in range(4):
        width_next = widths[level + 1]
        value = low_back(project(low(current), gates[level]) + gatebias[bias_start:bias_start + width_next])
        bias_start = bias_start + width_next
        current = value * factors[level + 1]
    branch = low_back(project(low(current), outweight) + outbias)
    middle = features + maskf * mixscale * branch
    second_in = low(maskf * layer_norm(middle, mlpgain, mlpshift))
    hidden = low_back(project(second_in, expandweight) + expandbias)
    activated = low(jax.nn.gelu(hidden, approximate=False))
    reduced = low_back(project(activated, reduceweight) + reducebias)
    return middle + maskf * mlpscale * reduced

def reference(features, validity, upstream, normgain, normshift, inweight, inbias, dwkernel, dwbias, gatefirst, gatesecond, gatethird, gatefourth, gatebias, outweight, outbias, mixscale, mlpgain, mlpshift, expandweight, expandbias, reduceweight, reducebias, mlpscale):
    params = tuple((p.astype(jnp.float32) for p in (normgain, normshift, inweight, inbias, dwkernel, dwbias, gatefirst, gatesecond, gatethird, gatefourth, gatebias, outweight, outbias, mixscale, mlpgain, mlpshift, expandweight, expandbias, reduceweight, reducebias, mlpscale)))
    group = math.gcd(IMAGES, max(1, 4096 // (H * W)))
    count = IMAGES // group
    feats = features.astype(jnp.float32).reshape(count, group, H, W, D)
    masks = validity.astype(jnp.float32).reshape(count, group, H, W, 1)
    grads_in = upstream.astype(jnp.float32).reshape(count, group, H, W, D)

    def advance(totals, block):
        feat, maskb, grad = block
        result, pullback = jax.vjp(lambda p, v: forward(p, v, maskb), params, feat)
        param_grads, feat_grad = pullback(grad)
        totals = jax.tree.map(lambda a, b: a + b, totals, param_grads)
        return (totals, (result.astype(jnp.bfloat16), feat_grad.astype(jnp.bfloat16)))
    zeros = jax.tree.map(jnp.zeros_like, params)
    totals, stacked = lax.scan(advance, zeros, (feats, masks, grads_in))
    produced = stacked[0].reshape(IMAGES, H, W, D)
    features_grad = stacked[1].reshape(IMAGES, H, W, D)
    return (produced, features_grad, totals[0], totals[1], totals[2], totals[3], totals[4], totals[5], totals[6], totals[7], totals[8], totals[9], totals[10], totals[11], totals[12], totals[13], totals[14], totals[15], totals[16], totals[17], totals[18], totals[19], totals[20])
```

```python
import functools
import math

import jax
import jax.numpy as jnp
from jax import lax
from jax.experimental import pallas as pl
from jax.experimental.pallas import tpu as pltpu
from jax.sharding import PartitionSpec as P

f32 = jnp.float32
bf16 = jnp.bfloat16
i32 = jnp.int32
norm_eps = 1e-06
conv_scale = 1.0 / 3.0
inv_root_two = 1.0 / math.sqrt(2.0)
inv_root_tau = 1.0 / math.sqrt(2.0 * math.pi)
vmem_bytes = 60 * 1024 * 1024


def dot(left, right):
    return jnp.dot(left, right, preferred_element_type=f32)


def dot_tn(left, right):
    return lax.dot_general(left, right, (((0,), (0,)), ((), ())), preferred_element_type=f32)


def dot_nt(left, right):
    return lax.dot_general(left, right, (((1,), (1,)), ((), ())), preferred_element_type=f32)


def column_sum(values):
    return jnp.sum(values, axis=0, keepdims=True)


def permutation():
    out = lax.broadcasted_iota(i32, (256, 256), 0)
    src = lax.broadcasted_iota(i32, (256, 256), 1)
    row_par, col_par = out >> 7, (out >> 6) & 1
    pair, ccp, img, blk = (out >> 5) & 1, (out >> 4) & 1, (out >> 3) & 1, out & 7
    want = img * 128 + (2 * pair + row_par) * 32 + 4 * blk + 2 * ccp + col_par
    return (src == want).astype(f32).astype(bf16)


def normalize(values):
    center = jnp.mean(values, axis=-1, keepdims=True)
    shifted = values - center
    spread = jnp.mean(shifted * shifted, axis=-1, keepdims=True)
    inverse = lax.rsqrt(spread + norm_eps)
    return shifted * inverse, inverse


def norm_backward(grad_norm, normed, inverse, gain):
    scaled = grad_norm * gain
    return inverse * (
        scaled
        - jnp.mean(scaled, axis=-1, keepdims=True)
        - normed * jnp.mean(scaled * normed, axis=-1, keepdims=True)
    )


def chunk_mask(size_ref, row_par, col_par, count=256, halo=False):
    at = lax.broadcasted_iota(i32, (count, 1), 0)
    pair, ccp, img, blk = at >> 5, (at >> 4) & 1, (at >> 3) & 1, at & 7
    row = 2 * pair + row_par
    col = 4 * blk + 2 * ccp + col_par
    first = 4 if halo else 0
    high = jnp.where(img == 1, size_ref[first + 1], size_ref[first])
    wide = jnp.where(img == 1, size_ref[3], size_ref[2])
    return jnp.where((row < high) & (col < wide), 1.0, 0.0).astype(f32)


def prepare_kernel(size_ref, x_ref, xh_ref, g_ref, vec_ref, xp_ref, gp_ref, y1_ref, y1h_ref):
    perm = permutation()
    gain, shift = vec_ref[0:1], vec_ref[1:2]
    for b in range(5):
        halo = b == 4
        if halo:
            block = jnp.concatenate([xh_ref[0], xh_ref[1]], axis=0)
        else:
            rows = slice(b * 128, (b + 1) * 128)
            block = jnp.concatenate([x_ref[0, rows], x_ref[1, rows]], axis=0)
            gblock = dot(perm, jnp.concatenate([g_ref[0, rows], g_ref[1, rows]], axis=0)).astype(bf16)
        block = dot(perm, block)
        lowered = block.astype(bf16)
        normed, _ = normalize(block)
        value = normed * gain + shift
        for q in range(4):
            part = slice(q * 64, (q + 1) * 64)
            at = lax.broadcasted_iota(i32, (64, 1), 0)
            pair, ccp, img, blk = at >> 5, (at >> 4) & 1, (at >> 3) & 1, at & 7
            row = 2 * pair + q // 2 + (0 if halo else 4 * b)
            col = 4 * blk + 2 * ccp + q % 2
            first = 4 if halo else 0
            high = jnp.where(img == 1, size_ref[first + 1], size_ref[first])
            wide = jnp.where(img == 1, size_ref[3], size_ref[2])
            mask = jnp.where((row < high) & (col < wide), 1.0, 0.0).astype(f32)
            masked = (mask * value[part]).astype(bf16)
            if halo:
                y1h_ref[q] = masked
            else:
                dest = slice(b * 64, (b + 1) * 64)
                xp_ref[q, dest] = lowered[part]
                gp_ref[q, dest] = gblock[part]
                y1_ref[q, dest] = masked


def whole(shape):
    return pl.BlockSpec(shape, lambda *_: (0,) * len(shape))


SMEM = pl.BlockSpec(memory_space=pltpu.SMEM)


def params():
    return pltpu.CompilerParams(vmem_limit_bytes=vmem_bytes)


def prepare(sizes, x, xh, g, vecs):
    return pl.pallas_call(
        prepare_kernel,
        out_shape=(
            jax.ShapeDtypeStruct((4, 256, 512), bf16),
            jax.ShapeDtypeStruct((4, 256, 512), bf16),
            jax.ShapeDtypeStruct((4, 256, 512), bf16),
            jax.ShapeDtypeStruct((4, 64, 512), bf16),
        ),
        in_specs=[SMEM] + [pl.BlockSpec(memory_space=pltpu.VMEM)] * 4,
        out_specs=tuple([pl.BlockSpec(memory_space=pltpu.VMEM)] * 4),
        compiler_params=params(),
        name="prepare",
    )(sizes, x, xh, g, vecs)


def low_lanes(shape):
    return lax.broadcasted_iota(i32, shape, len(shape) - 1) < 64


def swap_lanes(value):
    return pltpu.roll(value, 64, axis=1)


def shifted_block(value, step):
    if step == 0:
        return value
    blk = lax.broadcasted_iota(i32, value.shape, 1)
    if step > 0:
        return jnp.where(blk < 7, pltpu.roll(value, 7, axis=1), 0.0)
    return jnp.where(blk > 0, pltpu.roll(value, 1, axis=1), 0.0)


ODD = ((-1, 0), (-1, 1), (0, 0), (0, 1), (1, 0))
EVEN = ((-1, 1), (0, 0), (0, 1), (1, 0), (1, 1))


def lane_pairs(chunks):
    res = {}
    for row_par in range(2):
        odd, even = chunks[2 * row_par + 1], chunks[2 * row_par]
        odd_s, even_s = swap_lanes(odd), swap_lanes(even)
        res[row_par, 0] = (odd, even_s)
        res[row_par, 1] = (odd_s, even)
    return res


def fill_band(ref, lead, pairs, n, start, row_par):
    odd, even = (v.reshape(n, 2, 2, 8, 128) for v in pairs)
    half = 1 - row_par
    lanes = slice(half * 128, half * 128 + 128)
    low = low_lanes((n * 2, 8, 128))
    cache = {}

    def take(name, value, step, ccp):
        if (name, step, ccp) not in cache:
            cache[name, step, ccp] = shifted_block(value[:, ccp].reshape(n * 2, 8, 128), step)
        return cache[name, step, ccp]

    for k in range(5):
        both = jnp.where(low, take("o", odd, *ODD[k]), take("e", even, *EVEN[k]))
        ref[lead + (pl.ds(start, n), k, slice(None), lanes)] = both.reshape(n, 16, 128).astype(bf16)


def fill_group(ref, lead, own, halo, base):
    other = 6 - base
    for row_par in range(2):
        first = 2 + row_par
        half = 1 - row_par
        fill_band(ref, lead, own[row_par], 8, first, row_par)
        fill_band(ref, lead, halo[row_par], 2, base + first, row_par)
        ref[lead + (pl.ds(other + first, 2), slice(None), slice(None), slice(half * 128, half * 128 + 128))] = jnp.zeros(
            (2, 5, 16, 128), bf16
        )


def diagonal(rows):
    return (lax.broadcasted_iota(i32, (rows, 128), 0) % 64) == (lax.broadcasted_iota(i32, (rows, 128), 1) % 64)


def build_weights(w_ref, slot, rv_ref, group, zeros):
    mask = diagonal(64)
    for i in range(-1, 8):
        if i in (-1, 7) and not zeros:
            continue
        for jj in range(8):
            if i in (-1, 7):
                block = jnp.zeros((64, 128), bf16)
            else:
                at = (i + 1) * 8 + jj
                block = jnp.where(mask, jnp.broadcast_to(rv_ref[group, at : at + 1], (64, 128)), 0.0).astype(bf16)
            for out_par in range(2):
                top = i + out_par
                if 0 <= top <= 7:
                    ti, rp, tj, cp = top // 2, top % 2, jj // 2, jj % 2
                    rows = (rp * 2 + cp) * 64
                    w_ref[slot, ti * 4 + tj, rows : rows + 64, out_par * 128 : out_par * 128 + 128] = block


def band_block(ref, lead, ti, tj):
    return ref[lead + (slice(1 + ti, 9 + ti), slice(tj, tj + 2))].reshape(256, 256)


def convolve(ref, lead, w_ref, slot):
    total = None
    for ti in range(4):
        for tj in range(4):
            part = dot(band_block(ref, lead, ti, tj), w_ref[slot, ti * 4 + tj])
            total = part if total is None else total + part
    return total


def split_lanes(low_group, high_group):
    low = low_lanes((256, 128))
    chunks = []
    for rp in range(2):
        lg = low_group[:, rp * 128 : rp * 128 + 128]
        hg = high_group[:, rp * 128 : rp * 128 + 128]
        chunks.append(jnp.where(low, lg, swap_lanes(hg)))
        chunks.append(jnp.where(low, swap_lanes(lg), hg))
    return chunks


def forward_kernel(size_ref, y1_ref, y1h_ref, w_in_ref, bias_ref, rv_ref, dwb_ref, d_ref, band_ref, j0_ref, w_ref):
    step = pl.program_id(0)

    @pl.when(step == 0)
    def _():
        for slot in range(2):
            build_weights(w_ref, slot, rv_ref, 0, True)

    base = size_ref[6]
    weight = w_in_ref[...]
    bias = bias_ref[...]
    joined = [dot(y1_ref[q], weight) + bias for q in range(4)]

    @pl.when(step == 0)
    def _():
        for q in range(4):
            j0_ref[q] = joined[q][:, 0:128]

    own, halo = [], []
    for q in range(4):
        own.append((joined[q] * chunk_mask(size_ref, q // 2, q % 2)).astype(bf16).astype(f32))
        part = dot(y1h_ref[q], weight) + bias
        halo.append((part * chunk_mask(size_ref, q // 2, q % 2, 64, True)).astype(bf16).astype(f32))
    for tile in range(2):
        cols = slice(tile * 128, tile * 128 + 128)
        own_pairs = lane_pairs([v[:, cols] for v in own])
        halo_pairs = lane_pairs([v[:, cols] for v in halo])
        sums = []
        for side in range(2):
            group = tile * 2 + side
            fill_group(
                band_ref,
                (group,),
                [own_pairs[rp, side] for rp in range(2)],
                [halo_pairs[rp, side] for rp in range(2)],
                base,
            )
            build_weights(w_ref, side, rv_ref, group, False)
            sums.append(convolve(band_ref, (group,), w_ref, side))
        for q, value in enumerate(split_lanes(*sums)):
            d_ref[q, :, cols] = (value + dwb_ref[:, cols]) * conv_scale


def forward(sizes, y1, y1h, w_in, bias, rv, dwb):
    return pl.pallas_call(
        forward_kernel,
        grid=(4,),
        out_shape=(
            jax.ShapeDtypeStruct((4, 256, 1024), f32),
            jax.ShapeDtypeStruct((16, 13, 5, 16, 256), bf16),
            jax.ShapeDtypeStruct((4, 256, 128), f32),
        ),
        in_specs=[
            SMEM,
            whole((4, 256, 512)),
            whole((4, 64, 512)),
            pl.BlockSpec((512, 256), lambda t: (0, t)),
            pl.BlockSpec((1, 256), lambda t: (0, t)),
            pl.BlockSpec((4, 72, 128), lambda t: (t, 0, 0)),
            pl.BlockSpec((1, 256), lambda t: (0, t)),
        ],
        out_specs=(
            pl.BlockSpec((4, 256, 256), lambda t: (0, 0, t)),
            pl.BlockSpec((4, 13, 5, 16, 256), lambda t: (t, 0, 0, 0, 0)),
            whole((4, 256, 128)),
        ),
        scratch_shapes=[pltpu.VMEM((2, 16, 256, 256), bf16)],
        compiler_params=params(),
        name="forward",
    )(sizes, y1, y1h, w_in, bias, rv, dwb)


def middle_kernel(
    size_ref,
    d_ref,
    j0_ref,
    xp_ref,
    gp_ref,
    w_out_ref,
    w_exp_ref,
    w_red_ref,
    g1_ref,
    g2_ref,
    g3_ref,
    g4_ref,
    gb_ref,
    vec_ref,
    eb_ref,
    out_ref,
    act_ref,
    dh_ref,
    y2_ref,
    df_ref,
    dz_ref,
    u_ref,
    dv_ref,
    dd_ref,
    dx2_ref,
    s512_ref,
    s2048_ref,
    s1024_ref,
    held_ref,
):
    q = pl.program_id(0)
    mask = chunk_mask(size_ref, q // 2, q % 2)
    out_bias, mix, gain, shift, red_bias, ffn = (vec_ref[k : k + 1] for k in range(6))
    lane = lax.broadcasted_iota(i32, (256, 128), 1)
    is0 = (lane >= 32) & (lane < 64)
    is1 = lane >= 64

    @pl.when(q == 0)
    def _():
        s512_ref[...] = jnp.zeros_like(s512_ref)
        s2048_ref[...] = jnp.zeros_like(s2048_ref)
        s1024_ref[...] = jnp.zeros_like(s1024_ref)

    d01, d2, d3, d4 = d_ref[:, 0:128], d_ref[:, 128:256], d_ref[:, 256:512], d_ref[:, 512:1024]
    pointwise = pltpu.roll(j0_ref[...], 32, axis=1)
    u0 = jnp.where(is0, pointwise * d01, 0.0).astype(bf16)
    v1 = dot(u0, g1_ref[...]) + gb_ref[:, 0:128]
    u1 = jnp.where(is1, v1 * d01, 0.0).astype(bf16)
    v2 = dot(u1, g2_ref[...]) + gb_ref[:, 128:256]
    u2 = (v2 * d2).astype(bf16)
    v3 = dot(u2, g3_ref[...]) + gb_ref[:, 256:512]
    u3 = (v3 * d3).astype(bf16)
    v4 = dot(u3, g4_ref[...]) + gb_ref[:, 512:1024]
    u4 = (v4 * d4).astype(bf16)
    u_ref[:, 0:128] = jnp.where(is1, u1, u0)
    u_ref[:, 128:256] = u2
    u_ref[:, 256:512] = u3
    u_ref[:, 512:1024] = u4
    branch = dot(u4, w_out_ref[...]) + out_bias
    middle = xp_ref[...].astype(f32) + mask * mix * branch
    normed, inverse = normalize(middle)
    y2 = (mask * (normed * gain + shift)).astype(bf16)
    y2_ref[...] = y2
    grad = gp_ref[...].astype(f32)
    df = (mask * ffn * grad).astype(bf16)
    df_ref[...] = df
    reduced = red_bias
    back = jnp.zeros((256, 512), f32)
    for k in range(4):
        cols = slice(k * 512, (k + 1) * 512)
        hidden = dot(y2, w_exp_ref[:, cols]) + eb_ref[:, cols]
        cdf = 0.5 * (1.0 + lax.erf(hidden * inv_root_two))
        act = (hidden * cdf).astype(bf16)
        act_ref[:, cols] = act
        reduced = reduced + dot(act, w_red_ref[cols, :])
        density = jnp.exp(-0.5 * hidden * hidden) * inv_root_tau
        dh = (dot_nt(df, w_red_ref[cols, :]) * (cdf + hidden * density)).astype(bf16)
        dh_ref[:, cols] = dh
        s2048_ref[:, cols] += column_sum(dh.astype(f32))
        back = back + dot_nt(dh, w_exp_ref[:, cols])
    held_ref[q] = (middle + mask * ffn * reduced).astype(bf16)
    s512_ref[0:1] += column_sum(grad * mask * reduced)
    s512_ref[1:2] += column_sum(df.astype(f32))
    back = mask * back
    s512_ref[2:3] += column_sum(back * normed)
    s512_ref[3:4] += column_sum(back)
    dx2 = grad + norm_backward(back, normed, inverse, gain)
    dx2_ref[...] = dx2
    dz = (mask * mix * dx2).astype(bf16)
    dz_ref[...] = dz
    s512_ref[4:5] += column_sum(dx2 * mask * branch)
    s512_ref[5:6] += column_sum(dz.astype(f32))
    du4 = dot_nt(dz, w_out_ref[...])
    dv4 = (du4 * d4).astype(bf16)
    dd4 = (du4 * v4).astype(bf16)
    du3 = dot_nt(dv4, g4_ref[...])
    dv3 = (du3 * d3).astype(bf16)
    dd3 = (du3 * v3).astype(bf16)
    du2 = dot_nt(dv3, g3_ref[...])
    dv2 = (du2 * d2).astype(bf16)
    dd2 = (du2 * v2).astype(bf16)
    du1 = dot_nt(dv2, g2_ref[...])
    dv1 = (du1 * d01).astype(bf16)
    du0 = dot_nt(dv1, g1_ref[...])
    dpw = pltpu.roll(du0 * d01, 96, axis=1)
    dd01 = jnp.where(is1, du1 * v1, jnp.where(is0, du0 * pointwise, dpw)).astype(bf16)
    dv_ref[:, 0:128] = dv1
    dv_ref[:, 128:256] = dv2
    dv_ref[:, 256:512] = dv3
    dv_ref[:, 512:1024] = dv4
    dd_ref[:, 0:128] = dd01
    dd_ref[:, 128:256] = dd2
    dd_ref[:, 256:512] = dd3
    dd_ref[:, 512:1024] = dd4
    for k, ref in enumerate((dv_ref, dd_ref)):
        s1024_ref[k : k + 1] += column_sum(ref[...].astype(f32))

    @pl.when(q == 3)
    def _():
        unpermute(held_ref, out_ref)


def unpermute(held_ref, out_ref):
    perm = permutation()
    for b in range(4):
        block = jnp.concatenate([held_ref[k, b * 64 : (b + 1) * 64] for k in range(4)], axis=0)
        block = dot_tn(perm, block).astype(bf16)
        out_ref[0, b * 128 : (b + 1) * 128] = block[0:128]
        out_ref[1, b * 128 : (b + 1) * 128] = block[128:256]


def middle_call(sizes, d, j0, xp, gp, w_out, w_exp, w_red, g1, g2, g3, g4, gb, vecs, eb):
    def chunk(width):
        return pl.BlockSpec((None, 256, width), lambda q: (q, 0, 0))

    def out(width, dtype=bf16):
        return jax.ShapeDtypeStruct((4, 256, width), dtype)

    widths = (2048, 2048, 512, 512, 512, 1024, 1024, 1024)
    return pl.pallas_call(
        middle_kernel,
        grid=(4,),
        out_shape=(jax.ShapeDtypeStruct((2, 512, 512), bf16),)
        + tuple(out(w) for w in widths)
        + (
            out(512, f32),
            jax.ShapeDtypeStruct((8, 512), f32),
            jax.ShapeDtypeStruct((1, 2048), f32),
            jax.ShapeDtypeStruct((8, 1024), f32),
        ),
        in_specs=[SMEM, chunk(1024), chunk(128), chunk(512), chunk(512)]
        + [whole(v.shape) for v in (w_out, w_exp, w_red, g1, g2, g3, g4, gb, vecs, eb)],
        out_specs=(whole((2, 512, 512)),)
        + tuple(chunk(w) for w in widths)
        + (chunk(512), whole((8, 512)), whole((1, 2048)), whole((8, 1024))),
        scratch_shapes=[pltpu.VMEM((4, 256, 512), bf16)],
        compiler_params=params(),
        name="middle",
    )(sizes, d, j0, xp, gp, w_out, w_exp, w_red, g1, g2, g3, g4, gb, vecs, eb)


def feed_grads_kernel(act_ref, df_ref, y2_ref, dh_ref, red_ref, exp_ref):
    red_ref[...] = dot_tn(act_ref[...], df_ref[...]).astype(bf16)
    exp_ref[...] = dot_tn(y2_ref[...], dh_ref[...]).astype(bf16)


def feed_grads(act, df, y2, dh):
    block = pl.BlockSpec((1024, 512), lambda k: (0, k))
    return pl.pallas_call(
        feed_grads_kernel,
        grid=(4,),
        out_shape=(jax.ShapeDtypeStruct((2048, 512), bf16), jax.ShapeDtypeStruct((512, 2048), bf16)),
        in_specs=[block, whole((1024, 512)), whole((1024, 512)), block],
        out_specs=(pl.BlockSpec((512, 512), lambda k: (k, 0)), pl.BlockSpec((512, 512), lambda k: (0, k))),
        compiler_params=params(),
        name="feed_grads",
    )(act, df, y2, dh)


def gate_grads_kernel(u_ref, dz_ref, dv_ref, out_ref, g12_ref, g3_ref, g4_ref):
    out_ref[...] = dot_tn(u_ref[:, 512:1024], dz_ref[...]).astype(bf16)
    g12_ref[...] = dot_tn(u_ref[:, 0:128], dv_ref[:, 0:256])
    g3_ref[...] = dot_tn(u_ref[:, 128:256], dv_ref[:, 256:512])
    g4_ref[...] = dot_tn(u_ref[:, 256:512], dv_ref[:, 512:1024])


def gate_grads(u, dz, dv):
    return pl.pallas_call(
        gate_grads_kernel,
        out_shape=(
            jax.ShapeDtypeStruct((512, 512), bf16),
            jax.ShapeDtypeStruct((128, 256), f32),
            jax.ShapeDtypeStruct((128, 256), f32),
            jax.ShapeDtypeStruct((256, 512), f32),
        ),
        in_specs=[pl.BlockSpec(memory_space=pltpu.VMEM)] * 3,
        out_specs=tuple([pl.BlockSpec(memory_space=pltpu.VMEM)] * 4),
        compiler_params=params(),
        name="gate_grads",
    )(u, dz, dv)


def conv_back_kernel(size_ref, dd_ref, ddh_ref, band_ref, rv_ref, df_ref, dk_ref, w_ref, back_ref):
    step = pl.program_id(0)

    @pl.when(step == 0)
    def _():
        for slot in range(2):
            build_weights(w_ref, slot, rv_ref, 0, True)

    base = size_ref[6]
    low = low_lanes((256, 128))
    low8 = low_lanes((8, 128))
    wide = diagonal(256)
    masks = [chunk_mask(size_ref, q // 2, q % 2) for q in range(4)]
    lane = lax.broadcasted_iota(i32, (256, 128), 1)
    keep = (lane < 32) & (step == 0)
    for tile in range(2):
        cols = slice(tile * 128, tile * 128 + 128)
        own = [dd_ref[q, :, cols].astype(f32) for q in range(4)]
        own_pairs = lane_pairs(own)
        halo_pairs = lane_pairs([ddh_ref[q, :, cols].astype(f32) for q in range(4)])
        sums = []
        for side in range(2):
            group = tile * 2 + side
            fill_group(
                back_ref,
                (side,),
                [own_pairs[rp, side] for rp in range(2)],
                [halo_pairs[rp, side] for rp in range(2)],
                base,
            )
            build_weights(w_ref, side, rv_ref, group, False)
            sums.append(convolve(back_ref, (side,), w_ref, side))
            halves = []
            for rp in range(2):
                odd, even = own_pairs[rp, side]
                halves.append(jnp.where(low, swap_lanes(even), swap_lanes(odd)))
            left = jnp.concatenate(halves, axis=1).astype(bf16)
            rows = {}
            for ti in range(4):
                for tj in range(4):
                    cross = dot_tn(left, band_block(band_ref, (group,), ti, tj))
                    for rp in range(2):
                        half = jnp.where(wide, cross[:, rp * 128 : rp * 128 + 128], 0.0)
                        part = jnp.sum(half.reshape(4, 8, 8, 128), axis=1)
                        for out_rp in range(2):
                            i = 2 * ti + rp - out_rp
                            if 0 <= i <= 6:
                                for out_cp in range(2):
                                    key = (i, tj, out_cp)
                                    term = part[out_rp * 2 + out_cp]
                                    rows[key] = rows[key] + term if key in rows else term
            for i in range(7):
                turned = [swap_lanes(rows[i, tj, 1]) for tj in range(4)] + [jnp.zeros((8, 128), f32)]
                for tj in range(4):
                    value = rows[i, tj, 0] + jnp.where(low8, turned[tj], turned[tj + 1])
                    dk_ref[group, i * 4 + tj : i * 4 + tj + 1] = column_sum(value) * conv_scale
        for q, value in enumerate(split_lanes(*sums)):
            value = value * (masks[q] * conv_scale)
            if tile == 0:
                value = jnp.where(keep, own[q], value)
            df_ref[q, :, cols] = value.astype(bf16)


def conv_back(sizes, dd, ddh, band, rv):
    return pl.pallas_call(
        conv_back_kernel,
        grid=(4,),
        out_shape=(
            jax.ShapeDtypeStruct((4, 256, 1024), bf16),
            jax.ShapeDtypeStruct((16, 28, 128), f32),
        ),
        in_specs=[
            SMEM,
            pl.BlockSpec((4, 256, 256), lambda t: (0, 0, t)),
            pl.BlockSpec((4, 64, 256), lambda t: (0, 0, t)),
            pl.BlockSpec((4, 13, 5, 16, 256), lambda t: (t, 0, 0, 0, 0)),
            pl.BlockSpec((4, 72, 128), lambda t: (t, 0, 0)),
        ],
        out_specs=(
            pl.BlockSpec((4, 256, 256), lambda t: (0, 0, t)),
            pl.BlockSpec((4, 28, 128), lambda t: (t, 0, 0)),
        ),
        scratch_shapes=[pltpu.VMEM((2, 16, 256, 256), bf16), pltpu.VMEM((2, 13, 5, 16, 256), bf16)],
        compiler_params=params(),
        name="conv_back",
    )(sizes, dd, ddh, band, rv)


def in_grad_kernel(y1_ref, df_ref, out_ref):
    out_ref[...] = dot_tn(y1_ref[...], df_ref[...]).astype(bf16)


def in_grad(y1, df):
    return pl.pallas_call(
        in_grad_kernel,
        grid=(2,),
        out_shape=jax.ShapeDtypeStruct((512, 1024), bf16),
        in_specs=[whole((1024, 512)), pl.BlockSpec((1024, 512), lambda k: (0, k))],
        out_specs=pl.BlockSpec((512, 512), lambda k: (0, k)),
        compiler_params=params(),
        name="in_grad",
    )(y1, df)


def last_kernel(size_ref, df_ref, xp_ref, dx2_ref, w_in_ref, vec_ref, out_ref, s512_ref, s1024_ref, held_ref):
    q = pl.program_id(0)

    @pl.when(q == 0)
    def _():
        s512_ref[...] = jnp.zeros_like(s512_ref)
        s1024_ref[...] = jnp.zeros_like(s1024_ref)

    mask = chunk_mask(size_ref, q // 2, q % 2)
    df = df_ref[...]
    s1024_ref[0:1] += column_sum(df.astype(f32))
    grad = mask * dot_nt(df, w_in_ref[...])
    normed, inverse = normalize(xp_ref[...].astype(f32))
    s512_ref[0:1] += column_sum(grad * normed)
    s512_ref[1:2] += column_sum(grad)
    held_ref[q] = (dx2_ref[...] + norm_backward(grad, normed, inverse, vec_ref[0:1])).astype(bf16)

    @pl.when(q == 3)
    def _():
        unpermute(held_ref, out_ref)


def last_call(sizes, df, xp, dx2, w_in, vecs):
    def chunk(width):
        return pl.BlockSpec((None, 256, width), lambda q: (q, 0, 0))

    return pl.pallas_call(
        last_kernel,
        grid=(4,),
        out_shape=(
            jax.ShapeDtypeStruct((2, 512, 512), bf16),
            jax.ShapeDtypeStruct((8, 512), f32),
            jax.ShapeDtypeStruct((8, 1024), f32),
        ),
        in_specs=[SMEM, chunk(1024), chunk(512), chunk(512), whole(w_in.shape), whole(vecs.shape)],
        out_specs=(whole((2, 512, 512)), whole((8, 512)), whole((8, 1024))),
        scratch_shapes=[pltpu.VMEM((4, 256, 512), bf16)],
        compiler_params=params(),
        name="last",
    )(sizes, df, xp, dx2, w_in, vecs)


def bits_of(axis):
    return lax.axis_size(axis).bit_length() - 1


def swap_with(value, hop):
    axis, bit = hop
    size = lax.axis_size(axis)
    return lax.ppermute(value, axis, [(k, k ^ (1 << bit)) for k in range(size)])


def own_bit(hop):
    axis, bit = hop
    return (lax.axis_index(axis) >> bit) & 1


def img_hops():
    return [("img", b) for b in reversed(range(bits_of("img")))]


def hop_place(hop):
    axis, bit = hop
    return bits_of("img") if axis == "row" else bits_of("img") - 1 - bit


def gather_rows(shard, order):
    rows, cols = shard.shape
    places = []
    value = shard
    for hop in order:
        other = swap_with(value, hop)
        place = hop_place(hop)
        at = sum(1 for p in places if p < place)
        places.append(place)
        mine = own_bit(hop) == 0
        value = jnp.stack([jnp.where(mine, value, other), jnp.where(mine, other, value)], axis=at)
    return value.reshape(-1, cols)


def scatter_sum(whole_value, order, final=f32):
    count = bits_of("img") + 1
    rows, cols = whole_value.shape
    value = whole_value.reshape((2,) * count + (rows >> count, cols))
    places = list(range(count))
    for k, hop in enumerate(order):
        at = places.index(hop_place(hop))
        places.pop(at)
        bit = own_bit(hop)
        mine = lax.dynamic_index_in_dim(value, bit, at, keepdims=False)
        sent = lax.dynamic_index_in_dim(value, 1 - bit, at, keepdims=False)
        got = swap_with(sent, hop)
        total = mine.astype(f32) + got.astype(f32)
        value = total if k == count - 1 else total.astype(bf16)
    return value.astype(final)


def total_sum(flat, hops):
    count = bits_of("img") + 1
    size = flat.shape[0]
    unit = (1 << count) * 8 * 128
    padded = -(-size // unit) * unit
    table = jnp.pad(flat, (0, padded - size)).astype(bf16).reshape(-1, 128)
    part = scatter_sum(table, hops, bf16)
    return gather_rows(part, hops[::-1]).astype(f32).reshape(-1)[:size]


def per_device(
    features,
    validity,
    upstream,
    normgain,
    normshift,
    inweight,
    inbias,
    dwkernel,
    dwbias,
    gatefirst,
    gatesecond,
    gatethird,
    gatefourth,
    gatebias,
    outweight,
    outbias,
    mixscale,
    mlpgain,
    mlpshift,
    expandweight,
    expandbias,
    reduceweight,
    reducebias,
    mlpscale,
):
    hops = img_hops()
    row_hop = ("row", 0)
    turned = hops[:-2] + [hops[-1], hops[-2]]
    half_turn = hops[-2:] + hops[:-2]
    lower = lax.axis_index("row") == 1

    x = features.reshape(2, 512, 512)
    g = upstream.reshape(2, 512, 512)
    edge = jnp.where(lower, x[:, 0:128], x[:, 384:512])
    x_halo = swap_with(edge, row_hop)
    heights = jnp.sum(validity[:, :, 0], axis=1)
    widths = jnp.sum(validity[:, 0, :], axis=1)
    halo_heights = swap_with(heights, row_hop)
    base = jnp.where(lower, -2, 8).astype(i32)
    sizes = jnp.concatenate([heights, widths, halo_heights, jnp.stack([base, base])]).astype(i32)

    w_in = gather_rows(inweight, hops + [row_hop])
    w_out = gather_rows(outweight, turned + [row_hop])
    w_exp = gather_rows(expandweight, turned + [row_hop])
    w_red = gather_rows(reduceweight, half_turn + [row_hop])

    taps = jnp.pad(dwkernel.astype(f32), ((0, 0), (0, 0), (32, 0)))

    def row_vectors(kernel):
        kernel = kernel.reshape(7, 7, 16, 64)
        low = jnp.pad(kernel, ((1, 1), (0, 1), (0, 0), (0, 0)))
        high = jnp.pad(kernel, ((1, 1), (1, 0), (0, 0), (0, 0)))
        both = jnp.concatenate([low, high], axis=-1)
        return both.transpose(2, 0, 1, 3).reshape(16, 72, 128)

    rv = row_vectors(taps)
    rv_back = row_vectors(taps[::-1, ::-1])
    dwb = jnp.pad(dwbias.astype(f32), (32, 0)).reshape(1, 1024)
    in_bias = inbias.astype(f32).reshape(1, 1024)
    norm_vecs = jnp.stack([normgain, normshift]).astype(f32)
    vecs = jnp.stack([outbias, mixscale, mlpgain, mlpshift, reducebias, mlpscale]).astype(f32)
    gb = jnp.pad(gatebias.astype(f32), (64, 0)).reshape(1, 1024)
    g1 = jnp.pad(gatefirst, ((32, 64), (64, 0)))
    g2 = jnp.pad(gatesecond, ((64, 0), (0, 0)))
    eb = expandbias.astype(f32).reshape(1, 2048)

    xp, gp, y1, y1h = prepare(sizes, x, x_halo, g, norm_vecs)
    d, band, j0 = forward(sizes, y1, y1h, w_in, in_bias, rv, dwb)
    (produced, act, dh, y2, df, dz, u, dv, dd, dx2, s512, s2048, s1024) = middle_call(
        sizes, d, j0, xp, gp, w_out, w_exp, w_red, g1, g2, gatethird, gatefourth, gb, vecs, eb
    )
    dd_edge = jnp.where(lower, dd[:, 0:64], dd[:, 192:256])
    dd_halo = swap_with(dd_edge, row_hop)

    def flat(value):
        return value.reshape(1024, -1)

    red_part, exp_part = feed_grads(flat(act), flat(df), flat(y2), flat(dh))
    out_part, g12, g3, g4 = gate_grads(flat(u), flat(dz), flat(dv))
    red_sum = scatter_sum(red_part, [row_hop] + hops[::-1])
    exp_sum = scatter_sum(exp_part, [row_hop] + turned[::-1])
    out_sum = scatter_sum(out_part, [row_hop] + half_turn[::-1])
    early = (
        g12[32:64, 64:128],
        g12[64:128, 128:256],
        g3,
        g4,
        s1024[0, 64:],
        s1024[1, 32:] * conv_scale,
        s512[0:6],
        s2048,
    )
    early_shapes = [v.shape for v in early]
    early_sum = total_sum(jnp.concatenate([v.reshape(-1) for v in early]), [row_hop] + half_turn[::-1])

    dfused, dk = conv_back(sizes, dd, dd_halo, band, rv_back)
    in_part = in_grad(flat(y1), flat(dfused))
    in_sum = scatter_sum(in_part, [row_hop] + hops[::-1])
    fgrad, n512, n1024 = last_call(sizes, dfused, xp, dx2, w_in, norm_vecs)
    late = (dk, n512[0:2], n1024[0])
    late_shapes = [v.shape for v in late]
    late_sum = total_sum(jnp.concatenate([v.reshape(-1) for v in late]), [row_hop] + turned[::-1])

    def unpack(value, shapes):
        at, parts = 0, []
        for shape in shapes:
            size = math.prod(shape)
            parts.append(value[at : at + size].reshape(shape))
            at += size
        return parts

    gate1, gate2, gate3, gate4, gbias, dwb_sum, vec_sum, eb_sum = unpack(early_sum, early_shapes)
    dk_sum, norm_sum, inb_sum = unpack(late_sum, late_shapes)
    dk_sum = dk_sum.reshape(16, 7, 8, 64).transpose(1, 2, 0, 3).reshape(7, 8, 1024)[:, :7, 32:]
    return (
        produced.reshape(features.shape),
        fgrad.reshape(features.shape),
        norm_sum[0],
        norm_sum[1],
        in_sum,
        inb_sum,
        dk_sum,
        dwb_sum,
        gate1,
        gate2,
        gate3,
        gate4,
        gbias,
        out_sum,
        vec_sum[5],
        vec_sum[4],
        vec_sum[2],
        vec_sum[3],
        exp_sum,
        eb_sum.reshape(-1),
        red_sum,
        vec_sum[1],
        vec_sum[0],
    )


def solution(mesh):
    band = P("img", "row", None, None)
    rows = P(("img", "row"), None)
    copy = P()
    ins = [band, P("img", "row", None), band] + [copy] * 21
    for k in (5, 14, 19, 21):
        ins[k] = rows
    outs = [band, band] + [copy] * 21
    for k in (4, 13, 18, 20):
        outs[k] = rows
    return jax.shard_map(per_device, mesh=mesh, in_specs=tuple(ins), out_specs=tuple(outs), check_vma=False)
```

```python
import functools
import math

import jax
import jax.numpy as jnp
from jax import lax
from jax.experimental import pallas as pl
from jax.experimental.pallas import tpu as pltpu
from jax.sharding import PartitionSpec as P

f32 = jnp.float32
bf16 = jnp.bfloat16
i32 = jnp.int32
norm_eps = 1e-06
conv_scale = 1.0 / 3.0
inv_root_two = 1.0 / math.sqrt(2.0)
inv_root_tau = 1.0 / math.sqrt(2.0 * math.pi)
vmem_bytes = 60 * 1024 * 1024


def dot(left, right):
    return jnp.dot(left, right, preferred_element_type=f32)


def dot_tn(left, right):
    return lax.dot_general(left, right, (((0,), (0,)), ((), ())), preferred_element_type=f32)


def dot_nt(left, right):
    return lax.dot_general(left, right, (((1,), (1,)), ((), ())), preferred_element_type=f32)


def column_sum(values):
    return jnp.sum(values, axis=0, keepdims=True)


def permutation():
    out = lax.broadcasted_iota(i32, (256, 256), 0)
    src = lax.broadcasted_iota(i32, (256, 256), 1)
    row_par, col_par = out >> 7, (out >> 6) & 1
    pair, ccp, img, blk = (out >> 5) & 1, (out >> 4) & 1, (out >> 3) & 1, out & 7
    want = img * 128 + (2 * pair + row_par) * 32 + 4 * blk + 2 * ccp + col_par
    return (src == want).astype(f32).astype(bf16)


def normalize(values):
    center = jnp.mean(values, axis=-1, keepdims=True)
    shifted = values - center
    spread = jnp.mean(shifted * shifted, axis=-1, keepdims=True)
    inverse = lax.rsqrt(spread + norm_eps)
    return shifted * inverse, inverse


def norm_backward(grad_norm, normed, inverse, gain):
    scaled = grad_norm * gain
    return inverse * (
        scaled
        - jnp.mean(scaled, axis=-1, keepdims=True)
        - normed * jnp.mean(scaled * normed, axis=-1, keepdims=True)
    )


def extents(valid_ref):
    heights = [sum(valid_ref[16 * n + r, 0] for r in range(16)) for n in range(2)]
    widths = [sum(valid_ref[16 * n, c] for c in range(32)) for n in range(2)]
    return heights, widths


def chunk_mask(sizes, row_par, col_par, count=256, first_row=0):
    (high_a, high_b), (wide_a, wide_b) = sizes
    at = lax.broadcasted_iota(i32, (count, 1), 0)
    pair, ccp, img, blk = at >> 5, (at >> 4) & 1, (at >> 3) & 1, at & 7
    row = 2 * pair + row_par + first_row
    col = 4 * blk + 2 * ccp + col_par
    high = jnp.where(img == 1, high_b, high_a)
    wide = jnp.where(img == 1, wide_b, wide_a)
    return jnp.where((row < high) & (col < wide), 1.0, 0.0).astype(f32)


def halo_sizes(valid_ref, halo_ref):
    heights, widths = extents(valid_ref)
    below, _ = extents(halo_ref)
    upper = lax.axis_index("row") == 0
    return [jnp.where(upper, h, 4) for h in below], widths


def halo_base():
    return jnp.where(lax.axis_index("row") == 0, 8, -2).astype(i32)


def vectors_kernel(in_ref, dw_ref, gate_ref, exp_ref, *rest):
    small, out_ref = rest[:8], rest[8]

    def line(ref):
        return ref[...].astype(f32).reshape(1, ref.shape[0])

    out_ref[0:1] = line(in_ref)
    out_ref[1:2, 0:32] = jnp.zeros((1, 32), f32)
    out_ref[1:2, 32:1024] = line(dw_ref)
    out_ref[2:3, 0:64] = jnp.zeros((1, 64), f32)
    out_ref[2:3, 64:1024] = line(gate_ref)
    wide = line(exp_ref)
    out_ref[3:4] = wide[:, 0:1024]
    out_ref[4:5] = wide[:, 1024:2048]
    for k, ref in enumerate(small):
        out_ref[5 + k // 2 : 6 + k // 2, k % 2 * 512 : k % 2 * 512 + 512] = line(ref)


def gather_vectors(large, small, deps=()):
    vmem = pl.BlockSpec(memory_space=pltpu.VMEM)
    return launch(
        deps,
        vectors_kernel,
        out_shape=jax.ShapeDtypeStruct((9, 1024), f32),
        in_specs=[vmem] * 12,
        out_specs=vmem,
        cost_estimate=takes(1),
        name="vectors",
    )(*large, *small)


def prepare_kernel(valid_ref, halo_valid_ref, x_ref, xh_ref, g_ref, vec_ref, xp_ref, gp_ref, y1_ref, y1h_ref):
    perm = permutation()
    gain, shift = vec_ref[8:9, 0:512], vec_ref[8:9, 512:1024]
    own, halo = extents(valid_ref), halo_sizes(valid_ref, halo_valid_ref)
    start = pl.multiple_of(lax.axis_index("row") * 384, 128)
    for b in range(5):
        if b == 4:
            rows = pl.ds(start, 128)
            block = jnp.concatenate([xh_ref[0, rows], xh_ref[1, rows]], axis=0)
        else:
            rows = slice(b * 128, (b + 1) * 128)
            block = jnp.concatenate([x_ref[0, rows], x_ref[1, rows]], axis=0)
            gblock = dot(perm, jnp.concatenate([g_ref[0, rows], g_ref[1, rows]], axis=0)).astype(bf16)
        block = dot(perm, block)
        lowered = block.astype(bf16)
        normed, _ = normalize(block)
        value = normed * gain + shift
        for q in range(4):
            part = slice(q * 64, (q + 1) * 64)
            if b == 4:
                y1h_ref[q] = (chunk_mask(halo, q // 2, q % 2, 64) * value[part]).astype(bf16)
            else:
                dest = slice(b * 64, (b + 1) * 64)
                xp_ref[q, dest] = lowered[part]
                gp_ref[q, dest] = gblock[part]
                y1_ref[q, dest] = (chunk_mask(own, q // 2, q % 2, 64, 4 * b) * value[part]).astype(bf16)


def whole(shape):
    return pl.BlockSpec(shape, lambda *_: (0,) * len(shape))


SMEM = pl.BlockSpec(memory_space=pltpu.SMEM)


def params():
    return pltpu.CompilerParams(vmem_limit_bytes=vmem_bytes)


def takes(micros):
    return pl.CostEstimate(flops=int(micros * 1.0e9), bytes_accessed=0, transcendentals=0)


def launch(deps, kernel, *, out_shape, in_specs, out_specs, **rest):
    single = not isinstance(out_shape, tuple)
    shapes = (out_shape,) if single else out_shape
    specs = (out_specs,) if single else out_specs
    anywhere = pl.BlockSpec(memory_space=pl.ANY)
    count = len(in_specs)

    def body(*refs):
        at = count + len(deps)
        kernel(*refs[:count], *refs[at : at + len(shapes)], *refs[at + len(shapes) + 1 :])

    call = pl.pallas_call(
        body,
        out_shape=(*shapes, jax.ShapeDtypeStruct((8, 128), f32)),
        in_specs=list(in_specs) + [anywhere] * len(deps),
        out_specs=(*specs, anywhere),
        compiler_params=params(),
        **rest,
    )
    return lambda *args: call(*args, *deps)


def own_number(dealt):
    return lax.axis_index("img") * 2 + lax.axis_index("row") if dealt else 0


def place_rows(scratch, refs, order, number, rows):
    each = 32 // len(refs)
    for k, ref in enumerate(refs):
        for b in range(each):
            at = pl.multiple_of((order[k * each + b] ^ number) * rows, 16)
            scratch[pl.ds(at, rows), :] = ref[b * rows : (b + 1) * rows, :]


def dealt_owner(place, order):
    if order == "none":
        return place
    if order == "plain":
        return (2 * (place % 16) + place // 16) ^ lax.axis_index("row")
    return (2 * masks_of(order)[place % 16] + place // 16) ^ own_number(True)


def deal_rows(outs, lead, value_ref, order, rows):
    for p in range(32):
        at = pl.multiple_of(dealt_owner(p, order) * rows, 16)
        outs[p // 16][(slice(p % 16 * rows, (p % 16 + 1) * rows),) + lead] = value_ref[pl.ds(at, rows), :].astype(bf16)


def prepare(valid, halo_valid, x, xh, g, wide, deps=()):
    vmem = pl.BlockSpec(memory_space=pltpu.VMEM)
    return launch(
        deps,
        prepare_kernel,
        out_shape=(
            jax.ShapeDtypeStruct((4, 256, 512), bf16),
            jax.ShapeDtypeStruct((4, 256, 512), bf16),
            jax.ShapeDtypeStruct((4, 256, 512), bf16),
            jax.ShapeDtypeStruct((4, 64, 512), bf16),
        ),
        in_specs=[SMEM] * 2 + [vmem] * 4,
        out_specs=(vmem,) * 4,
        cost_estimate=takes(4),
        name="prepare",
    )(valid, halo_valid, x, xh, g, wide)


def low_lanes(shape):
    return lax.broadcasted_iota(i32, shape, len(shape) - 1) < 64


def swap_lanes(value):
    return pltpu.roll(value, 64, axis=1)


def shifted_block(value, step):
    if step == 0:
        return value
    blk = lax.broadcasted_iota(i32, value.shape, 1)
    if step > 0:
        return jnp.where(blk < 7, pltpu.roll(value, 7, axis=1), 0.0)
    return jnp.where(blk > 0, pltpu.roll(value, 1, axis=1), 0.0)


ODD = ((-1, 0), (-1, 1), (0, 0), (0, 1), (1, 0))
EVEN = ((-1, 1), (0, 0), (0, 1), (1, 0), (1, 1))


def lane_pairs(chunks):
    res = {}
    for row_par in range(2):
        odd, even = chunks[2 * row_par + 1], chunks[2 * row_par]
        odd_s, even_s = swap_lanes(odd), swap_lanes(even)
        res[row_par, 0] = (odd, even_s)
        res[row_par, 1] = (odd_s, even)
    return res


def fill_band(ref, lead, pairs, n, start, row_par):
    odd, even = (v.reshape(n, 2, 2, 8, 128) for v in pairs)
    half = 1 - row_par
    lanes = slice(half * 128, half * 128 + 128)
    low = low_lanes((n * 2, 8, 128))
    cache = {}

    def take(name, value, step, ccp):
        if (name, step, ccp) not in cache:
            cache[name, step, ccp] = shifted_block(value[:, ccp].reshape(n * 2, 8, 128), step)
        return cache[name, step, ccp]

    for k in range(5):
        both = jnp.where(low, take("o", odd, *ODD[k]), take("e", even, *EVEN[k]))
        ref[lead + (pl.ds(start, n), k, slice(None), lanes)] = both.reshape(n, 16, 128).astype(bf16)


def fill_group(ref, lead, own, halo, base):
    other = 6 - base
    for row_par in range(2):
        first = 2 + row_par
        half = 1 - row_par
        fill_band(ref, lead, own[row_par], 8, first, row_par)
        fill_band(ref, lead, halo[row_par], 2, base + first, row_par)
        ref[lead + (pl.ds(other + first, 2), slice(None), slice(None), slice(half * 128, half * 128 + 128))] = jnp.zeros(
            (2, 5, 16, 128), bf16
        )


def diagonal(rows):
    return (lax.broadcasted_iota(i32, (rows, 128), 0) % 64) == (lax.broadcasted_iota(i32, (rows, 128), 1) % 64)


def build_weights(w_ref, slot, tap_ref, group, flip=False):
    mask = diagonal(64)
    low = low_lanes((1, 128))
    tile, side = group // 2, group % 2
    cols = slice(tile * 128, tile * 128 + 128)
    for i in range(7):
        rows = tap_ref[6 - i if flip else i, :, cols]
        turned = swap_lanes(rows)
        first, second = (rows, turned) if side == 0 else (turned, rows)
        for jj in range(8):
            a, b = (6 - jj, 7 - jj) if flip else (jj, jj - 1)
            left = first[a : a + 1] if 0 <= a <= 6 else jnp.zeros((1, 128), f32)
            right = second[b : b + 1] if 0 <= b <= 6 else jnp.zeros((1, 128), f32)
            vector = jnp.where(low, left, right)
            block = jnp.where(mask, jnp.broadcast_to(vector, (64, 128)), 0.0).astype(bf16)
            for out_par in range(2):
                top = i + out_par
                ti, rp, tj, cp = top // 2, top % 2, jj // 2, jj % 2
                at = (rp * 2 + cp) * 64
                w_ref[slot, ti * 4 + tj, at : at + 64, out_par * 128 : out_par * 128 + 128] = block


def clear_weights(w_ref):
    for slot in range(2):
        for tj in range(4):
            w_ref[slot, tj, 0:128, 128:256] = jnp.zeros((128, 128), bf16)
            w_ref[slot, 12 + tj, 128:256, 0:128] = jnp.zeros((128, 128), bf16)


def band_block(ref, lead, ti, tj):
    return ref[lead + (slice(1 + ti, 9 + ti), slice(tj, tj + 2))].reshape(256, 256)


def convolve(ref, lead, w_ref, slot):
    total = None
    for ti in range(4):
        for tj in range(4):
            part = dot(band_block(ref, lead, ti, tj), w_ref[slot, ti * 4 + tj])
            total = part if total is None else total + part
    return total


def split_lanes(low_group, high_group):
    low = low_lanes((256, 128))
    chunks = []
    for rp in range(2):
        lg = low_group[:, rp * 128 : rp * 128 + 128]
        hg = high_group[:, rp * 128 : rp * 128 + 128]
        chunks.append(jnp.where(low, lg, swap_lanes(hg)))
        chunks.append(jnp.where(low, swap_lanes(lg), hg))
    return chunks


def forward_kernel(valid_ref, halo_valid_ref, y1_ref, y1h_ref, *rest, order, dealt):
    weights, (wide_ref, tap_ref, d_ref, band_ref, j0_ref, w_ref, win_ref) = rest[:8], rest[8:]
    step = pl.program_id(0)

    @pl.when(step == 0)
    def _():
        clear_weights(w_ref)

    base = halo_base()
    sizes, around = extents(valid_ref), halo_sizes(valid_ref, halo_valid_ref)
    place_rows(win_ref, weights, order, own_number(dealt), 16)
    weight = win_ref[...]
    bias = wide_ref[0:1]
    joined = [dot(y1_ref[q], weight) + bias for q in range(4)]

    @pl.when(step == 0)
    def _():
        for q in range(4):
            j0_ref[q] = joined[q][:, 0:128]

    own, halo = [], []
    for q in range(4):
        own.append((joined[q] * chunk_mask(sizes, q // 2, q % 2)).astype(bf16).astype(f32))
        part = dot(y1h_ref[q], weight) + bias
        halo.append((part * chunk_mask(around, q // 2, q % 2, 64)).astype(bf16).astype(f32))
    for tile in range(2):
        cols = slice(tile * 128, tile * 128 + 128)
        own_pairs = lane_pairs([v[:, cols] for v in own])
        halo_pairs = lane_pairs([v[:, cols] for v in halo])
        sums = []
        for side in range(2):
            group = tile * 2 + side
            fill_group(
                band_ref,
                (group,),
                [own_pairs[rp, side] for rp in range(2)],
                [halo_pairs[rp, side] for rp in range(2)],
                base,
            )
            build_weights(w_ref, side, tap_ref, group)
            sums.append(convolve(band_ref, (group,), w_ref, side))
        for q, value in enumerate(split_lanes(*sums)):
            d_ref[q, :, cols] = (value + wide_ref[1:2, cols]) * conv_scale


def forward(valid, halo_valid, y1, y1h, w_in, wide, taps, order, dealt, deps=()):
    return launch(
        deps,
        functools.partial(forward_kernel, order=order, dealt=dealt),
        grid=(4,),
        out_shape=(
            jax.ShapeDtypeStruct((4, 256, 1024), f32),
            jax.ShapeDtypeStruct((16, 13, 5, 16, 256), bf16),
            jax.ShapeDtypeStruct((4, 256, 128), f32),
        ),
        in_specs=[SMEM, SMEM, whole((4, 256, 512)), whole((4, 64, 512))]
        + [pl.BlockSpec((64, 256), lambda t: (0, t))] * 8
        + [pl.BlockSpec((9, 256), lambda t: (0, t)), pl.BlockSpec((7, 7, 256), lambda t: (0, 0, t))],
        out_specs=(
            pl.BlockSpec((4, 256, 256), lambda t: (0, 0, t)),
            pl.BlockSpec((4, 13, 5, 16, 256), lambda t: (t, 0, 0, 0, 0)),
            whole((4, 256, 128)),
        ),
        scratch_shapes=[pltpu.VMEM((2, 16, 256, 256), bf16), pltpu.VMEM((512, 256), bf16)],
        cost_estimate=takes(24),
        name="forward",
    )(valid, halo_valid, y1, y1h, *w_in, wide, taps)


def middle_kernel(
    valid_ref,
    d_ref,
    j0_ref,
    xp_ref,
    gp_ref,
    oa,
    ob,
    oc,
    od,
    ea,
    eb4,
    ec,
    ed,
    ra,
    rb,
    first_ref,
    second_ref,
    g3_ref,
    g4_ref,
    wide_ref,
    out_ref,
    act_ref,
    dh_ref,
    y2_ref,
    df_ref,
    dz_ref,
    u_ref,
    dv_ref,
    dd_ref,
    dx2_ref,
    s512_ref,
    s2048_ref,
    s1024_ref,
    held_ref,
    w_out_ref,
    w_exp_ref,
    w_red_ref,
    g1_ref,
    g2_ref,
    *,
    order,
    dealt,
):
    q = pl.program_id(0)
    mask = chunk_mask(extents(valid_ref), q // 2, q % 2)
    out_bias, mix, gain, shift, red_bias, ffn = (
        wide_ref[5 + k // 2 : 6 + k // 2, k % 2 * 512 : k % 2 * 512 + 512] for k in range(6)
    )
    lane = lax.broadcasted_iota(i32, (256, 128), 1)
    is0 = (lane >= 32) & (lane < 64)
    is1 = lane >= 64

    @pl.when(q == 0)
    def _():
        s512_ref[...] = jnp.zeros_like(s512_ref)
        s2048_ref[...] = jnp.zeros_like(s2048_ref)
        s1024_ref[...] = jnp.zeros_like(s1024_ref)
        g1_ref[...] = jnp.zeros_like(g1_ref)
        g2_ref[...] = jnp.zeros_like(g2_ref)
        g1_ref[32:64, 64:128] = first_ref[...]
        g2_ref[64:128] = second_ref[...]
        number = own_number(dealt)
        place_rows(w_out_ref, (oa, ob, oc, od), order, number, 16)
        place_rows(w_exp_ref, (ea, eb4, ec, ed), order, number, 16)
        for p in range(32):
            at = pl.multiple_of(dealt_owner(p, "plain" if dealt else "none") * 64, 64)
            w_red_ref[pl.ds(at, 64), :] = (ra, rb)[p // 16][p % 16 * 64 : (p % 16 + 1) * 64, :]

    d01, d2, d3, d4 = d_ref[:, 0:128], d_ref[:, 128:256], d_ref[:, 256:512], d_ref[:, 512:1024]
    pointwise = pltpu.roll(j0_ref[...], 32, axis=1)
    u0 = jnp.where(is0, pointwise * d01, 0.0).astype(bf16)
    v1 = dot(u0, g1_ref[...]) + wide_ref[2:3, 0:128]
    u1 = jnp.where(is1, v1 * d01, 0.0).astype(bf16)
    v2 = dot(u1, g2_ref[...]) + wide_ref[2:3, 128:256]
    u2 = (v2 * d2).astype(bf16)
    v3 = dot(u2, g3_ref[...]) + wide_ref[2:3, 256:512]
    u3 = (v3 * d3).astype(bf16)
    v4 = dot(u3, g4_ref[...]) + wide_ref[2:3, 512:1024]
    u4 = (v4 * d4).astype(bf16)
    u_ref[:, 0:128] = jnp.where(is1, u1, u0)
    u_ref[:, 128:256] = u2
    u_ref[:, 256:512] = u3
    u_ref[:, 512:1024] = u4
    branch = dot(u4, w_out_ref[...]) + out_bias
    middle = xp_ref[...].astype(f32) + mask * mix * branch
    normed, inverse = normalize(middle)
    y2 = (mask * (normed * gain + shift)).astype(bf16)
    y2_ref[...] = y2
    grad = gp_ref[...].astype(f32)
    df = (mask * ffn * grad).astype(bf16)
    df_ref[...] = df
    reduced = red_bias
    back = jnp.zeros((256, 512), f32)
    for k in range(4):
        cols = slice(k * 512, (k + 1) * 512)
        hidden = dot(y2, w_exp_ref[:, cols]) + wide_ref[3 + k // 2 : 4 + k // 2, k % 2 * 512 : k % 2 * 512 + 512]
        cdf = 0.5 * (1.0 + lax.erf(hidden * inv_root_two))
        act = (hidden * cdf).astype(bf16)
        act_ref[:, cols] = act
        reduced = reduced + dot(act, w_red_ref[cols, :])
        density = jnp.exp(-0.5 * hidden * hidden) * inv_root_tau
        dh = (dot_nt(df, w_red_ref[cols, :]) * (cdf + hidden * density)).astype(bf16)
        dh_ref[:, cols] = dh
        s2048_ref[:, cols] += column_sum(dh.astype(f32))
        back = back + dot_nt(dh, w_exp_ref[:, cols])
    held_ref[q] = (middle + mask * ffn * reduced).astype(bf16)
    s512_ref[0:1] += column_sum(grad * mask * reduced)
    s512_ref[1:2] += column_sum(df.astype(f32))
    back = mask * back
    s512_ref[2:3] += column_sum(back * normed)
    s512_ref[3:4] += column_sum(back)
    dx2 = grad + norm_backward(back, normed, inverse, gain)
    dx2_ref[...] = dx2
    dz = (mask * mix * dx2).astype(bf16)
    dz_ref[...] = dz
    s512_ref[4:5] += column_sum(dx2 * mask * branch)
    s512_ref[5:6] += column_sum(dz.astype(f32))
    du4 = dot_nt(dz, w_out_ref[...])
    dv4 = (du4 * d4).astype(bf16)
    dd4 = (du4 * v4).astype(bf16)
    du3 = dot_nt(dv4, g4_ref[...])
    dv3 = (du3 * d3).astype(bf16)
    dd3 = (du3 * v3).astype(bf16)
    du2 = dot_nt(dv3, g3_ref[...])
    dv2 = (du2 * d2).astype(bf16)
    dd2 = (du2 * v2).astype(bf16)
    du1 = dot_nt(dv2, g2_ref[...])
    dv1 = (du1 * d01).astype(bf16)
    du0 = dot_nt(dv1, g1_ref[...])
    dpw = pltpu.roll(du0 * d01, 96, axis=1)
    dd01 = jnp.where(is1, du1 * v1, jnp.where(is0, du0 * pointwise, dpw)).astype(bf16)
    dv_ref[:, 0:128] = dv1
    dv_ref[:, 128:256] = dv2
    dv_ref[:, 256:512] = dv3
    dv_ref[:, 512:1024] = dv4
    dd_ref[:, 0:128] = dd01
    dd_ref[:, 128:256] = dd2
    dd_ref[:, 256:512] = dd3
    dd_ref[:, 512:1024] = dd4
    for k, ref in enumerate((dv_ref, dd_ref)):
        s1024_ref[k : k + 1] += column_sum(ref[...].astype(f32))

    @pl.when(q == 3)
    def _():
        unpermute(held_ref, out_ref)


def unpermute(held_ref, out_ref):
    perm = permutation()
    for b in range(4):
        block = jnp.concatenate([held_ref[k, b * 64 : (b + 1) * 64] for k in range(4)], axis=0)
        block = dot_tn(perm, block).astype(bf16)
        out_ref[0, b * 128 : (b + 1) * 128] = block[0:128]
        out_ref[1, b * 128 : (b + 1) * 128] = block[128:256]


def middle_call(valid, d, j0, xp, gp, w_exp, w_red, g1, g2, g3, g4, wide, order, dealt, deps=()):
    def chunk(width):
        return pl.BlockSpec((None, 256, width), lambda q: (q, 0, 0))

    def out(width, dtype=bf16):
        return jax.ShapeDtypeStruct((4, 256, width), dtype)

    widths = (2048, 2048, 512, 512, 512, 1024, 1024, 1024)
    return launch(
        deps,
        functools.partial(middle_kernel, order=order, dealt=dealt),
        grid=(4,),
        out_shape=(jax.ShapeDtypeStruct((2, 512, 512), bf16),)
        + tuple(out(w) for w in widths)
        + (
            out(512, f32),
            jax.ShapeDtypeStruct((8, 512), f32),
            jax.ShapeDtypeStruct((1, 2048), f32),
            jax.ShapeDtypeStruct((8, 1024), f32),
        ),
        in_specs=[SMEM, chunk(1024), chunk(128), chunk(512), chunk(512)]
        + [pl.BlockSpec((128, 512), lambda q: (0, 4))] * 4
        + [pl.BlockSpec((128, 2048), lambda q: (0, 0))] * 4
        + [whole((1024, 512))] * 2
        + [whole(v.shape) for v in (g1, g2, g3, g4, wide)],
        out_specs=(whole((2, 512, 512)),)
        + tuple(chunk(w) for w in widths)
        + (chunk(512), whole((8, 512)), whole((1, 2048)), whole((8, 1024))),
        scratch_shapes=[
            pltpu.VMEM((4, 256, 512), bf16),
            pltpu.VMEM((512, 512), bf16),
            pltpu.VMEM((512, 2048), bf16),
            pltpu.VMEM((2048, 512), bf16),
            pltpu.VMEM((128, 128), bf16),
            pltpu.VMEM((128, 128), bf16),
        ],
        cost_estimate=takes(30),
        name="middle",
    )(valid, d, j0, xp, gp, *w_exp, *w_exp, *w_red, g1, g2, g3, g4, wide)


def expand_grad_kernel(y2_ref, dh_ref, keep, send, sum_ref, *, order):
    sum_ref[...] = dot_tn(y2_ref[...], dh_ref[...])
    deal_rows((keep, send), (slice(None),), sum_ref, order, 16)


def expand_grad(y2, dh, order, deps=()):
    return launch(
        deps,
        functools.partial(expand_grad_kernel, order=order),
        grid=(4,),
        out_shape=(jax.ShapeDtypeStruct((256, 2048), bf16),) * 2,
        in_specs=[whole((1024, 512)), pl.BlockSpec((1024, 512), lambda k: (0, k))],
        out_specs=(pl.BlockSpec((256, 512), lambda k: (0, k)),) * 2,
        scratch_shapes=[pltpu.VMEM((512, 512), f32)],
        cost_estimate=takes(5),
        name="expand_grad",
    )(y2, dh)


def reduce_grad_kernel(act_ref, df_ref, u_ref, dz_ref, keep, send, red_ref, out_ref, *, order):
    step = pl.program_id(0)
    red_ref[pl.ds(pl.multiple_of(step * 512, 512), 512), :] = dot_tn(act_ref[...], df_ref[...])

    @pl.when(step == 0)
    def _():
        out_ref[...] = dot_tn(u_ref[...], dz_ref[...])

    @pl.when(step == 3)
    def _():
        for p in range(32):
            owner = dealt_owner(p, order)
            ref, first = (keep, send)[p // 16], p % 16 * 80
            ref[first : first + 64] = red_ref[pl.ds(pl.multiple_of(owner * 64, 64), 64), :].astype(bf16)
            ref[first + 64 : first + 80] = out_ref[pl.ds(pl.multiple_of(owner * 16, 16), 16), :].astype(bf16)


def reduce_grad(act, df, u, dz, order, deps=()):
    return launch(
        deps,
        functools.partial(reduce_grad_kernel, order=order),
        grid=(4,),
        out_shape=(jax.ShapeDtypeStruct((1280, 512), bf16),) * 2,
        in_specs=[
            pl.BlockSpec((1024, 512), lambda k: (0, k)),
            whole((1024, 512)),
            pl.BlockSpec((1024, 512), lambda k: (0, 1)),
            whole((1024, 512)),
        ],
        out_specs=(whole((1280, 512)),) * 2,
        scratch_shapes=[pltpu.VMEM((2048, 512), f32), pltpu.VMEM((512, 512), f32)],
        cost_estimate=takes(6),
        name="reduce_grad",
    )(act, df, u, dz)


def kernel_grad_kernel(dd_ref, band_ref, dk_ref):
    low = low_lanes((256, 128))
    low8 = low_lanes((8, 128))
    wide = diagonal(256)
    for tile in range(2):
        cols = slice(tile * 128, tile * 128 + 128)
        own = [dd_ref[q, :, cols].astype(f32) for q in range(4)]
        turned_own = [swap_lanes(v) for v in own]
        for side in range(2):
            group = tile * 2 + side
            halves = []
            for rp in range(2):
                if side == 0:
                    halves.append(jnp.where(low, own[2 * rp], turned_own[2 * rp + 1]))
                else:
                    halves.append(jnp.where(low, turned_own[2 * rp], own[2 * rp + 1]))
            left = jnp.concatenate(halves, axis=1).astype(bf16)
            rows = {}
            for ti in range(4):
                for tj in range(4):
                    cross = dot_tn(left, band_block(band_ref, (group,), ti, tj))
                    for rp in range(2):
                        half = jnp.where(wide, cross[:, rp * 128 : rp * 128 + 128], 0.0)
                        part = jnp.sum(half.reshape(4, 8, 8, 128), axis=1)
                        for out_rp in range(2):
                            i = 2 * ti + rp - out_rp
                            if 0 <= i <= 6:
                                for out_cp in range(2):
                                    key = (i, tj, out_cp)
                                    term = part[out_rp * 2 + out_cp]
                                    rows[key] = rows[key] + term if key in rows else term
            for i in range(7):
                turned = [swap_lanes(rows[i, tj, 1]) for tj in range(4)] + [jnp.zeros((8, 128), f32)]
                for tj in range(4):
                    value = rows[i, tj, 0] + jnp.where(low8, turned[tj], turned[tj + 1])
                    dk_ref[group, i * 4 + tj : i * 4 + tj + 1] = column_sum(value) * conv_scale
            dk_ref[group, 28:32] = jnp.zeros((4, 128), f32)


def kernel_grad(dd, band, deps=()):
    return launch(
        deps,
        kernel_grad_kernel,
        grid=(4,),
        out_shape=jax.ShapeDtypeStruct((16, 32, 128), f32),
        in_specs=[
            pl.BlockSpec((4, 256, 256), lambda t: (0, 0, t)),
            pl.BlockSpec((4, 13, 5, 16, 256), lambda t: (t, 0, 0, 0, 0)),
        ],
        out_specs=pl.BlockSpec((4, 32, 128), lambda t: (t, 0, 0)),
        cost_estimate=takes(13),
        name="kernel_grad",
    )(dd, band)


def gate_grads_kernel(u_ref, dv_ref, s512_ref, s2048_ref, s1024_ref, dk_ref, keep, send, small_ref, *, order):
    small_ref[0:256] = dot_tn(u_ref[:, 256:512], dv_ref[:, 512:1024])
    g3 = dot_tn(u_ref[:, 128:256], dv_ref[:, 256:512])
    small_ref[256:320, 0:256] = g3[0:64]
    small_ref[256:320, 256:512] = g3[64:128]
    g12 = dot_tn(u_ref[:, 0:128], dv_ref[:, 0:256])
    for k in range(4):
        cols = slice(k * 128, (k + 1) * 128)
        small_ref[320:336, cols] = g12[64 + 16 * k : 80 + 16 * k, 128:256]
        small_ref[336:344, cols] = g12[32 + 8 * k : 40 + 8 * k, 0:128]
        small_ref[384:512, cols] = dk_ref[k * 128 : (k + 1) * 128]
        small_ref[352 + k : 353 + k] = s2048_ref[:, k * 512 : (k + 1) * 512]
        small_ref[356 + k : 357 + k] = s1024_ref[k // 2 : k // 2 + 1, k % 2 * 512 : k % 2 * 512 + 512]
    small_ref[344:352] = s512_ref[...]
    small_ref[360:384] = jnp.zeros((24, 512), f32)
    deal_rows((keep, send), (slice(None),), small_ref, order, 16)


def gate_grads(u, dv, s512, s2048, s1024, dk, order, deps=()):
    return launch(
        deps,
        functools.partial(gate_grads_kernel, order=order),
        grid=(1,),
        out_shape=(jax.ShapeDtypeStruct((256, 512), bf16),) * 2,
        in_specs=[whole((1024, 512))] + [whole(v.shape) for v in (dv, s512, s2048, s1024, dk)],
        out_specs=(whole((256, 512)),) * 2,
        scratch_shapes=[pltpu.VMEM((512, 512), f32)],
        cost_estimate=takes(3),
        name="gate_grads",
    )(u, dv, s512, s2048, s1024, dk)


def unpack_kernel(own_ref, oth_ref, *rest):
    outs, (table_ref, all_ref) = rest[:-2], rest[-2:]
    in_ref, dk_ref, dwb_ref, g1_ref, g2_ref, g3_ref, g4_ref, gb_ref = outs[:8]
    outb_ref, mix_ref, gain_ref, shift_ref, expb_ref, redb_ref, ffn_ref = outs[8:]
    row = lax.axis_index("row")
    total = own_ref[0:16, 0:1024].astype(f32)
    for k in range(1, 16):
        total = total + own_ref[k * 16 : (k + 1) * 16, 0:1024].astype(f32)
    in_ref[...] = total
    for k in range(16):
        block = slice(k * 16, (k + 1) * 16)
        table_ref[pl.ds(pl.multiple_of((2 * k + row) * 16, 16), 16), :] = own_ref[block, 1024:1536]
        table_ref[pl.ds(pl.multiple_of((2 * k + 1 - row) * 16, 16), 16), :] = oth_ref[block, 1024:1536]
    all_ref[...] = table_ref[...].astype(f32)
    g4_ref[...] = all_ref[0:256]
    g3_ref[0:64] = all_ref[256:320, 0:256]
    g3_ref[64:128] = all_ref[256:320, 256:512]
    for k in range(4):
        cols = slice(k * 128, (k + 1) * 128)
        g2_ref[16 * k : 16 * k + 16] = all_ref[320:336, cols]
        g1_ref[8 * k : 8 * k + 8] = swap_lanes(all_ref[336:344, cols])[:, 0:64]
        expb_ref[k * 512 : (k + 1) * 512] = all_ref[352 + k : 353 + k].reshape(512)
    for k, ref in enumerate((ffn_ref, redb_ref, gain_ref, shift_ref, mix_ref, outb_ref)):
        ref[...] = all_ref[344 + k : 345 + k].reshape(512)

    def line(first):
        return jnp.concatenate([all_ref[first : first + 1], all_ref[first + 1 : first + 2]], axis=1)

    gb_ref[...] = line(356)[:, 64:1024].reshape(960)
    dwb_ref[...] = line(358)[:, 32:1024].reshape(992) * conv_scale
    low = low_lanes((32, 128))
    lane = lax.broadcasted_iota(i32, (32, 128), 1)
    rows = []
    for t in range(8):
        cols = slice(t // 2 * 128, t // 2 * 128 + 128)
        first = 384 + t % 2 * 64
        left = all_ref[first : first + 32, cols]
        right = all_ref[first + 32 : first + 64, cols]
        pair = (jnp.where(low, left, swap_lanes(right)), jnp.where(low, swap_lanes(left), right))
        rows.append([pltpu.roll(v, 96, axis=1) for v in pair])
    for t in range(8):
        size = 128 if t < 7 else 96
        for odd in range(2):
            value = jnp.where(lane < 96, rows[t][odd], rows[t + 1][odd]) if t < 7 else rows[t][odd]
            for i in range(7):
                for j in range(odd, 7, 2):
                    at = i * 4 + j // 2
                    dk_ref[i, j : j + 1, t * 128 : t * 128 + size] = value[at : at + 1, 0:size]


def unpack(own, oth, deps=()):
    vmem = pl.BlockSpec(memory_space=pltpu.VMEM)
    shapes = ((16, 1024), (7, 7, 992), (992,), (32, 64), (64, 128), (128, 256), (256, 512), (960,))
    shapes += ((512,),) * 4 + ((2048,), (512,), (512,))
    return launch(
        deps,
        unpack_kernel,
        out_shape=tuple(jax.ShapeDtypeStruct(v, f32) for v in shapes),
        in_specs=[vmem] * 2,
        out_specs=(vmem,) * len(shapes),
        scratch_shapes=[pltpu.VMEM((512, 512), bf16), pltpu.VMEM((512, 512), f32)],
        cost_estimate=takes(3),
        name="unpack",
    )(own, oth)


def conv_back_kernel(valid_ref, dd_ref, ddh_ref, tap_ref, df_ref, w_ref, back_ref, *, offset):
    step = pl.program_id(0)

    @pl.when(step == 0)
    def _():
        clear_weights(w_ref)

    base = halo_base()
    sizes = extents(valid_ref)
    masks = [chunk_mask(sizes, q // 2, q % 2) for q in range(4)]
    lane = lax.broadcasted_iota(i32, (256, 128), 1)
    keep = (lane < 32) & (step == 0)
    for tile in range(2):
        cols = slice(tile * 128, tile * 128 + 128)
        own = [dd_ref[q, :, cols].astype(f32) for q in range(4)]
        own_pairs = lane_pairs(own)
        halo_pairs = lane_pairs([ddh_ref[q, :, cols].astype(f32) for q in range(4)])
        sums = []
        for side in range(2):
            group = tile * 2 + side
            fill_group(
                back_ref,
                (group,),
                [own_pairs[rp, side] for rp in range(2)],
                [halo_pairs[rp, side] for rp in range(2)],
                base,
            )
            build_weights(w_ref, side, tap_ref, group, True)
            sums.append(convolve(back_ref, (group,), w_ref, side))
        for q, value in enumerate(split_lanes(*sums)):
            value = value * (masks[q] * conv_scale)
            if tile == 0 and offset == 0:
                value = jnp.where(keep, own[q], value)
            df_ref[q, :, cols] = value.astype(bf16)


def conv_back(valid, dd, ddh, taps, offset, steps, deps=()):
    return launch(
        deps,
        functools.partial(conv_back_kernel, offset=offset),
        grid=(steps,),
        out_shape=jax.ShapeDtypeStruct((4, 256, 256 * steps), bf16),
        in_specs=[
            SMEM,
            pl.BlockSpec((4, 256, 256), lambda t: (0, 0, t + offset)),
            pl.BlockSpec((4, 64, 256), lambda t: (0, 0, t + offset)),
            pl.BlockSpec((7, 7, 256), lambda t: (0, 0, t + offset)),
        ],
        out_specs=pl.BlockSpec((4, 256, 256), lambda t: (0, 0, t)),
        scratch_shapes=[pltpu.VMEM((2, 16, 256, 256), bf16), pltpu.VMEM((4, 13, 5, 16, 256), bf16)],
        cost_estimate=takes(4.5 * steps),
        name="conv_back",
    )(valid, dd, ddh, taps)


def in_grad_kernel(y1_ref, da_ref, db_ref, keep, send, sum_ref, *, order):
    for k, ref in enumerate((da_ref, db_ref)):
        sum_ref[k] = dot_tn(y1_ref[...], ref[...])
        deal_rows((keep, send), (slice(k * 512, (k + 1) * 512),), sum_ref.at[k], order, 16)


def in_grad(y1, da, db, order, deps=()):
    vmem = pl.BlockSpec(memory_space=pltpu.VMEM)
    return launch(
        deps,
        functools.partial(in_grad_kernel, order=order),
        out_shape=(jax.ShapeDtypeStruct((256, 1024), bf16),) * 2,
        in_specs=[vmem] * 3,
        out_specs=(vmem, vmem),
        scratch_shapes=[pltpu.VMEM((2, 512, 512), f32)],
        cost_estimate=takes(4),
        name="in_grad",
    )(y1, da, db)


def last_kernel(valid_ref, da_ref, db_ref, xp_ref, dx2_ref, *rest, order, dealt):
    weights, (wide_ref, out_ref, late_ref, held_ref, win_ref) = rest[:8], rest[8:]
    q = pl.program_id(0)

    @pl.when(q == 0)
    def _():
        late_ref[...] = jnp.zeros_like(late_ref)
        place_rows(win_ref, weights, order, own_number(dealt), 16)

    mask = chunk_mask(extents(valid_ref), q // 2, q % 2)
    da, db = da_ref[...], db_ref[...]
    late_ref[2:3] += column_sum(da.astype(f32))
    late_ref[3:4] += column_sum(db.astype(f32))
    grad = mask * (dot_nt(da, win_ref[:, 0:512]) + dot_nt(db, win_ref[:, 512:1024]))
    normed, inverse = normalize(xp_ref[...].astype(f32))
    late_ref[0:1] += column_sum(grad * normed)
    late_ref[1:2] += column_sum(grad)
    held_ref[q] = (dx2_ref[...] + norm_backward(grad, normed, inverse, wide_ref[8:9, 0:512])).astype(bf16)

    @pl.when(q == 3)
    def _():
        unpermute(held_ref, out_ref)


def last_call(valid, da, db, xp, dx2, w_in, wide, order, dealt, deps=()):
    def chunk(width):
        return pl.BlockSpec((None, 256, width), lambda q: (q, 0, 0))

    return launch(
        deps,
        functools.partial(last_kernel, order=order, dealt=dealt),
        grid=(4,),
        out_shape=(jax.ShapeDtypeStruct((2, 512, 512), bf16), jax.ShapeDtypeStruct((8, 512), f32)),
        in_specs=[SMEM] + [chunk(512)] * 4 + [whole((64, 1024))] * 8 + [whole(wide.shape)],
        out_specs=(whole((2, 512, 512)), whole((8, 512))),
        scratch_shapes=[pltpu.VMEM((4, 256, 512), bf16), pltpu.VMEM((512, 1024), bf16)],
        cost_estimate=takes(7),
        name="last",
    )(valid, da, db, xp, dx2, *w_in, wide)


def repeat(value):
    rows, cols = value.shape
    return jnp.broadcast_to(value[None], (16, rows, cols)).reshape(16 * rows, cols)


def join_kernel(*refs, counts):
    ins = list(refs[: sum(counts)])
    for out, count in zip(refs[sum(counts) :], counts):
        at = 0
        for _ in range(count):
            ref = ins.pop(0)
            out[at : at + ref.shape[0]] = ref[...]
            at += ref.shape[0]


def join(*lists, deps=()):
    vmem = pl.BlockSpec(memory_space=pltpu.VMEM)
    shapes = [(sum(v.shape[0] for v in group), group[0].shape[1]) for group in lists]
    return launch(
        deps,
        functools.partial(join_kernel, counts=[len(v) for v in lists]),
        out_shape=tuple(jax.ShapeDtypeStruct(v, bf16) for v in shapes),
        in_specs=[vmem] * sum(len(v) for v in lists),
        out_specs=(vmem,) * len(lists),
        cost_estimate=takes(1),
        name="join",
    )(*sum((list(v) for v in lists), []))


def add_kernel(a_ref, b_ref, out_ref):
    out_ref[...] = a_ref[...] + b_ref[...]


def add(a, b, deps=()):
    vmem = pl.BlockSpec(memory_space=pltpu.VMEM)
    return launch(
        deps,
        add_kernel,
        out_shape=jax.ShapeDtypeStruct(a.shape, a.dtype),
        in_specs=[vmem] * 2,
        out_specs=vmem,
        cost_estimate=takes(1),
        name="add",
    )(a, b)


def combine_kernel(*refs, parts):
    count = len(parts)
    ins, outs = refs[: 2 * count], list(refs[2 * count :])
    for k, n in enumerate(parts):
        for part in range(n):
            total = ins[2 * k][part, 0].astype(f32) + ins[2 * k + 1][part, 0].astype(f32)
            outs.pop(0)[0] = total.astype(bf16)


def combine(*items, deps=()):
    steps = next(n for n in (4, 2, 1) if all(v.shape[0] % (16 * n * p) == 0 for v, _, p in items))
    ins, in_specs, outs, out_specs = [], [], [], []
    for keep, got, parts in items:
        rows, cols = keep.shape
        size = rows // parts // steps
        ins += [v.reshape(parts, steps, size, cols) for v in (keep, got)]
        in_specs += [pl.BlockSpec((parts, 1, size, cols), lambda t: (0, t, 0, 0))] * 2
        outs += [jax.ShapeDtypeStruct((steps, size, cols), bf16)] * parts
        out_specs += [pl.BlockSpec((1, size, cols), lambda t: (t, 0, 0))] * parts
    *values, token = launch(
        deps,
        functools.partial(combine_kernel, parts=[p for _, _, p in items]),
        grid=(steps,),
        out_shape=tuple(outs),
        in_specs=in_specs,
        out_specs=tuple(out_specs),
        cost_estimate=takes(2),
        name="combine",
    )(*ins)
    return [v.reshape(-1, v.shape[-1]) for v in values] + [token]


def merge_kernel(ro_a, ro_b, e_a, e_b, keep, send):
    for z in range(4):
        ref, first = (keep, send)[z // 2], z % 2 * 144
        rows = slice(z * 80, (z + 1) * 80)
        ref[first : first + 80] = (ro_a[rows].astype(f32) + ro_b[rows].astype(f32)).astype(bf16)
        total = e_a[z * 16 : (z + 1) * 16].astype(f32) + e_b[z * 16 : (z + 1) * 16].astype(f32)
        for c in range(4):
            at = first + 80 + c * 16
            ref[at : at + 16] = total[:, c * 512 : (c + 1) * 512].astype(bf16)


def merge(ro_a, ro_b, e_a, e_b, deps=()):
    vmem = pl.BlockSpec(memory_space=pltpu.VMEM)
    return launch(
        deps,
        merge_kernel,
        out_shape=(jax.ShapeDtypeStruct((288, 512), bf16),) * 2,
        in_specs=[vmem] * 4,
        out_specs=(vmem,) * 2,
        cost_estimate=takes(2),
        name="merge",
    )(ro_a, ro_b, e_a, e_b)


def finish_kernel(a_ref, b_ref, red_ref, out_ref, exp_ref):
    red_ref[...] = a_ref[0:64].astype(f32) + b_ref[0:64].astype(f32)
    out_ref[...] = a_ref[64:80].astype(f32) + b_ref[64:80].astype(f32)
    for c in range(4):
        rows = slice(80 + c * 16, 96 + c * 16)
        exp_ref[:, c * 512 : (c + 1) * 512] = a_ref[rows].astype(f32) + b_ref[rows].astype(f32)


def finish(a, b, deps=()):
    vmem = pl.BlockSpec(memory_space=pltpu.VMEM)
    shapes = ((64, 512), (16, 512), (16, 2048))
    return launch(
        deps,
        finish_kernel,
        out_shape=tuple(jax.ShapeDtypeStruct(v, f32) for v in shapes),
        in_specs=[vmem] * 2,
        out_specs=(vmem,) * 3,
        cost_estimate=takes(1),
        name="finish",
    )(a, b)


def deal_kernel(i_a, i_b, s_a, s_b, out_ref):
    small = (s_a[...].astype(f32) + s_b[...].astype(f32)).astype(bf16)
    out_ref[:, 0:1024] = (i_a[...].astype(f32) + i_b[...].astype(f32)).astype(bf16)
    for k in range(16):
        out_ref[k * 16 : (k + 1) * 16, 1024:1536] = small


def deal(i_a, i_b, s_a, s_b, deps=()):
    vmem = pl.BlockSpec(memory_space=pltpu.VMEM)
    return launch(
        deps,
        deal_kernel,
        out_shape=jax.ShapeDtypeStruct((256, 1536), bf16),
        in_specs=[vmem] * 4,
        out_specs=vmem,
        cost_estimate=takes(2),
        name="deal",
    )(i_a, i_b, s_a, s_b)


def late_kernel(a_ref, b_ref, gain_ref, shift_ref, bias_ref):
    total = a_ref[...] + b_ref[...]
    gain_ref[...] = total[0:1].reshape(512)
    shift_ref[...] = total[1:2].reshape(512)
    bias_ref[0:512] = total[2:3].reshape(512)
    bias_ref[512:1024] = total[3:4].reshape(512)


def late_sums(a, b, deps=()):
    vmem = pl.BlockSpec(memory_space=pltpu.VMEM)
    return launch(
        deps,
        late_kernel,
        out_shape=tuple(jax.ShapeDtypeStruct((v,), f32) for v in (512, 512, 1024)),
        in_specs=[vmem] * 2,
        out_specs=(vmem,) * 3,
        cost_estimate=takes(1),
        name="late",
    )(a, b)


ROW = "row"


def img_bits():
    return lax.axis_size("img").bit_length() - 1


def swap_img(value, mask):
    return lax.ppermute(value, "img", [(k, k ^ mask) for k in range(lax.axis_size("img"))])


def swap_row(value):
    return lax.ppermute(value, "row", [(0, 1), (1, 0)])


def masks_of(stage):
    masks = [0]
    for bit in stage:
        masks = [m | v for m in masks for v in (0, 1 << bit)]
    return masks


def gather_order(groups):
    rel = [0]
    for bits in groups:
        rel = [m ^ r for m in masks_of(bits) for r in rel]
    return [2 * r + side for side in (0, 1) for r in rel]


def swaps(value, bits):
    return [value] + [swap_img(value, m) for m in masks_of(bits)[1:]]


def after(value, *others):
    return lax.optimization_barrier((value, others))[0]


def spread(value):
    return lax.all_to_all(value, "img", split_axis=0, concat_axis=0, tiled=True)


def sum_all(value):
    value = value + swap_row(value)
    for bit in range(img_bits() - 1):
        value = value + swap_img(value, 1 << bit)
    return value, swap_img(value, 1 << (img_bits() - 1))


def own_bit(bit):
    return lax.axis_index("row") if bit == ROW else (lax.axis_index("img") >> bit) & 1


def swap_bit(value, bit):
    return swap_row(value) if bit == ROW else swap_img(value, 1 << bit)


def plain_gather(shard):
    value = shard
    for bit in [ROW] + list(range(img_bits())):
        other = swap_bit(value, bit)
        mine = own_bit(bit) == 0
        value = jnp.concatenate([jnp.where(mine, value, other), jnp.where(mine, other, value)], axis=0)
    return value


def plain_scatter(value):
    for bit in list(range(img_bits()))[::-1] + [ROW]:
        half = value.shape[0] // 2
        mine = own_bit(bit) == 0
        first, second = value[:half], value[half:]
        sent = swap_bit(jnp.where(mine, second, first).astype(bf16), bit)
        value = jnp.where(mine, first, second).astype(f32) + sent.astype(f32)
    return value


def per_device(
    features,
    validity,
    upstream,
    normgain,
    normshift,
    inweight,
    inbias,
    dwkernel,
    dwbias,
    gatefirst,
    gatesecond,
    gatethird,
    gatefourth,
    gatebias,
    outweight,
    outbias,
    mixscale,
    mlpgain,
    mlpshift,
    expandweight,
    expandbias,
    reduceweight,
    reducebias,
    mlpscale,
):
    bits = img_bits()
    dealt = bits == 4
    lower = lax.axis_index("row") == 1

    x = features.reshape(2, 512, 512)
    g = upstream.reshape(2, 512, 512)
    valid = validity.reshape(32, 32)
    x_halo = swap_row(x)
    halo_valid = swap_row(valid)
    taps = jnp.pad(dwkernel.astype(f32), ((0, 0), (0, 0), (32, 0)))
    wide, token = gather_vectors(
        (inbias, dwbias, gatebias, expandbias),
        (outbias, mixscale, mlpgain, mlpshift, reducebias, mlpscale, normgain, normshift),
    )
    exp_out = jnp.concatenate([expandweight, outweight], axis=1)
    deep, flat_pair = (3, 2), (1, 0)
    if dealt:
        in_order = gather_order((deep, flat_pair))
        exp_order = gather_order((deep, (1,), (0,)))
        in_z, token = join(swaps(inweight, deep))
        exp_parts = swaps(exp_out, deep)
        red_own = spread(repeat(reduceweight))
        w_in = swaps(in_z, flat_pair)
        xp, gp, y1, y1h, token = prepare(valid, halo_valid, x, x_halo, g, wide, [token])
        exp_z, token = join(exp_parts, deps=[token] + w_in[1:])
        w_in = w_in + [swap_row(v) for v in w_in]
        exp_y, token = join(swaps(exp_z, (1,)), deps=[token])
        w_exp = swaps(exp_y, (0,))
        d, band, j0, token = forward(
            valid, halo_valid, y1, y1h, w_in, wide, taps, in_order, dealt, [token]
        )
        w_exp = w_exp + [swap_row(w_exp[0]), swap_row(after(w_exp[1], d))]
        w_red = [red_own, swap_row(after(red_own, d))]
    else:
        in_order = exp_order = list(range(32))
        w_in = jnp.split(plain_gather(inweight), 8, axis=0)
        w_exp = jnp.split(plain_gather(exp_out), 4, axis=0)
        w_red = jnp.split(plain_gather(reduceweight), 2, axis=0)
        xp, gp, y1, y1h, token = prepare(valid, halo_valid, x, x_halo, g, wide)
        d, band, j0, token = forward(valid, halo_valid, y1, y1h, w_in, wide, taps, in_order, dealt)
    (produced, act, dh, y2, df, dz, u, dv, dd, dx2, s512, s2048, s1024, token) = middle_call(
        valid, d, j0, xp, gp, w_exp, w_red, gatefirst, gatesecond, gatethird, gatefourth, wide, exp_order, dealt
    )
    dd_halo = swap_row(jnp.where(lower, dd[:, 0:64], dd[:, 192:256]))

    def flat(value):
        return value.reshape(1024, -1)

    r_order, e_order, plain = ((1, 0, 3, 2), (0, 1, 3, 2), "plain") if dealt else ("none",) * 3
    dk, token = kernel_grad(dd, band)
    dk = dk.reshape(512, 128)
    s_keep, s_send, token = gate_grads(flat(u), flat(dv), s512, s2048, s1024, dk, e_order, [token])
    if dealt:
        s_got = swap_row(s_send)
        e_keep, e_send, token = expand_grad(flat(y2), flat(dh), e_order, [token])
        e_got = swap_row(e_send)
        s_keep, s_send, token = combine((s_keep, s_got, 2), deps=[token])
        s_got = swap_img(s_send, 1)
        r_keep, r_send, token = reduce_grad(flat(act), flat(df), flat(u), flat(dz), r_order, [token])
        r_got = swap_row(r_send)
        s_keep, s_send, token = combine((s_keep, s_got, 2), deps=[token])
        s_got = swap_img(s_send, 2)
        df_a, token = conv_back(valid, dd, dd_halo, taps, 0, 2, [token])
        r_keep, r_send, e_keep, e_send, s_keep, s_send, token = combine(
            (r_keep, r_got, 2), (e_keep, e_got, 2), (s_keep, s_got, 2), deps=[token]
        )
        r_got, e_got, s_got = swap_img(r_send, 2), swap_img(e_send, 1), swap_img(s_send, 8)
        df_b, token = conv_back(valid, dd, dd_halo, taps, 2, 2, [token])
        s_keep, s_send, token = combine((s_keep, s_got, 2), deps=[token])
        s_got = swap_img(s_send, 4)
        i_keep, i_send, token = in_grad(flat(y1), flat(df_a), flat(df_b), plain, [token])
        i_got = swap_row(i_send)
        r_keep, r_send, e_keep, e_send, token = combine((r_keep, r_got, 2), (e_keep, e_got, 2), deps=[token])
        r_got, e_got = swap_img(r_send, 1), swap_img(e_send, 2)
        dealt_rows, token = deal(i_keep, i_got, s_keep, s_got, [token])
        mixed = spread(dealt_rows)
        fgrad, late, token = last_call(valid, df_a, df_b, xp, dx2, w_in, wide, in_order, dealt, [token])
        got = swap_row(late)
        m_keep, m_send, token = merge(r_keep, r_got, e_keep, e_got, [token])
        m_got = swap_img(m_send, 8)
        late, token = add(late, got, [token])
        got = swap_img(late, 1)
        late, token = add(late, got, [token])
        got = swap_img(late, 2)
        late, token = add(late, got, [token])
        got = swap_img(late, 4)
        m_keep, m_send, token = combine((m_keep, m_got, 2), deps=[token])
        m_got = swap_img(m_send, 4)
        late, token = add(late, got, [token])
        got = swap_img(late, 8)
        red_sum, out_sum, exp_sum, token = finish(m_keep, m_got, [token])
        sums = late_sums(late, got, [token])
        own, oth = mixed, swap_row(after(mixed, late))
    else:

        def total(parts, rows):
            value = jnp.concatenate(parts, axis=0)
            return plain_scatter(value.reshape(32, -1, value.shape[1])[:, rows].reshape(-1, value.shape[1]))

        everything = slice(None)
        e_parts = expand_grad(flat(y2), flat(dh), e_order)[:2]
        r_parts = reduce_grad(flat(act), flat(df), flat(u), flat(dz), r_order)[:2]
        df_a, _ = conv_back(valid, dd, dd_halo, taps, 0, 2)
        df_b, _ = conv_back(valid, dd, dd_halo, taps, 2, 2)
        i_parts = in_grad(flat(y1), flat(df_a), flat(df_b), plain)[:2]
        fgrad, late, token = last_call(valid, df_a, df_b, xp, dx2, w_in, wide, in_order, dealt)
        sums = late_sums(*sum_all(late))
        exp_sum, in_sum = total(e_parts, everything), total(i_parts, everything)
        red_sum, out_sum = total(r_parts, slice(0, 64)), total(r_parts, slice(64, 80))
        small = plain_gather(total((s_keep, s_send), everything).astype(bf16)).reshape(16, 2, 16, 512)
        lower_row = lax.axis_index("row")
        own, oth = (
            jnp.pad(lax.dynamic_index_in_dim(small, v, 1, keepdims=False).reshape(256, 512), ((0, 0), (1024, 0)))
            for v in (lower_row, 1 - lower_row)
        )

    unpacked = unpack(own, oth)
    if dealt:
        in_sum = unpacked[0]
    dk_sum, dwb_sum, gate1, gate2, gate3, gate4, gb_sum, outb, mix, gain, shift, expb, redb, ffn = unpacked[1:-1]
    return (
        produced.reshape(features.shape),
        fgrad.reshape(features.shape),
        sums[0],
        sums[1],
        in_sum,
        sums[2],
        dk_sum,
        dwb_sum,
        gate1,
        gate2,
        gate3,
        gate4,
        gb_sum,
        out_sum,
        outb,
        mix,
        gain,
        shift,
        exp_sum,
        expb,
        red_sum,
        redb,
        ffn,
    )


def solution(mesh):
    band = P("img", "row", None, None)
    rows = P(("img", "row"), None)
    copy = P()
    ins = [band, P("img", "row", None), band] + [copy] * 21
    for k in (5, 14, 19, 21):
        ins[k] = rows
    outs = [band, band] + [copy] * 21
    for k in (4, 13, 18, 20):
        outs[k] = rows
    return jax.shard_map(per_device, mesh=mesh, in_specs=tuple(ins), out_specs=tuple(outs), check_vma=False)
```

```python
import functools
import math

import jax
import jax.numpy as jnp
from jax import lax
from jax.experimental import pallas as pl
from jax.experimental.pallas import tpu as pltpu
from jax.sharding import PartitionSpec as P

f32 = jnp.float32
bf16 = jnp.bfloat16
i32 = jnp.int32
norm_eps = 1e-06
conv_scale = 1.0 / 3.0
inv_root_two = 1.0 / math.sqrt(2.0)
inv_root_tau = 1.0 / math.sqrt(2.0 * math.pi)
vmem_bytes = 60 * 1024 * 1024


def dot(left, right):
    return jnp.dot(left, right, preferred_element_type=f32)


def dot_tn(left, right):
    return lax.dot_general(left, right, (((0,), (0,)), ((), ())), preferred_element_type=f32)


def dot_nt(left, right):
    return lax.dot_general(left, right, (((1,), (1,)), ((), ())), preferred_element_type=f32)


def column_sum(values):
    return jnp.sum(values, axis=0, keepdims=True)


def permutation():
    out = lax.broadcasted_iota(i32, (256, 256), 0)
    src = lax.broadcasted_iota(i32, (256, 256), 1)
    row_par, col_par = out >> 7, (out >> 6) & 1
    pair, ccp, img, blk = (out >> 5) & 1, (out >> 4) & 1, (out >> 3) & 1, out & 7
    want = img * 128 + (2 * pair + row_par) * 32 + 4 * blk + 2 * ccp + col_par
    return (src == want).astype(f32).astype(bf16)


def normalize(values):
    center = jnp.mean(values, axis=-1, keepdims=True)
    shifted = values - center
    spread = jnp.mean(shifted * shifted, axis=-1, keepdims=True)
    inverse = lax.rsqrt(spread + norm_eps)
    return shifted * inverse, inverse


def norm_backward(grad_norm, normed, inverse, gain):
    scaled = grad_norm * gain
    return inverse * (
        scaled
        - jnp.mean(scaled, axis=-1, keepdims=True)
        - normed * jnp.mean(scaled * normed, axis=-1, keepdims=True)
    )


def extents(valid_ref):
    heights = [sum(valid_ref[16 * n + r, 0] for r in range(16)) for n in range(2)]
    widths = [sum(valid_ref[16 * n, c] for c in range(32)) for n in range(2)]
    return heights, widths


def chunk_mask(sizes, row_par, col_par, count=256, first_row=0):
    (high_a, high_b), (wide_a, wide_b) = sizes
    at = lax.broadcasted_iota(i32, (count, 1), 0)
    pair, ccp, img, blk = at >> 5, (at >> 4) & 1, (at >> 3) & 1, at & 7
    row = 2 * pair + row_par + first_row
    col = 4 * blk + 2 * ccp + col_par
    high = jnp.where(img == 1, high_b, high_a)
    wide = jnp.where(img == 1, wide_b, wide_a)
    return jnp.where((row < high) & (col < wide), 1.0, 0.0).astype(f32)


def pair_mask(sizes, row_par):
    return jnp.concatenate([chunk_mask(sizes, row_par, col_par) for col_par in range(2)], axis=0)


def halo_sizes(valid_ref, halo_ref):
    heights, widths = extents(valid_ref)
    below, _ = extents(halo_ref)
    upper = lax.axis_index("row") == 0
    return [jnp.where(upper, h, 4) for h in below], widths


def is_upper():
    return jnp.where(lax.axis_index("row") == 0, 1.0, 0.0).astype(f32)


def vectors_kernel(in_ref, dw_ref, gate_ref, exp_ref, *rest):
    small, out_ref = rest[:8], rest[8]

    def line(ref):
        return ref[...].astype(f32).reshape(1, ref.shape[0])

    out_ref[0:1] = line(in_ref)
    out_ref[1:2, 0:32] = jnp.zeros((1, 32), f32)
    out_ref[1:2, 32:1024] = line(dw_ref)
    out_ref[2:3, 0:64] = jnp.zeros((1, 64), f32)
    out_ref[2:3, 64:1024] = line(gate_ref)
    wide = line(exp_ref)
    out_ref[3:4] = wide[:, 0:1024]
    out_ref[4:5] = wide[:, 1024:2048]
    for k, ref in enumerate(small):
        out_ref[5 + k // 2 : 6 + k // 2, k % 2 * 512 : k % 2 * 512 + 512] = line(ref)


def gather_vectors(large, small, deps=()):
    vmem = pl.BlockSpec(memory_space=pltpu.VMEM)
    return launch(
        deps,
        vectors_kernel,
        out_shape=jax.ShapeDtypeStruct((9, 1024), f32),
        in_specs=[vmem] * 12,
        out_specs=vmem,
        cost_estimate=takes(1),
        name="vectors",
    )(*large, *small)


def prepare_kernel(valid_ref, halo_valid_ref, x_ref, xh_ref, g_ref, vec_ref, xp_ref, gp_ref, y1_ref, y1h_ref, y1t_ref):
    perm = permutation()
    gain, shift = vec_ref[8:9, 0:512], vec_ref[8:9, 512:1024]
    own, halo = extents(valid_ref), halo_sizes(valid_ref, halo_valid_ref)
    start = pl.multiple_of(lax.axis_index("row") * 384, 128)
    for b in range(5):
        if b == 4:
            rows = pl.ds(start, 128)
            block = jnp.concatenate([xh_ref[0, rows], xh_ref[1, rows]], axis=0)
        else:
            rows = slice(b * 128, (b + 1) * 128)
            block = jnp.concatenate([x_ref[0, rows], x_ref[1, rows]], axis=0)
            gblock = dot(perm, jnp.concatenate([g_ref[0, rows], g_ref[1, rows]], axis=0)).astype(bf16)
        block = dot(perm, block)
        lowered = block.astype(bf16)
        normed, _ = normalize(block)
        value = normed * gain + shift
        for q in range(4):
            part = slice(q * 64, (q + 1) * 64)
            if b == 4:
                y1h_ref[q] = (chunk_mask(halo, q // 2, q % 2, 64) * value[part]).astype(bf16)
            else:
                dest = slice(b * 64, (b + 1) * 64)
                xp_ref[q, dest] = lowered[part]
                gp_ref[q, dest] = gblock[part]
                y1_ref[q, dest] = (chunk_mask(own, q // 2, q % 2, 64, 4 * b) * value[part]).astype(bf16)
    for q in range(4):
        y1t_ref[:, q * 256 : (q + 1) * 256] = y1_ref[q].T


def whole(shape):
    return pl.BlockSpec(shape, lambda *_: (0,) * len(shape))


SMEM = pl.BlockSpec(memory_space=pltpu.SMEM)


def params():
    return pltpu.CompilerParams(vmem_limit_bytes=vmem_bytes)


def takes(micros):
    return pl.CostEstimate(flops=int(micros * 1.0e9), bytes_accessed=0, transcendentals=0)


def launch(deps, kernel, *, out_shape, in_specs, out_specs, **rest):
    single = not isinstance(out_shape, tuple)
    shapes = (out_shape,) if single else out_shape
    specs = (out_specs,) if single else out_specs
    anywhere = pl.BlockSpec(memory_space=pl.ANY)
    count = len(in_specs)

    def body(*refs):
        at = count + len(deps)
        kernel(*refs[:count], *refs[at : at + len(shapes)], *refs[at + len(shapes) + 1 :])

    call = pl.pallas_call(
        body,
        out_shape=(*shapes, jax.ShapeDtypeStruct((8, 128), f32)),
        in_specs=list(in_specs) + [anywhere] * len(deps),
        out_specs=(*specs, anywhere),
        compiler_params=params(),
        **rest,
    )
    return lambda *args: call(*args, *deps)


def own_number(dealt):
    return lax.axis_index("img") * 2 + lax.axis_index("row") if dealt else 0


def place_rows(scratch, refs, order, number, rows):
    each = 32 // len(refs)
    for k, ref in enumerate(refs):
        for b in range(each):
            at = pl.multiple_of((order[k * each + b] ^ number) * rows, 16)
            scratch[pl.ds(at, rows), :] = ref[b * rows : (b + 1) * rows, :]


def dealt_owner(place, order):
    if order == "none":
        return place
    if order == "plain":
        return (2 * (place % 16) + place // 16) ^ lax.axis_index("row")
    return (2 * masks_of(order)[place % 16] + place // 16) ^ own_number(True)


def deal_rows(outs, lead, value_ref, order, rows):
    for p in range(32):
        at = pl.multiple_of(dealt_owner(p, order) * rows, 16)
        outs[p // 16][(slice(p % 16 * rows, (p % 16 + 1) * rows),) + lead] = value_ref[pl.ds(at, rows), :].astype(bf16)


def prepare(valid, halo_valid, x, xh, g, wide, deps=()):
    vmem = pl.BlockSpec(memory_space=pltpu.VMEM)
    return launch(
        deps,
        prepare_kernel,
        out_shape=(
            jax.ShapeDtypeStruct((4, 256, 512), bf16),
            jax.ShapeDtypeStruct((4, 256, 512), bf16),
            jax.ShapeDtypeStruct((4, 256, 512), bf16),
            jax.ShapeDtypeStruct((4, 64, 512), bf16),
            jax.ShapeDtypeStruct((512, 1024), bf16),
        ),
        in_specs=[SMEM] * 2 + [vmem] * 4,
        out_specs=(vmem,) * 5,
        cost_estimate=takes(4),
        name="prepare",
    )(valid, halo_valid, x, xh, g, wide)


def low_lanes(shape):
    return lax.broadcasted_iota(i32, shape, len(shape) - 1) < 64


def swap_lanes(value):
    return pltpu.roll(value, 64, axis=1)


def shifted_block(value, step):
    if step == 0:
        return value
    blk = lax.broadcasted_iota(i32, value.shape, 1)
    if step > 0:
        return jnp.where(blk < 7, pltpu.roll(value, 7, axis=1), 0.0)
    return jnp.where(blk > 0, pltpu.roll(value, 1, axis=1), 0.0)


ODD = ((-1, 0), (-1, 1), (0, 0), (0, 1), (1, 0))
EVEN = ((-1, 1), (0, 0), (0, 1), (1, 0), (1, 1))


def lane_pairs(chunks):
    res = {}
    for row_par in range(2):
        odd, even = chunks[2 * row_par + 1], chunks[2 * row_par]
        odd_s, even_s = swap_lanes(odd), swap_lanes(even)
        res[row_par, 0] = (odd, even_s)
        res[row_par, 1] = (odd_s, even)
    return res


def fill_band(ref, lead, pairs, n, start, row_par):
    odd, even = (v.reshape(n, 2, 2, 8, 128) for v in pairs)
    half = 1 - row_par
    lanes = slice(half * 128, half * 128 + 128)
    low = low_lanes((n * 2, 8, 128))
    cache = {}

    def take(name, value, step, ccp):
        if (name, step, ccp) not in cache:
            cache[name, step, ccp] = shifted_block(value[:, ccp].reshape(n * 2, 8, 128), step)
        return cache[name, step, ccp]

    def write(k):
        both = jnp.where(low, take("o", odd, *ODD[k]), take("e", even, *EVEN[k]))
        ref[lead + (slice(start, start + n), k, slice(None), lanes)] = both.reshape(n, 16, 128).astype(bf16)

    return [functools.partial(write, k) for k in range(5)]


def fill_group(ref, lead, own, halo, upper):
    steps = []
    for row_par in range(2):
        first = 2 + row_par
        steps += fill_band(ref, lead, own[row_par], 8, first, row_par)
        steps += fill_band(ref, lead, [v * (1.0 - upper) for v in halo[row_par]], 2, first - 2, row_par)
        steps += fill_band(ref, lead, [v * upper for v in halo[row_par]], 2, first + 8, row_par)
    return steps


def diagonal(rows):
    return (lax.broadcasted_iota(i32, (rows, 128), 0) % 64) == (lax.broadcasted_iota(i32, (rows, 128), 1) % 64)


def build_weights(w_ref, slot, tap_ref, group, flip=False):
    mask = diagonal(64)
    low = low_lanes((1, 128))
    tile, side = group // 2, group % 2
    cols = slice(tile * 128, tile * 128 + 128)

    def write(i, jj):
        rows = tap_ref[6 - i if flip else i, :, cols]
        turned = swap_lanes(rows)
        first, second = (rows, turned) if side == 0 else (turned, rows)
        a, b = (6 - jj, 7 - jj) if flip else (jj, jj - 1)
        left = first[a : a + 1] if 0 <= a <= 6 else jnp.zeros((1, 128), f32)
        right = second[b : b + 1] if 0 <= b <= 6 else jnp.zeros((1, 128), f32)
        vector = jnp.where(low, left, right)
        block = jnp.where(mask, jnp.broadcast_to(vector, (64, 128)), 0.0).astype(bf16)
        for out_par in range(2):
            top = i + out_par
            ti, rp, tj, cp = top // 2, top % 2, jj // 2, jj % 2
            at = (rp * 2 + cp) * 64
            w_ref[slot, ti * 4 + tj, at : at + 64, out_par * 128 : out_par * 128 + 128] = block

    return [functools.partial(write, i, jj) for i in range(7) for jj in range(8)]


def clear_weights(w_ref):
    for slot in range(2):
        for tj in range(4):
            w_ref[slot, tj, 0:128, 128:256] = jnp.zeros((128, 128), bf16)
            w_ref[slot, 12 + tj, 128:256, 0:128] = jnp.zeros((128, 128), bf16)


def band_block(ref, lead, ti, tj):
    return ref[lead + (slice(1 + ti, 9 + ti), slice(tj, tj + 2))].reshape(256, 256)


def convolve(ref, lead, w_ref, slot, meanwhile):
    total = None
    for k in range(16):
        part = dot(band_block(ref, lead, k // 4, k % 4), w_ref[slot, k])
        total = part if total is None else total + part
        for step in meanwhile[len(meanwhile) * k // 16 : len(meanwhile) * (k + 1) // 16]:
            step()
    return total


def convolve_groups(ref, w_ref, tap_ref, own, halo, upper, flip):
    def steps(group):
        cols = slice(group // 2 * 128, group // 2 * 128 + 128)
        own_pairs = lane_pairs([v[:, cols] for v in own])
        halo_pairs = lane_pairs([v[:, cols] for v in halo])
        side = group % 2
        band = [own_pairs[rp, side] for rp in range(2)], [halo_pairs[rp, side] for rp in range(2)]
        return fill_group(ref, (group,), *band, upper) + build_weights(w_ref, side, tap_ref, group, flip)

    for step in steps(0):
        step()
    return [convolve(ref, (group,), w_ref, group % 2, steps(group + 1) if group < 3 else []) for group in range(4)]


def split_lanes(low_group, high_group):
    low = low_lanes((256, 128))
    chunks = []
    for rp in range(2):
        lg = low_group[:, rp * 128 : rp * 128 + 128]
        hg = high_group[:, rp * 128 : rp * 128 + 128]
        chunks.append(jnp.where(low, lg, swap_lanes(hg)))
        chunks.append(jnp.where(low, swap_lanes(lg), hg))
    return chunks


def forward_kernel(valid_ref, halo_valid_ref, y1_ref, y1h_ref, *rest, order, dealt):
    weights, (wide_ref, tap_ref, d_ref, band_ref, j0_ref, w_ref, win_ref) = rest[:8], rest[8:]
    step = pl.program_id(0)

    @pl.when(step == 0)
    def _():
        clear_weights(w_ref)

    upper = is_upper()
    sizes, around = extents(valid_ref), halo_sizes(valid_ref, halo_valid_ref)
    place_rows(win_ref, weights, order, own_number(dealt), 16)
    weight = win_ref[...]
    bias = wide_ref[0:1]
    joined = dot(y1_ref[...].reshape(1024, 512), weight) + bias
    joined = [joined[q * 256 : (q + 1) * 256] for q in range(4)]
    around_rows = dot(y1h_ref[...].reshape(256, 512), weight) + bias

    @pl.when(step == 0)
    def _():
        for q in range(4):
            j0_ref[q] = joined[q][:, 0:128]

    own, halo = [], []
    for q in range(4):
        own.append((joined[q] * chunk_mask(sizes, q // 2, q % 2)).astype(bf16).astype(f32))
        part = around_rows[q * 64 : (q + 1) * 64]
        halo.append((part * chunk_mask(around, q // 2, q % 2, 64)).astype(bf16).astype(f32))
    sums = convolve_groups(band_ref, w_ref, tap_ref, own, halo, upper, False)
    for tile in range(2):
        cols = slice(tile * 128, tile * 128 + 128)
        for q, value in enumerate(split_lanes(*sums[2 * tile : 2 * tile + 2])):
            d_ref[q, :, cols] = (value + wide_ref[1:2, cols]) * conv_scale


def forward(valid, halo_valid, y1, y1h, w_in, wide, taps, order, dealt, deps=()):
    return launch(
        deps,
        functools.partial(forward_kernel, order=order, dealt=dealt),
        grid=(4,),
        out_shape=(
            jax.ShapeDtypeStruct((4, 256, 1024), f32),
            jax.ShapeDtypeStruct((16, 13, 5, 16, 256), bf16),
            jax.ShapeDtypeStruct((4, 256, 128), f32),
        ),
        in_specs=[SMEM, SMEM, whole((4, 256, 512)), whole((4, 64, 512))]
        + [pl.BlockSpec((64, 256), lambda t: (0, t))] * 8
        + [pl.BlockSpec((9, 256), lambda t: (0, t)), pl.BlockSpec((7, 7, 256), lambda t: (0, 0, t))],
        out_specs=(
            pl.BlockSpec((4, 256, 256), lambda t: (0, 0, t)),
            pl.BlockSpec((4, 13, 5, 16, 256), lambda t: (t, 0, 0, 0, 0)),
            whole((4, 256, 128)),
        ),
        scratch_shapes=[pltpu.VMEM((2, 16, 256, 256), bf16), pltpu.VMEM((512, 256), bf16)],
        cost_estimate=takes(24),
        name="forward",
    )(valid, halo_valid, y1, y1h, *w_in, wide, taps)


def middle_kernel(
    valid_ref,
    d_ref,
    j0_ref,
    xp_ref,
    gp_ref,
    oa,
    ob,
    oc,
    od,
    ea,
    eb4,
    ec,
    ed,
    ra,
    rb,
    first_ref,
    second_ref,
    g3_ref,
    g4_ref,
    wide_ref,
    out_ref,
    act_ref,
    y2_ref,
    u_ref,
    dh_ref,
    df_ref,
    dz_ref,
    dv_ref,
    dd_ref,
    dx2_ref,
    s512_ref,
    s2048_ref,
    s1024_ref,
    held_ref,
    w_out_ref,
    w_exp_ref,
    w_red_ref,
    g1_ref,
    g2_ref,
    *,
    order,
    dealt,
):
    q = pl.program_id(0)
    mask = pair_mask(extents(valid_ref), q)
    out_bias, mix, gain, shift, red_bias, ffn = (
        wide_ref[5 + k // 2 : 6 + k // 2, k % 2 * 512 : k % 2 * 512 + 512] for k in range(6)
    )
    lane = lax.broadcasted_iota(i32, (512, 128), 1)
    is0 = (lane >= 32) & (lane < 64)
    is1 = lane >= 64

    @pl.when(q == 0)
    def _():
        s512_ref[...] = jnp.zeros_like(s512_ref)
        s2048_ref[...] = jnp.zeros_like(s2048_ref)
        s1024_ref[...] = jnp.zeros_like(s1024_ref)
        g1_ref[...] = jnp.zeros_like(g1_ref)
        g2_ref[...] = jnp.zeros_like(g2_ref)
        g1_ref[32:64, 64:128] = first_ref[...]
        g2_ref[64:128] = second_ref[...]
        number = own_number(dealt)
        place_rows(w_out_ref, (oa, ob, oc, od), order, number, 16)
        place_rows(w_exp_ref, (ea, eb4, ec, ed), order, number, 16)
        for p in range(32):
            owner = dealt_owner(p, "plain" if dealt else "none")
            ref, first = (ra, rb)[p // 16], p % 16 * 64
            w_red_ref[pl.ds(pl.multiple_of(owner * 64, 64), 64), :] = ref[first : first + 64, :]

    d01, d2, d3, d4 = d_ref[:, 0:128], d_ref[:, 128:256], d_ref[:, 256:512], d_ref[:, 512:1024]
    pointwise = pltpu.roll(j0_ref[...], 32, axis=1)
    u0 = jnp.where(is0, pointwise * d01, 0.0).astype(bf16)
    v1 = dot(u0, g1_ref[...]) + wide_ref[2:3, 0:128]
    u1 = jnp.where(is1, v1 * d01, 0.0).astype(bf16)
    v2 = dot(u1, g2_ref[...]) + wide_ref[2:3, 128:256]
    u2 = (v2 * d2).astype(bf16)
    v3 = dot(u2, g3_ref[...]) + wide_ref[2:3, 256:512]
    u3 = (v3 * d3).astype(bf16)
    v4 = dot(u3, g4_ref[...]) + wide_ref[2:3, 512:1024]
    u4 = (v4 * d4).astype(bf16)
    u_ref[0:128] = jnp.where(is1, u1, u0).T
    u_ref[128:256] = u2.T
    u_ref[256:512] = u3.T
    u_ref[512:1024] = u4.T
    branch = dot(u4, w_out_ref[...]) + out_bias
    middle = xp_ref[...].astype(f32) + mask * mix * branch
    normed, inverse = normalize(middle)
    y2 = (mask * (normed * gain + shift)).astype(bf16)
    y2_ref[...] = y2.T
    grad = gp_ref[...].astype(f32)
    df = (mask * ffn * grad).astype(bf16)
    df_ref[...] = df
    reduced = red_bias
    back = jnp.zeros((512, 512), f32)
    for k in range(4):
        cols = slice(k * 512, (k + 1) * 512)
        hidden = dot(y2, w_exp_ref[:, cols]) + wide_ref[3 + k // 2 : 4 + k // 2, k % 2 * 512 : k % 2 * 512 + 512]
        cdf = 0.5 * (1.0 + lax.erf(hidden * inv_root_two))
        act = (hidden * cdf).astype(bf16)
        act_ref[cols, :] = act.T
        reduced = reduced + dot(act, w_red_ref[cols, :])
        density = jnp.exp(-0.5 * hidden * hidden) * inv_root_tau
        dh = (dot_nt(df, w_red_ref[cols, :]) * (cdf + hidden * density)).astype(bf16)
        dh_ref[:, cols] = dh
        s2048_ref[:, cols] += column_sum(dh.astype(f32))
        back = back + dot_nt(dh, w_exp_ref[:, cols])
    held_ref[pl.ds(2 * q, 2)] = (middle + mask * ffn * reduced).astype(bf16).reshape(2, 256, 512)
    s512_ref[0:1] += column_sum(grad * mask * reduced)
    s512_ref[1:2] += column_sum(df.astype(f32))
    back = mask * back
    s512_ref[2:3] += column_sum(back * normed)
    s512_ref[3:4] += column_sum(back)
    dx2 = grad + norm_backward(back, normed, inverse, gain)
    dx2_ref[...] = dx2
    dz = (mask * mix * dx2).astype(bf16)
    dz_ref[...] = dz
    s512_ref[4:5] += column_sum(dx2 * mask * branch)
    s512_ref[5:6] += column_sum(dz.astype(f32))
    du4 = dot_nt(dz, w_out_ref[...])
    dv4 = (du4 * d4).astype(bf16)
    dd4 = (du4 * v4).astype(bf16)
    du3 = dot_nt(dv4, g4_ref[...])
    dv3 = (du3 * d3).astype(bf16)
    dd3 = (du3 * v3).astype(bf16)
    du2 = dot_nt(dv3, g3_ref[...])
    dv2 = (du2 * d2).astype(bf16)
    dd2 = (du2 * v2).astype(bf16)
    du1 = dot_nt(dv2, g2_ref[...])
    dv1 = (du1 * d01).astype(bf16)
    du0 = dot_nt(dv1, g1_ref[...])
    dpw = pltpu.roll(du0 * d01, 96, axis=1)
    dd01 = jnp.where(is1, du1 * v1, jnp.where(is0, du0 * pointwise, dpw)).astype(bf16)
    dv_ref[:, 0:128] = dv1
    dv_ref[:, 128:256] = dv2
    dv_ref[:, 256:512] = dv3
    dv_ref[:, 512:1024] = dv4
    dd_ref[:, 0:128] = dd01
    dd_ref[:, 128:256] = dd2
    dd_ref[:, 256:512] = dd3
    dd_ref[:, 512:1024] = dd4
    for k, ref in enumerate((dv_ref, dd_ref)):
        s1024_ref[k : k + 1] += column_sum(ref[...].astype(f32))

    @pl.when(q == 1)
    def _():
        unpermute(held_ref, out_ref)


def unpermute(held_ref, out_ref):
    perm = permutation()
    for b in range(4):
        block = jnp.concatenate([held_ref[k, b * 64 : (b + 1) * 64] for k in range(4)], axis=0)
        block = dot_tn(perm, block).astype(bf16)
        out_ref[0, b * 128 : (b + 1) * 128] = block[0:128]
        out_ref[1, b * 128 : (b + 1) * 128] = block[128:256]


def middle_call(valid, d, j0, xp, gp, w_exp, w_red, g1, g2, g3, g4, wide, order, dealt, deps=()):
    def chunk(width):
        return pl.BlockSpec((512, width), lambda q: (q, 0))

    def out(width, dtype=bf16):
        return jax.ShapeDtypeStruct((1024, width), dtype)

    def turned(rows):
        return pl.BlockSpec((rows, 512), lambda q: (0, q))

    def out_turned(rows):
        return jax.ShapeDtypeStruct((rows, 1024), bf16)

    widths = (2048, 512, 512, 1024, 1024)
    rows = (2048, 512, 1024)
    return launch(
        deps,
        functools.partial(middle_kernel, order=order, dealt=dealt),
        grid=(2,),
        out_shape=(jax.ShapeDtypeStruct((2, 512, 512), bf16),)
        + tuple(out_turned(r) for r in rows)
        + tuple(out(w) for w in widths)
        + (
            out(512, f32),
            jax.ShapeDtypeStruct((8, 512), f32),
            jax.ShapeDtypeStruct((1, 2048), f32),
            jax.ShapeDtypeStruct((8, 1024), f32),
        ),
        in_specs=[SMEM, chunk(1024), chunk(128), chunk(512), chunk(512)]
        + [pl.BlockSpec((128, 512), lambda q: (0, 4))] * 4
        + [pl.BlockSpec((128, 2048), lambda q: (0, 0))] * 4
        + [whole((1024, 512))] * 2
        + [whole(v.shape) for v in (g1, g2, g3, g4, wide)],
        out_specs=(whole((2, 512, 512)),)
        + tuple(turned(r) for r in rows)
        + tuple(chunk(w) for w in widths)
        + (chunk(512), whole((8, 512)), whole((1, 2048)), whole((8, 1024))),
        scratch_shapes=[
            pltpu.VMEM((4, 256, 512), bf16),
            pltpu.VMEM((512, 512), bf16),
            pltpu.VMEM((512, 2048), bf16),
            pltpu.VMEM((2048, 512), bf16),
            pltpu.VMEM((128, 128), bf16),
            pltpu.VMEM((128, 128), bf16),
        ],
        cost_estimate=takes(30),
        name="middle",
    )(valid, *(v.reshape(1024, -1) for v in (d, j0, xp, gp)), *w_exp, *w_exp, *w_red, g1, g2, g3, g4, wide)


def expand_grad_kernel(y2_ref, dh_ref, keep, send, sum_ref, *, order):
    sum_ref[...] = dot(y2_ref[...], dh_ref[...])
    deal_rows((keep, send), (slice(None),), sum_ref, order, 16)


def expand_grad(y2, dh, order, deps=()):
    return launch(
        deps,
        functools.partial(expand_grad_kernel, order=order),
        grid=(4,),
        out_shape=(jax.ShapeDtypeStruct((256, 2048), bf16),) * 2,
        in_specs=[whole((512, 1024)), pl.BlockSpec((1024, 512), lambda k: (0, k))],
        out_specs=(pl.BlockSpec((256, 512), lambda k: (0, k)),) * 2,
        scratch_shapes=[pltpu.VMEM((512, 512), f32)],
        cost_estimate=takes(5),
        name="expand_grad",
    )(y2, dh)


def reduce_grad_kernel(act_ref, df_ref, u_ref, dz_ref, keep, send, red_ref, out_ref, *, order):
    step = pl.program_id(0)
    red_ref[pl.ds(pl.multiple_of(step * 512, 512), 512), :] = dot(act_ref[...], df_ref[...])

    @pl.when(step == 0)
    def _():
        out_ref[...] = dot(u_ref[...], dz_ref[...])

    @pl.when(step == 3)
    def _():
        for p in range(32):
            owner = dealt_owner(p, order)
            ref, first = (keep, send)[p // 16], p % 16 * 80
            ref[first : first + 64] = red_ref[pl.ds(pl.multiple_of(owner * 64, 64), 64), :].astype(bf16)
            ref[first + 64 : first + 80] = out_ref[pl.ds(pl.multiple_of(owner * 16, 16), 16), :].astype(bf16)


def reduce_grad(act, df, u, dz, order, deps=()):
    return launch(
        deps,
        functools.partial(reduce_grad_kernel, order=order),
        grid=(4,),
        out_shape=(jax.ShapeDtypeStruct((1280, 512), bf16),) * 2,
        in_specs=[
            pl.BlockSpec((512, 1024), lambda k: (k, 0)),
            whole((1024, 512)),
            pl.BlockSpec((512, 1024), lambda k: (1, 0)),
            whole((1024, 512)),
        ],
        out_specs=(whole((1280, 512)),) * 2,
        scratch_shapes=[pltpu.VMEM((2048, 512), f32), pltpu.VMEM((512, 512), f32)],
        cost_estimate=takes(6),
        name="reduce_grad",
    )(act, df, u, dz)


def kernel_grad_kernel(dd_ref, band_ref, dk_ref):
    low = low_lanes((256, 128))
    low8 = low_lanes((8, 128))
    wide = diagonal(256)
    for tile in range(2):
        cols = slice(tile * 128, tile * 128 + 128)
        own = [dd_ref[q, :, cols].astype(f32) for q in range(4)]
        turned_own = [swap_lanes(v) for v in own]
        for side in range(2):
            group = tile * 2 + side
            halves = []
            for rp in range(2):
                if side == 0:
                    halves.append(jnp.where(low, own[2 * rp], turned_own[2 * rp + 1]))
                else:
                    halves.append(jnp.where(low, turned_own[2 * rp], own[2 * rp + 1]))
            left = jnp.concatenate(halves, axis=1).astype(bf16)
            rows = {}
            for ti in range(4):
                for tj in range(4):
                    cross = dot_tn(left, band_block(band_ref, (group,), ti, tj))
                    for rp in range(2):
                        half = jnp.where(wide, cross[:, rp * 128 : rp * 128 + 128], 0.0)
                        part = jnp.sum(half.reshape(4, 8, 8, 128), axis=1)
                        for out_rp in range(2):
                            i = 2 * ti + rp - out_rp
                            if 0 <= i <= 6:
                                for out_cp in range(2):
                                    key = (i, tj, out_cp)
                                    term = part[out_rp * 2 + out_cp]
                                    rows[key] = rows[key] + term if key in rows else term
            for i in range(7):
                turned = [swap_lanes(rows[i, tj, 1]) for tj in range(4)] + [jnp.zeros((8, 128), f32)]
                for tj in range(4):
                    value = rows[i, tj, 0] + jnp.where(low8, turned[tj], turned[tj + 1])
                    dk_ref[group, i * 4 + tj : i * 4 + tj + 1] = column_sum(value) * conv_scale
            dk_ref[group, 28:32] = jnp.zeros((4, 128), f32)


def kernel_grad(dd, band, deps=()):
    return launch(
        deps,
        kernel_grad_kernel,
        grid=(4,),
        out_shape=jax.ShapeDtypeStruct((16, 32, 128), f32),
        in_specs=[
            pl.BlockSpec((4, 256, 256), lambda t: (0, 0, t)),
            pl.BlockSpec((4, 13, 5, 16, 256), lambda t: (t, 0, 0, 0, 0)),
        ],
        out_specs=pl.BlockSpec((4, 32, 128), lambda t: (t, 0, 0)),
        cost_estimate=takes(13),
        name="kernel_grad",
    )(dd, band)


def gate_grads_kernel(u_ref, dv_ref, s512_ref, s2048_ref, s1024_ref, dk_ref, keep, send, small_ref, *, order):
    small_ref[0:256] = dot(u_ref[256:512], dv_ref[:, 512:1024])
    g3 = dot(u_ref[128:256], dv_ref[:, 256:512])
    small_ref[256:320, 0:256] = g3[0:64]
    small_ref[256:320, 256:512] = g3[64:128]
    g12 = dot(u_ref[0:128], dv_ref[:, 0:256])
    for k in range(4):
        cols = slice(k * 128, (k + 1) * 128)
        small_ref[320:336, cols] = g12[64 + 16 * k : 80 + 16 * k, 128:256]
        small_ref[336:344, cols] = g12[32 + 8 * k : 40 + 8 * k, 0:128]
        small_ref[384:512, cols] = dk_ref[k * 128 : (k + 1) * 128]
        small_ref[352 + k : 353 + k] = s2048_ref[:, k * 512 : (k + 1) * 512]
        small_ref[356 + k : 357 + k] = s1024_ref[k // 2 : k // 2 + 1, k % 2 * 512 : k % 2 * 512 + 512]
    small_ref[344:352] = s512_ref[...]
    small_ref[360:384] = jnp.zeros((24, 512), f32)
    deal_rows((keep, send), (slice(None),), small_ref, order, 16)


def gate_grads(u, dv, s512, s2048, s1024, dk, order, deps=()):
    return launch(
        deps,
        functools.partial(gate_grads_kernel, order=order),
        grid=(1,),
        out_shape=(jax.ShapeDtypeStruct((256, 512), bf16),) * 2,
        in_specs=[whole((512, 1024))] + [whole(v.shape) for v in (dv, s512, s2048, s1024, dk)],
        out_specs=(whole((256, 512)),) * 2,
        scratch_shapes=[pltpu.VMEM((512, 512), f32)],
        cost_estimate=takes(3),
        name="gate_grads",
    )(u, dv, s512, s2048, s1024, dk)


def unpack_kernel(own_ref, oth_ref, *rest):
    outs, (table_ref, all_ref) = rest[:-2], rest[-2:]
    in_ref, dk_ref, dwb_ref, g1_ref, g2_ref, g3_ref, g4_ref, gb_ref = outs[:8]
    outb_ref, mix_ref, gain_ref, shift_ref, expb_ref, redb_ref, ffn_ref = outs[8:]
    row = lax.axis_index("row")
    total = own_ref[0:16, 0:1024].astype(f32)
    for k in range(1, 16):
        total = total + own_ref[k * 16 : (k + 1) * 16, 0:1024].astype(f32)
    in_ref[...] = total
    for k in range(16):
        block = slice(k * 16, (k + 1) * 16)
        table_ref[pl.ds(pl.multiple_of((2 * k + row) * 16, 16), 16), :] = own_ref[block, 1024:1536]
        table_ref[pl.ds(pl.multiple_of((2 * k + 1 - row) * 16, 16), 16), :] = oth_ref[block, 1024:1536]
    all_ref[...] = table_ref[...].astype(f32)
    g4_ref[...] = all_ref[0:256]
    g3_ref[0:64] = all_ref[256:320, 0:256]
    g3_ref[64:128] = all_ref[256:320, 256:512]
    for k in range(4):
        cols = slice(k * 128, (k + 1) * 128)
        g2_ref[16 * k : 16 * k + 16] = all_ref[320:336, cols]
        g1_ref[8 * k : 8 * k + 8] = swap_lanes(all_ref[336:344, cols])[:, 0:64]
        expb_ref[k * 512 : (k + 1) * 512] = all_ref[352 + k : 353 + k].reshape(512)
    for k, ref in enumerate((ffn_ref, redb_ref, gain_ref, shift_ref, mix_ref, outb_ref)):
        ref[...] = all_ref[344 + k : 345 + k].reshape(512)

    def line(first):
        return jnp.concatenate([all_ref[first : first + 1], all_ref[first + 1 : first + 2]], axis=1)

    gb_ref[...] = line(356)[:, 64:1024].reshape(960)
    dwb_ref[...] = line(358)[:, 32:1024].reshape(992) * conv_scale
    low = low_lanes((32, 128))
    lane = lax.broadcasted_iota(i32, (32, 128), 1)
    rows = []
    for t in range(8):
        cols = slice(t // 2 * 128, t // 2 * 128 + 128)
        first = 384 + t % 2 * 64
        left = all_ref[first : first + 32, cols]
        right = all_ref[first + 32 : first + 64, cols]
        pair = (jnp.where(low, left, swap_lanes(right)), jnp.where(low, swap_lanes(left), right))
        rows.append([pltpu.roll(v, 96, axis=1) for v in pair])
    for t in range(8):
        size = 128 if t < 7 else 96
        for odd in range(2):
            value = jnp.where(lane < 96, rows[t][odd], rows[t + 1][odd]) if t < 7 else rows[t][odd]
            for i in range(7):
                for j in range(odd, 7, 2):
                    at = i * 4 + j // 2
                    dk_ref[i, j : j + 1, t * 128 : t * 128 + size] = value[at : at + 1, 0:size]


def unpack(own, oth, deps=()):
    vmem = pl.BlockSpec(memory_space=pltpu.VMEM)
    shapes = ((16, 1024), (7, 7, 992), (992,), (32, 64), (64, 128), (128, 256), (256, 512), (960,))
    shapes += ((512,),) * 4 + ((2048,), (512,), (512,))
    return launch(
        deps,
        unpack_kernel,
        out_shape=tuple(jax.ShapeDtypeStruct(v, f32) for v in shapes),
        in_specs=[vmem] * 2,
        out_specs=(vmem,) * len(shapes),
        scratch_shapes=[pltpu.VMEM((512, 512), bf16), pltpu.VMEM((512, 512), f32)],
        cost_estimate=takes(3),
        name="unpack",
    )(own, oth)


def conv_back_kernel(valid_ref, dd_ref, ddh_ref, tap_ref, df_ref, w_ref, back_ref, *, offset):
    step = pl.program_id(0)

    @pl.when(step == 0)
    def _():
        clear_weights(w_ref)

    sizes = extents(valid_ref)
    lane = lax.broadcasted_iota(i32, (256, 128), 1)
    keep = (lane < 32) & (step == 0)
    own = [dd_ref[q].astype(f32) for q in range(4)]
    halo = [ddh_ref[q].astype(f32) for q in range(4)]
    sums = convolve_groups(back_ref, w_ref, tap_ref, own, halo, is_upper(), True)
    for tile in range(2):
        cols = slice(tile * 128, tile * 128 + 128)
        for q, value in enumerate(split_lanes(*sums[2 * tile : 2 * tile + 2])):
            value = value * (chunk_mask(sizes, q // 2, q % 2) * conv_scale)
            if tile == 0 and offset == 0:
                value = jnp.where(keep, own[q][:, cols], value)
            df_ref[q, :, cols] = value.astype(bf16)


def conv_back(valid, dd, ddh, taps, offset, steps, deps=()):
    return launch(
        deps,
        functools.partial(conv_back_kernel, offset=offset),
        grid=(steps,),
        out_shape=jax.ShapeDtypeStruct((4, 256, 256 * steps), bf16),
        in_specs=[
            SMEM,
            pl.BlockSpec((4, 256, 256), lambda t: (0, 0, t + offset)),
            pl.BlockSpec((4, 64, 256), lambda t: (0, 0, t + offset)),
            pl.BlockSpec((7, 7, 256), lambda t: (0, 0, t + offset)),
        ],
        out_specs=pl.BlockSpec((4, 256, 256), lambda t: (0, 0, t)),
        scratch_shapes=[pltpu.VMEM((2, 16, 256, 256), bf16), pltpu.VMEM((4, 13, 5, 16, 256), bf16)],
        cost_estimate=takes(4.5 * steps),
        name="conv_back",
    )(valid, dd, ddh, taps)


def in_grad_kernel(y1_ref, da_ref, db_ref, keep, send, sum_ref, *, order):
    for k, ref in enumerate((da_ref, db_ref)):
        sum_ref[k] = dot(y1_ref[...], ref[...])
        deal_rows((keep, send), (slice(k * 512, (k + 1) * 512),), sum_ref.at[k], order, 16)


def in_grad(y1, da, db, order, deps=()):
    vmem = pl.BlockSpec(memory_space=pltpu.VMEM)
    return launch(
        deps,
        functools.partial(in_grad_kernel, order=order),
        out_shape=(jax.ShapeDtypeStruct((256, 1024), bf16),) * 2,
        in_specs=[vmem] * 3,
        out_specs=(vmem, vmem),
        scratch_shapes=[pltpu.VMEM((2, 512, 512), f32)],
        cost_estimate=takes(4),
        name="in_grad",
    )(y1, da, db)


def last_kernel(valid_ref, da_ref, db_ref, xp_ref, dx2_ref, *rest, order, dealt):
    weights, (wide_ref, out_ref, late_ref, held_ref, win_ref) = rest[:8], rest[8:]
    q = pl.program_id(0)

    @pl.when(q == 0)
    def _():
        late_ref[...] = jnp.zeros_like(late_ref)
        place_rows(win_ref, weights, order, own_number(dealt), 16)

    mask = pair_mask(extents(valid_ref), q)
    da, db = da_ref[...], db_ref[...]
    late_ref[2:3] += column_sum(da.astype(f32))
    late_ref[3:4] += column_sum(db.astype(f32))
    grad = mask * (dot_nt(da, win_ref[:, 0:512]) + dot_nt(db, win_ref[:, 512:1024]))
    normed, inverse = normalize(xp_ref[...].astype(f32))
    late_ref[0:1] += column_sum(grad * normed)
    late_ref[1:2] += column_sum(grad)
    total = dx2_ref[...] + norm_backward(grad, normed, inverse, wide_ref[8:9, 0:512])
    held_ref[pl.ds(2 * q, 2)] = total.astype(bf16).reshape(2, 256, 512)

    @pl.when(q == 1)
    def _():
        unpermute(held_ref, out_ref)


def last_call(valid, da, db, xp, dx2, w_in, wide, order, dealt, deps=()):
    def chunk(width):
        return pl.BlockSpec((512, width), lambda q: (q, 0))

    return launch(
        deps,
        functools.partial(last_kernel, order=order, dealt=dealt),
        grid=(2,),
        out_shape=(jax.ShapeDtypeStruct((2, 512, 512), bf16), jax.ShapeDtypeStruct((8, 512), f32)),
        in_specs=[SMEM] + [chunk(512)] * 4 + [whole((64, 1024))] * 8 + [whole(wide.shape)],
        out_specs=(whole((2, 512, 512)), whole((8, 512))),
        scratch_shapes=[pltpu.VMEM((4, 256, 512), bf16), pltpu.VMEM((512, 1024), bf16)],
        cost_estimate=takes(7),
        name="last",
    )(valid, *(v.reshape(1024, -1) for v in (da, db, xp, dx2)), *w_in, wide)


def repeat(value):
    rows, cols = value.shape
    return jnp.broadcast_to(value[None], (16, rows, cols)).reshape(16 * rows, cols)


def join_kernel(*refs, counts):
    ins = list(refs[: sum(counts)])
    for out, count in zip(refs[sum(counts) :], counts):
        at = 0
        for _ in range(count):
            ref = ins.pop(0)
            out[at : at + ref.shape[0]] = ref[...]
            at += ref.shape[0]


def join(*lists, deps=()):
    vmem = pl.BlockSpec(memory_space=pltpu.VMEM)
    shapes = [(sum(v.shape[0] for v in group), group[0].shape[1]) for group in lists]
    return launch(
        deps,
        functools.partial(join_kernel, counts=[len(v) for v in lists]),
        out_shape=tuple(jax.ShapeDtypeStruct(v, bf16) for v in shapes),
        in_specs=[vmem] * sum(len(v) for v in lists),
        out_specs=(vmem,) * len(lists),
        cost_estimate=takes(1),
        name="join",
    )(*sum((list(v) for v in lists), []))


def add_kernel(a_ref, b_ref, out_ref):
    out_ref[...] = a_ref[...] + b_ref[...]


def add(a, b, deps=()):
    vmem = pl.BlockSpec(memory_space=pltpu.VMEM)
    return launch(
        deps,
        add_kernel,
        out_shape=jax.ShapeDtypeStruct(a.shape, a.dtype),
        in_specs=[vmem] * 2,
        out_specs=vmem,
        cost_estimate=takes(1),
        name="add",
    )(a, b)


def combine_kernel(*refs, items):
    at = sum(n for n, _ in items)
    ins, outs = list(refs[:at]), list(refs[at:])
    for count, parts in items:
        terms = [ins.pop(0) for _ in range(count)]
        for part in range(parts):
            total = functools.reduce(lambda a, b: a + b, [v[part, 0].astype(f32) for v in terms])
            outs.pop(0)[0] = total.astype(bf16)


def combine(*items, deps=()):
    steps = next(n for n in (4, 2, 1) if all(v[0].shape[0] % (16 * n * p) == 0 for v, p in items))
    ins, in_specs, outs, out_specs = [], [], [], []
    for terms, parts in items:
        rows, cols = terms[0].shape
        size = rows // parts // steps
        ins += [v.reshape(parts, steps, size, cols) for v in terms]
        in_specs += [pl.BlockSpec((parts, 1, size, cols), lambda t: (0, t, 0, 0))] * len(terms)
        outs += [jax.ShapeDtypeStruct((steps, size, cols), bf16)] * parts
        out_specs += [pl.BlockSpec((1, size, cols), lambda t: (t, 0, 0))] * parts
    *values, token = launch(
        deps,
        functools.partial(combine_kernel, items=[(len(v), p) for v, p in items]),
        grid=(steps,),
        out_shape=tuple(outs),
        in_specs=in_specs,
        out_specs=tuple(out_specs),
        cost_estimate=takes(2),
        name="combine",
    )(*ins)
    return [v.reshape(-1, v.shape[-1]) for v in values] + [token]


def merge_kernel(ro_a, ro_b, e_a, e_b, *outs):
    for z, ref in enumerate(outs):
        rows = slice(z * 80, (z + 1) * 80)
        ref[0:80] = (ro_a[rows].astype(f32) + ro_b[rows].astype(f32)).astype(bf16)
        total = e_a[z * 16 : (z + 1) * 16].astype(f32) + e_b[z * 16 : (z + 1) * 16].astype(f32)
        for c in range(4):
            at = 80 + c * 16
            ref[at : at + 16] = total[:, c * 512 : (c + 1) * 512].astype(bf16)


def merge(ro_a, ro_b, e_a, e_b, deps=()):
    vmem = pl.BlockSpec(memory_space=pltpu.VMEM)
    return launch(
        deps,
        merge_kernel,
        out_shape=(jax.ShapeDtypeStruct((144, 512), bf16),) * 4,
        in_specs=[vmem] * 4,
        out_specs=(vmem,) * 4,
        cost_estimate=takes(2),
        name="merge",
    )(ro_a, ro_b, e_a, e_b)


def finish_kernel(*refs):
    ins, (red_ref, out_ref, exp_ref) = refs[:-3], refs[-3:]
    total = functools.reduce(lambda a, b: a + b, [v[...].astype(f32) for v in ins])
    red_ref[...] = total[0:64]
    out_ref[...] = total[64:80]
    for c in range(4):
        exp_ref[:, c * 512 : (c + 1) * 512] = total[80 + c * 16 : 96 + c * 16]


def finish(parts, deps=()):
    vmem = pl.BlockSpec(memory_space=pltpu.VMEM)
    shapes = ((64, 512), (16, 512), (16, 2048))
    return launch(
        deps,
        finish_kernel,
        out_shape=tuple(jax.ShapeDtypeStruct(v, f32) for v in shapes),
        in_specs=[vmem] * len(parts),
        out_specs=(vmem,) * 3,
        cost_estimate=takes(1),
        name="finish",
    )(*parts)


def deal_kernel(i_a, i_b, *rest):
    parts, out_ref = rest[:-1], rest[-1]
    small = functools.reduce(lambda a, b: a + b, [v[...].astype(f32) for v in parts]).astype(bf16)
    out_ref[:, 0:1024] = (i_a[...].astype(f32) + i_b[...].astype(f32)).astype(bf16)
    for k in range(16):
        out_ref[k * 16 : (k + 1) * 16, 1024:1536] = small


def deal(i_a, i_b, parts, deps=()):
    vmem = pl.BlockSpec(memory_space=pltpu.VMEM)
    return launch(
        deps,
        deal_kernel,
        out_shape=jax.ShapeDtypeStruct((256, 1536), bf16),
        in_specs=[vmem] * (2 + len(parts)),
        out_specs=vmem,
        cost_estimate=takes(2),
        name="deal",
    )(i_a, i_b, *parts)


def late_kernel(a_ref, b_ref, gain_ref, shift_ref, bias_ref):
    total = a_ref[...] + b_ref[...]
    gain_ref[...] = total[0:1].reshape(512)
    shift_ref[...] = total[1:2].reshape(512)
    bias_ref[0:512] = total[2:3].reshape(512)
    bias_ref[512:1024] = total[3:4].reshape(512)


def late_sums(a, b, deps=()):
    vmem = pl.BlockSpec(memory_space=pltpu.VMEM)
    return launch(
        deps,
        late_kernel,
        out_shape=tuple(jax.ShapeDtypeStruct((v,), f32) for v in (512, 512, 1024)),
        in_specs=[vmem] * 2,
        out_specs=(vmem,) * 3,
        cost_estimate=takes(1),
        name="late",
    )(a, b)


ROW = "row"


def img_bits():
    return lax.axis_size("img").bit_length() - 1


def swap_img(value, mask):
    return lax.ppermute(value, "img", [(k, k ^ mask) for k in range(lax.axis_size("img"))])


def swap_row(value):
    return lax.ppermute(value, "row", [(0, 1), (1, 0)])


def masks_of(stage):
    masks = [0]
    for bit in stage:
        masks = [m | v for m in masks for v in (0, 1 << bit)]
    return masks


def gather_order(groups):
    rel = [0]
    for bits in groups:
        rel = [m ^ r for m in masks_of(bits) for r in rel]
    return [2 * r + side for side in (0, 1) for r in rel]


def swaps(value, bits):
    return [value] + [swap_img(value, m) for m in masks_of(bits)[1:]]


def after(value, *others):
    return lax.optimization_barrier((value, others))[0]


def spread(value):
    return lax.all_to_all(value, "img", split_axis=0, concat_axis=0, tiled=True)


def sum_img(value, bits):
    for bit in bits[:-1]:
        value = value + swap_img(value, 1 << bit)
    return value, swap_img(value, 1 << bits[-1])


def own_bit(bit):
    return lax.axis_index("row") if bit == ROW else (lax.axis_index("img") >> bit) & 1


def swap_bit(value, bit):
    return swap_row(value) if bit == ROW else swap_img(value, 1 << bit)


def plain_gather(shard):
    value = shard
    for bit in [ROW] + list(range(img_bits())):
        other = swap_bit(value, bit)
        mine = own_bit(bit) == 0
        value = jnp.concatenate([jnp.where(mine, value, other), jnp.where(mine, other, value)], axis=0)
    return value


def plain_scatter(value):
    for bit in list(range(img_bits()))[::-1] + [ROW]:
        half = value.shape[0] // 2
        mine = own_bit(bit) == 0
        first, second = value[:half], value[half:]
        sent = swap_bit(jnp.where(mine, second, first).astype(bf16), bit)
        value = jnp.where(mine, first, second).astype(f32) + sent.astype(f32)
    return value


def per_device(
    features,
    validity,
    upstream,
    normgain,
    normshift,
    inweight,
    inbias,
    dwkernel,
    dwbias,
    gatefirst,
    gatesecond,
    gatethird,
    gatefourth,
    gatebias,
    outweight,
    outbias,
    mixscale,
    mlpgain,
    mlpshift,
    expandweight,
    expandbias,
    reduceweight,
    reducebias,
    mlpscale,
):
    bits = img_bits()
    dealt = bits == 4
    lower = lax.axis_index("row") == 1

    x = features.reshape(2, 512, 512)
    g = upstream.reshape(2, 512, 512)
    valid = validity.reshape(32, 32)
    x_halo = swap_row(x)
    halo_valid = swap_row(valid)
    taps = jnp.pad(dwkernel.astype(f32), ((0, 0), (0, 0), (32, 0)))
    wide, token = gather_vectors(
        (inbias, dwbias, gatebias, expandbias),
        (outbias, mixscale, mlpgain, mlpshift, reducebias, mlpscale, normgain, normshift),
    )
    exp_out = jnp.concatenate([expandweight, outweight], axis=1)
    deep, flat_pair = (3, 2), (1, 0)
    if dealt:
        in_order = gather_order((deep, flat_pair))
        exp_order = gather_order((deep, (1,), (0,)))
        in_z, token = join(swaps(inweight, deep))
        exp_parts = swaps(exp_out, deep)
        red_own = spread(repeat(reduceweight))
        w_in = swaps(in_z, flat_pair)
        xp, gp, y1, y1h, y1t, token = prepare(valid, halo_valid, x, x_halo, g, wide, [token])
        exp_z, token = join(exp_parts, deps=[token] + w_in[1:])
        w_in = w_in + [swap_row(v) for v in w_in]
        exp_y, token = join(swaps(exp_z, (1,)), deps=[token])
        w_exp = swaps(exp_y, (0,))
        d, band, j0, token = forward(valid, halo_valid, y1, y1h, w_in, wide, taps, in_order, dealt, [token])
        w_exp = w_exp + [swap_row(w_exp[0]), swap_row(after(w_exp[1], d))]
        w_red = [red_own, swap_row(after(red_own, d))]
    else:
        in_order = exp_order = list(range(32))
        w_in = jnp.split(plain_gather(inweight), 8, axis=0)
        w_exp = jnp.split(plain_gather(exp_out), 4, axis=0)
        w_red = jnp.split(plain_gather(reduceweight), 2, axis=0)
        xp, gp, y1, y1h, y1t, token = prepare(valid, halo_valid, x, x_halo, g, wide)
        d, band, j0, token = forward(valid, halo_valid, y1, y1h, w_in, wide, taps, in_order, dealt)
    (produced, act, y2, u, dh, df, dz, dv, dd, dx2, s512, s2048, s1024, token) = middle_call(
        valid, d, j0, xp, gp, w_exp, w_red, gatefirst, gatesecond, gatethird, gatefourth, wide, exp_order, dealt
    )
    dd = dd.reshape(4, 256, 1024)
    dd_halo = swap_row(jnp.where(lower, dd[:, 0:64], dd[:, 192:256]))

    def flat(value):
        return value.reshape(1024, -1)

    r_order, e_order, plain = ((1, 0, 3, 2), (0, 1, 3, 2), "plain") if dealt else ("none",) * 3
    if dealt:
        e_keep, e_send, token = expand_grad(y2, flat(dh), e_order)
        e_got = swap_row(e_send)
        r_keep, r_send, token = reduce_grad(act, flat(df), u, flat(dz), r_order, [token])
        r_got = swap_row(r_send)
        dk, token = kernel_grad(dd, band, [token])
        r_keep, r_send, e_keep, e_send, token = combine(([r_keep, r_got], 2), ([e_keep, e_got], 2), deps=[token])
        r_got, e_got = swap_img(r_send, 2), swap_img(e_send, 1)
        s_keep, s_send, token = gate_grads(
            u, flat(dv), s512, s2048, s1024, dk.reshape(512, 128), flat_pair + deep, [token]
        )
        s_got = swap_row(s_send)
        df_a, token = conv_back(valid, dd, dd_halo, taps, 0, 2, [token])
        *small, token = combine(([s_keep, s_got], 4), deps=[token])
        small = small[:1] + [swap_img(v, m) for v, m in zip(small[1:], masks_of(flat_pair)[1:])]
        df_b, token = conv_back(valid, dd, dd_halo, taps, 2, 2, [token])
        r_keep, r_send, e_keep, e_send, *small, token = combine(
            ([r_keep, r_got], 2), ([e_keep, e_got], 2), (small, 4), deps=[token]
        )
        r_got, e_got = swap_img(r_send, 1), swap_img(e_send, 2)
        small = small[:1] + [swap_img(v, m) for v, m in zip(small[1:], masks_of(deep)[1:])]
        i_keep, i_send, token = in_grad(y1t, flat(df_a), flat(df_b), plain, [token])
        i_got = swap_row(i_send)
        *parts, token = merge(r_keep, r_got, e_keep, e_got, [token])
        parts = parts[:1] + [swap_img(v, m) for v, m in zip(parts[1:], masks_of(deep)[1:])]
        fgrad, late, token = last_call(valid, df_a, df_b, xp, dx2, w_in, wide, in_order, dealt, [token])
        red_sum, out_sum, exp_sum, token = finish(parts, [token])
        dealt_rows, token = deal(i_keep, i_got, small, [token])
        mixed = spread(dealt_rows)
        late, got = sum_img(late + swap_row(late), (0, 1, 2, 3))
        own, oth = mixed, swap_row(after(mixed, late))
        sums = late_sums(late, got, [token])
    else:

        def total(parts, rows):
            value = jnp.concatenate(parts, axis=0)
            return plain_scatter(value.reshape(32, -1, value.shape[1])[:, rows].reshape(-1, value.shape[1]))

        everything = slice(None)
        dk, token = kernel_grad(dd, band)
        s_keep, s_send, token = gate_grads(u, flat(dv), s512, s2048, s1024, dk.reshape(512, 128), plain)
        e_parts = expand_grad(y2, flat(dh), e_order)[:2]
        r_parts = reduce_grad(act, flat(df), u, flat(dz), r_order)[:2]
        df_a, _ = conv_back(valid, dd, dd_halo, taps, 0, 2)
        df_b, _ = conv_back(valid, dd, dd_halo, taps, 2, 2)
        i_parts = in_grad(y1t, flat(df_a), flat(df_b), plain)[:2]
        fgrad, late, token = last_call(valid, df_a, df_b, xp, dx2, w_in, wide, in_order, dealt)
        sums = late_sums(*sum_img(late + swap_row(late), list(range(bits))))
        exp_sum, in_sum = total(e_parts, everything), total(i_parts, everything)
        red_sum, out_sum = total(r_parts, slice(0, 64)), total(r_parts, slice(64, 80))
        small = plain_gather(total((s_keep, s_send), everything).astype(bf16)).reshape(16, 2, 16, 512)
        lower_row = lax.axis_index("row")
        own, oth = (
            jnp.pad(lax.dynamic_index_in_dim(small, v, 1, keepdims=False).reshape(256, 512), ((0, 0), (1024, 0)))
            for v in (lower_row, 1 - lower_row)
        )

    unpacked = unpack(own, oth)
    if dealt:
        in_sum = unpacked[0]
    dk_sum, dwb_sum, gate1, gate2, gate3, gate4, gb_sum, outb, mix, gain, shift, expb, redb, ffn = unpacked[1:-1]
    return (
        produced.reshape(features.shape),
        fgrad.reshape(features.shape),
        sums[0],
        sums[1],
        in_sum,
        sums[2],
        dk_sum,
        dwb_sum,
        gate1,
        gate2,
        gate3,
        gate4,
        gb_sum,
        out_sum,
        outb,
        mix,
        gain,
        shift,
        exp_sum,
        expb,
        red_sum,
        redb,
        ffn,
    )


def solution(mesh):
    band = P("img", "row", None, None)
    rows = P(("img", "row"), None)
    copy = P()
    ins = [band, P("img", "row", None), band] + [copy] * 21
    for k in (5, 14, 19, 21):
        ins[k] = rows
    outs = [band, band] + [copy] * 21
    for k in (4, 13, 18, 20):
        outs[k] = rows
    return jax.shard_map(per_device, mesh=mesh, in_specs=tuple(ins), out_specs=tuple(outs), check_vma=False)
```

```python
import functools
import math

import jax
import jax.numpy as jnp
from jax import lax
from jax.experimental import pallas as pl
from jax.experimental.pallas import tpu as pltpu
from jax.sharding import PartitionSpec as P

f32 = jnp.float32
bf16 = jnp.bfloat16
i32 = jnp.int32
norm_eps = 1e-06
conv_scale = 1.0 / 3.0
inv_root_two = 1.0 / math.sqrt(2.0)
inv_root_tau = 1.0 / math.sqrt(2.0 * math.pi)
vmem_bytes = 60 * 1024 * 1024


def dot(left, right):
    return jnp.dot(left, right, preferred_element_type=f32)


def dot_tn(left, right):
    return lax.dot_general(left, right, (((0,), (0,)), ((), ())), preferred_element_type=f32)


def dot_nt(left, right):
    return lax.dot_general(left, right, (((1,), (1,)), ((), ())), preferred_element_type=f32)


def column_sum(values):
    return jnp.sum(values, axis=0, keepdims=True)


def permutation():
    out = lax.broadcasted_iota(i32, (256, 256), 0)
    src = lax.broadcasted_iota(i32, (256, 256), 1)
    row_par, col_par = out >> 7, (out >> 6) & 1
    pair, ccp, img, blk = (out >> 5) & 1, (out >> 4) & 1, (out >> 3) & 1, out & 7
    want = img * 128 + (2 * pair + row_par) * 32 + 4 * blk + 2 * ccp + col_par
    return (src == want).astype(f32).astype(bf16)


def normalize(values):
    center = jnp.mean(values, axis=-1, keepdims=True)
    shifted = values - center
    spread = jnp.mean(shifted * shifted, axis=-1, keepdims=True)
    inverse = lax.rsqrt(spread + norm_eps)
    return shifted * inverse, inverse


def norm_backward(grad_norm, normed, inverse, gain):
    scaled = grad_norm * gain
    return inverse * (
        scaled
        - jnp.mean(scaled, axis=-1, keepdims=True)
        - normed * jnp.mean(scaled * normed, axis=-1, keepdims=True)
    )


def extents(valid_ref):
    heights = [sum(valid_ref[16 * n + r, 0] for r in range(16)) for n in range(2)]
    widths = [sum(valid_ref[16 * n, c] for c in range(32)) for n in range(2)]
    return heights, widths


def chunk_mask(sizes, row_par, col_par, count=256, first_row=0):
    (high_a, high_b), (wide_a, wide_b) = sizes
    at = lax.broadcasted_iota(i32, (count, 1), 0)
    pair, ccp, img, blk = at >> 5, (at >> 4) & 1, (at >> 3) & 1, at & 7
    row = 2 * pair + row_par + first_row
    col = 4 * blk + 2 * ccp + col_par
    high = jnp.where(img == 1, high_b, high_a)
    wide = jnp.where(img == 1, wide_b, wide_a)
    return jnp.where((row < high) & (col < wide), 1.0, 0.0).astype(f32)


def pair_mask(sizes, row_par):
    return jnp.concatenate([chunk_mask(sizes, row_par, col_par) for col_par in range(2)], axis=0)


def halo_sizes(valid_ref, halo_ref):
    heights, widths = extents(valid_ref)
    below, _ = extents(halo_ref)
    upper = lax.axis_index("row") == 0
    return [jnp.where(upper, h, 4) for h in below], widths


def is_upper():
    return jnp.where(lax.axis_index("row") == 0, 1.0, 0.0).astype(f32)


def vectors_kernel(in_ref, dw_ref, gate_ref, exp_ref, *rest):
    small, out_ref = rest[:8], rest[8]

    def line(ref):
        return ref[...].astype(f32).reshape(1, ref.shape[0])

    out_ref[0:1] = line(in_ref)
    out_ref[1:2, 0:32] = jnp.zeros((1, 32), f32)
    out_ref[1:2, 32:1024] = line(dw_ref)
    out_ref[2:3, 0:64] = jnp.zeros((1, 64), f32)
    out_ref[2:3, 64:1024] = line(gate_ref)
    wide = line(exp_ref)
    out_ref[3:4] = wide[:, 0:1024]
    out_ref[4:5] = wide[:, 1024:2048]
    for k, ref in enumerate(small):
        out_ref[5 + k // 2 : 6 + k // 2, k % 2 * 512 : k % 2 * 512 + 512] = line(ref)


def gather_vectors(large, small, deps=()):
    vmem = pl.BlockSpec(memory_space=pltpu.VMEM)
    return launch(
        deps,
        vectors_kernel,
        out_shape=jax.ShapeDtypeStruct((9, 1024), f32),
        in_specs=[vmem] * 12,
        out_specs=vmem,
        cost_estimate=takes(1),
        name="vectors",
    )(*large, *small)


def prepare_kernel(valid_ref, halo_valid_ref, x_ref, xh_ref, g_ref, vec_ref, xp_ref, gp_ref, y1_ref, y1h_ref, y1t_ref):
    perm = permutation()
    gain, shift = vec_ref[8:9, 0:512], vec_ref[8:9, 512:1024]
    own, halo = extents(valid_ref), halo_sizes(valid_ref, halo_valid_ref)
    start = pl.multiple_of(lax.axis_index("row") * 384, 128)
    for b in range(5):
        if b == 4:
            rows = pl.ds(start, 128)
            block = jnp.concatenate([xh_ref[0, rows], xh_ref[1, rows]], axis=0)
        else:
            rows = slice(b * 128, (b + 1) * 128)
            block = jnp.concatenate([x_ref[0, rows], x_ref[1, rows]], axis=0)
            gblock = dot(perm, jnp.concatenate([g_ref[0, rows], g_ref[1, rows]], axis=0)).astype(bf16)
        block = dot(perm, block)
        lowered = block.astype(bf16)
        normed, _ = normalize(block)
        value = normed * gain + shift
        for q in range(4):
            part = slice(q * 64, (q + 1) * 64)
            if b == 4:
                y1h_ref[q] = (chunk_mask(halo, q // 2, q % 2, 64) * value[part]).astype(bf16)
            else:
                dest = slice(b * 64, (b + 1) * 64)
                xp_ref[q, dest] = lowered[part]
                gp_ref[q, dest] = gblock[part]
                y1_ref[q, dest] = (chunk_mask(own, q // 2, q % 2, 64, 4 * b) * value[part]).astype(bf16)
    for q in range(4):
        y1t_ref[:, q * 256 : (q + 1) * 256] = y1_ref[q].T


def whole(shape):
    return pl.BlockSpec(shape, lambda *_: (0,) * len(shape))


SMEM = pl.BlockSpec(memory_space=pltpu.SMEM)


def params():
    return pltpu.CompilerParams(vmem_limit_bytes=vmem_bytes)


def takes(micros):
    return pl.CostEstimate(flops=int(micros * 1.0e9), bytes_accessed=0, transcendentals=0)


def launch(deps, kernel, *, out_shape, in_specs, out_specs, **rest):
    single = not isinstance(out_shape, tuple)
    shapes = (out_shape,) if single else out_shape
    specs = (out_specs,) if single else out_specs
    anywhere = pl.BlockSpec(memory_space=pl.ANY)
    count = len(in_specs)

    def body(*refs):
        at = count + len(deps)
        kernel(*refs[:count], *refs[at : at + len(shapes)], *refs[at + len(shapes) + 1 :])

    call = pl.pallas_call(
        body,
        out_shape=(*shapes, jax.ShapeDtypeStruct((8, 128), f32)),
        in_specs=list(in_specs) + [anywhere] * len(deps),
        out_specs=(*specs, anywhere),
        compiler_params=params(),
        **rest,
    )
    return lambda *args: call(*args, *deps)


def own_number(dealt):
    return lax.axis_index("img") * 2 + lax.axis_index("row") if dealt else 0


def place_rows(scratch, refs, order, number, rows):
    each = 32 // len(refs)
    for k, ref in enumerate(refs):
        for b in range(each):
            at = pl.multiple_of((order[k * each + b] ^ number) * rows, 16)
            scratch[pl.ds(at, rows), :] = ref[b * rows : (b + 1) * rows, :]


def dealt_owner(place, order):
    if order == "none":
        return place
    if order == "plain":
        return (2 * (place % 16) + place // 16) ^ lax.axis_index("row")
    return (2 * masks_of(order)[place % 16] + place // 16) ^ own_number(True)


def deal_rows(outs, lead, value_ref, order, rows):
    for p in range(32):
        at = pl.multiple_of(dealt_owner(p, order) * rows, 16)
        outs[p // 16][(slice(p % 16 * rows, (p % 16 + 1) * rows),) + lead] = value_ref[pl.ds(at, rows), :].astype(bf16)


def prepare(valid, halo_valid, x, xh, g, wide, deps=()):
    vmem = pl.BlockSpec(memory_space=pltpu.VMEM)
    return launch(
        deps,
        prepare_kernel,
        out_shape=(
            jax.ShapeDtypeStruct((4, 256, 512), bf16),
            jax.ShapeDtypeStruct((4, 256, 512), bf16),
            jax.ShapeDtypeStruct((4, 256, 512), bf16),
            jax.ShapeDtypeStruct((4, 64, 512), bf16),
            jax.ShapeDtypeStruct((512, 1024), bf16),
        ),
        in_specs=[SMEM] * 2 + [vmem] * 4,
        out_specs=(vmem,) * 5,
        cost_estimate=takes(4),
        name="prepare",
    )(valid, halo_valid, x, xh, g, wide)


def low_lanes(shape):
    return lax.broadcasted_iota(i32, shape, len(shape) - 1) < 64


def swap_lanes(value):
    return pltpu.roll(value, 64, axis=1)


def shifted_block(value, step):
    if step == 0:
        return value
    blk = lax.broadcasted_iota(i32, value.shape, 1)
    if step > 0:
        return jnp.where(blk < 7, pltpu.roll(value, 7, axis=1), 0.0)
    return jnp.where(blk > 0, pltpu.roll(value, 1, axis=1), 0.0)


ODD = ((-1, 0), (-1, 1), (0, 0), (0, 1), (1, 0))
EVEN = ((-1, 1), (0, 0), (0, 1), (1, 0), (1, 1))


def lane_pairs(chunks):
    res = {}
    for row_par in range(2):
        odd, even = chunks[2 * row_par + 1], chunks[2 * row_par]
        odd_s, even_s = swap_lanes(odd), swap_lanes(even)
        res[row_par, 0] = (odd, even_s)
        res[row_par, 1] = (odd_s, even)
    return res


def fill_band(ref, lead, pairs, n, start, row_par):
    odd, even = (v.reshape(n, 2, 2, 8, 128) for v in pairs)
    half = 1 - row_par
    lanes = slice(half * 128, half * 128 + 128)
    low = low_lanes((n * 2, 8, 128))
    cache = {}

    def take(name, value, step, ccp):
        if (name, step, ccp) not in cache:
            cache[name, step, ccp] = shifted_block(value[:, ccp].reshape(n * 2, 8, 128), step)
        return cache[name, step, ccp]

    def write(k):
        both = jnp.where(low, take("o", odd, *ODD[k]), take("e", even, *EVEN[k]))
        ref[lead + (slice(start, start + n), k, slice(None), lanes)] = both.reshape(n, 16, 128).astype(bf16)

    return [functools.partial(write, k) for k in range(5)]


def fill_group(ref, lead, own, halo, upper):
    steps = []
    for row_par in range(2):
        first = 2 + row_par
        steps += fill_band(ref, lead, own[row_par], 8, first, row_par)
        steps += fill_band(ref, lead, [v * (1.0 - upper) for v in halo[row_par]], 2, first - 2, row_par)
        steps += fill_band(ref, lead, [v * upper for v in halo[row_par]], 2, first + 8, row_par)
    return steps


def diagonal(rows):
    return (lax.broadcasted_iota(i32, (rows, 128), 0) % 64) == (lax.broadcasted_iota(i32, (rows, 128), 1) % 64)


def build_weights(w_ref, slot, tap_ref, group, flip=False):
    mask = diagonal(64)
    low = low_lanes((1, 128))
    tile, side = group // 2, group % 2
    cols = slice(tile * 128, tile * 128 + 128)

    def write(i, jj):
        rows = tap_ref[6 - i if flip else i, :, cols]
        turned = swap_lanes(rows)
        first, second = (rows, turned) if side == 0 else (turned, rows)
        a, b = (6 - jj, 7 - jj) if flip else (jj, jj - 1)
        left = first[a : a + 1] if 0 <= a <= 6 else jnp.zeros((1, 128), f32)
        right = second[b : b + 1] if 0 <= b <= 6 else jnp.zeros((1, 128), f32)
        vector = jnp.where(low, left, right)
        block = jnp.where(mask, jnp.broadcast_to(vector, (64, 128)), 0.0).astype(bf16)
        for out_par in range(2):
            top = i + out_par
            ti, rp, tj, cp = top // 2, top % 2, jj // 2, jj % 2
            at = (rp * 2 + cp) * 64
            w_ref[slot, ti * 4 + tj, at : at + 64, out_par * 128 : out_par * 128 + 128] = block

    return [functools.partial(write, i, jj) for i in range(7) for jj in range(8)]


def clear_weights(w_ref):
    for slot in range(2):
        for tj in range(4):
            w_ref[slot, tj, 0:128, 128:256] = jnp.zeros((128, 128), bf16)
            w_ref[slot, 12 + tj, 128:256, 0:128] = jnp.zeros((128, 128), bf16)


def band_block(ref, lead, ti, tj):
    return ref[lead + (slice(1 + ti, 9 + ti), slice(tj, tj + 2))].reshape(256, 256)


def convolve(ref, lead, w_ref, slot, meanwhile):
    total = None
    for k in range(16):
        part = dot(band_block(ref, lead, k // 4, k % 4), w_ref[slot, k])
        total = part if total is None else total + part
        for step in meanwhile[len(meanwhile) * k // 16 : len(meanwhile) * (k + 1) // 16]:
            step()
    return total


def convolve_groups(ref, w_ref, tap_ref, own, halo, upper, flip):
    def steps(group):
        cols = slice(group // 2 * 128, group // 2 * 128 + 128)
        own_pairs = lane_pairs([v[:, cols] for v in own])
        halo_pairs = lane_pairs([v[:, cols] for v in halo])
        side = group % 2
        band = [own_pairs[rp, side] for rp in range(2)], [halo_pairs[rp, side] for rp in range(2)]
        return fill_group(ref, (group,), *band, upper) + build_weights(w_ref, side, tap_ref, group, flip)

    for step in steps(0):
        step()
    return [convolve(ref, (group,), w_ref, group % 2, steps(group + 1) if group < 3 else []) for group in range(4)]


def split_lanes(low_group, high_group):
    low = low_lanes((256, 128))
    chunks = []
    for rp in range(2):
        lg = low_group[:, rp * 128 : rp * 128 + 128]
        hg = high_group[:, rp * 128 : rp * 128 + 128]
        chunks.append(jnp.where(low, lg, swap_lanes(hg)))
        chunks.append(jnp.where(low, swap_lanes(lg), hg))
    return chunks


def forward_kernel(valid_ref, halo_valid_ref, y1_ref, y1h_ref, *rest, order, dealt):
    weights, (wide_ref, tap_ref, d_ref, band_ref, j0_ref, w_ref, win_ref) = rest[:8], rest[8:]
    step = pl.program_id(0)

    @pl.when(step == 0)
    def _():
        clear_weights(w_ref)

    upper = is_upper()
    sizes, around = extents(valid_ref), halo_sizes(valid_ref, halo_valid_ref)
    place_rows(win_ref, weights, order, own_number(dealt), 16)
    weight = win_ref[...]
    bias = wide_ref[0:1]
    joined = dot(y1_ref[...].reshape(1024, 512), weight) + bias
    joined = [joined[q * 256 : (q + 1) * 256] for q in range(4)]
    around_rows = dot(y1h_ref[...].reshape(256, 512), weight) + bias

    @pl.when(step == 0)
    def _():
        for q in range(4):
            j0_ref[q] = joined[q][:, 0:128]

    own, halo = [], []
    for q in range(4):
        own.append((joined[q] * chunk_mask(sizes, q // 2, q % 2)).astype(bf16).astype(f32))
        part = around_rows[q * 64 : (q + 1) * 64]
        halo.append((part * chunk_mask(around, q // 2, q % 2, 64)).astype(bf16).astype(f32))
    sums = convolve_groups(band_ref, w_ref, tap_ref, own, halo, upper, False)
    for tile in range(2):
        cols = slice(tile * 128, tile * 128 + 128)
        for q, value in enumerate(split_lanes(*sums[2 * tile : 2 * tile + 2])):
            d_ref[q, :, cols] = (value + wide_ref[1:2, cols]) * conv_scale


def forward(valid, halo_valid, y1, y1h, w_in, wide, taps, order, dealt, deps=()):
    return launch(
        deps,
        functools.partial(forward_kernel, order=order, dealt=dealt),
        grid=(4,),
        out_shape=(
            jax.ShapeDtypeStruct((4, 256, 1024), f32),
            jax.ShapeDtypeStruct((16, 13, 5, 16, 256), bf16),
            jax.ShapeDtypeStruct((4, 256, 128), f32),
        ),
        in_specs=[SMEM, SMEM, whole((4, 256, 512)), whole((4, 64, 512))]
        + [pl.BlockSpec((64, 256), lambda t: (0, t))] * 8
        + [pl.BlockSpec((9, 256), lambda t: (0, t)), pl.BlockSpec((7, 7, 256), lambda t: (0, 0, t))],
        out_specs=(
            pl.BlockSpec((4, 256, 256), lambda t: (0, 0, t)),
            pl.BlockSpec((4, 13, 5, 16, 256), lambda t: (t, 0, 0, 0, 0)),
            whole((4, 256, 128)),
        ),
        scratch_shapes=[pltpu.VMEM((2, 16, 256, 256), bf16), pltpu.VMEM((512, 256), bf16)],
        cost_estimate=takes(24),
        name="forward",
    )(valid, halo_valid, y1, y1h, *w_in, wide, taps)


def middle_kernel(
    valid_ref,
    d_ref,
    j0_ref,
    xp_ref,
    gp_ref,
    oa,
    ob,
    oc,
    od,
    ea,
    eb4,
    ec,
    ed,
    ra,
    rb,
    first_ref,
    second_ref,
    g3_ref,
    g4_ref,
    wide_ref,
    out_ref,
    act_ref,
    y2_ref,
    u_ref,
    dh_ref,
    df_ref,
    dz_ref,
    dv_ref,
    dd_ref,
    dx2_ref,
    s512_ref,
    s2048_ref,
    s1024_ref,
    held_ref,
    w_out_ref,
    w_exp_ref,
    w_red_ref,
    g1_ref,
    g2_ref,
    *,
    order,
    dealt,
):
    q = pl.program_id(0)
    mask = pair_mask(extents(valid_ref), q)
    out_bias, mix, gain, shift, red_bias, ffn = (
        wide_ref[5 + k // 2 : 6 + k // 2, k % 2 * 512 : k % 2 * 512 + 512] for k in range(6)
    )
    lane = lax.broadcasted_iota(i32, (512, 128), 1)
    is0 = (lane >= 32) & (lane < 64)
    is1 = lane >= 64

    @pl.when(q == 0)
    def _():
        s512_ref[...] = jnp.zeros_like(s512_ref)
        s2048_ref[...] = jnp.zeros_like(s2048_ref)
        s1024_ref[...] = jnp.zeros_like(s1024_ref)
        g1_ref[...] = jnp.zeros_like(g1_ref)
        g2_ref[...] = jnp.zeros_like(g2_ref)
        g1_ref[32:64, 64:128] = first_ref[...]
        g2_ref[64:128] = second_ref[...]
        number = own_number(dealt)
        place_rows(w_out_ref, (oa, ob, oc, od), order, number, 16)
        place_rows(w_exp_ref, (ea, eb4, ec, ed), order, number, 16)
        for p in range(32):
            owner = dealt_owner(p, "plain" if dealt else "none")
            ref, first = (ra, rb)[p // 16], p % 16 * 64
            w_red_ref[pl.ds(pl.multiple_of(owner * 64, 64), 64), :] = ref[first : first + 64, :]

    d01, d2, d3, d4 = d_ref[:, 0:128], d_ref[:, 128:256], d_ref[:, 256:512], d_ref[:, 512:1024]
    pointwise = pltpu.roll(j0_ref[...], 32, axis=1)
    u0 = jnp.where(is0, pointwise * d01, 0.0).astype(bf16)
    v1 = dot(u0, g1_ref[...]) + wide_ref[2:3, 0:128]
    u1 = jnp.where(is1, v1 * d01, 0.0).astype(bf16)
    v2 = dot(u1, g2_ref[...]) + wide_ref[2:3, 128:256]
    u2 = (v2 * d2).astype(bf16)
    v3 = dot(u2, g3_ref[...]) + wide_ref[2:3, 256:512]
    u3 = (v3 * d3).astype(bf16)
    v4 = dot(u3, g4_ref[...]) + wide_ref[2:3, 512:1024]
    u4 = (v4 * d4).astype(bf16)
    u_ref[0:128] = jnp.where(is1, u1, u0).T
    u_ref[128:256] = u2.T
    u_ref[256:512] = u3.T
    u_ref[512:1024] = u4.T
    branch = dot(u4, w_out_ref[...]) + out_bias
    middle = xp_ref[...].astype(f32) + mask * mix * branch
    normed, inverse = normalize(middle)
    y2 = (mask * (normed * gain + shift)).astype(bf16)
    y2_ref[...] = y2.T
    grad = gp_ref[...].astype(f32)
    df = (mask * ffn * grad).astype(bf16)
    df_ref[...] = df
    reduced = red_bias
    back = jnp.zeros((512, 512), f32)
    for k in range(4):
        cols = slice(k * 512, (k + 1) * 512)
        hidden = dot(y2, w_exp_ref[:, cols]) + wide_ref[3 + k // 2 : 4 + k // 2, k % 2 * 512 : k % 2 * 512 + 512]
        cdf = 0.5 * (1.0 + lax.erf(hidden * inv_root_two))
        act = (hidden * cdf).astype(bf16)
        act_ref[cols, :] = act.T
        reduced = reduced + dot(act, w_red_ref[cols, :])
        density = jnp.exp(-0.5 * hidden * hidden) * inv_root_tau
        dh = (dot_nt(df, w_red_ref[cols, :]) * (cdf + hidden * density)).astype(bf16)
        dh_ref[:, cols] = dh
        s2048_ref[:, cols] += column_sum(dh.astype(f32))
        back = back + dot_nt(dh, w_exp_ref[:, cols])
    held_ref[pl.ds(2 * q, 2)] = (middle + mask * ffn * reduced).astype(bf16).reshape(2, 256, 512)
    s512_ref[0:1] += column_sum(grad * mask * reduced)
    s512_ref[1:2] += column_sum(df.astype(f32))
    back = mask * back
    s512_ref[2:3] += column_sum(back * normed)
    s512_ref[3:4] += column_sum(back)
    dx2 = grad + norm_backward(back, normed, inverse, gain)
    dx2_ref[...] = dx2
    dz = (mask * mix * dx2).astype(bf16)
    dz_ref[...] = dz
    s512_ref[4:5] += column_sum(dx2 * mask * branch)
    s512_ref[5:6] += column_sum(dz.astype(f32))
    du4 = dot_nt(dz, w_out_ref[...])
    dv4 = (du4 * d4).astype(bf16)
    dd4 = (du4 * v4).astype(bf16)
    du3 = dot_nt(dv4, g4_ref[...])
    dv3 = (du3 * d3).astype(bf16)
    dd3 = (du3 * v3).astype(bf16)
    du2 = dot_nt(dv3, g3_ref[...])
    dv2 = (du2 * d2).astype(bf16)
    dd2 = (du2 * v2).astype(bf16)
    du1 = dot_nt(dv2, g2_ref[...])
    dv1 = (du1 * d01).astype(bf16)
    du0 = dot_nt(dv1, g1_ref[...])
    dpw = pltpu.roll(du0 * d01, 96, axis=1)
    dd01 = jnp.where(is1, du1 * v1, jnp.where(is0, du0 * pointwise, dpw)).astype(bf16)
    dv_ref[:, 0:128] = dv1
    dv_ref[:, 128:256] = dv2
    dv_ref[:, 256:512] = dv3
    dv_ref[:, 512:1024] = dv4
    dd_ref[:, 0:128] = dd01
    dd_ref[:, 128:256] = dd2
    dd_ref[:, 256:512] = dd3
    dd_ref[:, 512:1024] = dd4
    for k, ref in enumerate((dv_ref, dd_ref)):
        s1024_ref[k : k + 1] += column_sum(ref[...].astype(f32))

    @pl.when(q == 1)
    def _():
        unpermute(held_ref, out_ref)


def unpermute(held_ref, out_ref):
    perm = permutation()
    for b in range(4):
        block = jnp.concatenate([held_ref[k, b * 64 : (b + 1) * 64] for k in range(4)], axis=0)
        block = dot_tn(perm, block).astype(bf16)
        out_ref[0, b * 128 : (b + 1) * 128] = block[0:128]
        out_ref[1, b * 128 : (b + 1) * 128] = block[128:256]


def middle_call(valid, d, j0, xp, gp, w_exp, w_red, g1, g2, g3, g4, wide, order, dealt, deps=()):
    def chunk(width):
        return pl.BlockSpec((512, width), lambda q: (q, 0))

    def out(width, dtype=bf16):
        return jax.ShapeDtypeStruct((1024, width), dtype)

    def turned(rows):
        return pl.BlockSpec((rows, 512), lambda q: (0, q))

    def out_turned(rows):
        return jax.ShapeDtypeStruct((rows, 1024), bf16)

    widths = (2048, 512, 512, 1024, 1024)
    rows = (2048, 512, 1024)
    return launch(
        deps,
        functools.partial(middle_kernel, order=order, dealt=dealt),
        grid=(2,),
        out_shape=(jax.ShapeDtypeStruct((2, 512, 512), bf16),)
        + tuple(out_turned(r) for r in rows)
        + tuple(out(w) for w in widths)
        + (
            out(512, f32),
            jax.ShapeDtypeStruct((8, 512), f32),
            jax.ShapeDtypeStruct((1, 2048), f32),
            jax.ShapeDtypeStruct((8, 1024), f32),
        ),
        in_specs=[SMEM, chunk(1024), chunk(128), chunk(512), chunk(512)]
        + [pl.BlockSpec((128, 512), lambda q: (0, 4))] * 4
        + [pl.BlockSpec((128, 2048), lambda q: (0, 0))] * 4
        + [whole((1024, 512))] * 2
        + [whole(v.shape) for v in (g1, g2, g3, g4, wide)],
        out_specs=(whole((2, 512, 512)),)
        + tuple(turned(r) for r in rows)
        + tuple(chunk(w) for w in widths)
        + (chunk(512), whole((8, 512)), whole((1, 2048)), whole((8, 1024))),
        scratch_shapes=[
            pltpu.VMEM((4, 256, 512), bf16),
            pltpu.VMEM((512, 512), bf16),
            pltpu.VMEM((512, 2048), bf16),
            pltpu.VMEM((2048, 512), bf16),
            pltpu.VMEM((128, 128), bf16),
            pltpu.VMEM((128, 128), bf16),
        ],
        cost_estimate=takes(30),
        name="middle",
    )(valid, *(v.reshape(1024, -1) for v in (d, j0, xp, gp)), *w_exp, *w_exp, *w_red, g1, g2, g3, g4, wide)


def feed_grads_kernel(
    y2_ref, dh_ref, act_ref, df_ref, u_ref, dz_ref, e_keep, e_send, r_keep, r_send, exp_ref, red_ref, out_ref, *, e_order, r_order
):
    step = pl.program_id(0)
    exp_ref[...] = dot(y2_ref[...], dh_ref[...])
    red_ref[pl.ds(pl.multiple_of(step * 512, 512), 512), :] = dot(act_ref[...], df_ref[...])
    deal_rows((e_keep, e_send), (slice(None),), exp_ref, e_order, 16)

    @pl.when(step == 0)
    def _():
        out_ref[...] = dot(u_ref[...], dz_ref[...])

    @pl.when(step == 3)
    def _():
        for p in range(32):
            owner = dealt_owner(p, r_order)
            ref, first = (r_keep, r_send)[p // 16], p % 16 * 80
            ref[first : first + 64] = red_ref[pl.ds(pl.multiple_of(owner * 64, 64), 64), :].astype(bf16)
            ref[first + 64 : first + 80] = out_ref[pl.ds(pl.multiple_of(owner * 16, 16), 16), :].astype(bf16)


def feed_grads(y2, dh, act, df, u, dz, e_order, r_order, deps=()):
    return launch(
        deps,
        functools.partial(feed_grads_kernel, e_order=e_order, r_order=r_order),
        grid=(4,),
        out_shape=(jax.ShapeDtypeStruct((256, 2048), bf16),) * 2 + (jax.ShapeDtypeStruct((1280, 512), bf16),) * 2,
        in_specs=[
            whole((512, 1024)),
            pl.BlockSpec((1024, 512), lambda k: (0, k)),
            pl.BlockSpec((512, 1024), lambda k: (k, 0)),
            whole((1024, 512)),
            pl.BlockSpec((512, 1024), lambda k: (1, 0)),
            whole((1024, 512)),
        ],
        out_specs=(pl.BlockSpec((256, 512), lambda k: (0, k)),) * 2 + (whole((1280, 512)),) * 2,
        scratch_shapes=[pltpu.VMEM((512, 512), f32), pltpu.VMEM((2048, 512), f32), pltpu.VMEM((512, 512), f32)],
        cost_estimate=takes(11),
        name="feed_grads",
    )(y2, dh, act, df, u, dz)


def kernel_grad_kernel(dd_ref, band_ref, dk_ref):
    low = low_lanes((256, 128))
    low8 = low_lanes((8, 128))
    wide = diagonal(256)
    for tile in range(2):
        cols = slice(tile * 128, tile * 128 + 128)
        own = [dd_ref[q, :, cols].astype(f32) for q in range(4)]
        turned_own = [swap_lanes(v) for v in own]
        for side in range(2):
            group = tile * 2 + side
            halves = []
            for rp in range(2):
                if side == 0:
                    halves.append(jnp.where(low, own[2 * rp], turned_own[2 * rp + 1]))
                else:
                    halves.append(jnp.where(low, turned_own[2 * rp], own[2 * rp + 1]))
            left = jnp.concatenate(halves, axis=1).astype(bf16)
            rows = {}
            for ti in range(4):
                for tj in range(4):
                    cross = dot_tn(left, band_block(band_ref, (group,), ti, tj))
                    for rp in range(2):
                        half = jnp.where(wide, cross[:, rp * 128 : rp * 128 + 128], 0.0)
                        part = jnp.sum(half.reshape(4, 8, 8, 128), axis=1)
                        for out_rp in range(2):
                            i = 2 * ti + rp - out_rp
                            if 0 <= i <= 6:
                                for out_cp in range(2):
                                    key = (i, tj, out_cp)
                                    term = part[out_rp * 2 + out_cp]
                                    rows[key] = rows[key] + term if key in rows else term
            for i in range(7):
                turned = [swap_lanes(rows[i, tj, 1]) for tj in range(4)] + [jnp.zeros((8, 128), f32)]
                for tj in range(4):
                    value = rows[i, tj, 0] + jnp.where(low8, turned[tj], turned[tj + 1])
                    dk_ref[group, i * 4 + tj : i * 4 + tj + 1] = column_sum(value) * conv_scale
            dk_ref[group, 28:32] = jnp.zeros((4, 128), f32)


def kernel_grad(dd, band, deps=()):
    return launch(
        deps,
        kernel_grad_kernel,
        grid=(4,),
        out_shape=jax.ShapeDtypeStruct((16, 32, 128), f32),
        in_specs=[
            pl.BlockSpec((4, 256, 256), lambda t: (0, 0, t)),
            pl.BlockSpec((4, 13, 5, 16, 256), lambda t: (t, 0, 0, 0, 0)),
        ],
        out_specs=pl.BlockSpec((4, 32, 128), lambda t: (t, 0, 0)),
        cost_estimate=takes(13),
        name="kernel_grad",
    )(dd, band)


def gate_grads_kernel(u_ref, dv_ref, s512_ref, s2048_ref, s1024_ref, dk_ref, keep, send, small_ref, *, order):
    small_ref[0:256] = dot(u_ref[256:512], dv_ref[:, 512:1024])
    g3 = dot(u_ref[128:256], dv_ref[:, 256:512])
    small_ref[256:320, 0:256] = g3[0:64]
    small_ref[256:320, 256:512] = g3[64:128]
    g12 = dot(u_ref[0:128], dv_ref[:, 0:256])
    for k in range(4):
        cols = slice(k * 128, (k + 1) * 128)
        small_ref[320:336, cols] = g12[64 + 16 * k : 80 + 16 * k, 128:256]
        small_ref[336:344, cols] = g12[32 + 8 * k : 40 + 8 * k, 0:128]
        small_ref[384:512, cols] = dk_ref[k * 128 : (k + 1) * 128]
        small_ref[352 + k : 353 + k] = s2048_ref[:, k * 512 : (k + 1) * 512]
        small_ref[356 + k : 357 + k] = s1024_ref[k // 2 : k // 2 + 1, k % 2 * 512 : k % 2 * 512 + 512]
    small_ref[344:352] = s512_ref[...]
    small_ref[360:384] = jnp.zeros((24, 512), f32)
    deal_rows((keep, send), (slice(None),), small_ref, order, 16)


def gate_grads(u, dv, s512, s2048, s1024, dk, order, deps=()):
    return launch(
        deps,
        functools.partial(gate_grads_kernel, order=order),
        grid=(1,),
        out_shape=(jax.ShapeDtypeStruct((256, 512), bf16),) * 2,
        in_specs=[whole((512, 1024))] + [whole(v.shape) for v in (dv, s512, s2048, s1024, dk)],
        out_specs=(whole((256, 512)),) * 2,
        scratch_shapes=[pltpu.VMEM((512, 512), f32)],
        cost_estimate=takes(3),
        name="gate_grads",
    )(u, dv, s512, s2048, s1024, dk)


def unpack_kernel(own_ref, oth_ref, *rest):
    outs, (table_ref, all_ref) = rest[:-2], rest[-2:]
    in_ref, dk_ref, dwb_ref, g1_ref, g2_ref, g3_ref, g4_ref, gb_ref = outs[:8]
    outb_ref, mix_ref, gain_ref, shift_ref, expb_ref, redb_ref, ffn_ref = outs[8:]
    row = lax.axis_index("row")
    total = own_ref[0:16, 0:1024].astype(f32)
    for k in range(1, 16):
        total = total + own_ref[k * 16 : (k + 1) * 16, 0:1024].astype(f32)
    in_ref[...] = total
    for k in range(16):
        block = slice(k * 16, (k + 1) * 16)
        table_ref[pl.ds(pl.multiple_of((2 * k + row) * 16, 16), 16), :] = own_ref[block, 1024:1536]
        table_ref[pl.ds(pl.multiple_of((2 * k + 1 - row) * 16, 16), 16), :] = oth_ref[block, 1024:1536]
    all_ref[...] = table_ref[...].astype(f32)
    g4_ref[...] = all_ref[0:256]
    g3_ref[0:64] = all_ref[256:320, 0:256]
    g3_ref[64:128] = all_ref[256:320, 256:512]
    for k in range(4):
        cols = slice(k * 128, (k + 1) * 128)
        g2_ref[16 * k : 16 * k + 16] = all_ref[320:336, cols]
        g1_ref[8 * k : 8 * k + 8] = swap_lanes(all_ref[336:344, cols])[:, 0:64]
        expb_ref[k * 512 : (k + 1) * 512] = all_ref[352 + k : 353 + k].reshape(512)
    for k, ref in enumerate((ffn_ref, redb_ref, gain_ref, shift_ref, mix_ref, outb_ref)):
        ref[...] = all_ref[344 + k : 345 + k].reshape(512)

    def line(first):
        return jnp.concatenate([all_ref[first : first + 1], all_ref[first + 1 : first + 2]], axis=1)

    gb_ref[...] = line(356)[:, 64:1024].reshape(960)
    dwb_ref[...] = line(358)[:, 32:1024].reshape(992) * conv_scale
    low = low_lanes((32, 128))
    lane = lax.broadcasted_iota(i32, (32, 128), 1)
    rows = []
    for t in range(8):
        cols = slice(t // 2 * 128, t // 2 * 128 + 128)
        first = 384 + t % 2 * 64
        left = all_ref[first : first + 32, cols]
        right = all_ref[first + 32 : first + 64, cols]
        pair = (jnp.where(low, left, swap_lanes(right)), jnp.where(low, swap_lanes(left), right))
        rows.append([pltpu.roll(v, 96, axis=1) for v in pair])
    for t in range(8):
        size = 128 if t < 7 else 96
        for odd in range(2):
            value = jnp.where(lane < 96, rows[t][odd], rows[t + 1][odd]) if t < 7 else rows[t][odd]
            for i in range(7):
                for j in range(odd, 7, 2):
                    at = i * 4 + j // 2
                    dk_ref[i, j : j + 1, t * 128 : t * 128 + size] = value[at : at + 1, 0:size]


def unpack(own, oth, deps=()):
    vmem = pl.BlockSpec(memory_space=pltpu.VMEM)
    shapes = ((16, 1024), (7, 7, 992), (992,), (32, 64), (64, 128), (128, 256), (256, 512), (960,))
    shapes += ((512,),) * 4 + ((2048,), (512,), (512,))
    return launch(
        deps,
        unpack_kernel,
        out_shape=tuple(jax.ShapeDtypeStruct(v, f32) for v in shapes),
        in_specs=[vmem] * 2,
        out_specs=(vmem,) * len(shapes),
        scratch_shapes=[pltpu.VMEM((512, 512), bf16), pltpu.VMEM((512, 512), f32)],
        cost_estimate=takes(3),
        name="unpack",
    )(own, oth)


def conv_back_kernel(valid_ref, dd_ref, ddh_ref, tap_ref, df_ref, w_ref, back_ref):
    step = pl.program_id(0)

    @pl.when(step == 0)
    def _():
        clear_weights(w_ref)

    sizes = extents(valid_ref)
    lane = lax.broadcasted_iota(i32, (256, 128), 1)
    keep = (lane < 32) & (step == 0)
    own = [dd_ref[q].astype(f32) for q in range(4)]
    halo = [ddh_ref[q].astype(f32) for q in range(4)]
    sums = convolve_groups(back_ref, w_ref, tap_ref, own, halo, is_upper(), True)
    for tile in range(2):
        cols = slice(tile * 128, tile * 128 + 128)
        for q, value in enumerate(split_lanes(*sums[2 * tile : 2 * tile + 2])):
            value = value * (chunk_mask(sizes, q // 2, q % 2) * conv_scale)
            if tile == 0:
                value = jnp.where(keep, own[q][:, cols], value)
            df_ref[q, :, cols] = value.astype(bf16)


def conv_back(valid, dd, ddh, taps, deps=()):
    return launch(
        deps,
        conv_back_kernel,
        grid=(4,),
        out_shape=jax.ShapeDtypeStruct((4, 256, 1024), bf16),
        in_specs=[
            SMEM,
            pl.BlockSpec((4, 256, 256), lambda t: (0, 0, t)),
            pl.BlockSpec((4, 64, 256), lambda t: (0, 0, t)),
            pl.BlockSpec((7, 7, 256), lambda t: (0, 0, t)),
        ],
        out_specs=pl.BlockSpec((4, 256, 256), lambda t: (0, 0, t)),
        scratch_shapes=[pltpu.VMEM((2, 16, 256, 256), bf16), pltpu.VMEM((4, 13, 5, 16, 256), bf16)],
        cost_estimate=takes(16),
        name="conv_back",
    )(valid, dd, ddh, taps)


def in_grad_kernel(y1_ref, df_ref, keep, send, sum_ref, *, order):
    sum_ref[...] = dot(y1_ref[...], df_ref[...])
    deal_rows((keep, send), (slice(None),), sum_ref, order, 16)


def in_grad(y1, df, order, deps=()):
    return launch(
        deps,
        functools.partial(in_grad_kernel, order=order),
        grid=(2,),
        out_shape=(jax.ShapeDtypeStruct((256, 1024), bf16),) * 2,
        in_specs=[whole((512, 1024)), pl.BlockSpec((1024, 512), lambda k: (0, k))],
        out_specs=(pl.BlockSpec((256, 512), lambda k: (0, k)),) * 2,
        scratch_shapes=[pltpu.VMEM((512, 512), f32)],
        cost_estimate=takes(4),
        name="in_grad",
    )(y1, df)


def last_kernel(valid_ref, df_ref, xp_ref, dx2_ref, *rest, order, dealt):
    weights, (wide_ref, out_ref, late_ref, held_ref, win_ref) = rest[:8], rest[8:]
    q = pl.program_id(0)

    @pl.when(q == 0)
    def _():
        late_ref[...] = jnp.zeros_like(late_ref)
        place_rows(win_ref, weights, order, own_number(dealt), 16)

    mask = pair_mask(extents(valid_ref), q)
    df = df_ref[...]
    sums = column_sum(df.astype(f32))
    late_ref[2:3] += sums[:, 0:512]
    late_ref[3:4] += sums[:, 512:1024]
    grad = mask * dot_nt(df, win_ref[...])
    normed, inverse = normalize(xp_ref[...].astype(f32))
    late_ref[0:1] += column_sum(grad * normed)
    late_ref[1:2] += column_sum(grad)
    total = dx2_ref[...] + norm_backward(grad, normed, inverse, wide_ref[8:9, 0:512])
    held_ref[pl.ds(2 * q, 2)] = total.astype(bf16).reshape(2, 256, 512)

    @pl.when(q == 1)
    def _():
        unpermute(held_ref, out_ref)


def last_call(valid, df, xp, dx2, w_in, wide, order, dealt, deps=()):
    def chunk(width):
        return pl.BlockSpec((512, width), lambda q: (q, 0))

    return launch(
        deps,
        functools.partial(last_kernel, order=order, dealt=dealt),
        grid=(2,),
        out_shape=(jax.ShapeDtypeStruct((2, 512, 512), bf16), jax.ShapeDtypeStruct((8, 512), f32)),
        in_specs=[SMEM, chunk(1024), chunk(512), chunk(512)] + [whole((64, 1024))] * 8 + [whole(wide.shape)],
        out_specs=(whole((2, 512, 512)), whole((8, 512))),
        scratch_shapes=[pltpu.VMEM((4, 256, 512), bf16), pltpu.VMEM((512, 1024), bf16)],
        cost_estimate=takes(7),
        name="last",
    )(valid, *(v.reshape(1024, -1) for v in (df, xp, dx2)), *w_in, wide)


def repeat(value):
    rows, cols = value.shape
    return jnp.broadcast_to(value[None], (16, rows, cols)).reshape(16 * rows, cols)


def join_kernel(*refs, counts):
    ins = list(refs[: sum(counts)])
    for out, count in zip(refs[sum(counts) :], counts):
        at = 0
        for _ in range(count):
            ref = ins.pop(0)
            out[at : at + ref.shape[0]] = ref[...]
            at += ref.shape[0]


def join(*lists, deps=()):
    vmem = pl.BlockSpec(memory_space=pltpu.VMEM)
    shapes = [(sum(v.shape[0] for v in group), group[0].shape[1]) for group in lists]
    return launch(
        deps,
        functools.partial(join_kernel, counts=[len(v) for v in lists]),
        out_shape=tuple(jax.ShapeDtypeStruct(v, bf16) for v in shapes),
        in_specs=[vmem] * sum(len(v) for v in lists),
        out_specs=(vmem,) * len(lists),
        cost_estimate=takes(1),
        name="join",
    )(*sum((list(v) for v in lists), []))


def add_kernel(a_ref, b_ref, out_ref):
    out_ref[...] = a_ref[...] + b_ref[...]


def add(a, b, deps=()):
    vmem = pl.BlockSpec(memory_space=pltpu.VMEM)
    return launch(
        deps,
        add_kernel,
        out_shape=jax.ShapeDtypeStruct(a.shape, a.dtype),
        in_specs=[vmem] * 2,
        out_specs=vmem,
        cost_estimate=takes(1),
        name="add",
    )(a, b)


def combine_kernel(*refs, items):
    at = sum(n for n, _ in items)
    ins, outs = list(refs[:at]), list(refs[at:])
    for count, parts in items:
        terms = [ins.pop(0) for _ in range(count)]
        for part in range(parts):
            total = functools.reduce(lambda a, b: a + b, [v[part, 0].astype(f32) for v in terms])
            outs.pop(0)[0] = total.astype(bf16)


def combine(*items, deps=()):
    steps = next(n for n in (4, 2, 1) if all(v[0].shape[0] % (16 * n * p) == 0 for v, p in items))
    ins, in_specs, outs, out_specs = [], [], [], []
    for terms, parts in items:
        rows, cols = terms[0].shape
        size = rows // parts // steps
        ins += [v.reshape(parts, steps, size, cols) for v in terms]
        in_specs += [pl.BlockSpec((parts, 1, size, cols), lambda t: (0, t, 0, 0))] * len(terms)
        outs += [jax.ShapeDtypeStruct((steps, size, cols), bf16)] * parts
        out_specs += [pl.BlockSpec((1, size, cols), lambda t: (t, 0, 0))] * parts
    *values, token = launch(
        deps,
        functools.partial(combine_kernel, items=[(len(v), p) for v, p in items]),
        grid=(steps,),
        out_shape=tuple(outs),
        in_specs=in_specs,
        out_specs=tuple(out_specs),
        cost_estimate=takes(2),
        name="combine",
    )(*ins)
    return [v.reshape(-1, v.shape[-1]) for v in values] + [token]


def merge_kernel(ro_a, ro_b, e_a, e_b, *outs):
    for z, ref in enumerate(outs):
        rows = slice(z * 80, (z + 1) * 80)
        ref[0:80] = (ro_a[rows].astype(f32) + ro_b[rows].astype(f32)).astype(bf16)
        total = e_a[z * 16 : (z + 1) * 16].astype(f32) + e_b[z * 16 : (z + 1) * 16].astype(f32)
        for c in range(4):
            at = 80 + c * 16
            ref[at : at + 16] = total[:, c * 512 : (c + 1) * 512].astype(bf16)


def merge(ro_a, ro_b, e_a, e_b, deps=()):
    vmem = pl.BlockSpec(memory_space=pltpu.VMEM)
    return launch(
        deps,
        merge_kernel,
        out_shape=(jax.ShapeDtypeStruct((144, 512), bf16),) * 4,
        in_specs=[vmem] * 4,
        out_specs=(vmem,) * 4,
        cost_estimate=takes(2),
        name="merge",
    )(ro_a, ro_b, e_a, e_b)


def finish_kernel(*refs):
    ins, (red_ref, out_ref, exp_ref) = refs[:-3], refs[-3:]
    total = functools.reduce(lambda a, b: a + b, [v[...].astype(f32) for v in ins])
    red_ref[...] = total[0:64]
    out_ref[...] = total[64:80]
    for c in range(4):
        exp_ref[:, c * 512 : (c + 1) * 512] = total[80 + c * 16 : 96 + c * 16]


def finish(parts, deps=()):
    vmem = pl.BlockSpec(memory_space=pltpu.VMEM)
    shapes = ((64, 512), (16, 512), (16, 2048))
    return launch(
        deps,
        finish_kernel,
        out_shape=tuple(jax.ShapeDtypeStruct(v, f32) for v in shapes),
        in_specs=[vmem] * len(parts),
        out_specs=(vmem,) * 3,
        cost_estimate=takes(1),
        name="finish",
    )(*parts)


def deal_kernel(i_a, i_b, *rest):
    parts, out_ref = rest[:-1], rest[-1]
    small = functools.reduce(lambda a, b: a + b, [v[...].astype(f32) for v in parts]).astype(bf16)
    out_ref[:, 0:1024] = (i_a[...].astype(f32) + i_b[...].astype(f32)).astype(bf16)
    for k in range(16):
        out_ref[k * 16 : (k + 1) * 16, 1024:1536] = small


def deal(i_a, i_b, parts, deps=()):
    vmem = pl.BlockSpec(memory_space=pltpu.VMEM)
    return launch(
        deps,
        deal_kernel,
        out_shape=jax.ShapeDtypeStruct((256, 1536), bf16),
        in_specs=[vmem] * (2 + len(parts)),
        out_specs=vmem,
        cost_estimate=takes(2),
        name="deal",
    )(i_a, i_b, *parts)


def late_kernel(a_ref, b_ref, gain_ref, shift_ref, bias_ref):
    total = a_ref[...] + b_ref[...]
    gain_ref[...] = total[0:1].reshape(512)
    shift_ref[...] = total[1:2].reshape(512)
    bias_ref[0:512] = total[2:3].reshape(512)
    bias_ref[512:1024] = total[3:4].reshape(512)


def late_sums(a, b, deps=()):
    vmem = pl.BlockSpec(memory_space=pltpu.VMEM)
    return launch(
        deps,
        late_kernel,
        out_shape=tuple(jax.ShapeDtypeStruct((v,), f32) for v in (512, 512, 1024)),
        in_specs=[vmem] * 2,
        out_specs=(vmem,) * 3,
        cost_estimate=takes(1),
        name="late",
    )(a, b)


ROW = "row"


def img_bits():
    return lax.axis_size("img").bit_length() - 1


def swap_img(value, mask):
    return lax.ppermute(value, "img", [(k, k ^ mask) for k in range(lax.axis_size("img"))])


def swap_row(value):
    return lax.ppermute(value, "row", [(0, 1), (1, 0)])


def masks_of(stage):
    masks = [0]
    for bit in stage:
        masks = [m | v for m in masks for v in (0, 1 << bit)]
    return masks


def gather_order(groups):
    rel = [0]
    for bits in groups:
        rel = [m ^ r for m in masks_of(bits) for r in rel]
    return [2 * r + side for side in (0, 1) for r in rel]


def swaps(value, bits):
    return [value] + [swap_img(value, m) for m in masks_of(bits)[1:]]


def after(value, *others):
    return lax.optimization_barrier((value, others))[0]


def spread(value):
    return lax.all_to_all(value, "img", split_axis=0, concat_axis=0, tiled=True)


def sum_img(value, bits):
    for bit in bits[:-1]:
        value = value + swap_img(value, 1 << bit)
    return value, swap_img(value, 1 << bits[-1])


def own_bit(bit):
    return lax.axis_index("row") if bit == ROW else (lax.axis_index("img") >> bit) & 1


def swap_bit(value, bit):
    return swap_row(value) if bit == ROW else swap_img(value, 1 << bit)


def plain_gather(shard):
    value = shard
    for bit in [ROW] + list(range(img_bits())):
        other = swap_bit(value, bit)
        mine = own_bit(bit) == 0
        value = jnp.concatenate([jnp.where(mine, value, other), jnp.where(mine, other, value)], axis=0)
    return value


def plain_scatter(value):
    for bit in list(range(img_bits()))[::-1] + [ROW]:
        half = value.shape[0] // 2
        mine = own_bit(bit) == 0
        first, second = value[:half], value[half:]
        sent = swap_bit(jnp.where(mine, second, first).astype(bf16), bit)
        value = jnp.where(mine, first, second).astype(f32) + sent.astype(f32)
    return value


def per_device(
    features,
    validity,
    upstream,
    normgain,
    normshift,
    inweight,
    inbias,
    dwkernel,
    dwbias,
    gatefirst,
    gatesecond,
    gatethird,
    gatefourth,
    gatebias,
    outweight,
    outbias,
    mixscale,
    mlpgain,
    mlpshift,
    expandweight,
    expandbias,
    reduceweight,
    reducebias,
    mlpscale,
):
    bits = img_bits()
    dealt = bits == 4
    lower = lax.axis_index("row") == 1

    x = features.reshape(2, 512, 512)
    g = upstream.reshape(2, 512, 512)
    valid = validity.reshape(32, 32)
    x_halo = swap_row(x)
    halo_valid = swap_row(valid)
    taps = jnp.pad(dwkernel.astype(f32), ((0, 0), (0, 0), (32, 0)))
    wide, token = gather_vectors(
        (inbias, dwbias, gatebias, expandbias),
        (outbias, mixscale, mlpgain, mlpshift, reducebias, mlpscale, normgain, normshift),
    )
    exp_out = jnp.concatenate([expandweight, outweight], axis=1)
    deep, flat_pair = (3, 2), (1, 0)
    if dealt:
        in_order = gather_order((deep, flat_pair))
        exp_order = gather_order((deep, (1,), (0,)))
        in_z, token = join(swaps(inweight, deep))
        exp_parts = swaps(exp_out, deep)
        red_own = spread(repeat(reduceweight))
        w_in = swaps(in_z, flat_pair)
        xp, gp, y1, y1h, y1t, token = prepare(valid, halo_valid, x, x_halo, g, wide, [token])
        exp_z, token = join(exp_parts, deps=[token] + w_in[1:])
        w_in = w_in + [swap_row(v) for v in w_in]
        exp_y, token = join(swaps(exp_z, (1,)), deps=[token])
        w_exp = swaps(exp_y, (0,))
        d, band, j0, token = forward(valid, halo_valid, y1, y1h, w_in, wide, taps, in_order, dealt, [token])
        w_exp = w_exp + [swap_row(w_exp[0]), swap_row(after(w_exp[1], d))]
        w_red = [red_own, swap_row(after(red_own, d))]
    else:
        in_order = exp_order = list(range(32))
        w_in = jnp.split(plain_gather(inweight), 8, axis=0)
        w_exp = jnp.split(plain_gather(exp_out), 4, axis=0)
        w_red = jnp.split(plain_gather(reduceweight), 2, axis=0)
        xp, gp, y1, y1h, y1t, token = prepare(valid, halo_valid, x, x_halo, g, wide)
        d, band, j0, token = forward(valid, halo_valid, y1, y1h, w_in, wide, taps, in_order, dealt)
    (produced, act, y2, u, dh, df, dz, dv, dd, dx2, s512, s2048, s1024, token) = middle_call(
        valid, d, j0, xp, gp, w_exp, w_red, gatefirst, gatesecond, gatethird, gatefourth, wide, exp_order, dealt
    )
    dd = dd.reshape(4, 256, 1024)
    dd_halo = swap_row(jnp.where(lower, dd[:, 0:64], dd[:, 192:256]))

    def flat(value):
        return value.reshape(1024, -1)

    r_order, e_order, plain = ((1, 0, 3, 2), (0, 1, 3, 2), "plain") if dealt else ("none",) * 3
    if dealt:
        e_keep, e_send, r_keep, r_send, token = feed_grads(
            y2, flat(dh), act, flat(df), u, flat(dz), e_order, r_order
        )
        e_got, r_got = swap_row(e_send), swap_row(r_send)
        dk, token = kernel_grad(dd, band, [token])
        s_keep, s_send, token = gate_grads(
            u, flat(dv), s512, s2048, s1024, dk.reshape(512, 128), flat_pair + deep, [token]
        )
        s_got = swap_row(s_send)
        r_keep, r_send, e_keep, e_send, *small, token = combine(
            ([r_keep, r_got], 2), ([e_keep, e_got], 2), ([s_keep, s_got], 4), deps=[token]
        )
        r_got, e_got = swap_img(r_send, 2), swap_img(e_send, 1)
        small = small[:1] + [swap_img(v, m) for v, m in zip(small[1:], masks_of(flat_pair)[1:])]
        dfused, token = conv_back(valid, dd, dd_halo, taps, [token])
        r_keep, r_send, e_keep, e_send, *small, token = combine(
            ([r_keep, r_got], 2), ([e_keep, e_got], 2), (small, 4), deps=[token]
        )
        r_got, e_got = swap_img(r_send, 1), swap_img(e_send, 2)
        small = small[:1] + [swap_img(v, m) for v, m in zip(small[1:], masks_of(deep)[1:])]
        i_keep, i_send, token = in_grad(y1t, flat(dfused), plain, [token])
        i_got = swap_row(i_send)
        *parts, token = merge(r_keep, r_got, e_keep, e_got, [token])
        parts = parts[:1] + [swap_img(v, m) for v, m in zip(parts[1:], masks_of(deep)[1:])]
        fgrad, late, token = last_call(
            valid, dfused, xp, dx2, w_in, wide, in_order, dealt, [token] + small[1:]
        )
        dealt_rows, token = deal(i_keep, i_got, small, [token] + parts[1:])
        mixed = spread(dealt_rows)
        red_sum, out_sum, exp_sum, token = finish(parts, [token])
        late, got = sum_img(late + swap_row(late), (0, 1, 2, 3))
        own, oth = mixed, swap_row(after(mixed, late))
        sums = late_sums(late, got, [token])
    else:

        def total(parts, rows):
            value = jnp.concatenate(parts, axis=0)
            return plain_scatter(value.reshape(32, -1, value.shape[1])[:, rows].reshape(-1, value.shape[1]))

        everything = slice(None)
        dk, token = kernel_grad(dd, band)
        s_keep, s_send, token = gate_grads(u, flat(dv), s512, s2048, s1024, dk.reshape(512, 128), plain)
        parts = feed_grads(y2, flat(dh), act, flat(df), u, flat(dz), e_order, r_order)
        e_parts, r_parts = parts[:2], parts[2:4]
        dfused, _ = conv_back(valid, dd, dd_halo, taps)
        i_parts = in_grad(y1t, flat(dfused), plain)[:2]
        fgrad, late, token = last_call(valid, dfused, xp, dx2, w_in, wide, in_order, dealt)
        sums = late_sums(*sum_img(late + swap_row(late), list(range(bits))))
        exp_sum, in_sum = total(e_parts, everything), total(i_parts, everything)
        red_sum, out_sum = total(r_parts, slice(0, 64)), total(r_parts, slice(64, 80))
        small = plain_gather(total((s_keep, s_send), everything).astype(bf16)).reshape(16, 2, 16, 512)
        lower_row = lax.axis_index("row")
        own, oth = (
            jnp.pad(lax.dynamic_index_in_dim(small, v, 1, keepdims=False).reshape(256, 512), ((0, 0), (1024, 0)))
            for v in (lower_row, 1 - lower_row)
        )

    unpacked = unpack(own, oth)
    if dealt:
        in_sum = unpacked[0]
    dk_sum, dwb_sum, gate1, gate2, gate3, gate4, gb_sum, outb, mix, gain, shift, expb, redb, ffn = unpacked[1:-1]
    return (
        produced.reshape(features.shape),
        fgrad.reshape(features.shape),
        sums[0],
        sums[1],
        in_sum,
        sums[2],
        dk_sum,
        dwb_sum,
        gate1,
        gate2,
        gate3,
        gate4,
        gb_sum,
        out_sum,
        outb,
        mix,
        gain,
        shift,
        exp_sum,
        expb,
        red_sum,
        redb,
        ffn,
    )


def solution(mesh):
    band = P("img", "row", None, None)
    rows = P(("img", "row"), None)
    copy = P()
    ins = [band, P("img", "row", None), band] + [copy] * 21
    for k in (5, 14, 19, 21):
        ins[k] = rows
    outs = [band, band] + [copy] * 21
    for k in (4, 13, 18, 20):
        outs[k] = rows
    return jax.shard_map(per_device, mesh=mesh, in_specs=tuple(ins), out_specs=tuple(outs), check_vma=False)
```

```python
import functools
import math

import jax
import jax.numpy as jnp
from jax import lax
from jax.experimental import pallas as pl
from jax.experimental.pallas import tpu as pltpu
from jax.sharding import PartitionSpec as P

f32 = jnp.float32
bf16 = jnp.bfloat16
i32 = jnp.int32
norm_eps = 1e-06
conv_scale = 1.0 / 3.0
inv_root_two = 1.0 / math.sqrt(2.0)
inv_root_tau = 1.0 / math.sqrt(2.0 * math.pi)
vmem_bytes = 60 * 1024 * 1024


def dot(left, right):
    return jnp.dot(left, right, preferred_element_type=f32)


def dot_tn(left, right):
    return lax.dot_general(left, right, (((0,), (0,)), ((), ())), preferred_element_type=f32)


def dot_nt(left, right):
    return lax.dot_general(left, right, (((1,), (1,)), ((), ())), preferred_element_type=f32)


def column_sum(values):
    return jnp.sum(values, axis=0, keepdims=True)


def permutation():
    out = lax.broadcasted_iota(i32, (256, 256), 0)
    src = lax.broadcasted_iota(i32, (256, 256), 1)
    row_par, col_par = out >> 7, (out >> 6) & 1
    pair, ccp, img, blk = (out >> 5) & 1, (out >> 4) & 1, (out >> 3) & 1, out & 7
    want = img * 128 + (2 * pair + row_par) * 32 + 4 * blk + 2 * ccp + col_par
    return (src == want).astype(f32).astype(bf16)


def normalize(values):
    center = jnp.mean(values, axis=-1, keepdims=True)
    shifted = values - center
    spread = jnp.mean(shifted * shifted, axis=-1, keepdims=True)
    inverse = lax.rsqrt(spread + norm_eps)
    return shifted * inverse, inverse


def norm_backward(grad_norm, normed, inverse, gain):
    scaled = grad_norm * gain
    return inverse * (
        scaled
        - jnp.mean(scaled, axis=-1, keepdims=True)
        - normed * jnp.mean(scaled * normed, axis=-1, keepdims=True)
    )


def extents(valid_ref):
    heights = [sum(valid_ref[16 * n + r, 0] for r in range(16)) for n in range(2)]
    widths = [sum(valid_ref[16 * n, c] for c in range(32)) for n in range(2)]
    return heights, widths


def chunk_mask(sizes, row_par, col_par, count=256, first_row=0):
    (high_a, high_b), (wide_a, wide_b) = sizes
    at = lax.broadcasted_iota(i32, (count, 1), 0)
    pair, ccp, img, blk = at >> 5, (at >> 4) & 1, (at >> 3) & 1, at & 7
    row = 2 * pair + row_par + first_row
    col = 4 * blk + 2 * ccp + col_par
    high = jnp.where(img == 1, high_b, high_a)
    wide = jnp.where(img == 1, wide_b, wide_a)
    return jnp.where((row < high) & (col < wide), 1.0, 0.0).astype(f32)


def pair_mask(sizes, row_par):
    return jnp.concatenate([chunk_mask(sizes, row_par, col_par) for col_par in range(2)], axis=0)


def halo_sizes(valid_ref, halo_ref):
    heights, widths = extents(valid_ref)
    below, _ = extents(halo_ref)
    upper = lax.axis_index("row") == 0
    return [jnp.where(upper, h, 4) for h in below], widths


def is_upper():
    return jnp.where(lax.axis_index("row") == 0, 1.0, 0.0).astype(f32)


def vectors_kernel(in_ref, dw_ref, gate_ref, exp_ref, *rest):
    small, out_ref = rest[:8], rest[8]

    def line(ref):
        return ref[...].astype(f32).reshape(1, ref.shape[0])

    out_ref[0:1] = line(in_ref)
    out_ref[1:2, 0:32] = jnp.zeros((1, 32), f32)
    out_ref[1:2, 32:1024] = line(dw_ref)
    out_ref[2:3, 0:64] = jnp.zeros((1, 64), f32)
    out_ref[2:3, 64:1024] = line(gate_ref)
    wide = line(exp_ref)
    out_ref[3:4] = wide[:, 0:1024]
    out_ref[4:5] = wide[:, 1024:2048]
    for k, ref in enumerate(small):
        out_ref[5 + k // 2 : 6 + k // 2, k % 2 * 512 : k % 2 * 512 + 512] = line(ref)


def gather_vectors(large, small, deps=()):
    vmem = pl.BlockSpec(memory_space=pltpu.VMEM)
    return launch(
        deps,
        vectors_kernel,
        out_shape=jax.ShapeDtypeStruct((9, 1024), f32),
        in_specs=[vmem] * 12,
        out_specs=vmem,
        cost_estimate=takes(1),
        name="vectors",
    )(*large, *small)


def prepare_kernel(valid_ref, halo_valid_ref, x_ref, xh_ref, g_ref, vec_ref, xp_ref, gp_ref, y1_ref, y1h_ref, y1t_ref):
    perm = permutation()
    gain, shift = vec_ref[8:9, 0:512], vec_ref[8:9, 512:1024]
    own, halo = extents(valid_ref), halo_sizes(valid_ref, halo_valid_ref)
    start = pl.multiple_of(lax.axis_index("row") * 384, 128)
    for b in range(5):
        if b == 4:
            rows = pl.ds(start, 128)
            block = jnp.concatenate([xh_ref[0, rows], xh_ref[1, rows]], axis=0)
        else:
            rows = slice(b * 128, (b + 1) * 128)
            block = jnp.concatenate([x_ref[0, rows], x_ref[1, rows]], axis=0)
            gblock = dot(perm, jnp.concatenate([g_ref[0, rows], g_ref[1, rows]], axis=0)).astype(bf16)
        block = dot(perm, block)
        lowered = block.astype(bf16)
        normed, _ = normalize(block)
        value = normed * gain + shift
        for q in range(4):
            part = slice(q * 64, (q + 1) * 64)
            if b == 4:
                y1h_ref[q] = (chunk_mask(halo, q // 2, q % 2, 64) * value[part]).astype(bf16)
            else:
                dest = slice(b * 64, (b + 1) * 64)
                xp_ref[q, dest] = lowered[part]
                gp_ref[q, dest] = gblock[part]
                y1_ref[q, dest] = (chunk_mask(own, q // 2, q % 2, 64, 4 * b) * value[part]).astype(bf16)
    for q in range(4):
        y1t_ref[:, q * 256 : (q + 1) * 256] = y1_ref[q].T


def whole(shape):
    return pl.BlockSpec(shape, lambda *_: (0,) * len(shape))


SMEM = pl.BlockSpec(memory_space=pltpu.SMEM)


def params():
    return pltpu.CompilerParams(vmem_limit_bytes=vmem_bytes)


def takes(micros):
    return pl.CostEstimate(flops=int(micros * 1.0e9), bytes_accessed=0, transcendentals=0)


def launch(deps, kernel, *, out_shape, in_specs, out_specs, **rest):
    single = not isinstance(out_shape, tuple)
    shapes = (out_shape,) if single else out_shape
    specs = (out_specs,) if single else out_specs
    anywhere = pl.BlockSpec(memory_space=pl.ANY)
    count = len(in_specs)

    def body(*refs):
        at = count + len(deps)
        kernel(*refs[:count], *refs[at : at + len(shapes)], *refs[at + len(shapes) + 1 :])

    call = pl.pallas_call(
        body,
        out_shape=(*shapes, jax.ShapeDtypeStruct((8, 128), f32)),
        in_specs=list(in_specs) + [anywhere] * len(deps),
        out_specs=(*specs, anywhere),
        compiler_params=params(),
        **rest,
    )
    return lambda *args: call(*args, *deps)


def own_number(dealt):
    return lax.axis_index("img") * 2 + lax.axis_index("row") if dealt else 0


def place_rows(scratch, refs, order, number, rows):
    each = 32 // len(refs)
    for k, ref in enumerate(refs):
        for b in range(each):
            at = pl.multiple_of((order[k * each + b] ^ number) * rows, 16)
            scratch[pl.ds(at, rows), :] = ref[b * rows : (b + 1) * rows, :]


def dealt_owner(place, order):
    if order == "none":
        return place
    if order == "plain":
        return (2 * (place % 16) + place // 16) ^ lax.axis_index("row")
    return (2 * masks_of(order)[place % 16] + place // 16) ^ own_number(True)


def deal_rows(outs, lead, value_ref, order, rows):
    for p in range(32):
        at = pl.multiple_of(dealt_owner(p, order) * rows, 16)
        outs[p // 16][(slice(p % 16 * rows, (p % 16 + 1) * rows),) + lead] = value_ref[pl.ds(at, rows), :].astype(bf16)


def prepare(valid, halo_valid, x, xh, g, wide, deps=()):
    vmem = pl.BlockSpec(memory_space=pltpu.VMEM)
    return launch(
        deps,
        prepare_kernel,
        out_shape=(
            jax.ShapeDtypeStruct((4, 256, 512), bf16),
            jax.ShapeDtypeStruct((4, 256, 512), bf16),
            jax.ShapeDtypeStruct((4, 256, 512), bf16),
            jax.ShapeDtypeStruct((4, 64, 512), bf16),
            jax.ShapeDtypeStruct((512, 1024), bf16),
        ),
        in_specs=[SMEM] * 2 + [vmem] * 4,
        out_specs=(vmem,) * 5,
        cost_estimate=takes(4),
        name="prepare",
    )(valid, halo_valid, x, xh, g, wide)


def low_lanes(shape):
    return lax.broadcasted_iota(i32, shape, len(shape) - 1) < 64


def swap_lanes(value):
    return pltpu.roll(value, 64, axis=1)


def shifted_block(value, step):
    if step == 0:
        return value
    blk = lax.broadcasted_iota(i32, value.shape, 1)
    if step > 0:
        return jnp.where(blk < 7, pltpu.roll(value, 7, axis=1), 0.0)
    return jnp.where(blk > 0, pltpu.roll(value, 1, axis=1), 0.0)


ODD = ((-1, 0), (-1, 1), (0, 0), (0, 1), (1, 0))
EVEN = ((-1, 1), (0, 0), (0, 1), (1, 0), (1, 1))


def lane_pairs(chunks):
    res = {}
    for row_par in range(2):
        odd, even = chunks[2 * row_par + 1], chunks[2 * row_par]
        odd_s, even_s = swap_lanes(odd), swap_lanes(even)
        res[row_par, 0] = (odd, even_s)
        res[row_par, 1] = (odd_s, even)
    return res


def fill_band(ref, lead, pairs, n, start, row_par):
    odd, even = (v.reshape(n, 2, 2, 8, 128) for v in pairs)
    half = 1 - row_par
    lanes = slice(half * 128, half * 128 + 128)
    low = low_lanes((n * 2, 8, 128))
    cache = {}

    def take(name, value, step, ccp):
        if (name, step, ccp) not in cache:
            cache[name, step, ccp] = shifted_block(value[:, ccp].reshape(n * 2, 8, 128), step)
        return cache[name, step, ccp]

    def write(k):
        both = jnp.where(low, take("o", odd, *ODD[k]), take("e", even, *EVEN[k]))
        ref[lead + (slice(start, start + n), k, slice(None), lanes)] = both.reshape(n, 16, 128).astype(bf16)

    return [functools.partial(write, k) for k in range(5)]


def fill_group(ref, lead, own, halo, upper):
    steps = []
    for row_par in range(2):
        first = 2 + row_par
        steps += fill_band(ref, lead, own[row_par], 8, first, row_par)
        steps += fill_band(ref, lead, [v * (1.0 - upper) for v in halo[row_par]], 2, first - 2, row_par)
        steps += fill_band(ref, lead, [v * upper for v in halo[row_par]], 2, first + 8, row_par)
    return steps


def diagonal(rows):
    return (lax.broadcasted_iota(i32, (rows, 128), 0) % 64) == (lax.broadcasted_iota(i32, (rows, 128), 1) % 64)


def build_weights(w_ref, slot, tap_ref, group, flip=False):
    mask = diagonal(64)
    low = low_lanes((1, 128))
    tile, side = group // 2, group % 2
    cols = slice(tile * 128, tile * 128 + 128)

    def write(i, jj):
        rows = tap_ref[6 - i if flip else i, :, cols]
        turned = swap_lanes(rows)
        first, second = (rows, turned) if side == 0 else (turned, rows)
        a, b = (6 - jj, 7 - jj) if flip else (jj, jj - 1)
        left = first[a : a + 1] if 0 <= a <= 6 else jnp.zeros((1, 128), f32)
        right = second[b : b + 1] if 0 <= b <= 6 else jnp.zeros((1, 128), f32)
        vector = jnp.where(low, left, right)
        block = jnp.where(mask, jnp.broadcast_to(vector, (64, 128)), 0.0).astype(bf16)
        for out_par in range(2):
            top = i + out_par
            ti, rp, tj, cp = top // 2, top % 2, jj // 2, jj % 2
            at = (rp * 2 + cp) * 64
            w_ref[slot, ti * 4 + tj, at : at + 64, out_par * 128 : out_par * 128 + 128] = block

    return [functools.partial(write, i, jj) for i in range(7) for jj in range(8)]


def clear_weights(w_ref):
    for slot in range(2):
        for tj in range(4):
            w_ref[slot, tj, 0:128, 128:256] = jnp.zeros((128, 128), bf16)
            w_ref[slot, 12 + tj, 128:256, 0:128] = jnp.zeros((128, 128), bf16)


def band_block(ref, lead, ti, tj):
    return ref[lead + (slice(1 + ti, 9 + ti), slice(tj, tj + 2))].reshape(256, 256)


def convolve(ref, lead, w_ref, slot, meanwhile):
    total = None
    for k in range(16):
        part = dot(band_block(ref, lead, k // 4, k % 4), w_ref[slot, k])
        total = part if total is None else total + part
        for step in meanwhile[len(meanwhile) * k // 16 : len(meanwhile) * (k + 1) // 16]:
            step()
    return total


def convolve_groups(ref, w_ref, tap_ref, own, halo, upper, flip):
    def steps(group):
        cols = slice(group // 2 * 128, group // 2 * 128 + 128)
        own_pairs = lane_pairs([v[:, cols] for v in own])
        halo_pairs = lane_pairs([v[:, cols] for v in halo])
        side = group % 2
        band = [own_pairs[rp, side] for rp in range(2)], [halo_pairs[rp, side] for rp in range(2)]
        return fill_group(ref, (group,), *band, upper) + build_weights(w_ref, side, tap_ref, group, flip)

    for step in steps(0):
        step()
    return [convolve(ref, (group,), w_ref, group % 2, steps(group + 1) if group < 3 else []) for group in range(4)]


def split_lanes(low_group, high_group):
    low = low_lanes((256, 128))
    chunks = []
    for rp in range(2):
        lg = low_group[:, rp * 128 : rp * 128 + 128]
        hg = high_group[:, rp * 128 : rp * 128 + 128]
        chunks.append(jnp.where(low, lg, swap_lanes(hg)))
        chunks.append(jnp.where(low, swap_lanes(lg), hg))
    return chunks


def forward_kernel(valid_ref, halo_valid_ref, y1_ref, y1h_ref, *rest, order, dealt):
    weights, (wide_ref, tap_ref, d_ref, band_ref, j0_ref, w_ref, win_ref) = rest[:8], rest[8:]
    step = pl.program_id(0)

    @pl.when(step == 0)
    def _():
        clear_weights(w_ref)

    upper = is_upper()
    sizes, around = extents(valid_ref), halo_sizes(valid_ref, halo_valid_ref)
    place_rows(win_ref, weights, order, own_number(dealt), 16)
    weight = win_ref[...]
    bias = wide_ref[0:1]
    joined = dot(y1_ref[...].reshape(1024, 512), weight) + bias
    joined = [joined[q * 256 : (q + 1) * 256] for q in range(4)]
    around_rows = dot(y1h_ref[...].reshape(256, 512), weight) + bias

    @pl.when(step == 0)
    def _():
        for q in range(4):
            j0_ref[q] = joined[q][:, 0:128]

    own, halo = [], []
    for q in range(4):
        own.append((joined[q] * chunk_mask(sizes, q // 2, q % 2)).astype(bf16).astype(f32))
        part = around_rows[q * 64 : (q + 1) * 64]
        halo.append((part * chunk_mask(around, q // 2, q % 2, 64)).astype(bf16).astype(f32))
    sums = convolve_groups(band_ref, w_ref, tap_ref, own, halo, upper, False)
    for tile in range(2):
        cols = slice(tile * 128, tile * 128 + 128)
        for q, value in enumerate(split_lanes(*sums[2 * tile : 2 * tile + 2])):
            d_ref[q, :, cols] = (value + wide_ref[1:2, cols]) * conv_scale


def forward(valid, halo_valid, y1, y1h, w_in, wide, taps, order, dealt, deps=()):
    return launch(
        deps,
        functools.partial(forward_kernel, order=order, dealt=dealt),
        grid=(4,),
        out_shape=(
            jax.ShapeDtypeStruct((4, 256, 1024), f32),
            jax.ShapeDtypeStruct((16, 13, 5, 16, 256), bf16),
            jax.ShapeDtypeStruct((4, 256, 128), f32),
        ),
        in_specs=[SMEM, SMEM, whole((4, 256, 512)), whole((4, 64, 512))]
        + [pl.BlockSpec((64, 256), lambda t: (0, t))] * 8
        + [pl.BlockSpec((9, 256), lambda t: (0, t)), pl.BlockSpec((7, 7, 256), lambda t: (0, 0, t))],
        out_specs=(
            pl.BlockSpec((4, 256, 256), lambda t: (0, 0, t)),
            pl.BlockSpec((4, 13, 5, 16, 256), lambda t: (t, 0, 0, 0, 0)),
            whole((4, 256, 128)),
        ),
        scratch_shapes=[pltpu.VMEM((2, 16, 256, 256), bf16), pltpu.VMEM((512, 256), bf16)],
        cost_estimate=takes(24),
        name="forward",
    )(valid, halo_valid, y1, y1h, *w_in, wide, taps)


def middle_kernel(
    valid_ref,
    d_ref,
    j0_ref,
    xp_ref,
    gp_ref,
    oa,
    ob,
    oc,
    od,
    ea,
    eb4,
    ec,
    ed,
    ra,
    rb,
    first_ref,
    second_ref,
    g3_ref,
    g4_ref,
    wide_ref,
    out_ref,
    act_ref,
    y2_ref,
    u_ref,
    dh_ref,
    df_ref,
    dz_ref,
    dv_ref,
    dd_ref,
    dx2_ref,
    s512_ref,
    s2048_ref,
    s1024_ref,
    held_ref,
    w_out_ref,
    w_exp_ref,
    w_red_ref,
    g1_ref,
    g2_ref,
    *,
    order,
    dealt,
):
    q = pl.program_id(0)
    mask = pair_mask(extents(valid_ref), q)
    out_bias, mix, gain, shift, red_bias, ffn = (
        wide_ref[5 + k // 2 : 6 + k // 2, k % 2 * 512 : k % 2 * 512 + 512] for k in range(6)
    )
    lane = lax.broadcasted_iota(i32, (512, 128), 1)
    is0 = (lane >= 32) & (lane < 64)
    is1 = lane >= 64

    @pl.when(q == 0)
    def _():
        s512_ref[...] = jnp.zeros_like(s512_ref)
        s2048_ref[...] = jnp.zeros_like(s2048_ref)
        s1024_ref[...] = jnp.zeros_like(s1024_ref)
        g1_ref[...] = jnp.zeros_like(g1_ref)
        g2_ref[...] = jnp.zeros_like(g2_ref)
        g1_ref[32:64, 64:128] = first_ref[...]
        g2_ref[64:128] = second_ref[...]
        number = own_number(dealt)
        place_rows(w_out_ref, (oa, ob, oc, od), order, number, 16)
        place_rows(w_exp_ref, (ea, eb4, ec, ed), order, number, 16)
        for p in range(32):
            owner = dealt_owner(p, "plain" if dealt else "none")
            ref, first = (ra, rb)[p // 16], p % 16 * 64
            w_red_ref[pl.ds(pl.multiple_of(owner * 64, 64), 64), :] = ref[first : first + 64, :]

    d01, d2, d3, d4 = d_ref[:, 0:128], d_ref[:, 128:256], d_ref[:, 256:512], d_ref[:, 512:1024]
    pointwise = pltpu.roll(j0_ref[...], 32, axis=1)
    u0 = jnp.where(is0, pointwise * d01, 0.0).astype(bf16)
    v1 = dot(u0, g1_ref[...]) + wide_ref[2:3, 0:128]
    u1 = jnp.where(is1, v1 * d01, 0.0).astype(bf16)
    v2 = dot(u1, g2_ref[...]) + wide_ref[2:3, 128:256]
    u2 = (v2 * d2).astype(bf16)
    v3 = dot(u2, g3_ref[...]) + wide_ref[2:3, 256:512]
    u3 = (v3 * d3).astype(bf16)
    v4 = dot(u3, g4_ref[...]) + wide_ref[2:3, 512:1024]
    u4 = (v4 * d4).astype(bf16)
    u_ref[0:128] = jnp.where(is1, u1, u0).T
    u_ref[128:256] = u2.T
    u_ref[256:512] = u3.T
    u_ref[512:1024] = u4.T
    branch = dot(u4, w_out_ref[...]) + out_bias
    middle = xp_ref[...].astype(f32) + mask * mix * branch
    normed, inverse = normalize(middle)
    y2 = (mask * (normed * gain + shift)).astype(bf16)
    y2_ref[...] = y2.T
    grad = gp_ref[...].astype(f32)
    df = (mask * ffn * grad).astype(bf16)
    df_ref[...] = df
    reduced = red_bias
    back = jnp.zeros((512, 512), f32)
    for k in range(4):
        cols = slice(k * 512, (k + 1) * 512)
        hidden = dot(y2, w_exp_ref[:, cols]) + wide_ref[3 + k // 2 : 4 + k // 2, k % 2 * 512 : k % 2 * 512 + 512]
        cdf = 0.5 * (1.0 + lax.erf(hidden * inv_root_two))
        act = (hidden * cdf).astype(bf16)
        act_ref[cols, :] = act.T
        reduced = reduced + dot(act, w_red_ref[cols, :])
        density = jnp.exp(-0.5 * hidden * hidden) * inv_root_tau
        dh = (dot_nt(df, w_red_ref[cols, :]) * (cdf + hidden * density)).astype(bf16)
        dh_ref[:, cols] = dh
        s2048_ref[:, cols] += column_sum(dh.astype(f32))
        back = back + dot_nt(dh, w_exp_ref[:, cols])
    held_ref[pl.ds(2 * q, 2)] = (middle + mask * ffn * reduced).astype(bf16).reshape(2, 256, 512)
    s512_ref[0:1] += column_sum(grad * mask * reduced)
    s512_ref[1:2] += column_sum(df.astype(f32))
    back = mask * back
    s512_ref[2:3] += column_sum(back * normed)
    s512_ref[3:4] += column_sum(back)
    dx2 = grad + norm_backward(back, normed, inverse, gain)
    dx2_ref[...] = dx2
    dz = (mask * mix * dx2).astype(bf16)
    dz_ref[...] = dz
    s512_ref[4:5] += column_sum(dx2 * mask * branch)
    s512_ref[5:6] += column_sum(dz.astype(f32))
    du4 = dot_nt(dz, w_out_ref[...])
    dv4 = (du4 * d4).astype(bf16)
    dd4 = (du4 * v4).astype(bf16)
    du3 = dot_nt(dv4, g4_ref[...])
    dv3 = (du3 * d3).astype(bf16)
    dd3 = (du3 * v3).astype(bf16)
    du2 = dot_nt(dv3, g3_ref[...])
    dv2 = (du2 * d2).astype(bf16)
    dd2 = (du2 * v2).astype(bf16)
    du1 = dot_nt(dv2, g2_ref[...])
    dv1 = (du1 * d01).astype(bf16)
    du0 = dot_nt(dv1, g1_ref[...])
    dpw = pltpu.roll(du0 * d01, 96, axis=1)
    dd01 = jnp.where(is1, du1 * v1, jnp.where(is0, du0 * pointwise, dpw)).astype(bf16)
    dv_ref[:, 0:128] = dv1
    dv_ref[:, 128:256] = dv2
    dv_ref[:, 256:512] = dv3
    dv_ref[:, 512:1024] = dv4
    dd_ref[:, 0:128] = dd01
    dd_ref[:, 128:256] = dd2
    dd_ref[:, 256:512] = dd3
    dd_ref[:, 512:1024] = dd4
    for k, ref in enumerate((dv_ref, dd_ref)):
        s1024_ref[k : k + 1] += column_sum(ref[...].astype(f32))

    @pl.when(q == 1)
    def _():
        unpermute(held_ref, out_ref)


def unpermute(held_ref, out_ref):
    perm = permutation()
    for b in range(4):
        block = jnp.concatenate([held_ref[k, b * 64 : (b + 1) * 64] for k in range(4)], axis=0)
        block = dot_tn(perm, block).astype(bf16)
        out_ref[0, b * 128 : (b + 1) * 128] = block[0:128]
        out_ref[1, b * 128 : (b + 1) * 128] = block[128:256]


def middle_call(valid, d, j0, xp, gp, w_exp, w_red, g1, g2, g3, g4, wide, order, dealt, deps=()):
    def chunk(width):
        return pl.BlockSpec((512, width), lambda q: (q, 0))

    def out(width, dtype=bf16):
        return jax.ShapeDtypeStruct((1024, width), dtype)

    def turned(rows):
        return pl.BlockSpec((rows, 512), lambda q: (0, q))

    def out_turned(rows):
        return jax.ShapeDtypeStruct((rows, 1024), bf16)

    widths = (2048, 512, 512, 1024, 1024)
    rows = (2048, 512, 1024)
    return launch(
        deps,
        functools.partial(middle_kernel, order=order, dealt=dealt),
        grid=(2,),
        out_shape=(jax.ShapeDtypeStruct((2, 512, 512), bf16),)
        + tuple(out_turned(r) for r in rows)
        + tuple(out(w) for w in widths)
        + (
            out(512, f32),
            jax.ShapeDtypeStruct((8, 512), f32),
            jax.ShapeDtypeStruct((1, 2048), f32),
            jax.ShapeDtypeStruct((8, 1024), f32),
        ),
        in_specs=[SMEM, chunk(1024), chunk(128), chunk(512), chunk(512)]
        + [pl.BlockSpec((128, 512), lambda q: (0, 4))] * 4
        + [pl.BlockSpec((128, 2048), lambda q: (0, 0))] * 4
        + [whole((1024, 512))] * 2
        + [whole(v.shape) for v in (g1, g2, g3, g4, wide)],
        out_specs=(whole((2, 512, 512)),)
        + tuple(turned(r) for r in rows)
        + tuple(chunk(w) for w in widths)
        + (chunk(512), whole((8, 512)), whole((1, 2048)), whole((8, 1024))),
        scratch_shapes=[
            pltpu.VMEM((4, 256, 512), bf16),
            pltpu.VMEM((512, 512), bf16),
            pltpu.VMEM((512, 2048), bf16),
            pltpu.VMEM((2048, 512), bf16),
            pltpu.VMEM((128, 128), bf16),
            pltpu.VMEM((128, 128), bf16),
        ],
        cost_estimate=takes(30),
        name="middle",
    )(valid, *(v.reshape(1024, -1) for v in (d, j0, xp, gp)), *w_exp, *w_exp, *w_red, g1, g2, g3, g4, wide)


def feed_grads_kernel(
    y2_ref, dh_ref, act_ref, df_ref, u_ref, dz_ref, e_keep, e_send, r_keep, r_send, exp_ref, red_ref, out_ref, *, e_order, r_order
):
    step = pl.program_id(0)
    exp_ref[...] = dot(y2_ref[...], dh_ref[...])
    red_ref[pl.ds(pl.multiple_of(step * 512, 512), 512), :] = dot(act_ref[...], df_ref[...])
    deal_rows((e_keep, e_send), (slice(None),), exp_ref, e_order, 16)

    @pl.when(step == 0)
    def _():
        out_ref[...] = dot(u_ref[...], dz_ref[...])

    @pl.when(step == 3)
    def _():
        for p in range(32):
            owner = dealt_owner(p, r_order)
            ref, first = (r_keep, r_send)[p // 16], p % 16 * 80
            ref[first : first + 64] = red_ref[pl.ds(pl.multiple_of(owner * 64, 64), 64), :].astype(bf16)
            ref[first + 64 : first + 80] = out_ref[pl.ds(pl.multiple_of(owner * 16, 16), 16), :].astype(bf16)


def feed_grads(y2, dh, act, df, u, dz, e_order, r_order, deps=()):
    return launch(
        deps,
        functools.partial(feed_grads_kernel, e_order=e_order, r_order=r_order),
        grid=(4,),
        out_shape=(jax.ShapeDtypeStruct((256, 2048), bf16),) * 2 + (jax.ShapeDtypeStruct((1280, 512), bf16),) * 2,
        in_specs=[
            whole((512, 1024)),
            pl.BlockSpec((1024, 512), lambda k: (0, k)),
            pl.BlockSpec((512, 1024), lambda k: (k, 0)),
            whole((1024, 512)),
            pl.BlockSpec((512, 1024), lambda k: (1, 0)),
            whole((1024, 512)),
        ],
        out_specs=(pl.BlockSpec((256, 512), lambda k: (0, k)),) * 2 + (whole((1280, 512)),) * 2,
        scratch_shapes=[pltpu.VMEM((512, 512), f32), pltpu.VMEM((2048, 512), f32), pltpu.VMEM((512, 512), f32)],
        cost_estimate=takes(11),
        name="feed_grads",
    )(y2, dh, act, df, u, dz)


def kernel_grad_kernel(dd_ref, band_ref, dk_ref):
    low = low_lanes((256, 128))
    low8 = low_lanes((8, 128))
    wide = diagonal(256)
    for tile in range(2):
        cols = slice(tile * 128, tile * 128 + 128)
        own = [dd_ref[q, :, cols].astype(f32) for q in range(4)]
        turned_own = [swap_lanes(v) for v in own]
        for side in range(2):
            group = tile * 2 + side
            halves = []
            for rp in range(2):
                if side == 0:
                    halves.append(jnp.where(low, own[2 * rp], turned_own[2 * rp + 1]))
                else:
                    halves.append(jnp.where(low, turned_own[2 * rp], own[2 * rp + 1]))
            left = jnp.concatenate(halves, axis=1).astype(bf16)
            rows = {}
            for ti in range(4):
                for tj in range(4):
                    cross = dot_tn(left, band_block(band_ref, (group,), ti, tj))
                    for rp in range(2):
                        half = jnp.where(wide, cross[:, rp * 128 : rp * 128 + 128], 0.0)
                        part = jnp.sum(half.reshape(4, 8, 8, 128), axis=1)
                        for out_rp in range(2):
                            i = 2 * ti + rp - out_rp
                            if 0 <= i <= 6:
                                for out_cp in range(2):
                                    key = (i, tj, out_cp)
                                    term = part[out_rp * 2 + out_cp]
                                    rows[key] = rows[key] + term if key in rows else term
            for i in range(7):
                turned = [swap_lanes(rows[i, tj, 1]) for tj in range(4)] + [jnp.zeros((8, 128), f32)]
                for tj in range(4):
                    value = rows[i, tj, 0] + jnp.where(low8, turned[tj], turned[tj + 1])
                    dk_ref[group, i * 4 + tj : i * 4 + tj + 1] = column_sum(value) * conv_scale
            dk_ref[group, 28:32] = jnp.zeros((4, 128), f32)


def kernel_grad(dd, band, deps=()):
    return launch(
        deps,
        kernel_grad_kernel,
        grid=(4,),
        out_shape=jax.ShapeDtypeStruct((16, 32, 128), f32),
        in_specs=[
            pl.BlockSpec((4, 256, 256), lambda t: (0, 0, t)),
            pl.BlockSpec((4, 13, 5, 16, 256), lambda t: (t, 0, 0, 0, 0)),
        ],
        out_specs=pl.BlockSpec((4, 32, 128), lambda t: (t, 0, 0)),
        cost_estimate=takes(13),
        name="kernel_grad",
    )(dd, band)


def gate_grads_kernel(u_ref, dv_ref, s512_ref, s2048_ref, s1024_ref, dk_ref, keep, send, small_ref, *, order):
    small_ref[0:256] = dot(u_ref[256:512], dv_ref[:, 512:1024])
    g3 = dot(u_ref[128:256], dv_ref[:, 256:512])
    small_ref[256:320, 0:256] = g3[0:64]
    small_ref[256:320, 256:512] = g3[64:128]
    g12 = dot(u_ref[0:128], dv_ref[:, 0:256])
    for k in range(4):
        cols = slice(k * 128, (k + 1) * 128)
        small_ref[320:336, cols] = g12[64 + 16 * k : 80 + 16 * k, 128:256]
        small_ref[336:344, cols] = g12[32 + 8 * k : 40 + 8 * k, 0:128]
        small_ref[384:512, cols] = dk_ref[k * 128 : (k + 1) * 128]
        small_ref[352 + k : 353 + k] = s2048_ref[:, k * 512 : (k + 1) * 512]
        small_ref[356 + k : 357 + k] = s1024_ref[k // 2 : k // 2 + 1, k % 2 * 512 : k % 2 * 512 + 512]
    small_ref[344:352] = s512_ref[...]
    small_ref[360:384] = jnp.zeros((24, 512), f32)
    deal_rows((keep, send), (slice(None),), small_ref, order, 16)


def gate_grads(u, dv, s512, s2048, s1024, dk, order, deps=()):
    return launch(
        deps,
        functools.partial(gate_grads_kernel, order=order),
        grid=(1,),
        out_shape=(jax.ShapeDtypeStruct((256, 512), bf16),) * 2,
        in_specs=[whole((512, 1024))] + [whole(v.shape) for v in (dv, s512, s2048, s1024, dk)],
        out_specs=(whole((256, 512)),) * 2,
        scratch_shapes=[pltpu.VMEM((512, 512), f32)],
        cost_estimate=takes(3),
        name="gate_grads",
    )(u, dv, s512, s2048, s1024, dk)


def unpack_kernel(own_ref, oth_ref, *rest):
    outs, (table_ref, all_ref) = rest[:-2], rest[-2:]
    in_ref, dk_ref, dwb_ref, g1_ref, g2_ref, g3_ref, g4_ref, gb_ref = outs[:8]
    outb_ref, mix_ref, gain_ref, shift_ref, expb_ref, redb_ref, ffn_ref = outs[8:15]
    first_gain_ref, first_shift_ref, inb_ref = outs[15:]
    row = lax.axis_index("row")
    total = own_ref[0:16, 0:1024].astype(f32)
    for k in range(1, 16):
        total = total + own_ref[k * 16 : (k + 1) * 16, 0:1024].astype(f32)
    in_ref[...] = total
    late = own_ref[0:16, 1536:1664].astype(f32)
    for k in range(1, 16):
        late = late + own_ref[k * 16 : (k + 1) * 16, 1536:1664].astype(f32)
    lines = [
        jnp.concatenate([late[r * 4 + c : r * 4 + c + 1] for c in range(4)], axis=1).reshape(512) for r in range(4)
    ]
    first_gain_ref[...] = lines[0]
    first_shift_ref[...] = lines[1]
    inb_ref[0:512] = lines[2]
    inb_ref[512:1024] = lines[3]
    for k in range(16):
        block = slice(k * 16, (k + 1) * 16)
        table_ref[pl.ds(pl.multiple_of((2 * k + row) * 16, 16), 16), :] = own_ref[block, 1024:1536]
        table_ref[pl.ds(pl.multiple_of((2 * k + 1 - row) * 16, 16), 16), :] = oth_ref[block, 1024:1536]
    all_ref[...] = table_ref[...].astype(f32)
    g4_ref[...] = all_ref[0:256]
    g3_ref[0:64] = all_ref[256:320, 0:256]
    g3_ref[64:128] = all_ref[256:320, 256:512]
    for k in range(4):
        cols = slice(k * 128, (k + 1) * 128)
        g2_ref[16 * k : 16 * k + 16] = all_ref[320:336, cols]
        g1_ref[8 * k : 8 * k + 8] = swap_lanes(all_ref[336:344, cols])[:, 0:64]
        expb_ref[k * 512 : (k + 1) * 512] = all_ref[352 + k : 353 + k].reshape(512)
    for k, ref in enumerate((ffn_ref, redb_ref, gain_ref, shift_ref, mix_ref, outb_ref)):
        ref[...] = all_ref[344 + k : 345 + k].reshape(512)

    def line(first):
        return jnp.concatenate([all_ref[first : first + 1], all_ref[first + 1 : first + 2]], axis=1)

    gb_ref[...] = line(356)[:, 64:1024].reshape(960)
    dwb_ref[...] = line(358)[:, 32:1024].reshape(992) * conv_scale
    low = low_lanes((32, 128))
    lane = lax.broadcasted_iota(i32, (32, 128), 1)
    rows = []
    for t in range(8):
        cols = slice(t // 2 * 128, t // 2 * 128 + 128)
        first = 384 + t % 2 * 64
        left = all_ref[first : first + 32, cols]
        right = all_ref[first + 32 : first + 64, cols]
        pair = (jnp.where(low, left, swap_lanes(right)), jnp.where(low, swap_lanes(left), right))
        rows.append([pltpu.roll(v, 96, axis=1) for v in pair])
    for t in range(8):
        size = 128 if t < 7 else 96
        for odd in range(2):
            value = jnp.where(lane < 96, rows[t][odd], rows[t + 1][odd]) if t < 7 else rows[t][odd]
            for i in range(7):
                for j in range(odd, 7, 2):
                    at = i * 4 + j // 2
                    dk_ref[i, j : j + 1, t * 128 : t * 128 + size] = value[at : at + 1, 0:size]


def unpack(own, oth, deps=()):
    vmem = pl.BlockSpec(memory_space=pltpu.VMEM)
    shapes = ((16, 1024), (7, 7, 992), (992,), (32, 64), (64, 128), (128, 256), (256, 512), (960,))
    shapes += ((512,),) * 4 + ((2048,), (512,), (512,), (512,), (512,), (1024,))
    return launch(
        deps,
        unpack_kernel,
        out_shape=tuple(jax.ShapeDtypeStruct(v, f32) for v in shapes),
        in_specs=[vmem] * 2,
        out_specs=(vmem,) * len(shapes),
        scratch_shapes=[pltpu.VMEM((512, 512), bf16), pltpu.VMEM((512, 512), f32)],
        cost_estimate=takes(3),
        name="unpack",
    )(own, oth)


def conv_back_kernel(valid_ref, dd_ref, ddh_ref, tap_ref, df_ref, w_ref, back_ref):
    step = pl.program_id(0)

    @pl.when(step == 0)
    def _():
        clear_weights(w_ref)

    sizes = extents(valid_ref)
    lane = lax.broadcasted_iota(i32, (256, 128), 1)
    keep = (lane < 32) & (step == 0)
    own = [dd_ref[q].astype(f32) for q in range(4)]
    halo = [ddh_ref[q].astype(f32) for q in range(4)]
    sums = convolve_groups(back_ref, w_ref, tap_ref, own, halo, is_upper(), True)
    for tile in range(2):
        cols = slice(tile * 128, tile * 128 + 128)
        for q, value in enumerate(split_lanes(*sums[2 * tile : 2 * tile + 2])):
            value = value * (chunk_mask(sizes, q // 2, q % 2) * conv_scale)
            if tile == 0:
                value = jnp.where(keep, own[q][:, cols], value)
            df_ref[q, :, cols] = value.astype(bf16)


def conv_back(valid, dd, ddh, taps, deps=()):
    return launch(
        deps,
        conv_back_kernel,
        grid=(4,),
        out_shape=jax.ShapeDtypeStruct((4, 256, 1024), bf16),
        in_specs=[
            SMEM,
            pl.BlockSpec((4, 256, 256), lambda t: (0, 0, t)),
            pl.BlockSpec((4, 64, 256), lambda t: (0, 0, t)),
            pl.BlockSpec((7, 7, 256), lambda t: (0, 0, t)),
        ],
        out_specs=pl.BlockSpec((4, 256, 256), lambda t: (0, 0, t)),
        scratch_shapes=[pltpu.VMEM((2, 16, 256, 256), bf16), pltpu.VMEM((4, 13, 5, 16, 256), bf16)],
        cost_estimate=takes(16),
        name="conv_back",
    )(valid, dd, ddh, taps)


def in_grad_kernel(y1_ref, df_ref, keep, send, sum_ref, *, order):
    sum_ref[...] = dot(y1_ref[...], df_ref[...])
    deal_rows((keep, send), (slice(None),), sum_ref, order, 16)


def in_grad(y1, df, order, deps=()):
    return launch(
        deps,
        functools.partial(in_grad_kernel, order=order),
        grid=(2,),
        out_shape=(jax.ShapeDtypeStruct((256, 1024), bf16),) * 2,
        in_specs=[whole((512, 1024)), pl.BlockSpec((1024, 512), lambda k: (0, k))],
        out_specs=(pl.BlockSpec((256, 512), lambda k: (0, k)),) * 2,
        scratch_shapes=[pltpu.VMEM((512, 512), f32)],
        cost_estimate=takes(4),
        name="in_grad",
    )(y1, df)


def last_kernel(valid_ref, df_ref, xp_ref, dx2_ref, *rest, order, dealt):
    weights, (wide_ref, out_ref, late_ref, held_ref, win_ref) = rest[:8], rest[8:]
    q = pl.program_id(0)

    @pl.when(q == 0)
    def _():
        late_ref[...] = jnp.zeros_like(late_ref)
        place_rows(win_ref, weights, order, own_number(dealt), 16)

    mask = pair_mask(extents(valid_ref), q)
    df = df_ref[...]
    sums = column_sum(df.astype(f32))
    late_ref[2:3] += sums[:, 0:512]
    late_ref[3:4] += sums[:, 512:1024]
    grad = mask * dot_nt(df, win_ref[...])
    normed, inverse = normalize(xp_ref[...].astype(f32))
    late_ref[0:1] += column_sum(grad * normed)
    late_ref[1:2] += column_sum(grad)
    total = dx2_ref[...] + norm_backward(grad, normed, inverse, wide_ref[8:9, 0:512])
    held_ref[pl.ds(2 * q, 2)] = total.astype(bf16).reshape(2, 256, 512)

    @pl.when(q == 1)
    def _():
        unpermute(held_ref, out_ref)


def last_call(valid, df, xp, dx2, w_in, wide, order, dealt, deps=()):
    def chunk(width):
        return pl.BlockSpec((512, width), lambda q: (q, 0))

    return launch(
        deps,
        functools.partial(last_kernel, order=order, dealt=dealt),
        grid=(2,),
        out_shape=(jax.ShapeDtypeStruct((2, 512, 512), bf16), jax.ShapeDtypeStruct((8, 512), f32)),
        in_specs=[SMEM, chunk(1024), chunk(512), chunk(512)] + [whole((64, 1024))] * 8 + [whole(wide.shape)],
        out_specs=(whole((2, 512, 512)), whole((8, 512))),
        scratch_shapes=[pltpu.VMEM((4, 256, 512), bf16), pltpu.VMEM((512, 1024), bf16)],
        cost_estimate=takes(7),
        name="last",
    )(valid, *(v.reshape(1024, -1) for v in (df, xp, dx2)), *w_in, wide)


def repeat(value):
    rows, cols = value.shape
    return jnp.broadcast_to(value[None], (16, rows, cols)).reshape(16 * rows, cols)


def join_kernel(*refs, counts):
    ins = list(refs[: sum(counts)])
    for out, count in zip(refs[sum(counts) :], counts):
        at = 0
        for _ in range(count):
            ref = ins.pop(0)
            out[at : at + ref.shape[0]] = ref[...]
            at += ref.shape[0]


def join(*lists, deps=()):
    vmem = pl.BlockSpec(memory_space=pltpu.VMEM)
    shapes = [(sum(v.shape[0] for v in group), group[0].shape[1]) for group in lists]
    return launch(
        deps,
        functools.partial(join_kernel, counts=[len(v) for v in lists]),
        out_shape=tuple(jax.ShapeDtypeStruct(v, bf16) for v in shapes),
        in_specs=[vmem] * sum(len(v) for v in lists),
        out_specs=(vmem,) * len(lists),
        cost_estimate=takes(1),
        name="join",
    )(*sum((list(v) for v in lists), []))


def add_kernel(a_ref, b_ref, out_ref):
    out_ref[...] = a_ref[...] + b_ref[...]


def add(a, b, deps=()):
    vmem = pl.BlockSpec(memory_space=pltpu.VMEM)
    return launch(
        deps,
        add_kernel,
        out_shape=jax.ShapeDtypeStruct(a.shape, a.dtype),
        in_specs=[vmem] * 2,
        out_specs=vmem,
        cost_estimate=takes(1),
        name="add",
    )(a, b)


def combine_kernel(*refs, items):
    at = sum(n for n, _ in items)
    ins, outs = list(refs[:at]), list(refs[at:])
    for count, parts in items:
        terms = [ins.pop(0) for _ in range(count)]
        for part in range(parts):
            total = functools.reduce(lambda a, b: a + b, [v[part, 0].astype(f32) for v in terms])
            outs.pop(0)[0] = total.astype(bf16)


def combine(*items, deps=()):
    steps = next(n for n in (4, 2, 1) if all(v[0].shape[0] % (16 * n * p) == 0 for v, p in items))
    ins, in_specs, outs, out_specs = [], [], [], []
    for terms, parts in items:
        rows, cols = terms[0].shape
        size = rows // parts // steps
        ins += [v.reshape(parts, steps, size, cols) for v in terms]
        in_specs += [pl.BlockSpec((parts, 1, size, cols), lambda t: (0, t, 0, 0))] * len(terms)
        outs += [jax.ShapeDtypeStruct((steps, size, cols), bf16)] * parts
        out_specs += [pl.BlockSpec((1, size, cols), lambda t: (t, 0, 0))] * parts
    *values, token = launch(
        deps,
        functools.partial(combine_kernel, items=[(len(v), p) for v, p in items]),
        grid=(steps,),
        out_shape=tuple(outs),
        in_specs=in_specs,
        out_specs=tuple(out_specs),
        cost_estimate=takes(2),
        name="combine",
    )(*ins)
    return [v.reshape(-1, v.shape[-1]) for v in values] + [token]


def merge_kernel(ro_a, ro_b, e_a, e_b, *outs):
    for z, ref in enumerate(outs):
        rows = slice(z * 80, (z + 1) * 80)
        ref[0:80] = (ro_a[rows].astype(f32) + ro_b[rows].astype(f32)).astype(bf16)
        total = e_a[z * 16 : (z + 1) * 16].astype(f32) + e_b[z * 16 : (z + 1) * 16].astype(f32)
        for c in range(4):
            at = 80 + c * 16
            ref[at : at + 16] = total[:, c * 512 : (c + 1) * 512].astype(bf16)


def merge(ro_a, ro_b, e_a, e_b, deps=()):
    vmem = pl.BlockSpec(memory_space=pltpu.VMEM)
    return launch(
        deps,
        merge_kernel,
        out_shape=(jax.ShapeDtypeStruct((144, 512), bf16),) * 4,
        in_specs=[vmem] * 4,
        out_specs=(vmem,) * 4,
        cost_estimate=takes(2),
        name="merge",
    )(ro_a, ro_b, e_a, e_b)


def finish_kernel(*refs):
    ins, (red_ref, out_ref, exp_ref) = refs[:-3], refs[-3:]
    total = functools.reduce(lambda a, b: a + b, [v[...].astype(f32) for v in ins])
    red_ref[...] = total[0:64]
    out_ref[...] = total[64:80]
    for c in range(4):
        exp_ref[:, c * 512 : (c + 1) * 512] = total[80 + c * 16 : 96 + c * 16]


def finish(parts, deps=()):
    vmem = pl.BlockSpec(memory_space=pltpu.VMEM)
    shapes = ((64, 512), (16, 512), (16, 2048))
    return launch(
        deps,
        finish_kernel,
        out_shape=tuple(jax.ShapeDtypeStruct(v, f32) for v in shapes),
        in_specs=[vmem] * len(parts),
        out_specs=(vmem,) * 3,
        cost_estimate=takes(1),
        name="finish",
    )(*parts)


def deal_kernel(i_a, i_b, late_a, late_b, *rest):
    parts, (out_ref, late_ref) = rest[:-2], rest[-2:]
    small = functools.reduce(lambda a, b: a + b, [v[...].astype(f32) for v in parts]).astype(bf16)
    late = late_a[...] + late_b[...]
    for r in range(4):
        for c in range(4):
            late_ref[r * 4 + c : r * 4 + c + 1] = late[r : r + 1, c * 128 : (c + 1) * 128]
    last = late_ref[...].astype(bf16)
    out_ref[:, 0:1024] = (i_a[...].astype(f32) + i_b[...].astype(f32)).astype(bf16)
    for k in range(16):
        out_ref[k * 16 : (k + 1) * 16, 1024:1536] = small
        out_ref[k * 16 : (k + 1) * 16, 1536:1664] = last


def deal(i_a, i_b, late_a, late_b, parts, deps=()):
    vmem = pl.BlockSpec(memory_space=pltpu.VMEM)
    return launch(
        deps,
        deal_kernel,
        out_shape=jax.ShapeDtypeStruct((256, 1664), bf16),
        in_specs=[vmem] * (4 + len(parts)),
        out_specs=vmem,
        scratch_shapes=[pltpu.VMEM((16, 128), f32)],
        cost_estimate=takes(2),
        name="deal",
    )(i_a, i_b, late_a, late_b, *parts)


def late_kernel(a_ref, b_ref, gain_ref, shift_ref, bias_ref):
    total = a_ref[...] + b_ref[...]
    gain_ref[...] = total[0:1].reshape(512)
    shift_ref[...] = total[1:2].reshape(512)
    bias_ref[0:512] = total[2:3].reshape(512)
    bias_ref[512:1024] = total[3:4].reshape(512)


def late_sums(a, b, deps=()):
    vmem = pl.BlockSpec(memory_space=pltpu.VMEM)
    return launch(
        deps,
        late_kernel,
        out_shape=tuple(jax.ShapeDtypeStruct((v,), f32) for v in (512, 512, 1024)),
        in_specs=[vmem] * 2,
        out_specs=(vmem,) * 3,
        cost_estimate=takes(1),
        name="late",
    )(a, b)


ROW = "row"


def img_bits():
    return lax.axis_size("img").bit_length() - 1


def swap_img(value, mask):
    return lax.ppermute(value, "img", [(k, k ^ mask) for k in range(lax.axis_size("img"))])


def swap_row(value):
    return lax.ppermute(value, "row", [(0, 1), (1, 0)])


def masks_of(stage):
    masks = [0]
    for bit in stage:
        masks = [m | v for m in masks for v in (0, 1 << bit)]
    return masks


def gather_order(groups):
    rel = [0]
    for bits in groups:
        rel = [m ^ r for m in masks_of(bits) for r in rel]
    return [2 * r + side for side in (0, 1) for r in rel]


def swaps(value, bits):
    return [value] + [swap_img(value, m) for m in masks_of(bits)[1:]]


def after(value, *others):
    return lax.optimization_barrier((value, others))[0]


def spread(value):
    return lax.all_to_all(value, "img", split_axis=0, concat_axis=0, tiled=True)


def sum_img(value, bits):
    for bit in bits[:-1]:
        value = value + swap_img(value, 1 << bit)
    return value, swap_img(value, 1 << bits[-1])


def own_bit(bit):
    return lax.axis_index("row") if bit == ROW else (lax.axis_index("img") >> bit) & 1


def swap_bit(value, bit):
    return swap_row(value) if bit == ROW else swap_img(value, 1 << bit)


def plain_gather(shard):
    value = shard
    for bit in [ROW] + list(range(img_bits())):
        other = swap_bit(value, bit)
        mine = own_bit(bit) == 0
        value = jnp.concatenate([jnp.where(mine, value, other), jnp.where(mine, other, value)], axis=0)
    return value


def plain_scatter(value):
    for bit in list(range(img_bits()))[::-1] + [ROW]:
        half = value.shape[0] // 2
        mine = own_bit(bit) == 0
        first, second = value[:half], value[half:]
        sent = swap_bit(jnp.where(mine, second, first).astype(bf16), bit)
        value = jnp.where(mine, first, second).astype(f32) + sent.astype(f32)
    return value


def per_device(
    features,
    validity,
    upstream,
    normgain,
    normshift,
    inweight,
    inbias,
    dwkernel,
    dwbias,
    gatefirst,
    gatesecond,
    gatethird,
    gatefourth,
    gatebias,
    outweight,
    outbias,
    mixscale,
    mlpgain,
    mlpshift,
    expandweight,
    expandbias,
    reduceweight,
    reducebias,
    mlpscale,
):
    bits = img_bits()
    dealt = bits == 4
    lower = lax.axis_index("row") == 1

    x = features.reshape(2, 512, 512)
    g = upstream.reshape(2, 512, 512)
    valid = validity.reshape(32, 32)
    x_halo = swap_row(x)
    halo_valid = swap_row(valid)
    taps = jnp.pad(dwkernel.astype(f32), ((0, 0), (0, 0), (32, 0)))
    wide, token = gather_vectors(
        (inbias, dwbias, gatebias, expandbias),
        (outbias, mixscale, mlpgain, mlpshift, reducebias, mlpscale, normgain, normshift),
    )
    exp_out = jnp.concatenate([expandweight, outweight], axis=1)
    deep, flat_pair = (3, 2), (1, 0)
    if dealt:
        in_order = gather_order((deep, flat_pair))
        exp_order = gather_order((deep, (1,), (0,)))
        in_z, token = join(swaps(inweight, deep))
        exp_parts = swaps(exp_out, deep)
        red_own = spread(repeat(reduceweight))
        w_in = swaps(in_z, flat_pair)
        xp, gp, y1, y1h, y1t, token = prepare(valid, halo_valid, x, x_halo, g, wide, [token])
        exp_z, token = join(exp_parts, deps=[token] + w_in[1:])
        w_in = w_in + [swap_row(v) for v in w_in]
        exp_y, token = join(swaps(exp_z, (1,)), deps=[token])
        w_exp = swaps(exp_y, (0,))
        d, band, j0, token = forward(valid, halo_valid, y1, y1h, w_in, wide, taps, in_order, dealt, [token])
        w_exp = w_exp + [swap_row(w_exp[0]), swap_row(after(w_exp[1], d))]
        w_red = [red_own, swap_row(after(red_own, d))]
    else:
        in_order = exp_order = list(range(32))
        w_in = jnp.split(plain_gather(inweight), 8, axis=0)
        w_exp = jnp.split(plain_gather(exp_out), 4, axis=0)
        w_red = jnp.split(plain_gather(reduceweight), 2, axis=0)
        xp, gp, y1, y1h, y1t, token = prepare(valid, halo_valid, x, x_halo, g, wide)
        d, band, j0, token = forward(valid, halo_valid, y1, y1h, w_in, wide, taps, in_order, dealt)
    (produced, act, y2, u, dh, df, dz, dv, dd, dx2, s512, s2048, s1024, token) = middle_call(
        valid, d, j0, xp, gp, w_exp, w_red, gatefirst, gatesecond, gatethird, gatefourth, wide, exp_order, dealt
    )
    dd = dd.reshape(4, 256, 1024)
    dd_halo = swap_row(jnp.where(lower, dd[:, 0:64], dd[:, 192:256]))

    def flat(value):
        return value.reshape(1024, -1)

    r_order, e_order, plain = ((1, 0, 3, 2), (0, 1, 3, 2), "plain") if dealt else ("none",) * 3
    if dealt:
        e_keep, e_send, r_keep, r_send, token = feed_grads(
            y2, flat(dh), act, flat(df), u, flat(dz), e_order, r_order
        )
        e_got, r_got = swap_row(e_send), swap_row(r_send)
        dk, token = kernel_grad(dd, band, [token])
        s_keep, s_send, token = gate_grads(
            u, flat(dv), s512, s2048, s1024, dk.reshape(512, 128), flat_pair + deep, [token]
        )
        s_got = swap_row(s_send)
        r_keep, r_send, e_keep, e_send, *small, token = combine(
            ([r_keep, r_got], 2), ([e_keep, e_got], 2), ([s_keep, s_got], 4), deps=[token]
        )
        r_got, e_got = swap_img(r_send, 2), swap_img(e_send, 1)
        small = small[:1] + [swap_img(v, m) for v, m in zip(small[1:], masks_of(flat_pair)[1:])]
        dfused, token = conv_back(valid, dd, dd_halo, taps, [token])
        r_keep, r_send, e_keep, e_send, *small, token = combine(
            ([r_keep, r_got], 2), ([e_keep, e_got], 2), (small, 4), deps=[token]
        )
        r_got, e_got = swap_img(r_send, 1), swap_img(e_send, 2)
        small = small[:1] + [swap_img(v, m) for v, m in zip(small[1:], masks_of(deep)[1:])]
        i_keep, i_send, token = in_grad(y1t, flat(dfused), plain, [token])
        i_got = swap_row(i_send)
        *parts, token = merge(r_keep, r_got, e_keep, e_got, [token])
        parts = parts[:1] + [swap_img(v, m) for v, m in zip(parts[1:], masks_of(deep)[1:])]
        fgrad, late, token = last_call(
            valid, dfused, xp, dx2, w_in, wide, in_order, dealt, [token] + small[1:]
        )
        dealt_rows, token = deal(i_keep, i_got, late, swap_row(late), small, [token] + parts[1:])
        mixed = spread(dealt_rows)
        red_sum, out_sum, exp_sum, token = finish(parts, [token])
        own, oth = mixed, swap_row(mixed)
    else:

        def total(parts, rows):
            value = jnp.concatenate(parts, axis=0)
            return plain_scatter(value.reshape(32, -1, value.shape[1])[:, rows].reshape(-1, value.shape[1]))

        everything = slice(None)
        dk, token = kernel_grad(dd, band)
        s_keep, s_send, token = gate_grads(u, flat(dv), s512, s2048, s1024, dk.reshape(512, 128), plain)
        parts = feed_grads(y2, flat(dh), act, flat(df), u, flat(dz), e_order, r_order)
        e_parts, r_parts = parts[:2], parts[2:4]
        dfused, _ = conv_back(valid, dd, dd_halo, taps)
        i_parts = in_grad(y1t, flat(dfused), plain)[:2]
        fgrad, late, token = last_call(valid, dfused, xp, dx2, w_in, wide, in_order, dealt)
        sums = late_sums(*sum_img(late + swap_row(late), list(range(bits))))
        exp_sum, in_sum = total(e_parts, everything), total(i_parts, everything)
        red_sum, out_sum = total(r_parts, slice(0, 64)), total(r_parts, slice(64, 80))
        small = plain_gather(total((s_keep, s_send), everything).astype(bf16)).reshape(16, 2, 16, 512)
        lower_row = lax.axis_index("row")
        own, oth = (
            jnp.pad(lax.dynamic_index_in_dim(small, v, 1, keepdims=False).reshape(256, 512), ((0, 0), (1024, 128)))
            for v in (lower_row, 1 - lower_row)
        )

    unpacked = unpack(own, oth)
    if dealt:
        in_sum, sums = unpacked[0], unpacked[15:18]
    dk_sum, dwb_sum, gate1, gate2, gate3, gate4, gb_sum, outb, mix, gain, shift, expb, redb, ffn = unpacked[1:15]
    return (
        produced.reshape(features.shape),
        fgrad.reshape(features.shape),
        sums[0],
        sums[1],
        in_sum,
        sums[2],
        dk_sum,
        dwb_sum,
        gate1,
        gate2,
        gate3,
        gate4,
        gb_sum,
        out_sum,
        outb,
        mix,
        gain,
        shift,
        exp_sum,
        expb,
        red_sum,
        redb,
        ffn,
    )


def solution(mesh):
    band = P("img", "row", None, None)
    rows = P(("img", "row"), None)
    copy = P()
    ins = [band, P("img", "row", None), band] + [copy] * 21
    for k in (5, 14, 19, 21):
        ins[k] = rows
    outs = [band, band] + [copy] * 21
    for k in (4, 13, 18, 20):
        outs[k] = rows
    return jax.shard_map(per_device, mesh=mesh, in_specs=tuple(ins), out_specs=tuple(outs), check_vma=False)
```

```python
import functools
import math

import jax
import jax.numpy as jnp
from jax import lax
from jax.experimental import pallas as pl
from jax.experimental.pallas import tpu as pltpu
from jax.sharding import PartitionSpec as P

f32 = jnp.float32
bf16 = jnp.bfloat16
i32 = jnp.int32
norm_eps = 1e-06
conv_scale = 1.0 / 3.0
inv_root_two = 1.0 / math.sqrt(2.0)
inv_root_tau = 1.0 / math.sqrt(2.0 * math.pi)
vmem_bytes = 60 * 1024 * 1024


def dot(left, right):
    return jnp.dot(left, right, preferred_element_type=f32)


def dot_tn(left, right):
    return lax.dot_general(left, right, (((0,), (0,)), ((), ())), preferred_element_type=f32)


def dot_nt(left, right):
    return lax.dot_general(left, right, (((1,), (1,)), ((), ())), preferred_element_type=f32)


def column_sum(values):
    return jnp.sum(values, axis=0, keepdims=True)


def permutation():
    out = lax.broadcasted_iota(i32, (256, 256), 0)
    src = lax.broadcasted_iota(i32, (256, 256), 1)
    row_par, col_par = out >> 7, (out >> 6) & 1
    pair, ccp, img, blk = (out >> 5) & 1, (out >> 4) & 1, (out >> 3) & 1, out & 7
    want = img * 128 + (2 * pair + row_par) * 32 + 4 * blk + 2 * ccp + col_par
    return (src == want).astype(f32).astype(bf16)


def normalize(values):
    center = jnp.mean(values, axis=-1, keepdims=True)
    shifted = values - center
    spread = jnp.mean(shifted * shifted, axis=-1, keepdims=True)
    inverse = lax.rsqrt(spread + norm_eps)
    return shifted * inverse, inverse


def norm_backward(grad_norm, normed, inverse, gain):
    scaled = grad_norm * gain
    return inverse * (
        scaled
        - jnp.mean(scaled, axis=-1, keepdims=True)
        - normed * jnp.mean(scaled * normed, axis=-1, keepdims=True)
    )


def extents(valid_ref):
    heights = [sum(valid_ref[16 * n + r, 0] for r in range(16)) for n in range(2)]
    widths = [sum(valid_ref[16 * n, c] for c in range(32)) for n in range(2)]
    return heights, widths


def chunk_mask(sizes, row_par, col_par, count=256, first_row=0):
    (high_a, high_b), (wide_a, wide_b) = sizes
    at = lax.broadcasted_iota(i32, (count, 1), 0)
    pair, ccp, img, blk = at >> 5, (at >> 4) & 1, (at >> 3) & 1, at & 7
    row = 2 * pair + row_par + first_row
    col = 4 * blk + 2 * ccp + col_par
    high = jnp.where(img == 1, high_b, high_a)
    wide = jnp.where(img == 1, wide_b, wide_a)
    return jnp.where((row < high) & (col < wide), 1.0, 0.0).astype(f32)


def pair_mask(sizes, row_par):
    return jnp.concatenate([chunk_mask(sizes, row_par, col_par) for col_par in range(2)], axis=0)


def halo_sizes(valid_ref, halo_ref):
    heights, widths = extents(valid_ref)
    below, _ = extents(halo_ref)
    upper = lax.axis_index("row") == 0
    return [jnp.where(upper, h, 4) for h in below], widths


def is_upper():
    return jnp.where(lax.axis_index("row") == 0, 1.0, 0.0).astype(f32)


def vectors_kernel(in_ref, dw_ref, gate_ref, exp_ref, *rest):
    small, out_ref = rest[:8], rest[8]

    def line(ref):
        return ref[...].astype(f32).reshape(1, ref.shape[0])

    out_ref[0:1] = line(in_ref)
    out_ref[1:2, 0:32] = jnp.zeros((1, 32), f32)
    out_ref[1:2, 32:1024] = line(dw_ref)
    out_ref[2:3, 0:64] = jnp.zeros((1, 64), f32)
    out_ref[2:3, 64:1024] = line(gate_ref)
    wide = line(exp_ref)
    out_ref[3:4] = wide[:, 0:1024]
    out_ref[4:5] = wide[:, 1024:2048]
    for k, ref in enumerate(small):
        out_ref[5 + k // 2 : 6 + k // 2, k % 2 * 512 : k % 2 * 512 + 512] = line(ref)


def prepare_kernel(valid_ref, halo_valid_ref, x_ref, xh_ref, g_ref, *rest):
    vectors, (xp_ref, gp_ref, y1_ref, y1h_ref, y1t_ref, wide_ref) = rest[:12], rest[12:]
    vectors_kernel(*vectors, wide_ref)
    perm = permutation()
    gain, shift = wide_ref[8:9, 0:512], wide_ref[8:9, 512:1024]
    own, halo = extents(valid_ref), halo_sizes(valid_ref, halo_valid_ref)
    start = pl.multiple_of(lax.axis_index("row") * 384, 128)
    for b in range(5):
        if b == 4:
            rows = pl.ds(start, 128)
            block = jnp.concatenate([xh_ref[0, rows], xh_ref[1, rows]], axis=0)
        else:
            rows = slice(b * 128, (b + 1) * 128)
            block = jnp.concatenate([x_ref[0, rows], x_ref[1, rows]], axis=0)
            gblock = dot(perm, jnp.concatenate([g_ref[0, rows], g_ref[1, rows]], axis=0)).astype(bf16)
        block = dot(perm, block)
        lowered = block.astype(bf16)
        normed, _ = normalize(block)
        value = normed * gain + shift
        for q in range(4):
            part = slice(q * 64, (q + 1) * 64)
            if b == 4:
                y1h_ref[q] = (chunk_mask(halo, q // 2, q % 2, 64) * value[part]).astype(bf16)
            else:
                dest = slice(b * 64, (b + 1) * 64)
                xp_ref[q, dest] = lowered[part]
                gp_ref[q, dest] = gblock[part]
                y1_ref[q, dest] = (chunk_mask(own, q // 2, q % 2, 64, 4 * b) * value[part]).astype(bf16)
    for q in range(4):
        y1t_ref[:, q * 256 : (q + 1) * 256] = y1_ref[q].T


def whole(shape):
    return pl.BlockSpec(shape, lambda *_: (0,) * len(shape))


SMEM = pl.BlockSpec(memory_space=pltpu.SMEM)


def params():
    return pltpu.CompilerParams(vmem_limit_bytes=vmem_bytes)


def takes(micros):
    return pl.CostEstimate(flops=int(micros * 1.0e9), bytes_accessed=0, transcendentals=0)


def launch(deps, kernel, *, out_shape, in_specs, out_specs, **rest):
    single = not isinstance(out_shape, tuple)
    shapes = (out_shape,) if single else out_shape
    specs = (out_specs,) if single else out_specs
    anywhere = pl.BlockSpec(memory_space=pl.ANY)
    count = len(in_specs)

    def body(*refs):
        at = count + len(deps)
        kernel(*refs[:count], *refs[at : at + len(shapes)], *refs[at + len(shapes) + 1 :])

    call = pl.pallas_call(
        body,
        out_shape=(*shapes, jax.ShapeDtypeStruct((8, 128), f32)),
        in_specs=list(in_specs) + [anywhere] * len(deps),
        out_specs=(*specs, anywhere),
        compiler_params=params(),
        **rest,
    )
    return lambda *args: call(*args, *deps)


def own_number(dealt):
    return lax.axis_index("img") * 2 + lax.axis_index("row") if dealt else 0


def place_rows(scratch, refs, order, number, rows):
    each = 32 // len(refs)
    for k, ref in enumerate(refs):
        for b in range(each):
            at = pl.multiple_of((order[k * each + b] ^ number) * rows, 16)
            scratch[pl.ds(at, rows), :] = ref[b * rows : (b + 1) * rows, :]


def dealt_owner(place, order):
    if order == "none":
        return place
    if order == "plain":
        return (2 * (place % 16) + place // 16) ^ lax.axis_index("row")
    return (2 * masks_of(order)[place % 16] + place // 16) ^ own_number(True)


def deal_rows(outs, lead, value_ref, order, rows):
    for p in range(32):
        at = pl.multiple_of(dealt_owner(p, order) * rows, 16)
        outs[p // 16][(slice(p % 16 * rows, (p % 16 + 1) * rows),) + lead] = value_ref[pl.ds(at, rows), :].astype(bf16)


def prepare(valid, halo_valid, x, xh, g, vectors, deps=()):
    vmem = pl.BlockSpec(memory_space=pltpu.VMEM)
    return launch(
        deps,
        prepare_kernel,
        out_shape=(
            jax.ShapeDtypeStruct((4, 256, 512), bf16),
            jax.ShapeDtypeStruct((4, 256, 512), bf16),
            jax.ShapeDtypeStruct((4, 256, 512), bf16),
            jax.ShapeDtypeStruct((4, 64, 512), bf16),
            jax.ShapeDtypeStruct((512, 1024), bf16),
            jax.ShapeDtypeStruct((9, 1024), f32),
        ),
        in_specs=[SMEM] * 2 + [vmem] * 15,
        out_specs=(vmem,) * 6,
        cost_estimate=takes(4),
        name="prepare",
    )(valid, halo_valid, x, xh, g, *vectors)


def low_lanes(shape):
    return lax.broadcasted_iota(i32, shape, len(shape) - 1) < 64


def swap_lanes(value):
    return pltpu.roll(value, 64, axis=1)


def shifted_block(value, step):
    if step == 0:
        return value
    blk = lax.broadcasted_iota(i32, value.shape, 1)
    if step > 0:
        return jnp.where(blk < 7, pltpu.roll(value, 7, axis=1), 0.0)
    return jnp.where(blk > 0, pltpu.roll(value, 1, axis=1), 0.0)


ODD = ((-1, 0), (-1, 1), (0, 0), (0, 1), (1, 0))
EVEN = ((-1, 1), (0, 0), (0, 1), (1, 0), (1, 1))


def lane_pairs(chunks):
    res = {}
    for row_par in range(2):
        odd, even = chunks[2 * row_par + 1], chunks[2 * row_par]
        odd_s, even_s = swap_lanes(odd), swap_lanes(even)
        res[row_par, 0] = (odd, even_s)
        res[row_par, 1] = (odd_s, even)
    return res


def fill_band(ref, lead, pairs, n, start, row_par):
    odd, even = (v.reshape(n, 2, 2, 8, 128) for v in pairs)
    half = 1 - row_par
    lanes = slice(half * 128, half * 128 + 128)
    low = low_lanes((n * 2, 8, 128))
    cache = {}

    def take(name, value, step, ccp):
        if (name, step, ccp) not in cache:
            cache[name, step, ccp] = shifted_block(value[:, ccp].reshape(n * 2, 8, 128), step)
        return cache[name, step, ccp]

    def write(k):
        both = jnp.where(low, take("o", odd, *ODD[k]), take("e", even, *EVEN[k]))
        ref[lead + (slice(start, start + n), k, slice(None), lanes)] = both.reshape(n, 16, 128).astype(bf16)

    return [functools.partial(write, k) for k in range(5)]


def fill_group(ref, lead, own, halo, upper):
    steps = []
    for row_par in range(2):
        first = 2 + row_par
        steps += fill_band(ref, lead, own[row_par], 8, first, row_par)
        steps += fill_band(ref, lead, [v * (1.0 - upper) for v in halo[row_par]], 2, first - 2, row_par)
        steps += fill_band(ref, lead, [v * upper for v in halo[row_par]], 2, first + 8, row_par)
    return steps


def diagonal(rows):
    return (lax.broadcasted_iota(i32, (rows, 128), 0) % 64) == (lax.broadcasted_iota(i32, (rows, 128), 1) % 64)


def build_weights(w_ref, slot, tap_ref, group, flip=False):
    mask = diagonal(64)
    low = low_lanes((1, 128))
    tile, side = group // 2, group % 2
    cols = slice(tile * 128, tile * 128 + 128)

    def write(i, jj):
        rows = tap_ref[6 - i if flip else i, :, cols]
        turned = swap_lanes(rows)
        first, second = (rows, turned) if side == 0 else (turned, rows)
        a, b = (6 - jj, 7 - jj) if flip else (jj, jj - 1)
        left = first[a : a + 1] if 0 <= a <= 6 else jnp.zeros((1, 128), f32)
        right = second[b : b + 1] if 0 <= b <= 6 else jnp.zeros((1, 128), f32)
        vector = jnp.where(low, left, right)
        block = jnp.where(mask, jnp.broadcast_to(vector, (64, 128)), 0.0).astype(bf16)
        for out_par in range(2):
            top = i + out_par
            ti, rp, tj, cp = top // 2, top % 2, jj // 2, jj % 2
            at = (rp * 2 + cp) * 64
            w_ref[slot, ti * 4 + tj, at : at + 64, out_par * 128 : out_par * 128 + 128] = block

    return [functools.partial(write, i, jj) for i in range(7) for jj in range(8)]


def clear_weights(w_ref):
    for slot in range(2):
        for tj in range(4):
            w_ref[slot, tj, 0:128, 128:256] = jnp.zeros((128, 128), bf16)
            w_ref[slot, 12 + tj, 128:256, 0:128] = jnp.zeros((128, 128), bf16)


def band_block(ref, lead, ti, tj):
    return ref[lead + (slice(1 + ti, 9 + ti), slice(tj, tj + 2))].reshape(256, 256)


def convolve(ref, lead, w_ref, slot, meanwhile):
    total = None
    for k in range(16):
        part = dot(band_block(ref, lead, k // 4, k % 4), w_ref[slot, k])
        total = part if total is None else total + part
        for step in meanwhile[len(meanwhile) * k // 16 : len(meanwhile) * (k + 1) // 16]:
            step()
    return total


def convolve_groups(ref, w_ref, tap_ref, own, halo, upper, flip):
    def steps(group):
        cols = slice(group // 2 * 128, group // 2 * 128 + 128)
        own_pairs = lane_pairs([v[:, cols] for v in own])
        halo_pairs = lane_pairs([v[:, cols] for v in halo])
        side = group % 2
        band = [own_pairs[rp, side] for rp in range(2)], [halo_pairs[rp, side] for rp in range(2)]
        return fill_group(ref, (group,), *band, upper) + build_weights(w_ref, side, tap_ref, group, flip)

    for step in steps(0):
        step()
    return [convolve(ref, (group,), w_ref, group % 2, steps(group + 1) if group < 3 else []) for group in range(4)]


def split_lanes(low_group, high_group):
    low = low_lanes((256, 128))
    chunks = []
    for rp in range(2):
        lg = low_group[:, rp * 128 : rp * 128 + 128]
        hg = high_group[:, rp * 128 : rp * 128 + 128]
        chunks.append(jnp.where(low, lg, swap_lanes(hg)))
        chunks.append(jnp.where(low, swap_lanes(lg), hg))
    return chunks


def forward_kernel(valid_ref, halo_valid_ref, y1_ref, y1h_ref, *rest, order, dealt):
    weights, (wide_ref, tap_ref, d_ref, band_ref, j0_ref, w_ref, win_ref) = rest[:8], rest[8:]
    step = pl.program_id(0)

    @pl.when(step == 0)
    def _():
        clear_weights(w_ref)

    upper = is_upper()
    sizes, around = extents(valid_ref), halo_sizes(valid_ref, halo_valid_ref)
    place_rows(win_ref, weights, order, own_number(dealt), 16)
    weight = win_ref[...]
    bias = wide_ref[0:1]
    joined = dot(y1_ref[...].reshape(1024, 512), weight) + bias
    joined = [joined[q * 256 : (q + 1) * 256] for q in range(4)]
    around_rows = dot(y1h_ref[...].reshape(256, 512), weight) + bias

    @pl.when(step == 0)
    def _():
        for q in range(4):
            j0_ref[q] = joined[q][:, 0:128]

    own, halo = [], []
    for q in range(4):
        own.append((joined[q] * chunk_mask(sizes, q // 2, q % 2)).astype(bf16).astype(f32))
        part = around_rows[q * 64 : (q + 1) * 64]
        halo.append((part * chunk_mask(around, q // 2, q % 2, 64)).astype(bf16).astype(f32))
    sums = convolve_groups(band_ref, w_ref, tap_ref, own, halo, upper, False)
    for tile in range(2):
        cols = slice(tile * 128, tile * 128 + 128)
        for q, value in enumerate(split_lanes(*sums[2 * tile : 2 * tile + 2])):
            d_ref[q, :, cols] = (value + wide_ref[1:2, cols]) * conv_scale


def forward(valid, halo_valid, y1, y1h, w_in, wide, taps, order, dealt, deps=()):
    return launch(
        deps,
        functools.partial(forward_kernel, order=order, dealt=dealt),
        grid=(4,),
        out_shape=(
            jax.ShapeDtypeStruct((4, 256, 1024), f32),
            jax.ShapeDtypeStruct((16, 13, 5, 16, 256), bf16),
            jax.ShapeDtypeStruct((4, 256, 128), f32),
        ),
        in_specs=[SMEM, SMEM, whole((4, 256, 512)), whole((4, 64, 512))]
        + [pl.BlockSpec((64, 256), lambda t: (0, t))] * 8
        + [pl.BlockSpec((9, 256), lambda t: (0, t)), pl.BlockSpec((7, 7, 256), lambda t: (0, 0, t))],
        out_specs=(
            pl.BlockSpec((4, 256, 256), lambda t: (0, 0, t)),
            pl.BlockSpec((4, 13, 5, 16, 256), lambda t: (t, 0, 0, 0, 0)),
            whole((4, 256, 128)),
        ),
        scratch_shapes=[pltpu.VMEM((2, 16, 256, 256), bf16), pltpu.VMEM((512, 256), bf16)],
        cost_estimate=takes(24),
        name="forward",
    )(valid, halo_valid, y1, y1h, *w_in, wide, taps)


def middle_kernel(
    valid_ref,
    d_ref,
    j0_ref,
    xp_ref,
    gp_ref,
    oa,
    ob,
    oc,
    od,
    ea,
    eb4,
    ec,
    ed,
    ra,
    rb,
    first_ref,
    second_ref,
    g3_ref,
    g4_ref,
    wide_ref,
    out_ref,
    act_ref,
    y2_ref,
    u_ref,
    dh_ref,
    df_ref,
    dz_ref,
    dv_ref,
    dd_ref,
    dx2_ref,
    s512_ref,
    s2048_ref,
    s1024_ref,
    held_ref,
    w_out_ref,
    w_exp_ref,
    w_red_ref,
    g1_ref,
    g2_ref,
    *,
    order,
    dealt,
):
    q = pl.program_id(0)
    mask = pair_mask(extents(valid_ref), q)
    out_bias, mix, gain, shift, red_bias, ffn = (
        wide_ref[5 + k // 2 : 6 + k // 2, k % 2 * 512 : k % 2 * 512 + 512] for k in range(6)
    )
    lane = lax.broadcasted_iota(i32, (512, 128), 1)
    is0 = (lane >= 32) & (lane < 64)
    is1 = lane >= 64

    @pl.when(q == 0)
    def _():
        s512_ref[...] = jnp.zeros_like(s512_ref)
        s2048_ref[...] = jnp.zeros_like(s2048_ref)
        s1024_ref[...] = jnp.zeros_like(s1024_ref)
        g1_ref[...] = jnp.zeros_like(g1_ref)
        g2_ref[...] = jnp.zeros_like(g2_ref)
        g1_ref[32:64, 64:128] = first_ref[...]
        g2_ref[64:128] = second_ref[...]
        number = own_number(dealt)
        place_rows(w_out_ref, (oa, ob, oc, od), order, number, 16)
        place_rows(w_exp_ref, (ea, eb4, ec, ed), order, number, 16)
        for p in range(32):
            owner = dealt_owner(p, "plain" if dealt else "none")
            ref, first = (ra, rb)[p // 16], p % 16 * 64
            w_red_ref[pl.ds(pl.multiple_of(owner * 64, 64), 64), :] = ref[first : first + 64, :]

    d01, d2, d3, d4 = d_ref[:, 0:128], d_ref[:, 128:256], d_ref[:, 256:512], d_ref[:, 512:1024]
    pointwise = pltpu.roll(j0_ref[...], 32, axis=1)
    u0 = jnp.where(is0, pointwise * d01, 0.0).astype(bf16)
    v1 = dot(u0, g1_ref[...]) + wide_ref[2:3, 0:128]
    u1 = jnp.where(is1, v1 * d01, 0.0).astype(bf16)
    v2 = dot(u1, g2_ref[...]) + wide_ref[2:3, 128:256]
    u2 = (v2 * d2).astype(bf16)
    v3 = dot(u2, g3_ref[...]) + wide_ref[2:3, 256:512]
    u3 = (v3 * d3).astype(bf16)
    v4 = dot(u3, g4_ref[...]) + wide_ref[2:3, 512:1024]
    u4 = (v4 * d4).astype(bf16)
    u_ref[0:128] = jnp.where(is1, u1, u0).T
    u_ref[128:256] = u2.T
    u_ref[256:512] = u3.T
    u_ref[512:1024] = u4.T
    branch = dot(u4, w_out_ref[...]) + out_bias
    middle = xp_ref[...].astype(f32) + mask * mix * branch
    normed, inverse = normalize(middle)
    y2 = (mask * (normed * gain + shift)).astype(bf16)
    y2_ref[...] = y2.T
    grad = gp_ref[...].astype(f32)
    df = (mask * ffn * grad).astype(bf16)
    df_ref[...] = df
    reduced = red_bias
    back = jnp.zeros((512, 512), f32)
    for k in range(4):
        cols = slice(k * 512, (k + 1) * 512)
        hidden = dot(y2, w_exp_ref[:, cols]) + wide_ref[3 + k // 2 : 4 + k // 2, k % 2 * 512 : k % 2 * 512 + 512]
        cdf = 0.5 * (1.0 + lax.erf(hidden * inv_root_two))
        act = (hidden * cdf).astype(bf16)
        act_ref[cols, :] = act.T
        reduced = reduced + dot(act, w_red_ref[cols, :])
        density = jnp.exp(-0.5 * hidden * hidden) * inv_root_tau
        dh = (dot_nt(df, w_red_ref[cols, :]) * (cdf + hidden * density)).astype(bf16)
        dh_ref[:, cols] = dh
        s2048_ref[:, cols] += column_sum(dh.astype(f32))
        back = back + dot_nt(dh, w_exp_ref[:, cols])
    held_ref[pl.ds(2 * q, 2)] = (middle + mask * ffn * reduced).astype(bf16).reshape(2, 256, 512)
    s512_ref[0:1] += column_sum(grad * mask * reduced)
    s512_ref[1:2] += column_sum(df.astype(f32))
    back = mask * back
    s512_ref[2:3] += column_sum(back * normed)
    s512_ref[3:4] += column_sum(back)
    dx2 = grad + norm_backward(back, normed, inverse, gain)
    dx2_ref[...] = dx2
    dz = (mask * mix * dx2).astype(bf16)
    dz_ref[...] = dz
    s512_ref[4:5] += column_sum(dx2 * mask * branch)
    s512_ref[5:6] += column_sum(dz.astype(f32))
    du4 = dot_nt(dz, w_out_ref[...])
    dv4 = (du4 * d4).astype(bf16)
    dd4 = (du4 * v4).astype(bf16)
    du3 = dot_nt(dv4, g4_ref[...])
    dv3 = (du3 * d3).astype(bf16)
    dd3 = (du3 * v3).astype(bf16)
    du2 = dot_nt(dv3, g3_ref[...])
    dv2 = (du2 * d2).astype(bf16)
    dd2 = (du2 * v2).astype(bf16)
    du1 = dot_nt(dv2, g2_ref[...])
    dv1 = (du1 * d01).astype(bf16)
    du0 = dot_nt(dv1, g1_ref[...])
    dpw = pltpu.roll(du0 * d01, 96, axis=1)
    dd01 = jnp.where(is1, du1 * v1, jnp.where(is0, du0 * pointwise, dpw)).astype(bf16)
    dv_ref[:, 0:128] = dv1
    dv_ref[:, 128:256] = dv2
    dv_ref[:, 256:512] = dv3
    dv_ref[:, 512:1024] = dv4
    dd_ref[:, 0:128] = dd01
    dd_ref[:, 128:256] = dd2
    dd_ref[:, 256:512] = dd3
    dd_ref[:, 512:1024] = dd4
    for k, ref in enumerate((dv_ref, dd_ref)):
        s1024_ref[k : k + 1] += column_sum(ref[...].astype(f32))

    @pl.when(q == 1)
    def _():
        unpermute(held_ref, out_ref)


def unpermute(held_ref, out_ref):
    perm = permutation()
    for b in range(4):
        block = jnp.concatenate([held_ref[k, b * 64 : (b + 1) * 64] for k in range(4)], axis=0)
        block = dot_tn(perm, block).astype(bf16)
        out_ref[0, b * 128 : (b + 1) * 128] = block[0:128]
        out_ref[1, b * 128 : (b + 1) * 128] = block[128:256]


def middle_call(valid, d, j0, xp, gp, w_exp, w_red, g1, g2, g3, g4, wide, order, dealt, deps=()):
    def chunk(width):
        return pl.BlockSpec((512, width), lambda q: (q, 0))

    def out(width, dtype=bf16):
        return jax.ShapeDtypeStruct((1024, width), dtype)

    def turned(rows):
        return pl.BlockSpec((rows, 512), lambda q: (0, q))

    def out_turned(rows):
        return jax.ShapeDtypeStruct((rows, 1024), bf16)

    widths = (2048, 512, 512, 1024, 1024)
    rows = (2048, 512, 1024)
    return launch(
        deps,
        functools.partial(middle_kernel, order=order, dealt=dealt),
        grid=(2,),
        out_shape=(jax.ShapeDtypeStruct((2, 512, 512), bf16),)
        + tuple(out_turned(r) for r in rows)
        + tuple(out(w) for w in widths)
        + (
            out(512, f32),
            jax.ShapeDtypeStruct((8, 512), f32),
            jax.ShapeDtypeStruct((1, 2048), f32),
            jax.ShapeDtypeStruct((8, 1024), f32),
        ),
        in_specs=[SMEM, chunk(1024), chunk(128), chunk(512), chunk(512)]
        + [pl.BlockSpec((128, 512), lambda q: (0, 4))] * 4
        + [pl.BlockSpec((128, 2048), lambda q: (0, 0))] * 4
        + [whole((1024, 512))] * 2
        + [whole(v.shape) for v in (g1, g2, g3, g4, wide)],
        out_specs=(whole((2, 512, 512)),)
        + tuple(turned(r) for r in rows)
        + tuple(chunk(w) for w in widths)
        + (chunk(512), whole((8, 512)), whole((1, 2048)), whole((8, 1024))),
        scratch_shapes=[
            pltpu.VMEM((4, 256, 512), bf16),
            pltpu.VMEM((512, 512), bf16),
            pltpu.VMEM((512, 2048), bf16),
            pltpu.VMEM((2048, 512), bf16),
            pltpu.VMEM((128, 128), bf16),
            pltpu.VMEM((128, 128), bf16),
        ],
        cost_estimate=takes(30),
        name="middle",
    )(valid, *(v.reshape(1024, -1) for v in (d, j0, xp, gp)), *w_exp, *w_exp, *w_red, g1, g2, g3, g4, wide)


def feed_grads_kernel(
    y2_ref, dh_ref, act_ref, df_ref, u_ref, dz_ref, e_keep, e_send, r_keep, r_send, exp_ref, red_ref, out_ref, *, e_order, r_order
):
    step = pl.program_id(0)
    exp_ref[...] = dot(y2_ref[...], dh_ref[...])
    red_ref[pl.ds(pl.multiple_of(step * 512, 512), 512), :] = dot(act_ref[...], df_ref[...])
    deal_rows((e_keep, e_send), (slice(None),), exp_ref, e_order, 16)

    @pl.when(step == 0)
    def _():
        out_ref[...] = dot(u_ref[...], dz_ref[...])

    @pl.when(step == 3)
    def _():
        for p in range(32):
            owner = dealt_owner(p, r_order)
            ref, first = (r_keep, r_send)[p // 16], p % 16 * 80
            ref[first : first + 64] = red_ref[pl.ds(pl.multiple_of(owner * 64, 64), 64), :].astype(bf16)
            ref[first + 64 : first + 80] = out_ref[pl.ds(pl.multiple_of(owner * 16, 16), 16), :].astype(bf16)


def feed_grads(y2, dh, act, df, u, dz, e_order, r_order, deps=()):
    return launch(
        deps,
        functools.partial(feed_grads_kernel, e_order=e_order, r_order=r_order),
        grid=(4,),
        out_shape=(jax.ShapeDtypeStruct((256, 2048), bf16),) * 2 + (jax.ShapeDtypeStruct((1280, 512), bf16),) * 2,
        in_specs=[
            whole((512, 1024)),
            pl.BlockSpec((1024, 512), lambda k: (0, k)),
            pl.BlockSpec((512, 1024), lambda k: (k, 0)),
            whole((1024, 512)),
            pl.BlockSpec((512, 1024), lambda k: (1, 0)),
            whole((1024, 512)),
        ],
        out_specs=(pl.BlockSpec((256, 512), lambda k: (0, k)),) * 2 + (whole((1280, 512)),) * 2,
        scratch_shapes=[pltpu.VMEM((512, 512), f32), pltpu.VMEM((2048, 512), f32), pltpu.VMEM((512, 512), f32)],
        cost_estimate=takes(11),
        name="feed_grads",
    )(y2, dh, act, df, u, dz)


def kernel_grad_kernel(dd_ref, band_ref, dk_ref):
    low = low_lanes((256, 128))
    low8 = low_lanes((8, 128))
    wide = diagonal(256)
    for tile in range(2):
        cols = slice(tile * 128, tile * 128 + 128)
        own = [dd_ref[q, :, cols].astype(f32) for q in range(4)]
        turned_own = [swap_lanes(v) for v in own]
        for side in range(2):
            group = tile * 2 + side
            halves = []
            for rp in range(2):
                if side == 0:
                    halves.append(jnp.where(low, own[2 * rp], turned_own[2 * rp + 1]))
                else:
                    halves.append(jnp.where(low, turned_own[2 * rp], own[2 * rp + 1]))
            left = jnp.concatenate(halves, axis=1).astype(bf16)
            rows = {}
            for ti in range(4):
                for tj in range(4):
                    cross = dot_tn(left, band_block(band_ref, (group,), ti, tj))
                    for rp in range(2):
                        half = jnp.where(wide, cross[:, rp * 128 : rp * 128 + 128], 0.0)
                        part = jnp.sum(half.reshape(4, 8, 8, 128), axis=1)
                        for out_rp in range(2):
                            i = 2 * ti + rp - out_rp
                            if 0 <= i <= 6:
                                for out_cp in range(2):
                                    key = (i, tj, out_cp)
                                    term = part[out_rp * 2 + out_cp]
                                    rows[key] = rows[key] + term if key in rows else term
            for i in range(7):
                turned = [swap_lanes(rows[i, tj, 1]) for tj in range(4)] + [jnp.zeros((8, 128), f32)]
                for tj in range(4):
                    value = rows[i, tj, 0] + jnp.where(low8, turned[tj], turned[tj + 1])
                    dk_ref[group, i * 4 + tj : i * 4 + tj + 1] = column_sum(value) * conv_scale
            dk_ref[group, 28:32] = jnp.zeros((4, 128), f32)


def kernel_grad(dd, band, deps=()):
    return launch(
        deps,
        kernel_grad_kernel,
        grid=(4,),
        out_shape=jax.ShapeDtypeStruct((16, 32, 128), f32),
        in_specs=[
            pl.BlockSpec((4, 256, 256), lambda t: (0, 0, t)),
            pl.BlockSpec((4, 13, 5, 16, 256), lambda t: (t, 0, 0, 0, 0)),
        ],
        out_specs=pl.BlockSpec((4, 32, 128), lambda t: (t, 0, 0)),
        cost_estimate=takes(13),
        name="kernel_grad",
    )(dd, band)


def gate_grads_kernel(u_ref, dv_ref, s512_ref, s2048_ref, s1024_ref, dk_ref, keep, send, small_ref, *, order):
    small_ref[0:256] = dot(u_ref[256:512], dv_ref[:, 512:1024])
    g3 = dot(u_ref[128:256], dv_ref[:, 256:512])
    small_ref[256:320, 0:256] = g3[0:64]
    small_ref[256:320, 256:512] = g3[64:128]
    g12 = dot(u_ref[0:128], dv_ref[:, 0:256])
    for k in range(4):
        cols = slice(k * 128, (k + 1) * 128)
        small_ref[320:336, cols] = g12[64 + 16 * k : 80 + 16 * k, 128:256]
        small_ref[336:344, cols] = g12[32 + 8 * k : 40 + 8 * k, 0:128]
        small_ref[384:512, cols] = dk_ref[k * 128 : (k + 1) * 128]
        small_ref[352 + k : 353 + k] = s2048_ref[:, k * 512 : (k + 1) * 512]
        small_ref[356 + k : 357 + k] = s1024_ref[k // 2 : k // 2 + 1, k % 2 * 512 : k % 2 * 512 + 512]
    small_ref[344:352] = s512_ref[...]
    small_ref[360:384] = jnp.zeros((24, 512), f32)
    deal_rows((keep, send), (slice(None),), small_ref, order, 16)


def gate_grads(u, dv, s512, s2048, s1024, dk, order, deps=()):
    return launch(
        deps,
        functools.partial(gate_grads_kernel, order=order),
        grid=(1,),
        out_shape=(jax.ShapeDtypeStruct((256, 512), bf16),) * 2,
        in_specs=[whole((512, 1024))] + [whole(v.shape) for v in (dv, s512, s2048, s1024, dk)],
        out_specs=(whole((256, 512)),) * 2,
        scratch_shapes=[pltpu.VMEM((512, 512), f32)],
        cost_estimate=takes(3),
        name="gate_grads",
    )(u, dv, s512, s2048, s1024, dk)


def unpack_kernel(own_ref, oth_ref, *rest):
    outs, (table_ref, all_ref) = rest[:-2], rest[-2:]
    in_ref, dk_ref, dwb_ref, g1_ref, g2_ref, g3_ref, g4_ref, gb_ref = outs[:8]
    outb_ref, mix_ref, gain_ref, shift_ref, expb_ref, redb_ref, ffn_ref = outs[8:15]
    first_gain_ref, first_shift_ref, inb_ref = outs[15:]
    row = lax.axis_index("row")
    total = own_ref[0:16, 0:1024].astype(f32)
    for k in range(1, 16):
        total = total + own_ref[k * 16 : (k + 1) * 16, 0:1024].astype(f32)
    in_ref[...] = total
    late = own_ref[0:16, 1536:1664].astype(f32)
    for k in range(1, 16):
        late = late + own_ref[k * 16 : (k + 1) * 16, 1536:1664].astype(f32)
    lines = [
        jnp.concatenate([late[r * 4 + c : r * 4 + c + 1] for c in range(4)], axis=1).reshape(512) for r in range(4)
    ]
    first_gain_ref[...] = lines[0]
    first_shift_ref[...] = lines[1]
    inb_ref[0:512] = lines[2]
    inb_ref[512:1024] = lines[3]
    for k in range(16):
        block = slice(k * 16, (k + 1) * 16)
        table_ref[pl.ds(pl.multiple_of((2 * k + row) * 16, 16), 16), :] = own_ref[block, 1024:1536]
        table_ref[pl.ds(pl.multiple_of((2 * k + 1 - row) * 16, 16), 16), :] = oth_ref[block, 1024:1536]
    all_ref[...] = table_ref[...].astype(f32)
    g4_ref[...] = all_ref[0:256]
    g3_ref[0:64] = all_ref[256:320, 0:256]
    g3_ref[64:128] = all_ref[256:320, 256:512]
    for k in range(4):
        cols = slice(k * 128, (k + 1) * 128)
        g2_ref[16 * k : 16 * k + 16] = all_ref[320:336, cols]
        g1_ref[8 * k : 8 * k + 8] = swap_lanes(all_ref[336:344, cols])[:, 0:64]
        expb_ref[k * 512 : (k + 1) * 512] = all_ref[352 + k : 353 + k].reshape(512)
    for k, ref in enumerate((ffn_ref, redb_ref, gain_ref, shift_ref, mix_ref, outb_ref)):
        ref[...] = all_ref[344 + k : 345 + k].reshape(512)

    def line(first):
        return jnp.concatenate([all_ref[first : first + 1], all_ref[first + 1 : first + 2]], axis=1)

    gb_ref[...] = line(356)[:, 64:1024].reshape(960)
    dwb_ref[...] = line(358)[:, 32:1024].reshape(992) * conv_scale
    low = low_lanes((32, 128))
    lane = lax.broadcasted_iota(i32, (32, 128), 1)
    rows = []
    for t in range(8):
        cols = slice(t // 2 * 128, t // 2 * 128 + 128)
        first = 384 + t % 2 * 64
        left = all_ref[first : first + 32, cols]
        right = all_ref[first + 32 : first + 64, cols]
        pair = (jnp.where(low, left, swap_lanes(right)), jnp.where(low, swap_lanes(left), right))
        rows.append([pltpu.roll(v, 96, axis=1) for v in pair])
    for t in range(8):
        size = 128 if t < 7 else 96
        for odd in range(2):
            value = jnp.where(lane < 96, rows[t][odd], rows[t + 1][odd]) if t < 7 else rows[t][odd]
            for i in range(7):
                for j in range(odd, 7, 2):
                    at = i * 4 + j // 2
                    dk_ref[i, j : j + 1, t * 128 : t * 128 + size] = value[at : at + 1, 0:size]


def unpack(own, oth, deps=()):
    vmem = pl.BlockSpec(memory_space=pltpu.VMEM)
    shapes = ((16, 1024), (7, 7, 992), (992,), (32, 64), (64, 128), (128, 256), (256, 512), (960,))
    shapes += ((512,),) * 4 + ((2048,), (512,), (512,), (512,), (512,), (1024,))
    return launch(
        deps,
        unpack_kernel,
        out_shape=tuple(jax.ShapeDtypeStruct(v, f32) for v in shapes),
        in_specs=[vmem] * 2,
        out_specs=(vmem,) * len(shapes),
        scratch_shapes=[pltpu.VMEM((512, 512), bf16), pltpu.VMEM((512, 512), f32)],
        cost_estimate=takes(3),
        name="unpack",
    )(own, oth)


def conv_back_kernel(valid_ref, dd_ref, ddh_ref, tap_ref, df_ref, w_ref, back_ref):
    step = pl.program_id(0)

    @pl.when(step == 0)
    def _():
        clear_weights(w_ref)

    sizes = extents(valid_ref)
    lane = lax.broadcasted_iota(i32, (256, 128), 1)
    keep = (lane < 32) & (step == 0)
    own = [dd_ref[q].astype(f32) for q in range(4)]
    halo = [ddh_ref[q].astype(f32) for q in range(4)]
    sums = convolve_groups(back_ref, w_ref, tap_ref, own, halo, is_upper(), True)
    for tile in range(2):
        cols = slice(tile * 128, tile * 128 + 128)
        for q, value in enumerate(split_lanes(*sums[2 * tile : 2 * tile + 2])):
            value = value * (chunk_mask(sizes, q // 2, q % 2) * conv_scale)
            if tile == 0:
                value = jnp.where(keep, own[q][:, cols], value)
            df_ref[q, :, cols] = value.astype(bf16)


def conv_back(valid, dd, ddh, taps, deps=()):
    return launch(
        deps,
        conv_back_kernel,
        grid=(4,),
        out_shape=jax.ShapeDtypeStruct((4, 256, 1024), bf16),
        in_specs=[
            SMEM,
            pl.BlockSpec((4, 256, 256), lambda t: (0, 0, t)),
            pl.BlockSpec((4, 64, 256), lambda t: (0, 0, t)),
            pl.BlockSpec((7, 7, 256), lambda t: (0, 0, t)),
        ],
        out_specs=pl.BlockSpec((4, 256, 256), lambda t: (0, 0, t)),
        scratch_shapes=[pltpu.VMEM((2, 16, 256, 256), bf16), pltpu.VMEM((4, 13, 5, 16, 256), bf16)],
        cost_estimate=takes(16),
        name="conv_back",
    )(valid, dd, ddh, taps)


def in_grad_kernel(y1_ref, df_ref, keep, send, sum_ref, *, order):
    sum_ref[...] = dot(y1_ref[...], df_ref[...])
    deal_rows((keep, send), (slice(None),), sum_ref, order, 16)


def in_grad(y1, df, order, deps=()):
    return launch(
        deps,
        functools.partial(in_grad_kernel, order=order),
        grid=(2,),
        out_shape=(jax.ShapeDtypeStruct((256, 1024), bf16),) * 2,
        in_specs=[whole((512, 1024)), pl.BlockSpec((1024, 512), lambda k: (0, k))],
        out_specs=(pl.BlockSpec((256, 512), lambda k: (0, k)),) * 2,
        scratch_shapes=[pltpu.VMEM((512, 512), f32)],
        cost_estimate=takes(4),
        name="in_grad",
    )(y1, df)


def last_kernel(valid_ref, df_ref, xp_ref, dx2_ref, *rest, order, dealt):
    weights, (wide_ref, out_ref, late_ref, held_ref, win_ref) = rest[:8], rest[8:]
    q = pl.program_id(0)

    @pl.when(q == 0)
    def _():
        late_ref[...] = jnp.zeros_like(late_ref)
        place_rows(win_ref, weights, order, own_number(dealt), 16)

    mask = pair_mask(extents(valid_ref), q)
    df = df_ref[...]
    sums = column_sum(df.astype(f32))
    late_ref[2:3] += sums[:, 0:512]
    late_ref[3:4] += sums[:, 512:1024]
    grad = mask * dot_nt(df, win_ref[...])
    normed, inverse = normalize(xp_ref[...].astype(f32))
    late_ref[0:1] += column_sum(grad * normed)
    late_ref[1:2] += column_sum(grad)
    total = dx2_ref[...] + norm_backward(grad, normed, inverse, wide_ref[8:9, 0:512])
    held_ref[pl.ds(2 * q, 2)] = total.astype(bf16).reshape(2, 256, 512)

    @pl.when(q == 1)
    def _():
        unpermute(held_ref, out_ref)


def last_call(valid, df, xp, dx2, w_in, wide, order, dealt, deps=()):
    def chunk(width):
        return pl.BlockSpec((512, width), lambda q: (q, 0))

    return launch(
        deps,
        functools.partial(last_kernel, order=order, dealt=dealt),
        grid=(2,),
        out_shape=(jax.ShapeDtypeStruct((2, 512, 512), bf16), jax.ShapeDtypeStruct((8, 512), f32)),
        in_specs=[SMEM, chunk(1024), chunk(512), chunk(512)] + [whole((64, 1024))] * 8 + [whole(wide.shape)],
        out_specs=(whole((2, 512, 512)), whole((8, 512))),
        scratch_shapes=[pltpu.VMEM((4, 256, 512), bf16), pltpu.VMEM((512, 1024), bf16)],
        cost_estimate=takes(7),
        name="last",
    )(valid, *(v.reshape(1024, -1) for v in (df, xp, dx2)), *w_in, wide)


def repeat(value):
    rows, cols = value.shape
    return jnp.broadcast_to(value[None], (16, rows, cols)).reshape(16 * rows, cols)


def join_kernel(*refs, counts):
    ins = list(refs[: sum(counts)])
    for out, count in zip(refs[sum(counts) :], counts):
        at = 0
        for _ in range(count):
            ref = ins.pop(0)
            out[at : at + ref.shape[0]] = ref[...]
            at += ref.shape[0]


def join(*lists, deps=()):
    vmem = pl.BlockSpec(memory_space=pltpu.VMEM)
    shapes = [(sum(v.shape[0] for v in group), group[0].shape[1]) for group in lists]
    return launch(
        deps,
        functools.partial(join_kernel, counts=[len(v) for v in lists]),
        out_shape=tuple(jax.ShapeDtypeStruct(v, bf16) for v in shapes),
        in_specs=[vmem] * sum(len(v) for v in lists),
        out_specs=(vmem,) * len(lists),
        cost_estimate=takes(1),
        name="join",
    )(*sum((list(v) for v in lists), []))


def add_kernel(a_ref, b_ref, out_ref):
    out_ref[...] = a_ref[...] + b_ref[...]


def add(a, b, deps=()):
    vmem = pl.BlockSpec(memory_space=pltpu.VMEM)
    return launch(
        deps,
        add_kernel,
        out_shape=jax.ShapeDtypeStruct(a.shape, a.dtype),
        in_specs=[vmem] * 2,
        out_specs=vmem,
        cost_estimate=takes(1),
        name="add",
    )(a, b)


def combine_kernel(*refs, items):
    at = sum(n for n, _ in items)
    ins, outs = list(refs[:at]), list(refs[at:])
    for count, parts in items:
        terms = [ins.pop(0) for _ in range(count)]
        for part in range(parts):
            total = functools.reduce(lambda a, b: a + b, [v[part, 0].astype(f32) for v in terms])
            outs.pop(0)[0] = total.astype(bf16)


def combine(*items, deps=()):
    steps = next(n for n in (4, 2, 1) if all(v[0].shape[0] % (16 * n * p) == 0 for v, p in items))
    ins, in_specs, outs, out_specs = [], [], [], []
    for terms, parts in items:
        rows, cols = terms[0].shape
        size = rows // parts // steps
        ins += [v.reshape(parts, steps, size, cols) for v in terms]
        in_specs += [pl.BlockSpec((parts, 1, size, cols), lambda t: (0, t, 0, 0))] * len(terms)
        outs += [jax.ShapeDtypeStruct((steps, size, cols), bf16)] * parts
        out_specs += [pl.BlockSpec((1, size, cols), lambda t: (t, 0, 0))] * parts
    *values, token = launch(
        deps,
        functools.partial(combine_kernel, items=[(len(v), p) for v, p in items]),
        grid=(steps,),
        out_shape=tuple(outs),
        in_specs=in_specs,
        out_specs=tuple(out_specs),
        cost_estimate=takes(2),
        name="combine",
    )(*ins)
    return [v.reshape(-1, v.shape[-1]) for v in values] + [token]


def merge_kernel(ro_a, ro_b, e_a, e_b, *outs):
    for z, ref in enumerate(outs):
        rows = slice(z * 80, (z + 1) * 80)
        ref[0:80] = (ro_a[rows].astype(f32) + ro_b[rows].astype(f32)).astype(bf16)
        total = e_a[z * 16 : (z + 1) * 16].astype(f32) + e_b[z * 16 : (z + 1) * 16].astype(f32)
        for c in range(4):
            at = 80 + c * 16
            ref[at : at + 16] = total[:, c * 512 : (c + 1) * 512].astype(bf16)


def merge(ro_a, ro_b, e_a, e_b, deps=()):
    vmem = pl.BlockSpec(memory_space=pltpu.VMEM)
    return launch(
        deps,
        merge_kernel,
        out_shape=(jax.ShapeDtypeStruct((144, 512), bf16),) * 4,
        in_specs=[vmem] * 4,
        out_specs=(vmem,) * 4,
        cost_estimate=takes(2),
        name="merge",
    )(ro_a, ro_b, e_a, e_b)


def finish_kernel(*refs):
    ins, (red_ref, out_ref, exp_ref) = refs[:-3], refs[-3:]
    total = functools.reduce(lambda a, b: a + b, [v[...].astype(f32) for v in ins])
    red_ref[...] = total[0:64]
    out_ref[...] = total[64:80]
    for c in range(4):
        exp_ref[:, c * 512 : (c + 1) * 512] = total[80 + c * 16 : 96 + c * 16]


def finish(parts, deps=()):
    vmem = pl.BlockSpec(memory_space=pltpu.VMEM)
    shapes = ((64, 512), (16, 512), (16, 2048))
    return launch(
        deps,
        finish_kernel,
        out_shape=tuple(jax.ShapeDtypeStruct(v, f32) for v in shapes),
        in_specs=[vmem] * len(parts),
        out_specs=(vmem,) * 3,
        cost_estimate=takes(1),
        name="finish",
    )(*parts)


def deal_kernel(i_a, i_b, late_a, late_b, *rest):
    parts, (out_ref, late_ref) = rest[:-2], rest[-2:]
    small = functools.reduce(lambda a, b: a + b, [v[...].astype(f32) for v in parts]).astype(bf16)
    late = late_a[...] + late_b[...]
    for r in range(4):
        for c in range(4):
            late_ref[r * 4 + c : r * 4 + c + 1] = late[r : r + 1, c * 128 : (c + 1) * 128]
    last = late_ref[...].astype(bf16)
    out_ref[:, 0:1024] = (i_a[...].astype(f32) + i_b[...].astype(f32)).astype(bf16)
    for k in range(16):
        out_ref[k * 16 : (k + 1) * 16, 1024:1536] = small
        out_ref[k * 16 : (k + 1) * 16, 1536:1664] = last


def deal(i_a, i_b, late_a, late_b, parts, deps=()):
    vmem = pl.BlockSpec(memory_space=pltpu.VMEM)
    return launch(
        deps,
        deal_kernel,
        out_shape=jax.ShapeDtypeStruct((256, 1664), bf16),
        in_specs=[vmem] * (4 + len(parts)),
        out_specs=vmem,
        scratch_shapes=[pltpu.VMEM((16, 128), f32)],
        cost_estimate=takes(2),
        name="deal",
    )(i_a, i_b, late_a, late_b, *parts)


def late_kernel(a_ref, b_ref, gain_ref, shift_ref, bias_ref):
    total = a_ref[...] + b_ref[...]
    gain_ref[...] = total[0:1].reshape(512)
    shift_ref[...] = total[1:2].reshape(512)
    bias_ref[0:512] = total[2:3].reshape(512)
    bias_ref[512:1024] = total[3:4].reshape(512)


def late_sums(a, b, deps=()):
    vmem = pl.BlockSpec(memory_space=pltpu.VMEM)
    return launch(
        deps,
        late_kernel,
        out_shape=tuple(jax.ShapeDtypeStruct((v,), f32) for v in (512, 512, 1024)),
        in_specs=[vmem] * 2,
        out_specs=(vmem,) * 3,
        cost_estimate=takes(1),
        name="late",
    )(a, b)


ROW = "row"


def img_bits():
    return lax.axis_size("img").bit_length() - 1


def swap_img(value, mask):
    return lax.ppermute(value, "img", [(k, k ^ mask) for k in range(lax.axis_size("img"))])


def swap_row(value):
    return lax.ppermute(value, "row", [(0, 1), (1, 0)])


def masks_of(stage):
    masks = [0]
    for bit in stage:
        masks = [m | v for m in masks for v in (0, 1 << bit)]
    return masks


def gather_order(groups):
    rel = [0]
    for bits in groups:
        rel = [m ^ r for m in masks_of(bits) for r in rel]
    return [2 * r + side for side in (0, 1) for r in rel]


def swaps(value, bits):
    return [value] + [swap_img(value, m) for m in masks_of(bits)[1:]]


def after(value, *others):
    return lax.optimization_barrier((value, others))[0]


def spread(value):
    return lax.all_to_all(value, "img", split_axis=0, concat_axis=0, tiled=True)


def sum_img(value, bits):
    for bit in bits[:-1]:
        value = value + swap_img(value, 1 << bit)
    return value, swap_img(value, 1 << bits[-1])


def own_bit(bit):
    return lax.axis_index("row") if bit == ROW else (lax.axis_index("img") >> bit) & 1


def swap_bit(value, bit):
    return swap_row(value) if bit == ROW else swap_img(value, 1 << bit)


def plain_gather(shard):
    value = shard
    for bit in [ROW] + list(range(img_bits())):
        other = swap_bit(value, bit)
        mine = own_bit(bit) == 0
        value = jnp.concatenate([jnp.where(mine, value, other), jnp.where(mine, other, value)], axis=0)
    return value


def plain_scatter(value):
    for bit in list(range(img_bits()))[::-1] + [ROW]:
        half = value.shape[0] // 2
        mine = own_bit(bit) == 0
        first, second = value[:half], value[half:]
        sent = swap_bit(jnp.where(mine, second, first).astype(bf16), bit)
        value = jnp.where(mine, first, second).astype(f32) + sent.astype(f32)
    return value


def per_device(
    features,
    validity,
    upstream,
    normgain,
    normshift,
    inweight,
    inbias,
    dwkernel,
    dwbias,
    gatefirst,
    gatesecond,
    gatethird,
    gatefourth,
    gatebias,
    outweight,
    outbias,
    mixscale,
    mlpgain,
    mlpshift,
    expandweight,
    expandbias,
    reduceweight,
    reducebias,
    mlpscale,
):
    bits = img_bits()
    dealt = bits == 4
    lower = lax.axis_index("row") == 1

    x = features.reshape(2, 512, 512)
    g = upstream.reshape(2, 512, 512)
    valid = validity.reshape(32, 32)
    x_halo = swap_row(x)
    halo_valid = swap_row(valid)
    taps = jnp.pad(dwkernel.astype(f32), ((0, 0), (0, 0), (32, 0)))
    vectors = (inbias, dwbias, gatebias, expandbias)
    vectors += (outbias, mixscale, mlpgain, mlpshift, reducebias, mlpscale, normgain, normshift)
    exp_out = jnp.concatenate([expandweight, outweight], axis=1)
    deep, flat_pair = (3, 2), (1, 0)
    if dealt:
        in_order = gather_order((deep, flat_pair))
        exp_order = gather_order((deep, (1,), (0,)))
        in_z, token = join(swaps(inweight, deep))
        exp_parts = swaps(exp_out, deep)
        red_own = spread(repeat(reduceweight))
        w_in = swaps(in_z, flat_pair)
        xp, gp, y1, y1h, y1t, wide, token = prepare(valid, halo_valid, x, x_halo, g, vectors, [token])
        exp_z, token = join(exp_parts, deps=[token] + w_in[1:])
        w_in = w_in + [swap_row(v) for v in w_in]
        exp_y, token = join(swaps(exp_z, (1,)), deps=[token])
        w_exp = swaps(exp_y, (0,))
        d, band, j0, token = forward(valid, halo_valid, y1, y1h, w_in, wide, taps, in_order, dealt, [token])
        w_exp = w_exp + [swap_row(w_exp[0]), swap_row(after(w_exp[1], d))]
        w_red = [red_own, swap_row(after(red_own, d))]
    else:
        in_order = exp_order = list(range(32))
        w_in = jnp.split(plain_gather(inweight), 8, axis=0)
        w_exp = jnp.split(plain_gather(exp_out), 4, axis=0)
        w_red = jnp.split(plain_gather(reduceweight), 2, axis=0)
        xp, gp, y1, y1h, y1t, wide, token = prepare(valid, halo_valid, x, x_halo, g, vectors)
        d, band, j0, token = forward(valid, halo_valid, y1, y1h, w_in, wide, taps, in_order, dealt)
    (produced, act, y2, u, dh, df, dz, dv, dd, dx2, s512, s2048, s1024, token) = middle_call(
        valid, d, j0, xp, gp, w_exp, w_red, gatefirst, gatesecond, gatethird, gatefourth, wide, exp_order, dealt
    )
    dd = dd.reshape(4, 256, 1024)
    dd_halo = swap_row(jnp.where(lower, dd[:, 0:64], dd[:, 192:256]))

    def flat(value):
        return value.reshape(1024, -1)

    r_order, e_order, plain = ((1, 0, 3, 2), (0, 1, 3, 2), "plain") if dealt else ("none",) * 3
    if dealt:
        e_keep, e_send, r_keep, r_send, token = feed_grads(
            y2, flat(dh), act, flat(df), u, flat(dz), e_order, r_order
        )
        e_got, r_got = swap_row(e_send), swap_row(r_send)
        dk, token = kernel_grad(dd, band, [token])
        s_keep, s_send, token = gate_grads(
            u, flat(dv), s512, s2048, s1024, dk.reshape(512, 128), flat_pair + deep, [token]
        )
        s_got = swap_row(s_send)
        r_keep, r_send, e_keep, e_send, *small, token = combine(
            ([r_keep, r_got], 2), ([e_keep, e_got], 2), ([s_keep, s_got], 4), deps=[token]
        )
        r_got, e_got = swap_img(r_send, 2), swap_img(e_send, 1)
        small = small[:1] + [swap_img(v, m) for v, m in zip(small[1:], masks_of(flat_pair)[1:])]
        dfused, token = conv_back(valid, dd, dd_halo, taps, [token])
        r_keep, r_send, e_keep, e_send, *small, token = combine(
            ([r_keep, r_got], 2), ([e_keep, e_got], 2), (small, 4), deps=[token]
        )
        r_got, e_got = swap_img(r_send, 1), swap_img(e_send, 2)
        small = small[:1] + [swap_img(v, m) for v, m in zip(small[1:], masks_of(deep)[1:])]
        i_keep, i_send, token = in_grad(y1t, flat(dfused), plain, [token])
        i_got = swap_row(i_send)
        *parts, token = merge(r_keep, r_got, e_keep, e_got, [token])
        parts = parts[:1] + [swap_img(v, m) for v, m in zip(parts[1:], masks_of(deep)[1:])]
        fgrad, late, token = last_call(
            valid, dfused, xp, dx2, w_in, wide, in_order, dealt, [token] + small[1:]
        )
        dealt_rows, token = deal(i_keep, i_got, late, swap_row(late), small, [token] + parts[1:])
        mixed = spread(dealt_rows)
        red_sum, out_sum, exp_sum, token = finish(parts, [token])
        own, oth = mixed, swap_row(mixed)
    else:

        def total(parts, rows):
            value = jnp.concatenate(parts, axis=0)
            return plain_scatter(value.reshape(32, -1, value.shape[1])[:, rows].reshape(-1, value.shape[1]))

        everything = slice(None)
        dk, token = kernel_grad(dd, band)
        s_keep, s_send, token = gate_grads(u, flat(dv), s512, s2048, s1024, dk.reshape(512, 128), plain)
        parts = feed_grads(y2, flat(dh), act, flat(df), u, flat(dz), e_order, r_order)
        e_parts, r_parts = parts[:2], parts[2:4]
        dfused, _ = conv_back(valid, dd, dd_halo, taps)
        i_parts = in_grad(y1t, flat(dfused), plain)[:2]
        fgrad, late, token = last_call(valid, dfused, xp, dx2, w_in, wide, in_order, dealt)
        sums = late_sums(*sum_img(late + swap_row(late), list(range(bits))))
        exp_sum, in_sum = total(e_parts, everything), total(i_parts, everything)
        red_sum, out_sum = total(r_parts, slice(0, 64)), total(r_parts, slice(64, 80))
        small = plain_gather(total((s_keep, s_send), everything).astype(bf16)).reshape(16, 2, 16, 512)
        lower_row = lax.axis_index("row")
        own, oth = (
            jnp.pad(lax.dynamic_index_in_dim(small, v, 1, keepdims=False).reshape(256, 512), ((0, 0), (1024, 128)))
            for v in (lower_row, 1 - lower_row)
        )

    unpacked = unpack(own, oth)
    if dealt:
        in_sum, sums = unpacked[0], unpacked[15:18]
    dk_sum, dwb_sum, gate1, gate2, gate3, gate4, gb_sum, outb, mix, gain, shift, expb, redb, ffn = unpacked[1:15]
    return (
        produced.reshape(features.shape),
        fgrad.reshape(features.shape),
        sums[0],
        sums[1],
        in_sum,
        sums[2],
        dk_sum,
        dwb_sum,
        gate1,
        gate2,
        gate3,
        gate4,
        gb_sum,
        out_sum,
        outb,
        mix,
        gain,
        shift,
        exp_sum,
        expb,
        red_sum,
        redb,
        ffn,
    )


def solution(mesh):
    band = P("img", "row", None, None)
    rows = P(("img", "row"), None)
    copy = P()
    ins = [band, P("img", "row", None), band] + [copy] * 21
    for k in (5, 14, 19, 21):
        ins[k] = rows
    outs = [band, band] + [copy] * 21
    for k in (4, 13, 18, 20):
        outs[k] = rows
    return jax.shard_map(per_device, mesh=mesh, in_specs=tuple(ins), out_specs=tuple(outs), check_vma=False)
```

```python
import functools
import math

import jax
import jax.numpy as jnp
from jax import lax
from jax.experimental import pallas as pl
from jax.experimental.pallas import tpu as pltpu
from jax.sharding import PartitionSpec as P

f32 = jnp.float32
bf16 = jnp.bfloat16
i32 = jnp.int32
norm_eps = 1e-06
conv_scale = 1.0 / 3.0
inv_root_two = 1.0 / math.sqrt(2.0)
inv_root_tau = 1.0 / math.sqrt(2.0 * math.pi)
vmem_bytes = 60 * 1024 * 1024


def dot(left, right):
    return jnp.dot(left, right, preferred_element_type=f32)


def dot_tn(left, right):
    return lax.dot_general(left, right, (((0,), (0,)), ((), ())), preferred_element_type=f32)


def dot_nt(left, right):
    return lax.dot_general(left, right, (((1,), (1,)), ((), ())), preferred_element_type=f32)


def column_sum(values):
    return jnp.sum(values, axis=0, keepdims=True)


def permutation():
    out = lax.broadcasted_iota(i32, (256, 256), 0)
    src = lax.broadcasted_iota(i32, (256, 256), 1)
    row_par, col_par = out >> 7, (out >> 6) & 1
    pair, ccp, img, blk = (out >> 5) & 1, (out >> 4) & 1, (out >> 3) & 1, out & 7
    want = img * 128 + (2 * pair + row_par) * 32 + 4 * blk + 2 * ccp + col_par
    return (src == want).astype(f32).astype(bf16)


def normalize(values):
    center = jnp.mean(values, axis=-1, keepdims=True)
    shifted = values - center
    spread = jnp.mean(shifted * shifted, axis=-1, keepdims=True)
    inverse = lax.rsqrt(spread + norm_eps)
    return shifted * inverse, inverse


def norm_backward(grad_norm, normed, inverse, gain):
    scaled = grad_norm * gain
    return inverse * (
        scaled
        - jnp.mean(scaled, axis=-1, keepdims=True)
        - normed * jnp.mean(scaled * normed, axis=-1, keepdims=True)
    )


def extents(valid_ref):
    heights = [sum(valid_ref[16 * n + r, 0] for r in range(16)) for n in range(2)]
    widths = [sum(valid_ref[16 * n, c] for c in range(32)) for n in range(2)]
    return heights, widths


def chunk_mask(sizes, row_par, col_par, count=256, first_row=0):
    (high_a, high_b), (wide_a, wide_b) = sizes
    at = lax.broadcasted_iota(i32, (count, 1), 0)
    pair, ccp, img, blk = at >> 5, (at >> 4) & 1, (at >> 3) & 1, at & 7
    row = 2 * pair + row_par + first_row
    col = 4 * blk + 2 * ccp + col_par
    high = jnp.where(img == 1, high_b, high_a)
    wide = jnp.where(img == 1, wide_b, wide_a)
    return jnp.where((row < high) & (col < wide), 1.0, 0.0).astype(f32)


def pair_mask(sizes, row_par):
    return jnp.concatenate([chunk_mask(sizes, row_par, col_par) for col_par in range(2)], axis=0)


def halo_sizes(valid_ref, halo_ref):
    heights, widths = extents(valid_ref)
    below, _ = extents(halo_ref)
    upper = lax.axis_index("row") == 0
    return [jnp.where(upper, h, 4) for h in below], widths


def is_upper():
    return jnp.where(lax.axis_index("row") == 0, 1.0, 0.0).astype(f32)


def vectors_kernel(in_ref, dw_ref, gate_ref, exp_ref, *rest):
    small, out_ref = rest[:8], rest[8]

    def line(ref):
        return ref[...].astype(f32).reshape(1, ref.shape[0])

    out_ref[0:1] = line(in_ref)
    out_ref[1:2, 0:32] = jnp.zeros((1, 32), f32)
    out_ref[1:2, 32:1024] = line(dw_ref)
    out_ref[2:3, 0:64] = jnp.zeros((1, 64), f32)
    out_ref[2:3, 64:1024] = line(gate_ref)
    wide = line(exp_ref)
    out_ref[3:4] = wide[:, 0:1024]
    out_ref[4:5] = wide[:, 1024:2048]
    for k, ref in enumerate(small):
        out_ref[5 + k // 2 : 6 + k // 2, k % 2 * 512 : k % 2 * 512 + 512] = line(ref)


def prepare_kernel(valid_ref, halo_valid_ref, x_ref, xh_ref, g_ref, *rest):
    vectors, (xp_ref, gp_ref, y1_ref, y1h_ref, y1t_ref, wide_ref) = rest[:12], rest[12:]
    vectors_kernel(*vectors, wide_ref)
    perm = permutation()
    gain, shift = wide_ref[8:9, 0:512], wide_ref[8:9, 512:1024]
    own, halo = extents(valid_ref), halo_sizes(valid_ref, halo_valid_ref)
    start = pl.multiple_of(lax.axis_index("row") * 384, 128)
    for b in range(5):
        if b == 4:
            rows = pl.ds(start, 128)
            block = jnp.concatenate([xh_ref[0, rows], xh_ref[1, rows]], axis=0)
        else:
            rows = slice(b * 128, (b + 1) * 128)
            block = jnp.concatenate([x_ref[0, rows], x_ref[1, rows]], axis=0)
            gblock = dot(perm, jnp.concatenate([g_ref[0, rows], g_ref[1, rows]], axis=0)).astype(bf16)
        block = dot(perm, block)
        lowered = block.astype(bf16)
        normed, _ = normalize(block)
        value = normed * gain + shift
        for q in range(4):
            part = slice(q * 64, (q + 1) * 64)
            if b == 4:
                y1h_ref[q] = (chunk_mask(halo, q // 2, q % 2, 64) * value[part]).astype(bf16)
            else:
                dest = slice(b * 64, (b + 1) * 64)
                xp_ref[q, dest] = lowered[part]
                gp_ref[q, dest] = gblock[part]
                y1_ref[q, dest] = (chunk_mask(own, q // 2, q % 2, 64, 4 * b) * value[part]).astype(bf16)
    for q in range(4):
        y1t_ref[:, q * 256 : (q + 1) * 256] = y1_ref[q].T


def whole(shape):
    return pl.BlockSpec(shape, lambda *_: (0,) * len(shape))


SMEM = pl.BlockSpec(memory_space=pltpu.SMEM)


def params():
    return pltpu.CompilerParams(vmem_limit_bytes=vmem_bytes)


def takes(micros):
    return pl.CostEstimate(flops=int(micros * 1.0e9), bytes_accessed=0, transcendentals=0)


def launch(deps, kernel, *, out_shape, in_specs, out_specs, **rest):
    single = not isinstance(out_shape, tuple)
    shapes = (out_shape,) if single else out_shape
    specs = (out_specs,) if single else out_specs
    anywhere = pl.BlockSpec(memory_space=pl.ANY)
    count = len(in_specs)

    def body(*refs):
        at = count + len(deps)
        kernel(*refs[:count], *refs[at : at + len(shapes)], *refs[at + len(shapes) + 1 :])

    call = pl.pallas_call(
        body,
        out_shape=(*shapes, jax.ShapeDtypeStruct((8, 128), f32)),
        in_specs=list(in_specs) + [anywhere] * len(deps),
        out_specs=(*specs, anywhere),
        compiler_params=params(),
        **rest,
    )
    return lambda *args: call(*args, *deps)


def own_number(dealt):
    return lax.axis_index("img") * 2 + lax.axis_index("row") if dealt else 0


def place_rows(scratch, refs, order, number, rows):
    each = 32 // len(refs)
    for k, ref in enumerate(refs):
        for b in range(each):
            at = pl.multiple_of((order[k * each + b] ^ number) * rows, 16)
            scratch[pl.ds(at, rows), :] = ref[b * rows : (b + 1) * rows, :]


def dealt_owner(place, order):
    if order == "none":
        return place
    if order == "plain":
        return (2 * (place % 16) + place // 16) ^ lax.axis_index("row")
    return (2 * masks_of(order)[place % 16] + place // 16) ^ own_number(True)


def deal_rows(outs, lead, value_ref, order, rows):
    for p in range(32):
        at = pl.multiple_of(dealt_owner(p, order) * rows, 16)
        outs[p // 16][(slice(p % 16 * rows, (p % 16 + 1) * rows),) + lead] = value_ref[pl.ds(at, rows), :].astype(bf16)


def prepare(valid, halo_valid, x, xh, g, vectors, deps=()):
    vmem = pl.BlockSpec(memory_space=pltpu.VMEM)
    return launch(
        deps,
        prepare_kernel,
        out_shape=(
            jax.ShapeDtypeStruct((4, 256, 512), bf16),
            jax.ShapeDtypeStruct((4, 256, 512), bf16),
            jax.ShapeDtypeStruct((4, 256, 512), bf16),
            jax.ShapeDtypeStruct((4, 64, 512), bf16),
            jax.ShapeDtypeStruct((512, 1024), bf16),
            jax.ShapeDtypeStruct((9, 1024), f32),
        ),
        in_specs=[SMEM] * 2 + [vmem] * 15,
        out_specs=(vmem,) * 6,
        cost_estimate=takes(4),
        name="prepare",
    )(valid, halo_valid, x, xh, g, *vectors)


def low_lanes(shape):
    return lax.broadcasted_iota(i32, shape, len(shape) - 1) < 64


def swap_lanes(value):
    return pltpu.roll(value, 64, axis=1)


def shifted_block(value, step):
    if step == 0:
        return value
    blk = lax.broadcasted_iota(i32, value.shape, 1)
    if step > 0:
        return jnp.where(blk < 7, pltpu.roll(value, 7, axis=1), 0.0)
    return jnp.where(blk > 0, pltpu.roll(value, 1, axis=1), 0.0)


ODD = ((-1, 0), (-1, 1), (0, 0), (0, 1), (1, 0))
EVEN = ((-1, 1), (0, 0), (0, 1), (1, 0), (1, 1))


def lane_pairs(chunks):
    res = {}
    for row_par in range(2):
        odd, even = chunks[2 * row_par + 1], chunks[2 * row_par]
        odd_s, even_s = swap_lanes(odd), swap_lanes(even)
        res[row_par, 0] = (odd, even_s)
        res[row_par, 1] = (odd_s, even)
    return res


def fill_band(ref, lead, pairs, n, start, row_par):
    odd, even = (v.reshape(n, 2, 2, 8, 128) for v in pairs)
    half = 1 - row_par
    lanes = slice(half * 128, half * 128 + 128)
    low = low_lanes((n * 2, 8, 128))
    cache = {}

    def take(name, value, step, ccp):
        if (name, step, ccp) not in cache:
            cache[name, step, ccp] = shifted_block(value[:, ccp].reshape(n * 2, 8, 128), step)
        return cache[name, step, ccp]

    def write(k):
        both = jnp.where(low, take("o", odd, *ODD[k]), take("e", even, *EVEN[k]))
        ref[lead + (slice(start, start + n), k, slice(None), lanes)] = both.reshape(n, 16, 128).astype(bf16)

    return [functools.partial(write, k) for k in range(5)]


def fill_group(ref, lead, own, halo, upper):
    steps = []
    for row_par in range(2):
        first = 2 + row_par
        steps += fill_band(ref, lead, own[row_par], 8, first, row_par)
        steps += fill_band(ref, lead, [v * (1.0 - upper) for v in halo[row_par]], 2, first - 2, row_par)
        steps += fill_band(ref, lead, [v * upper for v in halo[row_par]], 2, first + 8, row_par)
    return steps


def diagonal(rows):
    return (lax.broadcasted_iota(i32, (rows, 128), 0) % 64) == (lax.broadcasted_iota(i32, (rows, 128), 1) % 64)


def build_weights(w_ref, slot, tap_ref, group, flip=False):
    mask = diagonal(64)
    low = low_lanes((1, 128))
    tile, side = group // 2, group % 2
    cols = slice(tile * 128, tile * 128 + 128)

    def write(i, jj):
        rows = tap_ref[6 - i if flip else i, :, cols]
        turned = swap_lanes(rows)
        first, second = (rows, turned) if side == 0 else (turned, rows)
        a, b = (6 - jj, 7 - jj) if flip else (jj, jj - 1)
        left = first[a : a + 1] if 0 <= a <= 6 else jnp.zeros((1, 128), f32)
        right = second[b : b + 1] if 0 <= b <= 6 else jnp.zeros((1, 128), f32)
        vector = jnp.where(low, left, right)
        block = jnp.where(mask, jnp.broadcast_to(vector, (64, 128)), 0.0).astype(bf16)
        for out_par in range(2):
            top = i + out_par
            ti, rp, tj, cp = top // 2, top % 2, jj // 2, jj % 2
            at = (rp * 2 + cp) * 64
            w_ref[slot, ti * 4 + tj, at : at + 64, out_par * 128 : out_par * 128 + 128] = block

    return [functools.partial(write, i, jj) for i in range(7) for jj in range(8)]


def clear_weights(w_ref):
    for slot in range(2):
        for tj in range(4):
            w_ref[slot, tj, 0:128, 128:256] = jnp.zeros((128, 128), bf16)
            w_ref[slot, 12 + tj, 128:256, 0:128] = jnp.zeros((128, 128), bf16)


def band_block(ref, lead, ti, tj):
    return ref[lead + (slice(1 + ti, 9 + ti), slice(tj, tj + 2))].reshape(256, 256)


def convolve(ref, lead, w_ref, slot, meanwhile):
    total = None
    for k in range(16):
        part = dot(band_block(ref, lead, k // 4, k % 4), w_ref[slot, k])
        total = part if total is None else total + part
        for step in meanwhile[len(meanwhile) * k // 16 : len(meanwhile) * (k + 1) // 16]:
            step()
    return total


def convolve_groups(ref, w_ref, tap_ref, own, halo, upper, flip):
    def steps(group):
        cols = slice(group // 2 * 128, group // 2 * 128 + 128)
        own_pairs = lane_pairs([v[:, cols] for v in own])
        halo_pairs = lane_pairs([v[:, cols] for v in halo])
        side = group % 2
        band = [own_pairs[rp, side] for rp in range(2)], [halo_pairs[rp, side] for rp in range(2)]
        return fill_group(ref, (group,), *band, upper) + build_weights(w_ref, side, tap_ref, group, flip)

    for step in steps(0):
        step()
    return [convolve(ref, (group,), w_ref, group % 2, steps(group + 1) if group < 3 else []) for group in range(4)]


def split_lanes(low_group, high_group):
    low = low_lanes((256, 128))
    chunks = []
    for rp in range(2):
        lg = low_group[:, rp * 128 : rp * 128 + 128]
        hg = high_group[:, rp * 128 : rp * 128 + 128]
        chunks.append(jnp.where(low, lg, swap_lanes(hg)))
        chunks.append(jnp.where(low, swap_lanes(lg), hg))
    return chunks


def forward_kernel(valid_ref, halo_valid_ref, y1_ref, y1h_ref, *rest, order, dealt):
    weights, (wide_ref, tap_ref, d_ref, band_ref, j0_ref, w_ref, win_ref) = rest[:8], rest[8:]
    step = pl.program_id(0)

    @pl.when(step == 0)
    def _():
        clear_weights(w_ref)

    upper = is_upper()
    sizes, around = extents(valid_ref), halo_sizes(valid_ref, halo_valid_ref)
    place_rows(win_ref, weights, order, own_number(dealt), 16)
    weight = win_ref[...]
    bias = wide_ref[0:1]
    joined = dot(y1_ref[...].reshape(1024, 512), weight) + bias
    joined = [joined[q * 256 : (q + 1) * 256] for q in range(4)]
    around_rows = dot(y1h_ref[...].reshape(256, 512), weight) + bias

    @pl.when(step == 0)
    def _():
        for q in range(4):
            j0_ref[q] = joined[q][:, 0:128]

    own, halo = [], []
    for q in range(4):
        own.append((joined[q] * chunk_mask(sizes, q // 2, q % 2)).astype(bf16).astype(f32))
        part = around_rows[q * 64 : (q + 1) * 64]
        halo.append((part * chunk_mask(around, q // 2, q % 2, 64)).astype(bf16).astype(f32))
    sums = convolve_groups(band_ref, w_ref, tap_ref, own, halo, upper, False)
    for tile in range(2):
        cols = slice(tile * 128, tile * 128 + 128)
        for q, value in enumerate(split_lanes(*sums[2 * tile : 2 * tile + 2])):
            d_ref[q, :, cols] = (value + wide_ref[1:2, cols]) * conv_scale


def forward(valid, halo_valid, y1, y1h, w_in, wide, taps, order, dealt, deps=()):
    return launch(
        deps,
        functools.partial(forward_kernel, order=order, dealt=dealt),
        grid=(4,),
        out_shape=(
            jax.ShapeDtypeStruct((4, 256, 1024), f32),
            jax.ShapeDtypeStruct((16, 13, 5, 16, 256), bf16),
            jax.ShapeDtypeStruct((4, 256, 128), f32),
        ),
        in_specs=[SMEM, SMEM, whole((4, 256, 512)), whole((4, 64, 512))]
        + [pl.BlockSpec((64, 256), lambda t: (0, t))] * 8
        + [pl.BlockSpec((9, 256), lambda t: (0, t)), pl.BlockSpec((7, 7, 256), lambda t: (0, 0, t))],
        out_specs=(
            pl.BlockSpec((4, 256, 256), lambda t: (0, 0, t)),
            pl.BlockSpec((4, 13, 5, 16, 256), lambda t: (t, 0, 0, 0, 0)),
            whole((4, 256, 128)),
        ),
        scratch_shapes=[pltpu.VMEM((2, 16, 256, 256), bf16), pltpu.VMEM((512, 256), bf16)],
        cost_estimate=takes(24),
        name="forward",
    )(valid, halo_valid, y1, y1h, *w_in, wide, taps)


def middle_kernel(
    valid_ref,
    d_ref,
    j0_ref,
    xp_ref,
    gp_ref,
    oa,
    ob,
    oc,
    od,
    ea,
    eb4,
    ec,
    ed,
    ra,
    rb,
    first_ref,
    second_ref,
    g3_ref,
    g4_ref,
    wide_ref,
    out_ref,
    act_ref,
    y2_ref,
    u_ref,
    dh_ref,
    df_ref,
    dz_ref,
    dv_ref,
    dd_ref,
    dx2_ref,
    s512_ref,
    s2048_ref,
    s1024_ref,
    held_ref,
    w_out_ref,
    w_exp_ref,
    w_red_ref,
    g1_ref,
    g2_ref,
    *,
    order,
    dealt,
):
    q = pl.program_id(0)
    mask = pair_mask(extents(valid_ref), q)
    out_bias, mix, gain, shift, red_bias, ffn = (
        wide_ref[5 + k // 2 : 6 + k // 2, k % 2 * 512 : k % 2 * 512 + 512] for k in range(6)
    )
    lane = lax.broadcasted_iota(i32, (512, 128), 1)
    is0 = (lane >= 32) & (lane < 64)
    is1 = lane >= 64

    @pl.when(q == 0)
    def _():
        s512_ref[...] = jnp.zeros_like(s512_ref)
        s2048_ref[...] = jnp.zeros_like(s2048_ref)
        s1024_ref[...] = jnp.zeros_like(s1024_ref)
        g1_ref[...] = jnp.zeros_like(g1_ref)
        g2_ref[...] = jnp.zeros_like(g2_ref)
        g1_ref[32:64, 64:128] = first_ref[...]
        g2_ref[64:128] = second_ref[...]
        number = own_number(dealt)
        place_rows(w_out_ref, (oa, ob, oc, od), order, number, 16)
        place_rows(w_exp_ref, (ea, eb4, ec, ed), order, number, 16)
        for p in range(32):
            owner = dealt_owner(p, "plain" if dealt else "none")
            ref, first = (ra, rb)[p // 16], p % 16 * 64
            w_red_ref[pl.ds(pl.multiple_of(owner * 64, 64), 64), :] = ref[first : first + 64, :]

    d01, d2, d3, d4 = d_ref[:, 0:128], d_ref[:, 128:256], d_ref[:, 256:512], d_ref[:, 512:1024]
    pointwise = pltpu.roll(j0_ref[...], 32, axis=1)
    u0 = jnp.where(is0, pointwise * d01, 0.0).astype(bf16)
    v1 = dot(u0, g1_ref[...]) + wide_ref[2:3, 0:128]
    u1 = jnp.where(is1, v1 * d01, 0.0).astype(bf16)
    v2 = dot(u1, g2_ref[...]) + wide_ref[2:3, 128:256]
    u2 = (v2 * d2).astype(bf16)
    v3 = dot(u2, g3_ref[...]) + wide_ref[2:3, 256:512]
    u3 = (v3 * d3).astype(bf16)
    v4 = dot(u3, g4_ref[...]) + wide_ref[2:3, 512:1024]
    u4 = (v4 * d4).astype(bf16)
    u_ref[0:128] = jnp.where(is1, u1, u0).T
    u_ref[128:256] = u2.T
    u_ref[256:512] = u3.T
    u_ref[512:1024] = u4.T
    branch = dot(u4, w_out_ref[...]) + out_bias
    middle = xp_ref[...].astype(f32) + mask * mix * branch
    normed, inverse = normalize(middle)
    y2 = (mask * (normed * gain + shift)).astype(bf16)
    y2_ref[...] = y2.T
    grad = gp_ref[...].astype(f32)
    df = (mask * ffn * grad).astype(bf16)
    df_ref[...] = df
    reduced = red_bias
    back = jnp.zeros((512, 512), f32)
    for k in range(4):
        cols = slice(k * 512, (k + 1) * 512)
        hidden = dot(y2, w_exp_ref[:, cols]) + wide_ref[3 + k // 2 : 4 + k // 2, k % 2 * 512 : k % 2 * 512 + 512]
        cdf = 0.5 * (1.0 + lax.erf(hidden * inv_root_two))
        act = (hidden * cdf).astype(bf16)
        act_ref[cols, :] = act.T
        reduced = reduced + dot(act, w_red_ref[cols, :])
        density = jnp.exp(-0.5 * hidden * hidden) * inv_root_tau
        dh = (dot_nt(df, w_red_ref[cols, :]) * (cdf + hidden * density)).astype(bf16)
        dh_ref[:, cols] = dh
        s2048_ref[:, cols] += column_sum(dh.astype(f32))
        back = back + dot_nt(dh, w_exp_ref[:, cols])
    held_ref[pl.ds(2 * q, 2)] = (middle + mask * ffn * reduced).astype(bf16).reshape(2, 256, 512)
    s512_ref[0:1] += column_sum(grad * mask * reduced)
    s512_ref[1:2] += column_sum(df.astype(f32))
    back = mask * back
    s512_ref[2:3] += column_sum(back * normed)
    s512_ref[3:4] += column_sum(back)
    dx2 = grad + norm_backward(back, normed, inverse, gain)
    dx2_ref[...] = dx2
    dz = (mask * mix * dx2).astype(bf16)
    dz_ref[...] = dz
    s512_ref[4:5] += column_sum(dx2 * mask * branch)
    s512_ref[5:6] += column_sum(dz.astype(f32))
    du4 = dot_nt(dz, w_out_ref[...])
    dv4 = (du4 * d4).astype(bf16)
    dd4 = (du4 * v4).astype(bf16)
    du3 = dot_nt(dv4, g4_ref[...])
    dv3 = (du3 * d3).astype(bf16)
    dd3 = (du3 * v3).astype(bf16)
    du2 = dot_nt(dv3, g3_ref[...])
    dv2 = (du2 * d2).astype(bf16)
    dd2 = (du2 * v2).astype(bf16)
    du1 = dot_nt(dv2, g2_ref[...])
    dv1 = (du1 * d01).astype(bf16)
    du0 = dot_nt(dv1, g1_ref[...])
    dpw = pltpu.roll(du0 * d01, 96, axis=1)
    dd01 = jnp.where(is1, du1 * v1, jnp.where(is0, du0 * pointwise, dpw)).astype(bf16)
    dv_ref[:, 0:128] = dv1
    dv_ref[:, 128:256] = dv2
    dv_ref[:, 256:512] = dv3
    dv_ref[:, 512:1024] = dv4
    dd_ref[:, 0:128] = dd01
    dd_ref[:, 128:256] = dd2
    dd_ref[:, 256:512] = dd3
    dd_ref[:, 512:1024] = dd4
    for k, ref in enumerate((dv_ref, dd_ref)):
        s1024_ref[k : k + 1] += column_sum(ref[...].astype(f32))

    @pl.when(q == 1)
    def _():
        unpermute(held_ref, out_ref)


def unpermute(held_ref, out_ref):
    perm = permutation()
    for b in range(4):
        block = jnp.concatenate([held_ref[k, b * 64 : (b + 1) * 64] for k in range(4)], axis=0)
        block = dot_tn(perm, block).astype(bf16)
        out_ref[0, b * 128 : (b + 1) * 128] = block[0:128]
        out_ref[1, b * 128 : (b + 1) * 128] = block[128:256]


def middle_call(valid, d, j0, xp, gp, w_exp, w_red, g1, g2, g3, g4, wide, order, dealt, deps=()):
    def chunk(width):
        return pl.BlockSpec((512, width), lambda q: (q, 0))

    def out(width, dtype=bf16):
        return jax.ShapeDtypeStruct((1024, width), dtype)

    def turned(rows):
        return pl.BlockSpec((rows, 512), lambda q: (0, q))

    def out_turned(rows):
        return jax.ShapeDtypeStruct((rows, 1024), bf16)

    widths = (2048, 512, 512, 1024, 1024)
    rows = (2048, 512, 1024)
    return launch(
        deps,
        functools.partial(middle_kernel, order=order, dealt=dealt),
        grid=(2,),
        out_shape=(jax.ShapeDtypeStruct((2, 512, 512), bf16),)
        + tuple(out_turned(r) for r in rows)
        + tuple(out(w) for w in widths)
        + (
            out(512, f32),
            jax.ShapeDtypeStruct((8, 512), f32),
            jax.ShapeDtypeStruct((1, 2048), f32),
            jax.ShapeDtypeStruct((8, 1024), f32),
        ),
        in_specs=[SMEM, chunk(1024), chunk(128), chunk(512), chunk(512)]
        + [pl.BlockSpec((128, 512), lambda q: (0, 4))] * 4
        + [pl.BlockSpec((128, 2048), lambda q: (0, 0))] * 4
        + [whole((1024, 512))] * 2
        + [whole(v.shape) for v in (g1, g2, g3, g4, wide)],
        out_specs=(whole((2, 512, 512)),)
        + tuple(turned(r) for r in rows)
        + tuple(chunk(w) for w in widths)
        + (chunk(512), whole((8, 512)), whole((1, 2048)), whole((8, 1024))),
        scratch_shapes=[
            pltpu.VMEM((4, 256, 512), bf16),
            pltpu.VMEM((512, 512), bf16),
            pltpu.VMEM((512, 2048), bf16),
            pltpu.VMEM((2048, 512), bf16),
            pltpu.VMEM((128, 128), bf16),
            pltpu.VMEM((128, 128), bf16),
        ],
        cost_estimate=takes(30),
        name="middle",
    )(valid, *(v.reshape(1024, -1) for v in (d, j0, xp, gp)), *w_exp, *w_exp, *w_red, g1, g2, g3, g4, wide)


def feed_grads_kernel(
    y2_ref, dh_ref, act_ref, df_ref, u_ref, dz_ref, e_keep, e_send, r_keep, r_send, exp_ref, red_ref, out_ref, *, e_order, r_order
):
    step = pl.program_id(0)
    exp_ref[...] = dot(y2_ref[...], dh_ref[...])
    red_ref[pl.ds(pl.multiple_of(step * 512, 512), 512), :] = dot(act_ref[...], df_ref[...])
    deal_rows((e_keep, e_send), (slice(None),), exp_ref, e_order, 16)

    @pl.when(step == 0)
    def _():
        out_ref[...] = dot(u_ref[...], dz_ref[...])

    @pl.when(step == 3)
    def _():
        for p in range(32):
            owner = dealt_owner(p, r_order)
            ref, first = (r_keep, r_send)[p // 16], p % 16 * 80
            ref[first : first + 64] = red_ref[pl.ds(pl.multiple_of(owner * 64, 64), 64), :].astype(bf16)
            ref[first + 64 : first + 80] = out_ref[pl.ds(pl.multiple_of(owner * 16, 16), 16), :].astype(bf16)


def feed_grads(y2, dh, act, df, u, dz, e_order, r_order, deps=()):
    return launch(
        deps,
        functools.partial(feed_grads_kernel, e_order=e_order, r_order=r_order),
        grid=(4,),
        out_shape=(jax.ShapeDtypeStruct((256, 2048), bf16),) * 2 + (jax.ShapeDtypeStruct((1280, 512), bf16),) * 2,
        in_specs=[
            whole((512, 1024)),
            pl.BlockSpec((1024, 512), lambda k: (0, k)),
            pl.BlockSpec((512, 1024), lambda k: (k, 0)),
            whole((1024, 512)),
            pl.BlockSpec((512, 1024), lambda k: (1, 0)),
            whole((1024, 512)),
        ],
        out_specs=(pl.BlockSpec((256, 512), lambda k: (0, k)),) * 2 + (whole((1280, 512)),) * 2,
        scratch_shapes=[pltpu.VMEM((512, 512), f32), pltpu.VMEM((2048, 512), f32), pltpu.VMEM((512, 512), f32)],
        cost_estimate=takes(11),
        name="feed_grads",
    )(y2, dh, act, df, u, dz)


def kernel_grad_kernel(dd_ref, band_ref, dk_ref):
    low = low_lanes((256, 128))
    low8 = low_lanes((8, 128))
    wide = diagonal(256)
    for tile in range(2):
        cols = slice(tile * 128, tile * 128 + 128)
        own = [dd_ref[q, :, cols].astype(f32) for q in range(4)]
        turned_own = [swap_lanes(v) for v in own]
        for side in range(2):
            group = tile * 2 + side
            halves = []
            for rp in range(2):
                if side == 0:
                    halves.append(jnp.where(low, own[2 * rp], turned_own[2 * rp + 1]))
                else:
                    halves.append(jnp.where(low, turned_own[2 * rp], own[2 * rp + 1]))
            left = jnp.concatenate(halves, axis=1).astype(bf16)
            rows = {}
            for ti in range(4):
                for tj in range(4):
                    cross = dot_tn(left, band_block(band_ref, (group,), ti, tj))
                    for rp in range(2):
                        half = jnp.where(wide, cross[:, rp * 128 : rp * 128 + 128], 0.0)
                        part = jnp.sum(half.reshape(4, 8, 8, 128), axis=1)
                        for out_rp in range(2):
                            i = 2 * ti + rp - out_rp
                            if 0 <= i <= 6:
                                for out_cp in range(2):
                                    key = (i, tj, out_cp)
                                    term = part[out_rp * 2 + out_cp]
                                    rows[key] = rows[key] + term if key in rows else term
            for i in range(7):
                turned = [swap_lanes(rows[i, tj, 1]) for tj in range(4)] + [jnp.zeros((8, 128), f32)]
                for tj in range(4):
                    value = rows[i, tj, 0] + jnp.where(low8, turned[tj], turned[tj + 1])
                    dk_ref[group, i * 4 + tj : i * 4 + tj + 1] = column_sum(value) * conv_scale
            dk_ref[group, 28:32] = jnp.zeros((4, 128), f32)


def kernel_grad(dd, band, deps=()):
    return launch(
        deps,
        kernel_grad_kernel,
        grid=(4,),
        out_shape=jax.ShapeDtypeStruct((16, 32, 128), f32),
        in_specs=[
            pl.BlockSpec((4, 256, 256), lambda t: (0, 0, t)),
            pl.BlockSpec((4, 13, 5, 16, 256), lambda t: (t, 0, 0, 0, 0)),
        ],
        out_specs=pl.BlockSpec((4, 32, 128), lambda t: (t, 0, 0)),
        cost_estimate=takes(13),
        name="kernel_grad",
    )(dd, band)


def gate_grads_kernel(u_ref, dv_ref, s512_ref, s2048_ref, s1024_ref, dk_ref, keep, send, small_ref, *, order):
    small_ref[0:256] = dot(u_ref[256:512], dv_ref[:, 512:1024])
    g3 = dot(u_ref[128:256], dv_ref[:, 256:512])
    small_ref[256:320, 0:256] = g3[0:64]
    small_ref[256:320, 256:512] = g3[64:128]
    g12 = dot(u_ref[0:128], dv_ref[:, 0:256])
    for k in range(4):
        cols = slice(k * 128, (k + 1) * 128)
        small_ref[320:336, cols] = g12[64 + 16 * k : 80 + 16 * k, 128:256]
        small_ref[336:344, cols] = g12[32 + 8 * k : 40 + 8 * k, 0:128]
        small_ref[384:512, cols] = dk_ref[k * 128 : (k + 1) * 128]
        small_ref[352 + k : 353 + k] = s2048_ref[:, k * 512 : (k + 1) * 512]
        small_ref[356 + k : 357 + k] = s1024_ref[k // 2 : k // 2 + 1, k % 2 * 512 : k % 2 * 512 + 512]
    small_ref[344:352] = s512_ref[...]
    small_ref[360:384] = jnp.zeros((24, 512), f32)
    deal_rows((keep, send), (slice(None),), small_ref, order, 16)


def gate_grads(u, dv, s512, s2048, s1024, dk, order, deps=()):
    return launch(
        deps,
        functools.partial(gate_grads_kernel, order=order),
        grid=(1,),
        out_shape=(jax.ShapeDtypeStruct((256, 512), bf16),) * 2,
        in_specs=[whole((512, 1024))] + [whole(v.shape) for v in (dv, s512, s2048, s1024, dk)],
        out_specs=(whole((256, 512)),) * 2,
        scratch_shapes=[pltpu.VMEM((512, 512), f32)],
        cost_estimate=takes(3),
        name="gate_grads",
    )(u, dv, s512, s2048, s1024, dk)


def unpack_kernel(own_ref, oth_ref, *rest):
    outs, (table_ref, all_ref) = rest[:-2], rest[-2:]
    in_ref, dk_ref, dwb_ref, g1_ref, g2_ref, g3_ref, g4_ref, gb_ref = outs[:8]
    outb_ref, mix_ref, gain_ref, shift_ref, expb_ref, redb_ref, ffn_ref = outs[8:15]
    first_gain_ref, first_shift_ref, inb_ref = outs[15:]
    row = lax.axis_index("row")
    total = own_ref[0:16, 0:1024].astype(f32)
    for k in range(1, 16):
        total = total + own_ref[k * 16 : (k + 1) * 16, 0:1024].astype(f32)
    in_ref[...] = total
    late = own_ref[0:16, 1536:1664].astype(f32)
    for k in range(1, 16):
        late = late + own_ref[k * 16 : (k + 1) * 16, 1536:1664].astype(f32)
    lines = [
        jnp.concatenate([late[r * 4 + c : r * 4 + c + 1] for c in range(4)], axis=1).reshape(512) for r in range(4)
    ]
    first_gain_ref[...] = lines[0]
    first_shift_ref[...] = lines[1]
    inb_ref[0:512] = lines[2]
    inb_ref[512:1024] = lines[3]
    for k in range(16):
        block = slice(k * 16, (k + 1) * 16)
        table_ref[pl.ds(pl.multiple_of((2 * k + row) * 16, 16), 16), :] = own_ref[block, 1024:1536]
        table_ref[pl.ds(pl.multiple_of((2 * k + 1 - row) * 16, 16), 16), :] = oth_ref[block, 1024:1536]
    all_ref[...] = table_ref[...].astype(f32)
    g4_ref[...] = all_ref[0:256]
    g3_ref[0:64] = all_ref[256:320, 0:256]
    g3_ref[64:128] = all_ref[256:320, 256:512]
    for k in range(4):
        cols = slice(k * 128, (k + 1) * 128)
        g2_ref[16 * k : 16 * k + 16] = all_ref[320:336, cols]
        g1_ref[8 * k : 8 * k + 8] = swap_lanes(all_ref[336:344, cols])[:, 0:64]
        expb_ref[k * 512 : (k + 1) * 512] = all_ref[352 + k : 353 + k].reshape(512)
    for k, ref in enumerate((ffn_ref, redb_ref, gain_ref, shift_ref, mix_ref, outb_ref)):
        ref[...] = all_ref[344 + k : 345 + k].reshape(512)

    def line(first):
        return jnp.concatenate([all_ref[first : first + 1], all_ref[first + 1 : first + 2]], axis=1)

    gb_ref[...] = line(356)[:, 64:1024].reshape(960)
    dwb_ref[...] = line(358)[:, 32:1024].reshape(992) * conv_scale
    low = low_lanes((32, 128))
    lane = lax.broadcasted_iota(i32, (32, 128), 1)
    rows = []
    for t in range(8):
        cols = slice(t // 2 * 128, t // 2 * 128 + 128)
        first = 384 + t % 2 * 64
        left = all_ref[first : first + 32, cols]
        right = all_ref[first + 32 : first + 64, cols]
        pair = (jnp.where(low, left, swap_lanes(right)), jnp.where(low, swap_lanes(left), right))
        rows.append([pltpu.roll(v, 96, axis=1) for v in pair])
    for t in range(8):
        size = 128 if t < 7 else 96
        for odd in range(2):
            value = jnp.where(lane < 96, rows[t][odd], rows[t + 1][odd]) if t < 7 else rows[t][odd]
            for i in range(7):
                for j in range(odd, 7, 2):
                    at = i * 4 + j // 2
                    dk_ref[i, j : j + 1, t * 128 : t * 128 + size] = value[at : at + 1, 0:size]


def unpack(own, oth, deps=()):
    vmem = pl.BlockSpec(memory_space=pltpu.VMEM)
    shapes = ((16, 1024), (7, 7, 992), (992,), (32, 64), (64, 128), (128, 256), (256, 512), (960,))
    shapes += ((512,),) * 4 + ((2048,), (512,), (512,), (512,), (512,), (1024,))
    return launch(
        deps,
        unpack_kernel,
        out_shape=tuple(jax.ShapeDtypeStruct(v, f32) for v in shapes),
        in_specs=[vmem] * 2,
        out_specs=(vmem,) * len(shapes),
        scratch_shapes=[pltpu.VMEM((512, 512), bf16), pltpu.VMEM((512, 512), f32)],
        cost_estimate=takes(3),
        name="unpack",
    )(own, oth)


def conv_back_kernel(valid_ref, dd_ref, ddh_ref, tap_ref, df_ref, w_ref, back_ref):
    step = pl.program_id(0)

    @pl.when(step == 0)
    def _():
        clear_weights(w_ref)

    sizes = extents(valid_ref)
    lane = lax.broadcasted_iota(i32, (256, 128), 1)
    keep = (lane < 32) & (step == 0)
    own = [dd_ref[q].astype(f32) for q in range(4)]
    halo = [ddh_ref[q].astype(f32) for q in range(4)]
    sums = convolve_groups(back_ref, w_ref, tap_ref, own, halo, is_upper(), True)
    for tile in range(2):
        cols = slice(tile * 128, tile * 128 + 128)
        for q, value in enumerate(split_lanes(*sums[2 * tile : 2 * tile + 2])):
            value = value * (chunk_mask(sizes, q // 2, q % 2) * conv_scale)
            if tile == 0:
                value = jnp.where(keep, own[q][:, cols], value)
            df_ref[q, :, cols] = value.astype(bf16)


def conv_back(valid, dd, ddh, taps, deps=()):
    return launch(
        deps,
        conv_back_kernel,
        grid=(4,),
        out_shape=jax.ShapeDtypeStruct((4, 256, 1024), bf16),
        in_specs=[
            SMEM,
            pl.BlockSpec((4, 256, 256), lambda t: (0, 0, t)),
            pl.BlockSpec((4, 64, 256), lambda t: (0, 0, t)),
            pl.BlockSpec((7, 7, 256), lambda t: (0, 0, t)),
        ],
        out_specs=pl.BlockSpec((4, 256, 256), lambda t: (0, 0, t)),
        scratch_shapes=[pltpu.VMEM((2, 16, 256, 256), bf16), pltpu.VMEM((4, 13, 5, 16, 256), bf16)],
        cost_estimate=takes(16),
        name="conv_back",
    )(valid, dd, ddh, taps)


def in_grad_kernel(y1_ref, df_ref, keep, send, sum_ref, *, order):
    sum_ref[...] = dot(y1_ref[...], df_ref[...])
    deal_rows((keep, send), (slice(None),), sum_ref, order, 16)


def in_grad(y1, df, order, deps=()):
    return launch(
        deps,
        functools.partial(in_grad_kernel, order=order),
        grid=(2,),
        out_shape=(jax.ShapeDtypeStruct((256, 1024), bf16),) * 2,
        in_specs=[whole((512, 1024)), pl.BlockSpec((1024, 512), lambda k: (0, k))],
        out_specs=(pl.BlockSpec((256, 512), lambda k: (0, k)),) * 2,
        scratch_shapes=[pltpu.VMEM((512, 512), f32)],
        cost_estimate=takes(4),
        name="in_grad",
    )(y1, df)


def last_kernel(valid_ref, df_ref, xp_ref, dx2_ref, *rest, order, dealt):
    weights, (wide_ref, out_ref, late_ref, held_ref, win_ref) = rest[:8], rest[8:]
    q = pl.program_id(0)

    @pl.when(q == 0)
    def _():
        late_ref[...] = jnp.zeros_like(late_ref)
        place_rows(win_ref, weights, order, own_number(dealt), 16)

    mask = pair_mask(extents(valid_ref), q)
    df = df_ref[...]
    sums = column_sum(df.astype(f32))
    late_ref[2:3] += sums[:, 0:512]
    late_ref[3:4] += sums[:, 512:1024]
    grad = mask * dot_nt(df, win_ref[...])
    normed, inverse = normalize(xp_ref[...].astype(f32))
    late_ref[0:1] += column_sum(grad * normed)
    late_ref[1:2] += column_sum(grad)
    total = dx2_ref[...] + norm_backward(grad, normed, inverse, wide_ref[8:9, 0:512])
    held_ref[pl.ds(2 * q, 2)] = total.astype(bf16).reshape(2, 256, 512)

    @pl.when(q == 1)
    def _():
        unpermute(held_ref, out_ref)


def last_call(valid, df, xp, dx2, w_in, wide, order, dealt, deps=()):
    def chunk(width):
        return pl.BlockSpec((512, width), lambda q: (q, 0))

    return launch(
        deps,
        functools.partial(last_kernel, order=order, dealt=dealt),
        grid=(2,),
        out_shape=(jax.ShapeDtypeStruct((2, 512, 512), bf16), jax.ShapeDtypeStruct((8, 512), f32)),
        in_specs=[SMEM, chunk(1024), chunk(512), chunk(512)] + [whole((64, 1024))] * 8 + [whole(wide.shape)],
        out_specs=(whole((2, 512, 512)), whole((8, 512))),
        scratch_shapes=[pltpu.VMEM((4, 256, 512), bf16), pltpu.VMEM((512, 1024), bf16)],
        cost_estimate=takes(7),
        name="last",
    )(valid, *(v.reshape(1024, -1) for v in (df, xp, dx2)), *w_in, wide)


def repeat(value):
    rows, cols = value.shape
    return jnp.broadcast_to(value[None], (16, rows, cols)).reshape(16 * rows, cols)


def join_kernel(*refs, counts):
    ins = list(refs[: sum(counts)])
    for out, count in zip(refs[sum(counts) :], counts):
        at = 0
        for _ in range(count):
            ref = ins.pop(0)
            out[at : at + ref.shape[0]] = ref[...]
            at += ref.shape[0]


def join(*lists, deps=()):
    vmem = pl.BlockSpec(memory_space=pltpu.VMEM)
    shapes = [(sum(v.shape[0] for v in group), group[0].shape[1]) for group in lists]
    return launch(
        deps,
        functools.partial(join_kernel, counts=[len(v) for v in lists]),
        out_shape=tuple(jax.ShapeDtypeStruct(v, bf16) for v in shapes),
        in_specs=[vmem] * sum(len(v) for v in lists),
        out_specs=(vmem,) * len(lists),
        cost_estimate=takes(1),
        name="join",
    )(*sum((list(v) for v in lists), []))


def add_kernel(a_ref, b_ref, out_ref):
    out_ref[...] = a_ref[...] + b_ref[...]


def add(a, b, deps=()):
    vmem = pl.BlockSpec(memory_space=pltpu.VMEM)
    return launch(
        deps,
        add_kernel,
        out_shape=jax.ShapeDtypeStruct(a.shape, a.dtype),
        in_specs=[vmem] * 2,
        out_specs=vmem,
        cost_estimate=takes(1),
        name="add",
    )(a, b)


def combine_kernel(*refs, items):
    at = sum(n for n, _ in items)
    ins, outs = list(refs[:at]), list(refs[at:])
    for count, parts in items:
        terms = [ins.pop(0) for _ in range(count)]
        for part in range(parts):
            total = functools.reduce(lambda a, b: a + b, [v[part, 0].astype(f32) for v in terms])
            outs.pop(0)[0] = total.astype(bf16)


def combine(*items, deps=()):
    steps = next(n for n in (2, 1) if all(v[0].shape[0] % (16 * n * p) == 0 for v, p in items))
    ins, in_specs, outs, out_specs = [], [], [], []
    for terms, parts in items:
        rows, cols = terms[0].shape
        size = rows // parts // steps
        ins += [v.reshape(parts, steps, size, cols) for v in terms]
        in_specs += [pl.BlockSpec((parts, 1, size, cols), lambda t: (0, t, 0, 0))] * len(terms)
        outs += [jax.ShapeDtypeStruct((steps, size, cols), bf16)] * parts
        out_specs += [pl.BlockSpec((1, size, cols), lambda t: (t, 0, 0))] * parts
    *values, token = launch(
        deps,
        functools.partial(combine_kernel, items=[(len(v), p) for v, p in items]),
        grid=(steps,),
        out_shape=tuple(outs),
        in_specs=in_specs,
        out_specs=tuple(out_specs),
        cost_estimate=takes(2),
        name="combine",
    )(*ins)
    return [v.reshape(-1, v.shape[-1]) for v in values] + [token]


def merge_kernel(ro_a, ro_b, e_a, e_b, *outs):
    for z, ref in enumerate(outs):
        rows = slice(z * 80, (z + 1) * 80)
        ref[0:80] = (ro_a[rows].astype(f32) + ro_b[rows].astype(f32)).astype(bf16)
        total = e_a[z * 16 : (z + 1) * 16].astype(f32) + e_b[z * 16 : (z + 1) * 16].astype(f32)
        for c in range(4):
            at = 80 + c * 16
            ref[at : at + 16] = total[:, c * 512 : (c + 1) * 512].astype(bf16)


def merge(ro_a, ro_b, e_a, e_b, deps=()):
    vmem = pl.BlockSpec(memory_space=pltpu.VMEM)
    return launch(
        deps,
        merge_kernel,
        out_shape=(jax.ShapeDtypeStruct((144, 512), bf16),) * 4,
        in_specs=[vmem] * 4,
        out_specs=(vmem,) * 4,
        cost_estimate=takes(2),
        name="merge",
    )(ro_a, ro_b, e_a, e_b)


def finish_kernel(*refs):
    ins, (red_ref, out_ref, exp_ref) = refs[:-3], refs[-3:]
    total = functools.reduce(lambda a, b: a + b, [v[...].astype(f32) for v in ins])
    red_ref[...] = total[0:64]
    out_ref[...] = total[64:80]
    for c in range(4):
        exp_ref[:, c * 512 : (c + 1) * 512] = total[80 + c * 16 : 96 + c * 16]


def finish(parts, deps=()):
    vmem = pl.BlockSpec(memory_space=pltpu.VMEM)
    shapes = ((64, 512), (16, 512), (16, 2048))
    return launch(
        deps,
        finish_kernel,
        out_shape=tuple(jax.ShapeDtypeStruct(v, f32) for v in shapes),
        in_specs=[vmem] * len(parts),
        out_specs=(vmem,) * 3,
        cost_estimate=takes(1),
        name="finish",
    )(*parts)


def deal_kernel(i_a, i_b, late_a, late_b, *rest):
    parts, (out_ref, late_ref) = rest[:-2], rest[-2:]
    small = functools.reduce(lambda a, b: a + b, [v[...].astype(f32) for v in parts]).astype(bf16)
    late = late_a[...] + late_b[...]
    for r in range(4):
        for c in range(4):
            late_ref[r * 4 + c : r * 4 + c + 1] = late[r : r + 1, c * 128 : (c + 1) * 128]
    last = late_ref[...].astype(bf16)
    out_ref[:, 0:1024] = (i_a[...].astype(f32) + i_b[...].astype(f32)).astype(bf16)
    for k in range(16):
        out_ref[k * 16 : (k + 1) * 16, 1024:1536] = small
        out_ref[k * 16 : (k + 1) * 16, 1536:1664] = last


def deal(i_a, i_b, late_a, late_b, parts, deps=()):
    vmem = pl.BlockSpec(memory_space=pltpu.VMEM)
    return launch(
        deps,
        deal_kernel,
        out_shape=jax.ShapeDtypeStruct((256, 1664), bf16),
        in_specs=[vmem] * (4 + len(parts)),
        out_specs=vmem,
        scratch_shapes=[pltpu.VMEM((16, 128), f32)],
        cost_estimate=takes(2),
        name="deal",
    )(i_a, i_b, late_a, late_b, *parts)


def late_kernel(a_ref, b_ref, gain_ref, shift_ref, bias_ref):
    total = a_ref[...] + b_ref[...]
    gain_ref[...] = total[0:1].reshape(512)
    shift_ref[...] = total[1:2].reshape(512)
    bias_ref[0:512] = total[2:3].reshape(512)
    bias_ref[512:1024] = total[3:4].reshape(512)


def late_sums(a, b, deps=()):
    vmem = pl.BlockSpec(memory_space=pltpu.VMEM)
    return launch(
        deps,
        late_kernel,
        out_shape=tuple(jax.ShapeDtypeStruct((v,), f32) for v in (512, 512, 1024)),
        in_specs=[vmem] * 2,
        out_specs=(vmem,) * 3,
        cost_estimate=takes(1),
        name="late",
    )(a, b)


ROW = "row"


def img_bits():
    return lax.axis_size("img").bit_length() - 1


def swap_img(value, mask):
    return lax.ppermute(value, "img", [(k, k ^ mask) for k in range(lax.axis_size("img"))])


def swap_row(value):
    return lax.ppermute(value, "row", [(0, 1), (1, 0)])


def masks_of(stage):
    masks = [0]
    for bit in stage:
        masks = [m | v for m in masks for v in (0, 1 << bit)]
    return masks


def gather_order(groups):
    rel = [0]
    for bits in groups:
        rel = [m ^ r for m in masks_of(bits) for r in rel]
    return [2 * r + side for side in (0, 1) for r in rel]


def swaps(value, bits):
    return [value] + [swap_img(value, m) for m in masks_of(bits)[1:]]


def after(value, *others):
    return lax.optimization_barrier((value, others))[0]


def spread(value):
    return lax.all_to_all(value, "img", split_axis=0, concat_axis=0, tiled=True)


def sum_img(value, bits):
    for bit in bits[:-1]:
        value = value + swap_img(value, 1 << bit)
    return value, swap_img(value, 1 << bits[-1])


def own_bit(bit):
    return lax.axis_index("row") if bit == ROW else (lax.axis_index("img") >> bit) & 1


def swap_bit(value, bit):
    return swap_row(value) if bit == ROW else swap_img(value, 1 << bit)


def plain_gather(shard):
    value = shard
    for bit in [ROW] + list(range(img_bits())):
        other = swap_bit(value, bit)
        mine = own_bit(bit) == 0
        value = jnp.concatenate([jnp.where(mine, value, other), jnp.where(mine, other, value)], axis=0)
    return value


def plain_scatter(value):
    for bit in list(range(img_bits()))[::-1] + [ROW]:
        half = value.shape[0] // 2
        mine = own_bit(bit) == 0
        first, second = value[:half], value[half:]
        sent = swap_bit(jnp.where(mine, second, first).astype(bf16), bit)
        value = jnp.where(mine, first, second).astype(f32) + sent.astype(f32)
    return value


def per_device(
    features,
    validity,
    upstream,
    normgain,
    normshift,
    inweight,
    inbias,
    dwkernel,
    dwbias,
    gatefirst,
    gatesecond,
    gatethird,
    gatefourth,
    gatebias,
    outweight,
    outbias,
    mixscale,
    mlpgain,
    mlpshift,
    expandweight,
    expandbias,
    reduceweight,
    reducebias,
    mlpscale,
):
    bits = img_bits()
    dealt = bits == 4
    lower = lax.axis_index("row") == 1

    x = features.reshape(2, 512, 512)
    g = upstream.reshape(2, 512, 512)
    valid = validity.reshape(32, 32)
    x_halo = swap_row(x)
    halo_valid = swap_row(valid)
    taps = jnp.pad(dwkernel.astype(f32), ((0, 0), (0, 0), (32, 0)))
    vectors = (inbias, dwbias, gatebias, expandbias)
    vectors += (outbias, mixscale, mlpgain, mlpshift, reducebias, mlpscale, normgain, normshift)
    exp_out = jnp.concatenate([expandweight, outweight], axis=1)
    deep, flat_pair = (3, 2), (1, 0)
    if dealt:
        in_order = gather_order((deep, flat_pair))
        exp_order = gather_order((deep, (1,), (0,)))
        in_z, token = join(swaps(inweight, deep))
        exp_parts = swaps(exp_out, deep)
        red_own = spread(repeat(reduceweight))
        w_in = swaps(in_z, flat_pair)
        xp, gp, y1, y1h, y1t, wide, token = prepare(valid, halo_valid, x, x_halo, g, vectors, [token])
        exp_z, token = join(exp_parts, deps=[token] + w_in[1:])
        w_in = w_in + [swap_row(v) for v in w_in]
        exp_y, token = join(swaps(exp_z, (1,)), deps=[token])
        w_exp = swaps(exp_y, (0,))
        d, band, j0, token = forward(valid, halo_valid, y1, y1h, w_in, wide, taps, in_order, dealt, [token])
        w_exp = w_exp + [swap_row(w_exp[0]), swap_row(after(w_exp[1], d))]
        w_red = [red_own, swap_row(after(red_own, d))]
    else:
        in_order = exp_order = list(range(32))
        w_in = jnp.split(plain_gather(inweight), 8, axis=0)
        w_exp = jnp.split(plain_gather(exp_out), 4, axis=0)
        w_red = jnp.split(plain_gather(reduceweight), 2, axis=0)
        xp, gp, y1, y1h, y1t, wide, token = prepare(valid, halo_valid, x, x_halo, g, vectors)
        d, band, j0, token = forward(valid, halo_valid, y1, y1h, w_in, wide, taps, in_order, dealt)
    (produced, act, y2, u, dh, df, dz, dv, dd, dx2, s512, s2048, s1024, token) = middle_call(
        valid, d, j0, xp, gp, w_exp, w_red, gatefirst, gatesecond, gatethird, gatefourth, wide, exp_order, dealt
    )
    dd = dd.reshape(4, 256, 1024)
    dd_halo = swap_row(jnp.where(lower, dd[:, 0:64], dd[:, 192:256]))

    def flat(value):
        return value.reshape(1024, -1)

    r_order, e_order, plain = ((1, 0, 3, 2), (0, 1, 3, 2), "plain") if dealt else ("none",) * 3
    if dealt:
        e_keep, e_send, r_keep, r_send, token = feed_grads(
            y2, flat(dh), act, flat(df), u, flat(dz), e_order, r_order
        )
        e_got, r_got = swap_row(e_send), swap_row(r_send)
        dk, token = kernel_grad(dd, band, [token])
        s_keep, s_send, token = gate_grads(
            u, flat(dv), s512, s2048, s1024, dk.reshape(512, 128), flat_pair + deep, [token]
        )
        s_got = swap_row(s_send)
        r_keep, r_send, e_keep, e_send, *small, token = combine(
            ([r_keep, r_got], 2), ([e_keep, e_got], 2), ([s_keep, s_got], 4), deps=[token]
        )
        r_got, e_got = swap_img(r_send, 2), swap_img(e_send, 1)
        small = small[:1] + [swap_img(v, m) for v, m in zip(small[1:], masks_of(flat_pair)[1:])]
        dfused, token = conv_back(valid, dd, dd_halo, taps, [token])
        r_keep, r_send, e_keep, e_send, *small, token = combine(
            ([r_keep, r_got], 2), ([e_keep, e_got], 2), (small, 4), deps=[token]
        )
        r_got, e_got = swap_img(r_send, 1), swap_img(e_send, 2)
        small = small[:1] + [swap_img(v, m) for v, m in zip(small[1:], masks_of(deep)[1:])]
        i_keep, i_send, token = in_grad(y1t, flat(dfused), plain, [token])
        i_got = swap_row(i_send)
        *parts, token = merge(r_keep, r_got, e_keep, e_got, [token])
        parts = parts[:1] + [swap_img(v, m) for v, m in zip(parts[1:], masks_of(deep)[1:])]
        fgrad, late, token = last_call(
            valid, dfused, xp, dx2, w_in, wide, in_order, dealt, [token] + small[1:]
        )
        dealt_rows, token = deal(i_keep, i_got, late, swap_row(late), small, [token] + parts[1:])
        mixed = spread(dealt_rows)
        red_sum, out_sum, exp_sum, token = finish(parts, [token])
        own, oth = mixed, swap_row(mixed)
    else:

        def total(parts, rows):
            value = jnp.concatenate(parts, axis=0)
            return plain_scatter(value.reshape(32, -1, value.shape[1])[:, rows].reshape(-1, value.shape[1]))

        everything = slice(None)
        dk, token = kernel_grad(dd, band)
        s_keep, s_send, token = gate_grads(u, flat(dv), s512, s2048, s1024, dk.reshape(512, 128), plain)
        parts = feed_grads(y2, flat(dh), act, flat(df), u, flat(dz), e_order, r_order)
        e_parts, r_parts = parts[:2], parts[2:4]
        dfused, _ = conv_back(valid, dd, dd_halo, taps)
        i_parts = in_grad(y1t, flat(dfused), plain)[:2]
        fgrad, late, token = last_call(valid, dfused, xp, dx2, w_in, wide, in_order, dealt)
        sums = late_sums(*sum_img(late + swap_row(late), list(range(bits))))
        exp_sum, in_sum = total(e_parts, everything), total(i_parts, everything)
        red_sum, out_sum = total(r_parts, slice(0, 64)), total(r_parts, slice(64, 80))
        small = plain_gather(total((s_keep, s_send), everything).astype(bf16)).reshape(16, 2, 16, 512)
        lower_row = lax.axis_index("row")
        own, oth = (
            jnp.pad(lax.dynamic_index_in_dim(small, v, 1, keepdims=False).reshape(256, 512), ((0, 0), (1024, 128)))
            for v in (lower_row, 1 - lower_row)
        )

    unpacked = unpack(own, oth)
    if dealt:
        in_sum, sums = unpacked[0], unpacked[15:18]
    dk_sum, dwb_sum, gate1, gate2, gate3, gate4, gb_sum, outb, mix, gain, shift, expb, redb, ffn = unpacked[1:15]
    return (
        produced.reshape(features.shape),
        fgrad.reshape(features.shape),
        sums[0],
        sums[1],
        in_sum,
        sums[2],
        dk_sum,
        dwb_sum,
        gate1,
        gate2,
        gate3,
        gate4,
        gb_sum,
        out_sum,
        outb,
        mix,
        gain,
        shift,
        exp_sum,
        expb,
        red_sum,
        redb,
        ffn,
    )


def solution(mesh):
    band = P("img", "row", None, None)
    rows = P(("img", "row"), None)
    copy = P()
    ins = [band, P("img", "row", None), band] + [copy] * 21
    for k in (5, 14, 19, 21):
        ins[k] = rows
    outs = [band, band] + [copy] * 21
    for k in (4, 13, 18, 20):
        outs[k] = rows
    return jax.shard_map(per_device, mesh=mesh, in_specs=tuple(ins), out_specs=tuple(outs), check_vma=False)
```
